32 devices in a mesh: dp: 8 (over z, x), tp: 4 (over y, core).
Axes of the slice: x: 2, y: 2, z: 4, core: 2. Of those that a mesh axis runs over, the one named last changes fastest.
Arguments:
- layer_input: bfloat16 [8192, 2048], P(('dp', 'tp'))
- out_grad: bfloat16 [8192, 2048], P(('dp', 'tp'))
- segment_ids: int32 [8192], P('dp'), may hold values from 0 to 2, as said below
- positions: int32 [8192], P('dp'), may hold values from 0 to 1999, as said below
- w_query: float32 [2048, 2048], P('dp', 'tp'), may hold values from -0.125 to 0.125
- w_key: float32 [2048, 512], P('dp', 'tp'), may hold values from -0.125 to 0.125
- w_value: float32 [2048, 512], P('dp', 'tp'), may hold values from -0.125 to 0.125
- w_out: float32 [2048, 2048], P('tp', 'dp'), may hold values from -0.5 to 0.5
- w_gate: float32 [2048, 8192], P('dp', 'tp'), may hold values from -0.125 to 0.125
- w_up: float32 [2048, 8192], P('dp', 'tp'), may hold values from -0.125 to 0.125
- w_down: float32 [8192, 2048], P('tp', 'dp'), may hold values from -0.0625 to 0.0625
- m_query: float32 [2048, 2048], P('dp', 'tp'), may hold values from -56 to 56
- m_key: float32 [2048, 512], P('dp', 'tp'), may hold values from -112 to 112
- m_value: float32 [2048, 512], P('dp', 'tp'), may hold values from -256 to 256
- m_out: float32 [2048, 2048], P('tp', 'dp'), may hold values from -14 to 14
- m_gate: float32 [2048, 8192], P('dp', 'tp'), may hold values from -14 to 14
- m_up: float32 [2048, 8192], P('dp', 'tp'), may hold values from -16 to 16
- m_down: float32 [8192, 2048], P('tp', 'dp'), may hold values from -32 to 32
- v_query: float32 [2048, 2048], P('dp', 'tp'), may hold values from 245.76 to 3276.8
- v_key: float32 [2048, 512], P('dp', 'tp'), may hold values from 983.04 to 13107.2
- v_value: float32 [2048, 512], P('dp', 'tp'), may hold values from 6144 to 81920
- v_out: float32 [2048, 2048], P('tp', 'dp'), may hold values from 16.384 to 204.8
- v_gate: float32 [2048, 8192], P('dp', 'tp'), may hold values from 16.384 to 204.8
- v_up: float32 [2048, 8192], P('dp', 'tp'), may hold values from 24.576 to 294.912
- v_down: float32 [8192, 2048], P('tp', 'dp'), may hold values from 90.112 to 1228.8
- gain_attn: float32 [2048], replicated, may hold values from 0.5 to 1.5
- gain_ffn: float32 [2048], replicated, may hold values from 0.5 to 1.5
- m_gain_attn: float32 [2048], replicated, may hold values from -56 to 56
- m_gain_ffn: float32 [2048], replicated, may hold values from -56 to 56
- v_gain_attn: float32 [2048], replicated, may hold values from 409.6 to 6553.6
- v_gain_ffn: float32 [2048], replicated, may hold values from 245.76 to 3276.8
Outputs:
- out_value: bfloat16 [8192, 2048], P(('dp', 'tp'))
- in_grad: float32 [8192, 2048], P(('dp', 'tp'))
- grad_query: float32 [2048, 2048], P('dp', 'tp')
- grad_key: float32 [2048, 512], P('dp', 'tp')
- grad_value: float32 [2048, 512], P('dp', 'tp')
- grad_out: float32 [2048, 2048], P('tp', 'dp')
- grad_gate: float32 [2048, 8192], P('dp', 'tp')
- grad_up: float32 [2048, 8192], P('dp', 'tp')
- grad_down: float32 [8192, 2048], P('tp', 'dp')
- next_query: float32 [2048, 2048], P('dp', 'tp')
- next_key: float32 [2048, 512], P('dp', 'tp')
- next_value: float32 [2048, 512], P('dp', 'tp')
- next_out: float32 [2048, 2048], P('tp', 'dp')
- next_gate: float32 [2048, 8192], P('dp', 'tp')
- next_up: float32 [2048, 8192], P('dp', 'tp')
- next_down: float32 [8192, 2048], P('tp', 'dp')
- next_m_query: float32 [2048, 2048], P('dp', 'tp')
- next_m_key: float32 [2048, 512], P('dp', 'tp')
- next_m_value: float32 [2048, 512], P('dp', 'tp')
- next_m_out: float32 [2048, 2048], P('tp', 'dp')
- next_m_gate: float32 [2048, 8192], P('dp', 'tp')
- next_m_up: float32 [2048, 8192], P('dp', 'tp')
- next_m_down: float32 [8192, 2048], P('tp', 'dp')
- next_v_query: float32 [2048, 2048], P('dp', 'tp')
- next_v_key: float32 [2048, 512], P('dp', 'tp')
- next_v_value: float32 [2048, 512], P('dp', 'tp')
- next_v_out: float32 [2048, 2048], P('tp', 'dp')
- next_v_gate: float32 [2048, 8192], P('dp', 'tp')
- next_v_up: float32 [2048, 8192], P('dp', 'tp')
- next_v_down: float32 [8192, 2048], P('tp', 'dp')
- grad_gain_attn: float32 [2048], replicated
- grad_gain_ffn: float32 [2048], replicated
- next_gain_attn: float32 [2048], replicated
- next_gain_ffn: float32 [2048], replicated
- next_m_gain_attn: float32 [2048], replicated
- next_m_gain_ffn: float32 [2048], replicated
- next_v_gain_attn: float32 [2048], replicated
- next_v_gain_ffn: float32 [2048], replicated
The draws below stay inside these ranges and needn't reach their ends.
Inputs may be any that keep to these rules, and one draw needn't show every extreme that they name: `segment_ids`: within each sequence of 512 consecutive tokens the ids start at 0 and rise by one at each document boundary; ids of different sequences are unrelated. Within a segment positions rise by one from token to token; every segment except the first of a sequence starts at 0.
All inputs are finite; a program needn't handle non-finite values.
Results may differ from the reference program's by a relative error of at most 0.019.
Values may be sent and summed in bfloat16 or wider, within the bound.
No kernel may reach another device: no remote copies, remote signals or barrier semaphores. Data moves between devices by JAX's collectives and lax.ppermute only.
A program may use at most 256 MiB of HBM per device.

```python
import math
import jax
import jax.numpy as jnp
from jax import lax

D = 2048
H = 32
KV = 8
HD = 64
FF = 8192
LEN = 512
MIN_DOC = 200
MAX_DOC = 2000
STEP = 5
TOKENS = 8192


def draw_layer_input(key, part):
    row_logs = jax.random.uniform(jax.random.fold_in(key, 11), (TOKENS, 1), jnp.float32, math.log(0.3), math.log(3.0))
    col_logs = jax.random.uniform(jax.random.fold_in(key, 12), (1, D), jnp.float32, math.log(0.3), math.log(3.0))
    base = jax.random.normal(jax.random.fold_in(key, 13), (TOKENS, D), jnp.float32)
    values = base * jnp.exp(row_logs) * jnp.exp(col_logs)
    return values.astype(jnp.bfloat16)


def draw_out_grad(key, part):
    ramp = jnp.arange(TOKENS, dtype=jnp.float32)[:, None] / TOKENS
    base = jax.random.normal(jax.random.fold_in(key, 21), (TOKENS, D), jnp.float32)
    values = base * jnp.exp(math.log(3.0) * ramp) * 0.6
    return values.astype(jnp.bfloat16)


def packing(key):
    count = TOKENS // LEN
    first = jax.random.randint(jax.random.fold_in(key, 901), (count,), 1, LEN - MIN_DOC + 1)
    first = first.at[0].set(jax.random.randint(jax.random.fold_in(key, 902), (), 1, MIN_DOC // 2))
    upper_bound = jnp.maximum(MIN_DOC + 1, LEN - first + 1)
    second = jax.random.randint(jax.random.fold_in(key, 903), (count,), MIN_DOC, upper_bound)
    second = jnp.minimum(second, LEN - first)
    second = second.at[0].set(jax.random.randint(jax.random.fold_in(key, 904), (), MIN_DOC, MIN_DOC * 3 // 2))
    offset = jax.random.randint(jax.random.fold_in(key, 905), (count,), 0, MAX_DOC - first + 1)
    offset = offset.at[0].set(MAX_DOC - first[0])
    row_index = jnp.arange(LEN, dtype=jnp.int32)[None, :]
    cut_one = first[:, None]
    cut_two = (first + second)[:, None]
    segments = (row_index >= cut_one).astype(jnp.int32) + (row_index >= cut_two).astype(jnp.int32)
    places = jnp.where(row_index < cut_one, offset[:, None] + row_index, jnp.where(row_index < cut_two, row_index - cut_one, row_index - cut_two))
    return (segments.reshape(TOKENS).astype(jnp.int32), places.reshape(TOKENS).astype(jnp.int32))


def draw_segment_ids(key, part):
    return packing(key)[0]


def draw_positions(key, part):
    return packing(key)[1]


def level_of(key, extent, split, least, high):
    def one(position, parts):
        steps = jax.random.uniform(jax.random.fold_in(jax.random.fold_in(key, 6), position), (parts,), jnp.float32, least / len(split), high / len(split))
        return jnp.repeat(jnp.exp(steps), extent[position] // parts).reshape((-1,) + (1,) * (len(extent) - position - 1))

    gain = one(*split[0])
    for cut in split[1:]:
        gain = gain * one(*cut)
    return gain


def centred(rng, dims, spread, bound, cuts=(), held_as=jnp.bfloat16):
    result = jax.random.normal(rng, dims, jnp.float32) * spread
    if len(cuts) > 0:
        result = level_of(rng, dims, cuts, -0.22, 0.18) * result
    return jnp.clip(result, min=-bound, max=bound).astype(held_as)


def setup_inputs(seed: int = 0) -> dict:
    splits = jax.random.split(jax.random.key(seed), 32)
    layer_input = draw_layer_input(jax.random.fold_in(splits[31], 71), 0)
    out_grad = draw_out_grad(jax.random.fold_in(splits[31], 71), 0)
    segment_ids = draw_segment_ids(jax.random.fold_in(splits[31], 71), 0)
    positions = draw_positions(jax.random.fold_in(splits[31], 71), 0)
    w_query = centred(splits[4], (D, H * HD), D ** -0.5, 0.125, ((0, 8), (1, 4)), jnp.float32)
    w_key = centred(splits[5], (D, KV * HD), D ** -0.5, 0.125, ((0, 8), (1, 4)), jnp.float32)
    w_value = centred(splits[6], (D, KV * HD), D ** -0.5, 0.125, ((0, 8), (1, 4)), jnp.float32)
    w_out = centred(splits[7], (H * HD, D), (H * HD // 16) ** -0.5, 0.5, ((0, 4), (1, 8)), jnp.float32)
    w_gate = centred(splits[8], (D, FF), D ** -0.5, 0.125, ((0, 8), (1, 4)), jnp.float32)
    w_up = centred(splits[9], (D, FF), D ** -0.5, 0.125, ((0, 8), (1, 4)), jnp.float32)
    w_down = centred(splits[10], (FF, D), FF ** -0.5, 0.0625, ((0, 4), (1, 8)), jnp.float32)
    m_query = centred(splits[11], (D, H * HD), (0.1 * TOKENS ** 0.5), 56.0, ((0, 8), (1, 4)), jnp.float32)
    m_key = centred(splits[12], (D, KV * HD), (0.2 * TOKENS ** 0.5), 112.0, ((0, 8), (1, 4)), jnp.float32)
    m_value = centred(splits[13], (D, KV * HD), (0.5 * TOKENS ** 0.5), 256.0, ((0, 8), (1, 4)), jnp.float32)
    m_out = centred(splits[14], (H * HD, D), (0.025 * TOKENS ** 0.5), 14.0, ((0, 4), (1, 8)), jnp.float32)
    m_gate = centred(splits[15], (D, FF), (0.025 * TOKENS ** 0.5), 14.0, ((0, 8), (1, 4)), jnp.float32)
    m_up = centred(splits[16], (D, FF), (0.03 * TOKENS ** 0.5), 16.0, ((0, 8), (1, 4)), jnp.float32)
    m_down = centred(splits[17], (FF, D), (0.06 * TOKENS ** 0.5), 32.0, ((0, 4), (1, 8)), jnp.float32)
    v_query = jnp.clip(jnp.exp(math.log(3276.8) - 2.5902672 * jax.random.uniform(splits[18], (D, H * HD), jnp.float32) ** level_of(splits[18], (D, H * HD), ((0, 8), (1, 4)), -0.2, 0.2)), 245.76, 3276.8)
    v_key = jnp.clip(jnp.exp(math.log(13107.2) - 2.5902672 * jax.random.uniform(splits[19], (D, KV * HD), jnp.float32) ** level_of(splits[19], (D, KV * HD), ((0, 8), (1, 4)), -0.2, 0.2)), 983.04, 13107.2)
    v_value = jnp.clip(jnp.exp(math.log(81920.0) - 2.5902672 * jax.random.uniform(splits[20], (D, KV * HD), jnp.float32) ** level_of(splits[20], (D, KV * HD), ((0, 8), (1, 4)), -0.2, 0.2)), 6144.0, 81920.0)
    v_out = jnp.clip(jnp.exp(math.log(204.8) - 2.5257286 * jax.random.uniform(splits[21], (H * HD, D), jnp.float32) ** level_of(splits[21], (H * HD, D), ((0, 4), (1, 8)), -0.2, 0.2)), 16.384, 204.8)
    v_gate = jnp.clip(jnp.exp(math.log(204.8) - 2.5257286 * jax.random.uniform(splits[22], (D, FF), jnp.float32) ** level_of(splits[22], (D, FF), ((0, 8), (1, 4)), -0.2, 0.2)), 16.384, 204.8)
    v_up = jnp.clip(jnp.exp(math.log(294.912) - 2.4849066 * jax.random.uniform(splits[23], (D, FF), jnp.float32) ** level_of(splits[23], (D, FF), ((0, 8), (1, 4)), -0.2, 0.2)), 24.576, 294.912)
    v_down = jnp.clip(jnp.exp(math.log(1228.8) - 2.61274 * jax.random.uniform(splits[24], (FF, D), jnp.float32) ** level_of(splits[24], (FF, D), ((0, 4), (1, 8)), -0.2, 0.2)), 90.112, 1228.8)
    gain_attn = jnp.clip(1.0 + 0.1 * jax.random.normal(splits[25], (D,), jnp.float32), 0.5, 1.5)
    gain_ffn = jnp.clip(1.0 + 0.1 * jax.random.normal(splits[26], (D,), jnp.float32), 0.5, 1.5)
    m_gain_attn = centred(splits[27], (D,), (0.1 * TOKENS ** 0.5), 56.0, (), jnp.float32)
    m_gain_ffn = centred(splits[28], (D,), (0.1 * TOKENS ** 0.5), 56.0, (), jnp.float32)
    v_gain_attn = jnp.clip(jnp.exp(jax.random.uniform(splits[29], (D,), jnp.float32, math.log(409.6), math.log(6553.6))), 409.6, 6553.6)
    v_gain_ffn = jnp.clip(jnp.exp(jax.random.uniform(splits[30], (D,), jnp.float32, math.log(245.76), math.log(3276.8))), 245.76, 3276.8)
    return {"layer_input": layer_input, "out_grad": out_grad, "segment_ids": segment_ids, "positions": positions, "w_query": w_query, "w_key": w_key, "w_value": w_value, "w_out": w_out, "w_gate": w_gate, "w_up": w_up, "w_down": w_down, "m_query": m_query, "m_key": m_key, "m_value": m_value, "m_out": m_out, "m_gate": m_gate, "m_up": m_up, "m_down": m_down, "v_query": v_query, "v_key": v_key, "v_value": v_value, "v_out": v_out, "v_gate": v_gate, "v_up": v_up, "v_down": v_down, "gain_attn": gain_attn, "gain_ffn": gain_ffn, "m_gain_attn": m_gain_attn, "m_gain_ffn": m_gain_ffn, "v_gain_attn": v_gain_attn, "v_gain_ffn": v_gain_ffn}


NORM_EPS = 1e-05
ROPE_BASE = 500000.0
BETA_ONE = 0.9
BETA_TWO = 0.95
LEARN_RATE = 0.02
GAIN_RATE = 0.5
WEIGHT_DECAY = 0.1
ADAM_EPS = 1e-08

@jax.custom_vjp
def low(v):
    return lax.optimization_barrier(v.astype(jnp.bfloat16)).astype(jnp.float32)

@jax.custom_vjp
def low_back(v):
    return v

def low_keep(v):
    return (low(v), None)

def low_pass(kept, grad):
    return (grad,)

def back_keep(v):
    return (v, None)

def back_low(kept, grad):
    return (low(grad),)
low.defvjp(low_keep, low_pass)
low_back.defvjp(back_keep, back_low)

def rope_tables(positions):
    half_dim = HD // 2
    inverse_freq = ROPE_BASE ** (-2.0 * jnp.arange(half_dim, dtype=jnp.float32) / HD)
    angles = positions.astype(jnp.float32)[:, None] * inverse_freq[None, :]
    cos_half = jnp.cos(angles)
    sin_half = jnp.sin(angles)
    return (jnp.concatenate([cos_half, cos_half], 1), jnp.concatenate([sin_half, sin_half], 1))

def rotate_heads(values, cos_table, sin_table):
    half_dim = values.shape[-1] // 2
    turned = jnp.concatenate([-values[..., half_dim:], values[..., :half_dim]], -1)
    return values * cos_table[:, None, :] + turned * sin_table[:, None, :]

def norm_rows(values, gain_vec):
    row_scale = lax.rsqrt(lax.optimization_barrier(jnp.mean(values * values, axis=1, keepdims=True)) + NORM_EPS)
    return values * row_scale * gain_vec

def sequence_attention(entries):
    queries, key_rows, value_rows, seg_row = entries
    scores = jnp.einsum('qkgd,pkd->kgqp', queries, key_rows, precision=lax.Precision.HIGHEST) * HD ** (-0.5)
    scores = low_back(scores)
    row_index = jnp.arange(LEN)
    allowed = (seg_row[:, None] == seg_row[None, :]) & (row_index[None, :] <= row_index[:, None])
    masked = jnp.where(allowed, scores, -1e+30)
    top_score = lax.optimization_barrier(jnp.max(masked, axis=-1, keepdims=True))
    weights = jnp.exp(masked - top_score)
    prob_rows = low(weights / lax.optimization_barrier(jnp.sum(weights, axis=-1, keepdims=True)))
    return jnp.einsum('kgqp,pkd->qkgd', prob_rows, value_rows, precision=lax.Precision.HIGHEST)

def layer_forward(inputs_x, weights_x, gains_x, seg_block, cos_table, sin_table):
    query_w, key_w, value_w, out_w, gate_w, up_w, down_w = weights_x
    row_total = inputs_x.shape[0]
    seq_count = row_total // LEN
    normed = low(norm_rows(inputs_x, gains_x[0]))
    queries = low_back(jnp.dot(normed, query_w, precision=lax.Precision.HIGHEST))
    queries = low(rotate_heads(queries.reshape(row_total, H, HD), cos_table, sin_table))
    key_rows = low_back(jnp.dot(normed, key_w, precision=lax.Precision.HIGHEST))
    key_rows = low(rotate_heads(key_rows.reshape(row_total, KV, HD), cos_table, sin_table))
    value_rows = low(low_back(jnp.dot(normed, value_w, precision=lax.Precision.HIGHEST)))
    context = lax.map(jax.checkpoint(sequence_attention), (queries.reshape(seq_count, LEN, KV, H // KV, HD), key_rows.reshape(seq_count, LEN, KV, HD), value_rows.reshape(seq_count, LEN, KV, HD), seg_block.reshape(seq_count, LEN)))
    context = low(low_back(context.reshape(row_total, H * HD)))
    residual = inputs_x + low_back(jnp.dot(context, out_w, precision=lax.Precision.HIGHEST))
    normed_two = low(norm_rows(residual, gains_x[1]))
    gate_pre = low_back(jnp.dot(normed_two, gate_w, precision=lax.Precision.HIGHEST))
    lifted = low_back(jnp.dot(normed_two, up_w, precision=lax.Precision.HIGHEST))
    act = low(gate_pre * jax.nn.sigmoid(gate_pre) * lifted)
    return residual + low_back(jnp.dot(act, down_w, precision=lax.Precision.HIGHEST))

def adamw_update(master, grad_sum, first_mom, second_mom, decay_rate, step_rate):
    next_first = BETA_ONE * first_mom + (1.0 - BETA_ONE) * grad_sum
    next_second = BETA_TWO * second_mom + (1.0 - BETA_TWO) * grad_sum * grad_sum
    first_hat = next_first / (1.0 - BETA_ONE ** STEP)
    second_hat = next_second / (1.0 - BETA_TWO ** STEP)
    next_master = master - step_rate * (first_hat / (jnp.sqrt(second_hat) + ADAM_EPS) + decay_rate * master)
    return (next_master, next_first, next_second)

def reference(layer_input, out_grad, segment_ids, positions, w_query, w_key, w_value, w_out, w_gate, w_up, w_down, m_query, m_key, m_value, m_out, m_gate, m_up, m_down, v_query, v_key, v_value, v_out, v_gate, v_up, v_down, gain_attn, gain_ffn, m_gain_attn, m_gain_ffn, v_gain_attn, v_gain_ffn):
    masters = (w_query, w_key, w_value, w_out, w_gate, w_up, w_down)
    weights = tuple((lax.optimization_barrier(master.astype(jnp.bfloat16)).astype(jnp.float32) for master in masters))
    gains = (gain_attn, gain_ffn)
    seq_total = TOKENS // LEN
    per_block = max((divisor for divisor in range(1, 9) if seq_total % divisor == 0))
    block_rows = per_block * LEN
    blocks = TOKENS // block_rows
    cos_all, sin_all = rope_tables(positions)
    inputs_f = layer_input.astype(jnp.float32).reshape(blocks, block_rows, D)
    grads_f = out_grad.astype(jnp.float32).reshape(blocks, block_rows, D)

    def block_step(running, entries):
        inputs_b, grad_b, seg_b, cos_b, sin_b = entries

        def forward_fn(inputs_x, weights_x, gains_x):
            return layer_forward(inputs_x, weights_x, gains_x, seg_b, cos_b, sin_b)
        output, pull_back = jax.vjp(forward_fn, inputs_b, weights, gains)
        input_part, weight_part, gain_part = pull_back(grad_b)
        running = jax.tree.map(lambda summed, addend: summed + addend, running, (weight_part, gain_part))
        return (running, (output.astype(jnp.bfloat16), input_part))
    zero_grads = jax.tree.map(jnp.zeros_like, (weights, gains))
    (weight_grads, gain_grads), (out_blocks, in_blocks) = lax.scan(block_step, zero_grads, (inputs_f, grads_f, segment_ids.reshape(blocks, block_rows), cos_all.reshape(blocks, block_rows, HD), sin_all.reshape(blocks, block_rows, HD)))
    out_value = out_blocks.reshape(TOKENS, D)
    in_grad = in_blocks.reshape(TOKENS, D)
    grad_query, grad_key, grad_value, grad_out, grad_gate, grad_up, grad_down = weight_grads
    grad_gain_attn, grad_gain_ffn = gain_grads
    next_query, next_m_query, next_v_query = adamw_update(w_query, grad_query, m_query, v_query, WEIGHT_DECAY, LEARN_RATE)
    next_key, next_m_key, next_v_key = adamw_update(w_key, grad_key, m_key, v_key, WEIGHT_DECAY, LEARN_RATE)
    next_value, next_m_value, next_v_value = adamw_update(w_value, grad_value, m_value, v_value, WEIGHT_DECAY, LEARN_RATE)
    next_out, next_m_out, next_v_out = adamw_update(w_out, grad_out, m_out, v_out, WEIGHT_DECAY, LEARN_RATE)
    next_gate, next_m_gate, next_v_gate = adamw_update(w_gate, grad_gate, m_gate, v_gate, WEIGHT_DECAY, LEARN_RATE)
    next_up, next_m_up, next_v_up = adamw_update(w_up, grad_up, m_up, v_up, WEIGHT_DECAY, LEARN_RATE)
    next_down, next_m_down, next_v_down = adamw_update(w_down, grad_down, m_down, v_down, WEIGHT_DECAY, LEARN_RATE)
    next_gain_attn, next_m_gain_attn, next_v_gain_attn = adamw_update(gain_attn, grad_gain_attn, m_gain_attn, v_gain_attn, 0.0, GAIN_RATE)
    next_gain_ffn, next_m_gain_ffn, next_v_gain_ffn = adamw_update(gain_ffn, grad_gain_ffn, m_gain_ffn, v_gain_ffn, 0.0, GAIN_RATE)
    return (out_value, in_grad, grad_query, grad_key, grad_value, grad_out, grad_gate, grad_up, grad_down, next_query, next_key, next_value, next_out, next_gate, next_up, next_down, next_m_query, next_m_key, next_m_value, next_m_out, next_m_gate, next_m_up, next_m_down, next_v_query, next_v_key, next_v_value, next_v_out, next_v_gate, next_v_up, next_v_down, grad_gain_attn, grad_gain_ffn, next_gain_attn, next_gain_ffn, next_m_gain_attn, next_m_gain_ffn, next_v_gain_attn, next_v_gain_ffn)
```

```python
import functools

import jax
import jax.numpy as jnp
from jax import lax
from jax.experimental import pallas as pl
from jax.experimental.pallas import tpu as pltpu
from jax.sharding import Mesh
from jax.sharding import PartitionSpec as P

HD = 64
LEN = 512
STEP = 5
CHUNKS = 2

NORM_EPS = 1e-05
ROPE_BASE = 500000.0
BETA_ONE = 0.9
BETA_TWO = 0.95
LEARN_RATE = 0.02
GAIN_RATE = 0.5
WEIGHT_DECAY = 0.1
ADAM_EPS = 1e-08

LOW = jnp.bfloat16
F32 = jnp.float32
MIB = 1024 * 1024

NEAR = [(0, 1), (1, 0), (2, 3), (3, 2)]
MIDDLE = [(1, 2), (2, 1)]
OUTWARD = [(1, 0), (2, 3)]
INWARD = [(0, 1), (3, 2)]
PAIR = [(0, 1), (1, 0)]


def dot(lhs, rhs, lhs_dim, rhs_dim):
    return lax.dot_general(
        lhs, rhs, (((lhs_dim,), (rhs_dim,)), ((), ())), preferred_element_type=F32
    )


def cat(parts, axis):
    return jnp.concatenate(parts, axis)


def line_gather(own):
    near = lax.ppermute(own, "do", NEAR)
    across = lax.ppermute(own, "do", MIDDLE)
    across_near = lax.ppermute(near, "do", MIDDLE)
    out = lax.ppermute(across, "do", OUTWARD)
    out_near = lax.ppermute(across_near, "do", OUTWARD)
    place = lax.axis_index("do")
    inner = (place == 1) | (place == 2)
    return [
        own,
        near,
        jnp.where(inner, across_near, out),
        jnp.where(inner, across, out_near),
    ]


def line_reduce(parts):
    def add(part, *arrived):
        total = part.astype(F32)
        for piece in arrived:
            total = total + piece.astype(F32)
        return total

    far = lax.ppermute(parts[3], "do", INWARD)
    second = add(parts[2], far).astype(LOW)
    crossed = lax.ppermute(second, "do", MIDDLE)
    inward = lax.ppermute(second, "do", INWARD)
    third = add(parts[3], inward).astype(LOW)
    first = add(parts[1], crossed).astype(LOW)
    from_near = lax.ppermute(first, "do", NEAR)
    from_across = lax.ppermute(third, "do", MIDDLE)
    return add(parts[0], from_near, from_across)


class Plan:
    def __init__(self, outer, width, per_device):
        self.outer = outer
        self.width = width
        self.rows = per_device
        self.block = 2 * per_device
        self.line = outer == 4 and per_device % 128 == 0

    def reorder(self, values):
        if not self.line:
            return values
        place = lax.axis_index("do")
        quarter = values.shape[-1] // 4
        a, b, c, d = (values[..., i * quarter : (i + 1) * quarter] for i in range(4))
        values = jnp.where(place % 2 == 1, cat([b, a, d, c], -1), values)
        half = 2 * quarter
        turned = cat([values[..., half:], values[..., :half]], -1)
        return jnp.where(place >= 2, turned, values)

    def by_x(self, low, high):
        return jnp.where(lax.axis_index("di") == 0, low, high)

    def gather(self, row_parts, col_parts):
        if not self.line:
            row_full, col_full = [], []
            for own, other in row_parts:
                theirs = lax.ppermute(other, "di", PAIR)
                block = cat([self.by_x(own, theirs), self.by_x(theirs, own)], 0)
                row_full.append(lax.all_gather(block, "do", axis=0, tiled=True))
            for own, other in col_parts:
                theirs = lax.ppermute(other, "di", PAIR)
                block = cat([self.by_x(own, theirs), self.by_x(theirs, own)], 1)
                col_full.append(lax.all_gather(block, "do", axis=1, tiled=True))
            return row_full, col_full
        rows = self.rows

        def pack(which):
            pieces = [part[which] for part in row_parts]
            for part in col_parts:
                both = part[which]
                pieces += [both[i : i + rows] for i in range(0, both.shape[0], rows)]
            return cat(pieces, 1)

        mine, other = pack(0), pack(1)
        theirs = lax.ppermute(other, "di", PAIR)
        block = cat([self.by_x(mine, theirs), self.by_x(theirs, mine)], 0)
        slots = line_gather(block)
        row_full, col_full, start = [], [], 0
        for own, _ in row_parts:
            stop = start + own.shape[1]
            row_full.append(cat([slot[:, start:stop] for slot in slots], 0))
            start = stop
        for own, _ in col_parts:
            bands = []
            for _ in range(0, own.shape[0], rows):
                bands.append(
                    cat(
                        [
                            slot[x * rows : (x + 1) * rows, start : start + rows]
                            for slot in slots
                            for x in range(2)
                        ],
                        1,
                    )
                )
                start += rows
            col_full.append(cat(bands, 0))
        return row_full, col_full

    def reduce(self, row_grads, col_grads):
        rows = self.rows
        if not self.line:
            row_out, col_out = [], []
            for grad in row_grads:
                total = lax.psum_scatter(grad, "do", scatter_dimension=0, tiled=True)
                row_out.append(self.trade(total[:rows], total[rows:]))
            for grad in col_grads:
                total = lax.psum_scatter(grad, "do", scatter_dimension=1, tiled=True)
                col_out.append(self.trade(total[:, :rows], total[:, rows:]))
            return row_out, col_out
        block = self.block
        parts = []
        for k in range(4):
            pieces = [grad[k * block : (k + 1) * block] for grad in row_grads]
            for grad in col_grads:
                for i in range(0, grad.shape[0], rows):
                    at = k * block
                    pieces.append(
                        cat(
                            [
                                grad[i : i + rows, at : at + rows],
                                grad[i : i + rows, at + rows : at + block],
                            ],
                            0,
                        )
                    )
            parts.append(cat(pieces, 1))
        total = line_reduce(parts)
        mine, theirs = self.trade(total[:rows], total[rows:])
        row_out, col_out, start = [], [], 0
        for grad in row_grads:
            stop = start + grad.shape[1]
            row_out.append((mine[:, start:stop], theirs[:, start:stop]))
            start = stop
        for grad in col_grads:
            own, other = [], []
            for _ in range(0, grad.shape[0], rows):
                own.append(mine[:, start : start + rows])
                other.append(theirs[:, start : start + rows])
                start += rows
            col_out.append((cat(own, 0), cat(other, 0)))
        return row_out, col_out

    def trade(self, low, high):
        mine = self.by_x(low, high).astype(F32)
        theirs = lax.ppermute(self.by_x(high, low).astype(LOW), "di", PAIR)
        return mine, theirs.astype(F32)


def rope_tables(positions):
    half_dim = HD // 2
    inverse_freq = ROPE_BASE ** (-2.0 * jnp.arange(half_dim, dtype=F32) / HD)
    angles = positions.astype(F32)[:, None] * inverse_freq[None, :]
    cosine, sine = jnp.cos(angles), jnp.sin(angles)
    return cat([cosine] * 4, 1), cat([-sine, sine] * 2, 1)


def lanes_of(shape):
    return lax.broadcasted_iota(jnp.int32, shape, 1)


def shuffle_halves(values):
    wide = values.shape[1]
    up = pltpu.roll(values, wide - HD // 2, 1)
    down = pltpu.roll(values, HD // 2, 1)
    return jnp.where(lanes_of(values.shape) % HD < HD // 2, up, down)


def tables(cos_ref, sin_ref, pairs):
    cosine, sine = cos_ref[...], sin_ref[...]
    is_key = lanes_of(cosine.shape) < HD
    return (
        cat([cosine] * pairs + [jnp.where(is_key, cosine, 1.0)], 1),
        cat([sine] * pairs + [jnp.where(is_key, sine, 0.0)], 1),
    )


def split_kv(both):
    is_key = lanes_of(both.shape) < HD
    blank = jnp.zeros_like(both)
    key_low = jnp.where(is_key, both, blank)
    value_high = jnp.where(is_key, blank, both)
    return (
        (key_low, pltpu.roll(key_low.astype(F32), HD, 1).astype(LOW)),
        (pltpu.roll(value_high.astype(F32), HD, 1).astype(LOW), value_high),
    )


def allowed_pairs(seg_col, seg_row):
    shape = (seg_col.shape[0], seg_row.shape[1])
    key_at = lax.broadcasted_iota(jnp.int32, shape, 1)
    query_at = lax.broadcasted_iota(jnp.int32, shape, 0)
    return (seg_col == seg_row) & (key_at <= query_at)


def attn_forward_kernel(
    pairs, x_ref, wqkv_ref, wout_ref, cos_ref, sin_ref, col_ref, row_ref,
    part_ref, ctx_ref, q_ref, kv_ref, lse_ref,
):
    cosine, sine = tables(cos_ref, sin_ref, pairs)
    qkv = dot(x_ref[...], wqkv_ref[...], 1, 0)
    rotated = (qkv * cosine + shuffle_halves(qkv) * sine).astype(LOW)
    queries, both = rotated[:, : pairs * 128], rotated[:, pairs * 128 :]
    q_ref[...] = queries
    kv_ref[...] = both
    keys, values = split_kv(both)
    allowed = allowed_pairs(col_ref[...], row_ref[0])
    lane = lanes_of((both.shape[0], 128))
    log_sums = jnp.zeros((both.shape[0], 128), F32)
    contexts = []
    for pair in range(pairs):
        heads = queries[:, pair * 128 : (pair + 1) * 128]
        context = None
        for side in range(2):
            scores = dot(heads, keys[side], 1, 1) * HD**-0.5
            masked = jnp.where(allowed, scores, -1e30)
            top = jnp.max(masked, axis=1, keepdims=True)
            weights = jnp.exp(masked - top)
            totals = jnp.sum(weights, axis=1, keepdims=True)
            probs = (weights * (1.0 / totals)).astype(LOW)
            piece = dot(probs, values[side], 1, 0)
            context = piece if context is None else context + piece
            log_sums = jnp.where(lane == 2 * pair + side, top + jnp.log(totals), log_sums)
        contexts.append(context.astype(LOW))
    lse_ref[...] = log_sums
    context_low = cat(contexts, 1)
    ctx_ref[...] = context_low
    part_ref[...] = dot(context_low, wout_ref[...], 1, 0).astype(LOW)


def attn_backward_kernel(
    pairs, res_ref, x_ref, ctx_ref, q_ref, kv_ref, lse_ref, wqkv_ref, wout_ref, cos_ref, sin_ref,
    col_ref, row_ref,
    part_ref, gqkv_ref, gout_ref, gain_ref, acc_qkv, acc_out,
):
    step = pl.program_id(0)

    @pl.when(step == 0)
    def _():
        acc_qkv[...] = jnp.zeros_like(acc_qkv)
        acc_out[...] = jnp.zeros_like(acc_out)

    cosine, sine = tables(cos_ref, sin_ref, pairs)
    scale = HD**-0.5
    res = res_ref[...]
    acc_out[...] += dot(ctx_ref[...], res, 0, 0)
    ctx_grad = dot(res, wout_ref[...], 1, 1).astype(LOW)
    keys, values = split_kv(kv_ref[...])
    allowed = allowed_pairs(col_ref[...], row_ref[0])
    lane = lanes_of((res.shape[0], 128))
    log_sums = lse_ref[...]
    query_grads, key_grad, value_grad = [], None, None
    for pair in range(pairs):
        heads = q_ref[:, pair * 128 : (pair + 1) * 128]
        grads = ctx_grad[:, pair * 128 : (pair + 1) * 128]
        query_grad = None
        for side in range(2):
            here = (lane < HD) if side == 0 else (lane >= HD)
            head = jnp.where(here, heads, jnp.zeros_like(heads))
            grad = jnp.where(here, grads, jnp.zeros_like(grads))
            at = 2 * pair + side
            scores = dot(heads, keys[side], 1, 1) * scale
            probs = jnp.where(allowed, jnp.exp(scores - log_sums[:, at : at + 1]), 0.0)
            prob_grad = dot(grads, values[side], 1, 1)
            delta = jnp.sum(probs * prob_grad, axis=1, keepdims=True)
            score_grad = (probs * (prob_grad - delta)).astype(LOW)
            to_value = dot(probs.astype(LOW), grad, 0, 0)
            to_key = dot(score_grad, head, 0, 0)
            to_query = dot(score_grad, keys[side], 1, 0)
            value_grad = to_value if value_grad is None else value_grad + to_value
            key_grad = to_key if key_grad is None else key_grad + to_key
            query_grad = to_query if query_grad is None else query_grad + to_query
        query_grads.append(query_grad * scale)
    key_grad = (key_grad + pltpu.roll(key_grad, HD, 1)) * scale
    value_grad = value_grad + pltpu.roll(value_grad, HD, 1)
    joined = cat(query_grads + [jnp.where(lane < HD, key_grad, value_grad)], 1)
    low = (joined * cosine - shuffle_halves(joined) * sine).astype(LOW)
    part_ref[...] = dot(low, wqkv_ref[...], 1, 1).astype(LOW)
    acc_qkv[...] += dot(x_ref[...], low, 0, 0)

    @pl.when(step == pl.num_programs(0) - 1)
    def _():
        total = acc_qkv[...]
        gqkv_ref[...] = total.astype(LOW)
        gout_ref[...] = acc_out[...].astype(LOW)
        gain_ref[...] = jnp.sum(total * wqkv_ref[...].astype(F32), axis=1, keepdims=True)


def once(shape):
    return pl.BlockSpec(shape, lambda i: (0,) * len(shape), pipeline_mode=pl.Buffered(1))


def per_seq(shape):
    return pl.BlockSpec(shape, lambda i: (i,) + (0,) * (len(shape) - 1))


def attn_forward(normed, wqkv, wout, cosine, sine, seg_col, seg_row):
    rows, width = normed.shape
    heads = wout.shape[0]
    pairs = heads // 128
    seqs = rows // LEN
    return pl.pallas_call(
        functools.partial(attn_forward_kernel, pairs),
        grid=(seqs,),
        in_specs=[
            per_seq((LEN, width)),
            once(wqkv.shape),
            once(wout.shape),
            per_seq((LEN, 128)),
            per_seq((LEN, 128)),
            per_seq((LEN, 1)),
            per_seq((1, 1, LEN)),
        ],
        out_specs=[
            per_seq((LEN, width)),
            per_seq((LEN, heads)),
            per_seq((LEN, heads)),
            per_seq((LEN, 128)),
            per_seq((LEN, 128)),
        ],
        out_shape=[
            jax.ShapeDtypeStruct((rows, width), LOW),
            jax.ShapeDtypeStruct((rows, heads), LOW),
            jax.ShapeDtypeStruct((rows, heads), LOW),
            jax.ShapeDtypeStruct((rows, 128), LOW),
            jax.ShapeDtypeStruct((rows, 128), F32),
        ],
        compiler_params=pltpu.CompilerParams(vmem_limit_bytes=48 * MIB),
        cost_estimate=pl.CostEstimate(
            flops=20 * rows * width * heads, bytes_accessed=10 * rows * width, transcendentals=0
        ),
        name="attn_forward",
    )(normed, wqkv, wout, cosine, sine, seg_col, seg_row)


def attn_backward(res_all, normed, ctx, queries, both, lse, wqkv, wout, cosine, sine, seg_col, seg_row):
    rows, width = normed.shape
    heads = wout.shape[0]
    pairs = heads // 128
    seqs = rows // LEN
    return pl.pallas_call(
        functools.partial(attn_backward_kernel, pairs),
        grid=(seqs,),
        in_specs=[
            per_seq((LEN, width)),
            per_seq((LEN, width)),
            per_seq((LEN, heads)),
            per_seq((LEN, heads)),
            per_seq((LEN, 128)),
            per_seq((LEN, 128)),
            once(wqkv.shape),
            once(wout.shape),
            per_seq((LEN, 128)),
            per_seq((LEN, 128)),
            per_seq((LEN, 1)),
            per_seq((1, 1, LEN)),
        ],
        out_specs=[
            per_seq((LEN, width)),
            once(wqkv.shape),
            once(wout.shape),
            once((width, 1)),
        ],
        out_shape=[
            jax.ShapeDtypeStruct((rows, width), LOW),
            jax.ShapeDtypeStruct(wqkv.shape, LOW),
            jax.ShapeDtypeStruct(wout.shape, LOW),
            jax.ShapeDtypeStruct((width, 1), F32),
        ],
        scratch_shapes=[pltpu.VMEM(wqkv.shape, F32), pltpu.VMEM(wout.shape, F32)],
        compiler_params=pltpu.CompilerParams(vmem_limit_bytes=52 * MIB),
        cost_estimate=pl.CostEstimate(
            flops=40 * rows * width * heads, bytes_accessed=16 * rows * width, transcendentals=0
        ),
        name="attn_backward",
    )(res_all, normed, ctx, queries, both, lse, wqkv, wout, cosine, sine, seg_col, seg_row)


def norm_rows(values, gain_vec):
    row_scale = lax.rsqrt(jnp.mean(values * values, axis=1, keepdims=True) + NORM_EPS)
    return values * row_scale * gain_vec, row_scale


def norm_back(row_grad, values, row_scale, gain_vec):
    scaled_grad = row_grad * gain_vec
    return row_scale * scaled_grad - values * row_scale**3 * jnp.mean(
        scaled_grad * values, axis=1, keepdims=True
    )


def adamw_update(master, grad_sum, first_mom, second_mom, decay_rate, step_rate):
    next_first = BETA_ONE * first_mom + (1.0 - BETA_ONE) * grad_sum
    next_second = BETA_TWO * second_mom + (1.0 - BETA_TWO) * grad_sum * grad_sum
    first_hat = next_first / (1.0 - BETA_ONE**STEP)
    second_hat = next_second / (1.0 - BETA_TWO**STEP)
    next_master = master - step_rate * (
        first_hat / (jnp.sqrt(second_hat) + ADAM_EPS) + decay_rate * master
    )
    return (next_master, next_first, next_second)


def sum_everywhere(values, sizes):
    for axis, size in sizes:
        step = 1
        while step < size:
            values = values + lax.ppermute(values, axis, [(i, i ^ step) for i in range(size)])
            step *= 2
    return values


def on_device(
    sizes,
    layer_input, out_grad, segment_ids, positions,
    w_query, w_key, w_value, w_out, w_gate, w_up, w_down,
    m_query, m_key, m_value, m_out, m_gate, m_up, m_down,
    v_query, v_key, v_value, v_out, v_gate, v_up, v_down,
    gain_attn, gain_ffn, m_gain_attn, m_gain_ffn, v_gain_attn, v_gain_ffn,
):
    width = layer_input.shape[1]
    plan = Plan(sizes["do"], width, w_query.shape[0])
    by_x = plan.by_x
    plane = ("di", "tp")

    def col_halves(weight):
        half = weight.shape[1] // 2
        low = weight.astype(LOW)
        return by_x(low[:, :half], low[:, half:]), by_x(low[:, half:], low[:, :half])

    def row_halves(weight):
        half = weight.shape[0] // 2
        low = weight.astype(LOW)
        return by_x(low[:half], low[half:]), by_x(low[half:], low[:half])

    def col_cut(pair, chunk):
        size = pair[0].shape[1] // CHUNKS
        return tuple(part[:, chunk * size : (chunk + 1) * size] for part in pair)

    def row_cut(pair, chunk):
        size = pair[0].shape[0] // CHUNKS
        return tuple(part[chunk * size : (chunk + 1) * size] for part in pair)

    halves_q, halves_k, halves_v = col_halves(w_query), col_halves(w_key), col_halves(w_value)
    qkv_parts = tuple(cat([q, k, v], 1) for q, k, v in zip(halves_q, halves_k, halves_v))
    (wqkv,), (wout,) = plan.gather([qkv_parts], [row_halves(w_out)])
    halves_g, halves_u, halves_d = col_halves(w_gate), col_halves(w_up), row_halves(w_down)
    ffn_weights = []
    for chunk in range(CHUNKS):
        (gate_up,), (down,) = plan.gather(
            [
                tuple(
                    cat([g, u], 1)
                    for g, u in zip(col_cut(halves_g, chunk), col_cut(halves_u, chunk))
                )
            ],
            [row_cut(halves_d, chunk)],
        )
        ffn_weights.append((gate_up, down))

    marks = cat([segment_ids[None, :], positions[None, :]], 0)
    marks_other = lax.ppermute(marks, "di", PAIR)
    marks_all = cat([by_x(marks, marks_other), by_x(marks_other, marks)], 1)
    seg_all, pos_all = marks_all[0], marks_all[1]
    rows = seg_all.shape[0]
    seqs = rows // LEN
    seg_col, seg_row = seg_all.reshape(rows, 1), seg_all.reshape(seqs, 1, LEN)
    cosine, sine = rope_tables(pos_all)

    gain_one, gain_two = plan.reorder(gain_attn), plan.reorder(gain_ffn)
    inputs_f = plan.reorder(layer_input).astype(F32)
    grad_low = plan.reorder(out_grad)
    normed, scale_one = norm_rows(inputs_f, gain_one)
    normed_all = lax.all_gather(normed.astype(LOW), plane, axis=0, tiled=True)
    grad_all = lax.all_gather(grad_low, plane, axis=0, tiled=True)

    attn_part, ctx, queries, both, lse = attn_forward(
        normed_all, wqkv, wout, cosine, sine, seg_col, seg_row
    )
    residual = inputs_f + lax.psum_scatter(
        attn_part, plane, scatter_dimension=0, tiled=True
    ).astype(F32)
    normed_two, scale_two = norm_rows(residual, gain_two)
    two_all = lax.all_gather(normed_two.astype(LOW), plane, axis=0, tiled=True)

    out_part, back_part, gain_two_part, ffn_grads = None, None, None, []
    for gate_up, down in ffn_weights:
        hidden = down.shape[0]
        pre = dot(two_all, gate_up, 1, 0)
        gate_pre, lifted = pre[:, :hidden], pre[:, hidden:]
        sigmoid_gate = jax.nn.sigmoid(gate_pre)
        silu_gate = gate_pre * sigmoid_gate
        act = (silu_gate * lifted).astype(LOW)
        act_grad = dot(grad_all, down, 1, 1)
        gate_grad = act_grad * lifted * sigmoid_gate * (1.0 + gate_pre * (1.0 - sigmoid_gate))
        both_grad = cat([gate_grad.astype(LOW), (act_grad * silu_gate).astype(LOW)], 1)
        piece = dot(act, down, 1, 0)
        out_part = piece if out_part is None else out_part + piece
        piece = dot(both_grad, gate_up, 1, 1)
        back_part = piece if back_part is None else back_part + piece
        local_gate_up = dot(two_all, both_grad, 0, 0)
        local_down = dot(act, grad_all, 0, 0)
        piece = jnp.sum(local_gate_up * gate_up.astype(F32), axis=1)
        gain_two_part = piece if gain_two_part is None else gain_two_part + piece
        (gate_up_pair,), (down_pair,) = plan.reduce(
            [local_gate_up.astype(LOW)], [local_down.astype(LOW)]
        )
        ffn_grads.append((gate_up_pair, down_pair))

    normed_two_grad = lax.psum_scatter(
        back_part.astype(LOW), plane, scatter_dimension=0, tiled=True
    ).astype(F32)
    out_value = (
        residual
        + lax.psum_scatter(
            out_part.astype(LOW), plane, scatter_dimension=0, tiled=True
        ).astype(F32)
    ).astype(LOW)
    residual_grad = grad_low.astype(F32) + norm_back(normed_two_grad, residual, scale_two, gain_two)
    res_all = lax.all_gather(residual_grad.astype(LOW), plane, axis=0, tiled=True)

    back_one_part, local_qkv, local_out, gain_one_part = attn_backward(
        res_all, normed_all, ctx, queries, both, lse, wqkv, wout, cosine, sine, seg_col, seg_row
    )
    (qkv_pair,), (out_pair,) = plan.reduce([local_qkv], [local_out])
    normed_grad = lax.psum_scatter(
        back_one_part, plane, scatter_dimension=0, tiled=True
    ).astype(F32)
    in_grad = residual_grad + norm_back(normed_grad, inputs_f, scale_one, gain_one)

    gain_parts = jnp.stack([gain_one_part[:, 0] / gain_one, gain_two_part / gain_two])
    gain_sums = sum_everywhere(plan.reorder(gain_parts), list(sizes.items()))
    grad_gain_attn, grad_gain_ffn = gain_sums[0], gain_sums[1]

    def join(pair, axis):
        own, other = pair
        return by_x(cat([own, other], axis), cat([other, own], axis))

    def from_chunks(pairs, axis):
        own = cat([pair[0] for pair in pairs], axis)
        other = cat([pair[1] for pair in pairs], axis)
        return join((own, other), axis)

    def cut(pair, start, stop):
        return tuple(part[:, start:stop] for part in pair)

    at_k = halves_q[0].shape[1]
    at_v = at_k + halves_k[0].shape[1]
    end = at_v + halves_v[0].shape[1]
    grad_query = join(cut(qkv_pair, 0, at_k), 1)
    grad_key = join(cut(qkv_pair, at_k, at_v), 1)
    grad_value = join(cut(qkv_pair, at_v, end), 1)
    grad_out = join(out_pair, 0)
    hidden = ffn_weights[0][1].shape[0]
    grad_gate = from_chunks([cut(gu, 0, hidden) for gu, _ in ffn_grads], 1)
    grad_up = from_chunks([cut(gu, hidden, 2 * hidden) for gu, _ in ffn_grads], 1)
    grad_down = from_chunks([down for _, down in ffn_grads], 0)

    grads = (grad_query, grad_key, grad_value, grad_out, grad_gate, grad_up, grad_down)
    masters = (w_query, w_key, w_value, w_out, w_gate, w_up, w_down)
    firsts = (m_query, m_key, m_value, m_out, m_gate, m_up, m_down)
    seconds = (v_query, v_key, v_value, v_out, v_gate, v_up, v_down)
    updated = [
        adamw_update(w, g, m, v, WEIGHT_DECAY, LEARN_RATE)
        for w, g, m, v in zip(masters, grads, firsts, seconds)
    ]
    gain_updated = [
        adamw_update(gain_attn, grad_gain_attn, m_gain_attn, v_gain_attn, 0.0, GAIN_RATE),
        adamw_update(gain_ffn, grad_gain_ffn, m_gain_ffn, v_gain_ffn, 0.0, GAIN_RATE),
    ]
    return (
        plan.reorder(out_value),
        plan.reorder(in_grad),
        *grads,
        *[u[0] for u in updated],
        *[u[1] for u in updated],
        *[u[2] for u in updated],
        grad_gain_attn,
        grad_gain_ffn,
        *[u[0] for u in gain_updated],
        *[u[1] for u in gain_updated],
        *[u[2] for u in gain_updated],
    )


def solution(mesh):
    dp, tp = mesh.shape["dp"], mesh.shape["tp"]
    split = Mesh(mesh.devices.reshape(dp // 2, 2, tp), ("do", "di", "tp"))
    sizes = {"do": dp // 2, "di": 2, "tp": tp}
    dp_axes = ("do", "di")
    tokens = P(("do", "di", "tp"), None)
    by_rows, by_cols = P(dp_axes, "tp"), P("tp", dp_axes)
    weights = (by_rows, by_rows, by_rows, by_cols, by_rows, by_rows, by_cols)
    gains = (P(),) * 6
    in_specs = (tokens, tokens, P(dp_axes), P(dp_axes)) + weights * 3 + gains
    out_specs = (tokens, tokens) + weights * 4 + (P(),) * 2 + gains
    return jax.shard_map(
        functools.partial(on_device, sizes),
        mesh=split,
        in_specs=in_specs,
        out_specs=out_specs,
        check_vma=False,
    )
```

```python
import functools

import jax
import jax.numpy as jnp
from jax import lax
from jax.experimental import pallas as pl
from jax.experimental.pallas import tpu as pltpu
from jax.sharding import Mesh
from jax.sharding import PartitionSpec as P

HD = 64
LEN = 512
STEP = 5
CHUNKS = 2

NORM_EPS = 1e-05
ROPE_BASE = 500000.0
BETA_ONE = 0.9
BETA_TWO = 0.95
LEARN_RATE = 0.02
GAIN_RATE = 0.5
WEIGHT_DECAY = 0.1
ADAM_EPS = 1e-08

LOW = jnp.bfloat16
F32 = jnp.float32
MIB = 1024 * 1024

NEAR = [(0, 1), (1, 0), (2, 3), (3, 2)]
MIDDLE = [(1, 2), (2, 1)]
OUTWARD = [(1, 0), (2, 3)]
INWARD = [(0, 1), (3, 2)]
PAIR = [(0, 1), (1, 0)]


def dot(lhs, rhs, lhs_dim, rhs_dim):
    return lax.dot_general(
        lhs, rhs, (((lhs_dim,), (rhs_dim,)), ((), ())), preferred_element_type=F32
    )


def cat(parts, axis):
    return jnp.concatenate(parts, axis)


def after(value, *earlier):
    return lax.optimization_barrier((value, earlier))[0]


def line_near(own):
    return lax.ppermute(own, "do", NEAR), lax.ppermute(own, "do", MIDDLE)


def line_far(near, across):
    return lax.ppermute(near, "do", MIDDLE), lax.ppermute(across, "do", OUTWARD)


def line_last(across_near):
    return lax.ppermute(across_near, "do", OUTWARD)


def add(part, *arrived):
    total = part.astype(F32)
    for piece in arrived:
        total = total + piece.astype(F32)
    return total


def sum_far(parts):
    return lax.ppermute(parts[3], "do", INWARD)


def sum_middle(parts, far):
    second = add(parts[2], far).astype(LOW)
    return lax.ppermute(second, "do", MIDDLE), lax.ppermute(second, "do", INWARD)


def sum_near(parts, crossed, inward):
    first = add(parts[1], crossed).astype(LOW)
    third = add(parts[3], inward).astype(LOW)
    return lax.ppermute(first, "do", NEAR), lax.ppermute(third, "do", MIDDLE)


def sum_own(parts, from_near, from_across):
    return add(parts[0], from_near, from_across)


class Plan:
    def __init__(self, outer, per_device):
        self.rows = per_device
        self.block = 2 * per_device
        self.line = outer == 4 and per_device == 256

    def reorder(self, values):
        if not self.line:
            return values
        place = lax.axis_index("do")
        quarter = values.shape[-1] // 4
        a, b, c, d = (values[..., i * quarter : (i + 1) * quarter] for i in range(4))
        values = jnp.where(place % 2 == 1, cat([b, a, d, c], -1), values)
        half = 2 * quarter
        turned = cat([values[..., half:], values[..., :half]], -1)
        return jnp.where(place >= 2, turned, values)

    def by_x(self, low, high):
        return jnp.where(lax.axis_index("di") == 0, low, high)

    def inner(self):
        place = lax.axis_index("do")
        return ((place == 1) | (place == 2)).astype(jnp.int32).reshape(1)

    def blocks(self, row_part, col_part):
        if not self.line:
            out = []
            for (own, other), axis in ((row_part, 0), (col_part, 1)):
                theirs = lax.ppermute(other, "di", PAIR)
                out.append(cat([self.by_x(own, theirs), self.by_x(theirs, own)], axis))
            return tuple(out)
        rows = self.rows

        def pack(which):
            side = col_part[which]
            pieces = [side[i : i + rows] for i in range(0, side.shape[0], rows)]
            return cat([row_part[which]] + pieces, 1)

        mine, other = pack(0), pack(1)
        theirs = lax.ppermute(other, "di", PAIR)
        return cat([self.by_x(mine, theirs), self.by_x(theirs, mine)], 0)

    def plain_gather(self, blocks):
        return (
            lax.all_gather(blocks[0], "do", axis=0, tiled=True),
            lax.all_gather(blocks[1], "do", axis=1, tiled=True),
        )

    def plain_sum(self, grads):
        row, col = grads
        row = lax.psum_scatter(row, "do", scatter_dimension=0, tiled=True)
        col = lax.psum_scatter(col, "do", scatter_dimension=1, tiled=True)
        rows = self.rows
        return self.trade(row[:rows], row[rows:]), self.trade(col[:, :rows], col[:, rows:])

    def unpack(self, total, wide):
        rows = self.rows
        mine, theirs = self.trade(total[:rows], total[rows:])
        cuts = range(wide, total.shape[1], rows)
        return (
            (mine[:, :wide], theirs[:, :wide]),
            tuple(cat([side[:, i : i + rows] for i in cuts], 0) for side in (mine, theirs)),
        )

    def trade(self, low, high):
        mine = self.by_x(low, high).astype(F32)
        theirs = lax.ppermute(self.by_x(high, low).astype(LOW), "di", PAIR)
        return mine, theirs.astype(F32)


ANY = pl.BlockSpec(memory_space=pl.ANY)
SMALL = pl.CostEstimate(flops=1, bytes_accessed=1, transcendentals=0)


class Loader:
    def __init__(self, plan, weights, row_shape, col_shape):
        self.plan, self.row_shape, self.col_shape = plan, row_shape, col_shape
        rows, wide = plan.rows, row_shape[1]
        self.moves = []
        if plan.line:
            self.operands = [plan.inner(), *weights]
            for k in range(4):
                at = k * plan.block
                self.moves.append((k, 0, (0, 0), (at, 0), (plan.block, wide)))
                for i in range(0, col_shape[0], rows):
                    for x in range(2):
                        self.moves.append(
                            (k, 1, (x * rows, wide + i), (i, at + x * rows), (rows, rows))
                        )
        else:
            self.operands = list(weights)
            self.moves.append((0, 0, (0, 0), (0, 0), row_shape))
            self.moves.append((1, 1, (0, 0), (0, 0), col_shape))
        self.count = len(self.operands)

    def specs(self):
        if not self.plan.line:
            return [ANY] * 2
        return [pl.BlockSpec(memory_space=pltpu.SMEM)] + [ANY] * 6

    def scratch(self):
        return [
            pltpu.VMEM(self.row_shape, LOW),
            pltpu.VMEM(self.col_shape, LOW),
            pltpu.SemaphoreType.DMA((len(self.moves),)),
        ]

    def load(self, refs, row_ref, col_ref, sems):
        def copies(sources, chosen):
            made = []
            for i, (k, which, here, there, size) in enumerate(self.moves):
                if k in chosen:
                    target = (row_ref, col_ref)[which]
                    made.append(
                        pltpu.make_async_copy(
                            sources[k].at[pl.ds(here[0], size[0]), pl.ds(here[1], size[1])],
                            target.at[pl.ds(there[0], size[0]), pl.ds(there[1], size[1])],
                            sems.at[i],
                        )
                    )
            return made

        if not self.plan.line:
            for copy in copies(refs, (0, 1)):
                copy.start()
            for copy in copies(refs, (0, 1)):
                copy.wait()
            return
        inner, own, near, across_near, out, across, out_near = refs
        is_inner = inner[0] == 1
        for copy in copies((own, near), (0, 1)):
            copy.start()

        @pl.when(is_inner)
        def _():
            for copy in copies((None, None, across_near, across), (2, 3)):
                copy.start()

        @pl.when(jnp.logical_not(is_inner))
        def _():
            for copy in copies((None, None, out, out_near), (2, 3)):
                copy.start()

        for copy in copies((own, near, out, out_near), (0, 1, 2, 3)):
            copy.wait()


def pack_grads(plan, row_grad, col_grad, out_refs):
    if not plan.line:
        out_refs[0][...] = row_grad[...].astype(LOW)
        out_refs[1][...] = col_grad[...].astype(LOW)
        return
    rows, block, wide = plan.rows, plan.block, row_grad.shape[1]
    for k, out in enumerate(out_refs):
        at = k * block
        out[:, :wide] = row_grad[at : at + block, :].astype(LOW)
        for i in range(0, col_grad.shape[0], rows):
            for x in range(2):
                out[x * rows : (x + 1) * rows, wide + i : wide + i + rows] = col_grad[
                    i : i + rows, at + x * rows : at + (x + 1) * rows
                ].astype(LOW)


def packed_shapes(plan, row_shape, col_shape):
    if not plan.line:
        return [row_shape, col_shape]
    return [(plan.block, row_shape[1] + col_shape[0])] * 4


def rope_tables(positions):
    half_dim = HD // 2
    inverse_freq = ROPE_BASE ** (-2.0 * jnp.arange(half_dim, dtype=F32) / HD)
    angles = positions.astype(F32)[:, None] * inverse_freq[None, :]
    cosine, sine = jnp.cos(angles), jnp.sin(angles)
    return cat([cosine] * 4, 1), cat([-sine, sine] * 2, 1)


def lanes_of(shape):
    return lax.broadcasted_iota(jnp.int32, shape, 1)


def shuffle_halves(values):
    wide = values.shape[1]
    up = pltpu.roll(values, wide - HD // 2, 1)
    down = pltpu.roll(values, HD // 2, 1)
    return jnp.where(lanes_of(values.shape) % HD < HD // 2, up, down)


def tables(cos_ref, sin_ref, pairs):
    cosine, sine = cos_ref[...], sin_ref[...]
    is_key = lanes_of(cosine.shape) < HD
    return (
        cat([cosine] * pairs + [jnp.where(is_key, cosine, 1.0)], 1),
        cat([sine] * pairs + [jnp.where(is_key, sine, 0.0)], 1),
    )


def split_kv(both):
    is_key = lanes_of(both.shape) < HD
    blank = jnp.zeros_like(both)
    key_low = jnp.where(is_key, both, blank)
    value_high = jnp.where(is_key, blank, both)
    return (
        (key_low, pltpu.roll(key_low.astype(F32), HD, 1).astype(LOW)),
        (pltpu.roll(value_high.astype(F32), HD, 1).astype(LOW), value_high),
    )


def allowed_pairs(seg_col, seg_row):
    shape = (seg_col.shape[0], seg_row.shape[1])
    key_at = lax.broadcasted_iota(jnp.int32, shape, 1)
    query_at = lax.broadcasted_iota(jnp.int32, shape, 0)
    return (seg_col == seg_row) & (key_at <= query_at)


def attn_forward_kernel(pairs, loader, *refs):
    weights, refs = refs[: loader.count], refs[loader.count :]
    x_ref, cos_ref, sin_ref, col_ref, row_ref = refs[:5]
    part_ref, ctx_ref, q_ref, kv_ref, lse_ref, wqkv_ref, wout_ref, sems = refs[5:]

    @pl.when(pl.program_id(0) == 0)
    def _():
        loader.load(weights, wqkv_ref, wout_ref, sems)

    cosine, sine = tables(cos_ref, sin_ref, pairs)
    qkv = dot(x_ref[...], wqkv_ref[...], 1, 0)
    rotated = (qkv * cosine + shuffle_halves(qkv) * sine).astype(LOW)
    queries, both = rotated[:, : pairs * 128], rotated[:, pairs * 128 :]
    q_ref[...] = queries
    kv_ref[...] = both
    keys, values = split_kv(both)
    allowed = allowed_pairs(col_ref[...], row_ref[0])
    lane = lanes_of((both.shape[0], 128))
    log_sums = jnp.zeros((both.shape[0], 128), F32)
    contexts = []
    for pair in range(pairs):
        heads = queries[:, pair * 128 : (pair + 1) * 128]
        context = None
        for side in range(2):
            scores = dot(heads, keys[side], 1, 1) * HD**-0.5
            masked = jnp.where(allowed, scores, -1e30)
            top = jnp.max(masked, axis=1, keepdims=True)
            weights = jnp.exp(masked - top)
            totals = jnp.sum(weights, axis=1, keepdims=True)
            probs = (weights * (1.0 / totals)).astype(LOW)
            piece = dot(probs, values[side], 1, 0)
            context = piece if context is None else context + piece
            log_sums = jnp.where(lane == 2 * pair + side, top + jnp.log(totals), log_sums)
        contexts.append(context.astype(LOW))
    lse_ref[...] = log_sums
    context_low = cat(contexts, 1)
    ctx_ref[...] = context_low
    part_ref[...] = dot(context_low, wout_ref[...], 1, 0).astype(LOW)


def attn_backward_kernel(pairs, loader, *refs):
    weights, refs = refs[: loader.count], refs[loader.count :]
    res_ref, x_ref, ctx_ref, q_ref, kv_ref, lse_ref, cos_ref, sin_ref, col_ref, row_ref = refs[:10]
    part_ref, gain_ref, *grad_refs = refs[10:-5]
    wqkv_ref, wout_ref, sems, acc_qkv, acc_out = refs[-5:]
    step = pl.program_id(0)

    @pl.when(step == 0)
    def _():
        loader.load(weights, wqkv_ref, wout_ref, sems)
        acc_qkv[...] = jnp.zeros_like(acc_qkv)
        acc_out[...] = jnp.zeros_like(acc_out)

    cosine, sine = tables(cos_ref, sin_ref, pairs)
    scale = HD**-0.5
    res = res_ref[...]
    acc_out[...] += dot(ctx_ref[...], res, 0, 0)
    ctx_grad = dot(res, wout_ref[...], 1, 1).astype(LOW)
    keys, values = split_kv(kv_ref[...])
    allowed = allowed_pairs(col_ref[...], row_ref[0])
    lane = lanes_of((res.shape[0], 128))
    log_sums = lse_ref[...]
    query_grads, key_grad, value_grad = [], None, None
    for pair in range(pairs):
        heads = q_ref[:, pair * 128 : (pair + 1) * 128]
        grads = ctx_grad[:, pair * 128 : (pair + 1) * 128]
        query_grad = None
        for side in range(2):
            here = (lane < HD) if side == 0 else (lane >= HD)
            head = jnp.where(here, heads, jnp.zeros_like(heads))
            grad = jnp.where(here, grads, jnp.zeros_like(grads))
            at = 2 * pair + side
            scores = dot(heads, keys[side], 1, 1) * scale
            probs = jnp.where(allowed, jnp.exp(scores - log_sums[:, at : at + 1]), 0.0)
            prob_grad = dot(grads, values[side], 1, 1)
            delta = jnp.sum(probs * prob_grad, axis=1, keepdims=True)
            score_grad = (probs * (prob_grad - delta)).astype(LOW)
            to_value = dot(probs.astype(LOW), grad, 0, 0)
            to_key = dot(score_grad, head, 0, 0)
            to_query = dot(score_grad, keys[side], 1, 0)
            value_grad = to_value if value_grad is None else value_grad + to_value
            key_grad = to_key if key_grad is None else key_grad + to_key
            query_grad = to_query if query_grad is None else query_grad + to_query
        query_grads.append(query_grad * scale)
    key_grad = (key_grad + pltpu.roll(key_grad, HD, 1)) * scale
    value_grad = value_grad + pltpu.roll(value_grad, HD, 1)
    joined = cat(query_grads + [jnp.where(lane < HD, key_grad, value_grad)], 1)
    low = (joined * cosine - shuffle_halves(joined) * sine).astype(LOW)
    part_ref[...] = dot(low, wqkv_ref[...], 1, 1).astype(LOW)
    acc_qkv[...] += dot(x_ref[...], low, 0, 0)

    @pl.when(step == pl.num_programs(0) - 1)
    def _():
        pack_grads(loader.plan, acc_qkv, acc_out, grad_refs)
        gain_ref[...] = jnp.sum(acc_qkv[...] * wqkv_ref[...].astype(F32), axis=1, keepdims=True)


def once(shape):
    return pl.BlockSpec(shape, lambda i: (0,) * len(shape), pipeline_mode=pl.Buffered(1))


def per_seq(shape):
    return pl.BlockSpec(shape, lambda i: (i,) + (0,) * (len(shape) - 1))


def attn_forward(loader, normed, cosine, sine, seg_col, seg_row):
    rows, width = normed.shape
    heads = loader.col_shape[0]
    return pl.pallas_call(
        functools.partial(attn_forward_kernel, heads // 128, loader),
        grid=(rows // LEN,),
        in_specs=[
            *loader.specs(),
            per_seq((LEN, width)),
            per_seq((LEN, 128)),
            per_seq((LEN, 128)),
            per_seq((LEN, 1)),
            per_seq((1, 1, LEN)),
        ],
        out_specs=[
            per_seq((LEN, width)),
            per_seq((LEN, heads)),
            per_seq((LEN, heads)),
            per_seq((LEN, 128)),
            per_seq((LEN, 128)),
        ],
        out_shape=[
            jax.ShapeDtypeStruct((rows, width), LOW),
            jax.ShapeDtypeStruct((rows, heads), LOW),
            jax.ShapeDtypeStruct((rows, heads), LOW),
            jax.ShapeDtypeStruct((rows, 128), LOW),
            jax.ShapeDtypeStruct((rows, 128), F32),
        ],
        scratch_shapes=loader.scratch(),
        compiler_params=pltpu.CompilerParams(vmem_limit_bytes=48 * MIB),
        cost_estimate=SMALL,
        name="attn_forward",
    )(*loader.operands, normed, cosine, sine, seg_col, seg_row)


def attn_backward(loader, res_all, normed, ctx, queries, both, lse, cosine, sine, seg_col, seg_row):
    rows, width = normed.shape
    heads = loader.col_shape[0]
    grads = packed_shapes(loader.plan, loader.row_shape, loader.col_shape)
    return pl.pallas_call(
        functools.partial(attn_backward_kernel, heads // 128, loader),
        grid=(rows // LEN,),
        in_specs=[
            *loader.specs(),
            per_seq((LEN, width)),
            per_seq((LEN, width)),
            per_seq((LEN, heads)),
            per_seq((LEN, heads)),
            per_seq((LEN, 128)),
            per_seq((LEN, 128)),
            per_seq((LEN, 128)),
            per_seq((LEN, 128)),
            per_seq((LEN, 1)),
            per_seq((1, 1, LEN)),
        ],
        out_specs=[per_seq((LEN, width)), once((width, 1))] + [once(shape) for shape in grads],
        out_shape=[
            jax.ShapeDtypeStruct((rows, width), LOW),
            jax.ShapeDtypeStruct((width, 1), F32),
        ]
        + [jax.ShapeDtypeStruct(shape, LOW) for shape in grads],
        scratch_shapes=[
            *loader.scratch(),
            pltpu.VMEM(loader.row_shape, F32),
            pltpu.VMEM(loader.col_shape, F32),
        ],
        compiler_params=pltpu.CompilerParams(vmem_limit_bytes=52 * MIB),
        cost_estimate=SMALL,
        name="attn_backward",
    )(*loader.operands, res_all, normed, ctx, queries, both, lse, cosine, sine, seg_col, seg_row)


TILE = 512


def ffn_main_kernel(loader, more, *refs):
    weights, refs = refs[: loader.count], refs[loader.count :]
    x_ref, grad_ref = refs[:2]
    back_ref, act_ref, both_ref, gate_up_ref, down_ref, sems = refs[2 + more :]

    @pl.when(pl.program_id(0) == 0)
    def _():
        loader.load(weights, gate_up_ref, down_ref, sems)

    hidden = down_ref.shape[0]
    pre = dot(x_ref[...], gate_up_ref[...], 1, 0)
    gate_pre, lifted = pre[:, :hidden], pre[:, hidden:]
    sigmoid_gate = jax.nn.sigmoid(gate_pre)
    silu_gate = gate_pre * sigmoid_gate
    act_ref[...] = (silu_gate * lifted).astype(LOW)
    act_grad = dot(grad_ref[...], down_ref[...], 1, 1)
    gate_grad = act_grad * lifted * sigmoid_gate * (1.0 + gate_pre * (1.0 - sigmoid_gate))
    both_grad = cat([gate_grad.astype(LOW), (act_grad * silu_gate).astype(LOW)], 1)
    both_ref[...] = both_grad
    back = dot(both_grad, gate_up_ref[...], 1, 1)
    if more:
        back = back + refs[2][...].astype(F32)
    back_ref[...] = back.astype(LOW)


def ffn_main(loader, tokens, grads, earlier):
    rows, width = tokens.shape
    hidden = loader.col_shape[0]
    more = [] if earlier is None else [earlier]
    return pl.pallas_call(
        functools.partial(ffn_main_kernel, loader, len(more)),
        grid=(rows // TILE,),
        in_specs=[
            *loader.specs(),
            per_seq((TILE, width)),
            per_seq((TILE, width)),
            *[per_seq((TILE, width))] * len(more),
        ],
        out_specs=[
            per_seq((TILE, width)),
            per_seq((TILE, hidden)),
            per_seq((TILE, 2 * hidden)),
        ],
        out_shape=[
            jax.ShapeDtypeStruct((rows, width), LOW),
            jax.ShapeDtypeStruct((rows, hidden), LOW),
            jax.ShapeDtypeStruct((rows, 2 * hidden), LOW),
        ],
        scratch_shapes=loader.scratch(),
        compiler_params=pltpu.CompilerParams(vmem_limit_bytes=58 * MIB),
        cost_estimate=SMALL,
        name="ffn_main",
    )(*loader.operands, tokens, grads, *more)


def ffn_weights_kernel(loader, more, *refs):
    weights, refs = refs[: loader.count], refs[loader.count :]
    x_ref, grad_ref, act_ref, both_ref = refs[:4]
    out_ref, gain_ref, *grad_refs = refs[4 + more : -5]
    gate_up_ref, down_ref, sems, acc_gate_up, acc_down = refs[-5:]
    step = pl.program_id(0)

    @pl.when(step == 0)
    def _():
        loader.load(weights, gate_up_ref, down_ref, sems)
        acc_gate_up[...] = jnp.zeros_like(acc_gate_up)
        acc_down[...] = jnp.zeros_like(acc_down)

    act = act_ref[...]
    acc_down[...] += dot(act, grad_ref[...], 0, 0)
    acc_gate_up[...] += dot(x_ref[...], both_ref[...], 0, 0)
    out = dot(act, down_ref[...], 1, 0)
    if more:
        out = out + refs[4][...].astype(F32)
    out_ref[...] = out.astype(LOW)

    @pl.when(step == pl.num_programs(0) - 1)
    def _():
        pack_grads(loader.plan, acc_gate_up, acc_down, grad_refs)
        gain_ref[...] = jnp.sum(
            acc_gate_up[...] * gate_up_ref[...].astype(F32), axis=1, keepdims=True
        )


def ffn_weights(loader, tokens, grads, act, both_grad, earlier):
    rows, width = tokens.shape
    hidden = loader.col_shape[0]
    more = [] if earlier is None else [earlier]
    packed = packed_shapes(loader.plan, loader.row_shape, loader.col_shape)
    return pl.pallas_call(
        functools.partial(ffn_weights_kernel, loader, len(more)),
        grid=(rows // TILE,),
        in_specs=[
            *loader.specs(),
            per_seq((TILE, width)),
            per_seq((TILE, width)),
            per_seq((TILE, hidden)),
            per_seq((TILE, 2 * hidden)),
            *[per_seq((TILE, width))] * len(more),
        ],
        out_specs=[per_seq((TILE, width)), once((width, 1))] + [once(shape) for shape in packed],
        out_shape=[
            jax.ShapeDtypeStruct((rows, width), LOW),
            jax.ShapeDtypeStruct((width, 1), F32),
        ]
        + [jax.ShapeDtypeStruct(shape, LOW) for shape in packed],
        scratch_shapes=[
            *loader.scratch(),
            pltpu.VMEM(loader.row_shape, F32),
            pltpu.VMEM(loader.col_shape, F32),
        ],
        compiler_params=pltpu.CompilerParams(vmem_limit_bytes=60 * MIB),
        cost_estimate=SMALL,
        name="ffn_weights",
    )(*loader.operands, tokens, grads, act, both_grad, *more)


def norm_rows(values, gain_vec):
    row_scale = lax.rsqrt(jnp.mean(values * values, axis=1, keepdims=True) + NORM_EPS)
    return values * row_scale * gain_vec, row_scale


def norm_back(row_grad, values, row_scale, gain_vec):
    scaled_grad = row_grad * gain_vec
    return row_scale * scaled_grad - values * row_scale**3 * jnp.mean(
        scaled_grad * values, axis=1, keepdims=True
    )


def adamw_update(master, grad_sum, first_mom, second_mom, decay_rate, step_rate):
    next_first = BETA_ONE * first_mom + (1.0 - BETA_ONE) * grad_sum
    next_second = BETA_TWO * second_mom + (1.0 - BETA_TWO) * grad_sum * grad_sum
    first_hat = next_first / (1.0 - BETA_ONE**STEP)
    second_hat = next_second / (1.0 - BETA_TWO**STEP)
    next_master = master - step_rate * (
        first_hat / (jnp.sqrt(second_hat) + ADAM_EPS) + decay_rate * master
    )
    return (next_master, next_first, next_second)


def sum_everywhere(values, sizes):
    for axis, size in sizes:
        step = 1
        while step < size:
            values = values + lax.ppermute(values, axis, [(i, i ^ step) for i in range(size)])
            step *= 2
    return values


def pick(index, low, high):
    return jnp.where(index == 0, low, high)


class Plane:
    def __init__(self, tp):
        self.tp = tp
        self.half = tp // 2
        self.x = lax.axis_index("di")
        self.y = lax.axis_index("tp") // self.half
        self.far = [(i, (i + self.half) % tp) for i in range(tp)]

    def swap_y(self, value):
        return lax.ppermute(value, "tp", self.far)

    def swap_x(self, value):
        return lax.ppermute(value, "di", PAIR)

    def swap_core(self, value):
        return lax.ppermute(value, "tp", [(i, i ^ 1) for i in range(self.tp)])


def on_device(
    sizes,
    layer_input, out_grad, segment_ids, positions,
    w_query, w_key, w_value, w_out, w_gate, w_up, w_down,
    m_query, m_key, m_value, m_out, m_gate, m_up, m_down,
    v_query, v_key, v_value, v_out, v_gate, v_up, v_down,
    gain_attn, gain_ffn, m_gain_attn, m_gain_ffn, v_gain_attn, v_gain_ffn,
):
    width = layer_input.shape[1]
    plan = Plan(sizes["do"], w_query.shape[0])
    by_x = plan.by_x
    axes = ("di", "tp")
    plane = Plane(sizes["tp"])

    gain_one, gain_two = plan.reorder(gain_attn), plan.reorder(gain_ffn)
    inputs_f = plan.reorder(layer_input).astype(F32)
    grad_low = plan.reorder(out_grad)
    normed, scale_one = norm_rows(inputs_f, gain_one)
    normed_all = lax.all_gather(normed.astype(LOW), axes, axis=0, tiled=True)

    marks = cat([segment_ids[None, :], positions[None, :]], 0)
    marks_other = lax.ppermute(marks, "di", PAIR)
    marks_all = cat([by_x(marks, marks_other), by_x(marks_other, marks)], 1)
    seg_all, pos_all = marks_all[0], marks_all[1]
    rows = seg_all.shape[0]
    seqs = rows // LEN
    seg_col, seg_row = seg_all.reshape(rows, 1), seg_all.reshape(seqs, 1, LEN)
    cosine, sine = rope_tables(pos_all)

    def col_halves(weight):
        half = weight.shape[1] // 2
        low = weight.astype(LOW)
        return by_x(low[:, :half], low[:, half:]), by_x(low[:, half:], low[:, :half])

    def row_halves(weight):
        half = weight.shape[0] // 2
        low = weight.astype(LOW)
        return by_x(low[:half], low[half:]), by_x(low[half:], low[:half])

    def col_cut(pair, chunk):
        size = pair[0].shape[1] // CHUNKS
        return tuple(part[:, chunk * size : (chunk + 1) * size] for part in pair)

    def row_cut(pair, chunk):
        size = pair[0].shape[0] // CHUNKS
        return tuple(part[chunk * size : (chunk + 1) * size] for part in pair)

    halves_q, halves_k, halves_v = col_halves(w_query), col_halves(w_key), col_halves(w_value)
    qkv_parts = tuple(cat([q, k, v], 1) for q, k, v in zip(halves_q, halves_k, halves_v))
    out_parts = row_halves(w_out)
    halves_g, halves_u, halves_d = col_halves(w_gate), col_halves(w_up), row_halves(w_down)

    def ffn_parts(chunk):
        gate_up = tuple(
            cat([g, u], 1) for g, u in zip(col_cut(halves_g, chunk), col_cut(halves_u, chunk))
        )
        return gate_up, row_cut(halves_d, chunk)

    attn_block = plan.blocks(qkv_parts, out_parts)
    ffn_blocks = [plan.blocks(*ffn_parts(chunk)) for chunk in range(CHUNKS)]
    hidden = halves_d[0].shape[0] // CHUNKS
    attn_shapes = (width, qkv_parts[0].shape[1]), (out_parts[0].shape[0], width)
    ffn_shapes = (width, 2 * hidden), (hidden, width)

    if plan.line:
        near, across = line_near(attn_block)
        across_near, out = line_far(near, across)
        out_near = line_last(across_near)
        attn_weights = (attn_block, near, across_near, out, across, out_near)
        first_block = after(ffn_blocks[0], out_near)
        near_1, across_1 = line_near(first_block)
    else:
        attn_weights = plan.plain_gather(attn_block)
    attn_loader = Loader(plan, attn_weights, *attn_shapes)

    attn_part, ctx, queries, both, lse = attn_forward(
        attn_loader, normed_all, cosine, sine, seg_col, seg_row
    )
    attn_sum = lax.psum_scatter(attn_part, axes, scatter_dimension=0, tiled=True)

    grad_y = plane.swap_y(after(grad_low, normed_all))
    grad_half = cat([pick(plane.y, grad_low, grad_y), pick(plane.y, grad_y, grad_low)], 0)

    if plan.line:
        near_1, across_1 = after((near_1, across_1), attn_part)
        across_near_1, out_1 = line_far(near_1, across_1)
        attn_sum = after(attn_sum, across_near_1, out_1, grad_y)
        second_block = after(ffn_blocks[1], out_1, across_near_1)
        near_2, across_2 = line_near(second_block)
        out_near_1 = line_last(across_near_1)
        first_weights = (first_block, near_1, across_near_1, out_1, across_1, out_near_1)
    else:
        first_weights = plan.plain_gather(ffn_blocks[0])
        second_weights = plan.plain_gather(ffn_blocks[1])

    residual = inputs_f + attn_sum.astype(F32)
    normed_two, scale_two = norm_rows(residual, gain_two)
    two_all = lax.all_gather(normed_two.astype(LOW), axes, axis=0, tiled=True)

    grad_x = plane.swap_x(grad_half)
    grad_core = cat([by_x(grad_half, grad_x), by_x(grad_x, grad_half)], 0)
    grad_other = plane.swap_core(grad_core)
    own_rows = layer_input.shape[0]
    core = lax.axis_index("tp") % 2
    groups = (rows // own_rows // 2, 1, own_rows, width)
    mine, theirs = grad_core.reshape(groups), grad_other.reshape(groups)
    grad_all = cat([pick(core, mine, theirs), pick(core, theirs, mine)], 1).reshape(rows, width)

    first = Loader(plan, first_weights, *ffn_shapes)
    if plan.line:
        two_all = after(two_all, near_2, across_2)
        across_near_2, out_2 = line_far(near_2, across_2)
    back_1, act_1, both_1 = ffn_main(first, two_all, grad_all, None)
    if plan.line:
        act_1 = after(act_1, across_near_2, out_2)
        out_near_2 = line_last(across_near_2)
        second_weights = (second_block, near_2, across_near_2, out_2, across_2, out_near_2)
    out_1_part, gain_1, *grads_1 = ffn_weights(first, two_all, grad_all, act_1, both_1, None)
    second = Loader(plan, second_weights, *ffn_shapes)
    if plan.line:
        far_1 = sum_far(grads_1)
        back_1 = after(back_1, out_1_part)
    back_2, act_2, both_2 = ffn_main(second, two_all, grad_all, back_1)
    back_sum = lax.psum_scatter(back_2, axes, scatter_dimension=0, tiled=True)
    if plan.line:
        far_1 = after(far_1, back_2)
        crossed_1, inward_1 = sum_middle(grads_1, far_1)
        act_2 = after(act_2, far_1)
    out_2_part, gain_2, *grads_2 = ffn_weights(second, two_all, grad_all, act_2, both_2, out_1_part)
    if plan.line:
        far_2 = sum_far(grads_2)
        crossed_1, inward_1 = after((crossed_1, inward_1), out_2_part)
        near_sum_1, across_sum_1 = sum_near(grads_1, crossed_1, inward_1)
        back_sum = after(back_sum, crossed_1, inward_1, far_2)
        crossed_2, inward_2 = sum_middle(grads_2, far_2)

    out_shape = (rows // own_rows // 2, 2, own_rows, width)
    parts = out_2_part.reshape(out_shape)
    mine, theirs = pick(core, parts[:, 0], parts[:, 1]), pick(core, parts[:, 1], parts[:, 0])
    summed = add(mine, plane.swap_core(theirs)).astype(LOW)
    low, high = summed[: out_shape[0] // 2], summed[out_shape[0] // 2 :]
    summed = add(by_x(low, high), plane.swap_x(by_x(high, low))).astype(LOW)
    low, high = summed[: summed.shape[0] // 2], summed[summed.shape[0] // 2 :]
    summed = add(pick(plane.y, low, high), plane.swap_y(pick(plane.y, high, low)))
    out_value = (residual + summed.reshape(own_rows, width)).astype(LOW)

    normed_two_grad = back_sum.astype(F32)
    residual_grad = grad_low.astype(F32) + norm_back(normed_two_grad, residual, scale_two, gain_two)
    res_all = lax.all_gather(residual_grad.astype(LOW), axes, axis=0, tiled=True)
    if plan.line:
        res_all = after(res_all, near_sum_1, across_sum_1, crossed_2, inward_2)
        near_sum_2, across_sum_2 = sum_near(grads_2, crossed_2, inward_2)

    back_one_part, gain_one_part, *grads_attn = attn_backward(
        attn_loader, res_all, normed_all, ctx, queries, both, lse, cosine, sine, seg_col, seg_row
    )
    back_one = lax.psum_scatter(back_one_part, axes, scatter_dimension=0, tiled=True)
    if plan.line:
        far = sum_far(grads_attn)
        total_1 = sum_own(grads_1, near_sum_1, across_sum_1)
        total_2 = sum_own(grads_2, near_sum_2, across_sum_2)
        crossed, inward = sum_middle(grads_attn, far)
        from_near, from_across = sum_near(grads_attn, crossed, inward)
        total = sum_own(grads_attn, from_near, from_across)
        qkv_pair, out_pair = plan.unpack(total, attn_shapes[0][1])
        ffn_grads = [plan.unpack(each, 2 * hidden) for each in (total_1, total_2)]
    else:
        qkv_pair, out_pair = plan.plain_sum(grads_attn)
        ffn_grads = [plan.plain_sum(each) for each in (grads_1, grads_2)]
    in_grad = residual_grad + norm_back(back_one.astype(F32), inputs_f, scale_one, gain_one)

    gain_parts = jnp.stack(
        [gain_one_part[:, 0] / gain_one, (gain_1[:, 0] + gain_2[:, 0]) / gain_two]
    )
    gain_sums = sum_everywhere(plan.reorder(gain_parts), list(sizes.items()))
    grad_gain_attn, grad_gain_ffn = gain_sums[0], gain_sums[1]

    def join(pair, axis):
        own, other = pair
        return by_x(cat([own, other], axis), cat([other, own], axis))

    def from_chunks(pairs, axis):
        own = cat([pair[0] for pair in pairs], axis)
        other = cat([pair[1] for pair in pairs], axis)
        return join((own, other), axis)

    def cut(pair, start, stop):
        return tuple(part[:, start:stop] for part in pair)

    at_k = halves_q[0].shape[1]
    at_v = at_k + halves_k[0].shape[1]
    end = at_v + halves_v[0].shape[1]
    grad_query = join(cut(qkv_pair, 0, at_k), 1)
    grad_key = join(cut(qkv_pair, at_k, at_v), 1)
    grad_value = join(cut(qkv_pair, at_v, end), 1)
    grad_out = join(out_pair, 0)
    grad_gate = from_chunks([cut(gu, 0, hidden) for gu, _ in ffn_grads], 1)
    grad_up = from_chunks([cut(gu, hidden, 2 * hidden) for gu, _ in ffn_grads], 1)
    grad_down = from_chunks([down for _, down in ffn_grads], 0)

    grads = (grad_query, grad_key, grad_value, grad_out, grad_gate, grad_up, grad_down)
    masters = (w_query, w_key, w_value, w_out, w_gate, w_up, w_down)
    firsts = (m_query, m_key, m_value, m_out, m_gate, m_up, m_down)
    seconds = (v_query, v_key, v_value, v_out, v_gate, v_up, v_down)
    updated = [
        adamw_update(w, g, m, v, WEIGHT_DECAY, LEARN_RATE)
        for w, g, m, v in zip(masters, grads, firsts, seconds)
    ]
    gain_updated = [
        adamw_update(gain_attn, grad_gain_attn, m_gain_attn, v_gain_attn, 0.0, GAIN_RATE),
        adamw_update(gain_ffn, grad_gain_ffn, m_gain_ffn, v_gain_ffn, 0.0, GAIN_RATE),
    ]
    return (
        plan.reorder(out_value),
        plan.reorder(in_grad),
        *grads,
        *[u[0] for u in updated],
        *[u[1] for u in updated],
        *[u[2] for u in updated],
        grad_gain_attn,
        grad_gain_ffn,
        *[u[0] for u in gain_updated],
        *[u[1] for u in gain_updated],
        *[u[2] for u in gain_updated],
    )


def solution(mesh):
    dp, tp = mesh.shape["dp"], mesh.shape["tp"]
    split = Mesh(mesh.devices.reshape(dp // 2, 2, tp), ("do", "di", "tp"))
    sizes = {"do": dp // 2, "di": 2, "tp": tp}
    dp_axes = ("do", "di")
    tokens = P(("do", "di", "tp"), None)
    by_rows, by_cols = P(dp_axes, "tp"), P("tp", dp_axes)
    weights = (by_rows, by_rows, by_rows, by_cols, by_rows, by_rows, by_cols)
    gains = (P(),) * 6
    in_specs = (tokens, tokens, P(dp_axes), P(dp_axes)) + weights * 3 + gains
    out_specs = (tokens, tokens) + weights * 4 + (P(),) * 2 + gains
    return jax.shard_map(
        functools.partial(on_device, sizes),
        mesh=split,
        in_specs=in_specs,
        out_specs=out_specs,
        check_vma=False,
    )
```

```python
import functools

import jax
import jax.numpy as jnp
from jax import lax
from jax.experimental import pallas as pl
from jax.experimental.pallas import tpu as pltpu
from jax.sharding import Mesh
from jax.sharding import PartitionSpec as P

HD = 64
LEN = 512
STEP = 5
CHUNKS = 2

NORM_EPS = 1e-05
ROPE_BASE = 500000.0
BETA_ONE = 0.9
BETA_TWO = 0.95
LEARN_RATE = 0.02
GAIN_RATE = 0.5
WEIGHT_DECAY = 0.1
ADAM_EPS = 1e-08

LOW = jnp.bfloat16
F32 = jnp.float32
MIB = 1024 * 1024

NEAR = [(0, 1), (1, 0), (2, 3), (3, 2)]
MIDDLE = [(1, 2), (2, 1)]
OUTWARD = [(1, 0), (2, 3)]
INWARD = [(0, 1), (3, 2)]
CROSS = [(0, 2), (1, 3), (2, 0), (3, 1)]
MIRROR = [(0, 3), (1, 2), (2, 1), (3, 0)]
PAIR = [(0, 1), (1, 0)]


def dot(lhs, rhs, lhs_dim, rhs_dim):
    return lax.dot_general(
        lhs, rhs, (((lhs_dim,), (rhs_dim,)), ((), ())), preferred_element_type=F32
    )


def cat(parts, axis):
    return jnp.concatenate(parts, axis)


def fence(*values):
    return lax.optimization_barrier(values)


def line_near(own):
    return lax.ppermute(own, "do", NEAR), lax.ppermute(own, "do", MIDDLE)


def line_far(near, across):
    return lax.ppermute(near, "do", MIDDLE), lax.ppermute(across, "do", OUTWARD)


def line_last(across_near):
    return lax.ppermute(across_near, "do", OUTWARD)


def add(part, *arrived):
    total = part.astype(F32)
    for piece in arrived:
        total = total + piece.astype(F32)
    return total


def sum_far(parts):
    return lax.ppermute(parts[3], "do", INWARD)


def sum_middle(parts, far):
    second = add(parts[2], far).astype(LOW)
    return lax.ppermute(second, "do", MIDDLE), lax.ppermute(second, "do", INWARD)


def sum_near(parts, crossed, inward):
    first = add(parts[1], crossed).astype(LOW)
    third = add(parts[3], inward).astype(LOW)
    return lax.ppermute(first, "do", NEAR), lax.ppermute(third, "do", MIDDLE)


def sum_own(parts, from_near, from_across):
    return add(parts[0], from_near, from_across)


def send_direct(parts):
    return [
        lax.ppermute(part, "do", perm) for part, perm in zip(parts[1:], (NEAR, CROSS, MIRROR))
    ]


class Plan:
    def __init__(self, outer, per_device):
        self.rows = per_device
        self.block = 2 * per_device
        self.line = outer == 4 and per_device == 256
        self.cuts = 4 if self.line else 1

    def reorder(self, values):
        if not self.line:
            return values
        place = lax.axis_index("do")
        quarter = values.shape[-1] // 4
        a, b, c, d = (values[..., i * quarter : (i + 1) * quarter] for i in range(4))
        values = jnp.where(place % 2 == 1, cat([b, a, d, c], -1), values)
        half = 2 * quarter
        turned = cat([values[..., half:], values[..., :half]], -1)
        return jnp.where(place >= 2, turned, values)

    def by_x(self, low, high):
        return jnp.where(lax.axis_index("di") == 0, low, high)

    def inner(self):
        place = lax.axis_index("do")
        return ((place == 1) | (place == 2)).astype(jnp.int32).reshape(1)

    def pack(self, row_part, col_part):
        rows, packs = self.rows, []
        for row_side, side in zip(row_part, col_part):
            pieces = [side[i : i + rows] for i in range(0, side.shape[0], rows)]
            packs.append(cat([row_side] + pieces, 1))
        return packs

    def swap(self, other):
        return lax.ppermute(other, "di", PAIR)

    def join(self, own, theirs, axis=0):
        return cat([self.by_x(own, theirs), self.by_x(theirs, own)], axis)

    def plain_gather(self, row_part, col_part):
        full = []
        for (own, other), axis in ((row_part, 0), (col_part, 1)):
            block = self.join(own, self.swap(other), axis)
            full.append(lax.all_gather(block, "do", axis=axis, tiled=True))
        return tuple(full)

    def unpack(self, total, wide):
        rows = self.rows
        mine, theirs = self.trade(total[:rows], total[rows:])
        cuts = range(wide, total.shape[1], rows)
        return (
            (mine[:, :wide], theirs[:, :wide]),
            tuple(cat([side[:, i : i + rows] for i in cuts], 0) for side in (mine, theirs)),
        )

    def plain_sum_row(self, grad):
        total = lax.psum_scatter(grad, "do", scatter_dimension=0, tiled=True)
        return self.trade(total[: self.rows], total[self.rows :])

    def plain_sum_col(self, grad):
        total = lax.psum_scatter(grad, "do", scatter_dimension=1, tiled=True)
        return self.trade(total[:, : self.rows], total[:, self.rows :])

    def trade(self, low, high):
        mine = self.by_x(low, high).astype(F32)
        theirs = lax.ppermute(self.by_x(high, low).astype(LOW), "di", PAIR)
        return mine, theirs.astype(F32)


ANY = pl.BlockSpec(memory_space=pl.ANY)
SMALL = pl.CostEstimate(flops=1, bytes_accessed=1, transcendentals=0)


class Loader:
    def __init__(self, plan, weights, row_shape, col_shape):
        self.plan, self.row_shape, self.col_shape = plan, row_shape, col_shape
        rows, wide = plan.rows, row_shape[1]
        self.moves = []
        if plan.line:
            self.operands = [plan.inner(), *weights]
            for k in range(4):
                at = k * plan.block
                self.moves.append((k, 0, (0, 0), (at, 0), (plan.block, wide)))
                for i in range(0, col_shape[0], rows):
                    for x in range(2):
                        self.moves.append(
                            (k, 1, (x * rows, wide + i), (i, at + x * rows), (rows, rows))
                        )
        else:
            self.operands = list(weights)
            self.moves.append((0, 0, (0, 0), (0, 0), row_shape))
            self.moves.append((1, 1, (0, 0), (0, 0), col_shape))
        self.count = len(self.operands)

    def specs(self):
        if not self.plan.line:
            return [ANY] * 2
        return [pl.BlockSpec(memory_space=pltpu.SMEM)] + [ANY] * 6

    def scratch(self):
        return [
            pltpu.VMEM(self.row_shape, LOW),
            pltpu.VMEM(self.col_shape, LOW),
            pltpu.SemaphoreType.DMA((len(self.moves),)),
        ]

    def load(self, refs, row_ref, col_ref, sems):
        def copies(sources, chosen):
            made = []
            for i, (k, which, here, there, size) in enumerate(self.moves):
                if k in chosen:
                    target = (row_ref, col_ref)[which]
                    made.append(
                        pltpu.make_async_copy(
                            sources[k].at[pl.ds(here[0], size[0]), pl.ds(here[1], size[1])],
                            target.at[pl.ds(there[0], size[0]), pl.ds(there[1], size[1])],
                            sems.at[i],
                        )
                    )
            return made

        if not self.plan.line:
            for copy in copies(refs, (0, 1)):
                copy.start()
            for copy in copies(refs, (0, 1)):
                copy.wait()
            return
        inner, own, near, across_near, out, across, out_near = refs
        is_inner = inner[0] == 1
        for copy in copies((own, near), (0, 1)):
            copy.start()

        @pl.when(is_inner)
        def _():
            for copy in copies((None, None, across_near, across), (2, 3)):
                copy.start()

        @pl.when(jnp.logical_not(is_inner))
        def _():
            for copy in copies((None, None, out, out_near), (2, 3)):
                copy.start()

        for copy in copies((own, near, out, out_near), (0, 1, 2, 3)):
            copy.wait()


def pack_grads(plan, row_grad, col_grad, out_refs):
    if not plan.line:
        out_refs[0][...] = row_grad[...].astype(LOW)
        out_refs[1][...] = col_grad[...].astype(LOW)
        return
    rows, block, wide = plan.rows, plan.block, row_grad.shape[1]
    for k, out in enumerate(out_refs):
        at = k * block
        out[:, :wide] = row_grad[at : at + block, :].astype(LOW)
        for i in range(0, col_grad.shape[0], rows):
            for x in range(2):
                out[x * rows : (x + 1) * rows, wide + i : wide + i + rows] = col_grad[
                    i : i + rows, at + x * rows : at + (x + 1) * rows
                ].astype(LOW)


def packed_shapes(plan, row_shape, col_shape):
    if not plan.line:
        return [row_shape, col_shape]
    return [(plan.block, row_shape[1] + col_shape[0])] * 4


def rope_tables(positions):
    half_dim = HD // 2
    inverse_freq = ROPE_BASE ** (-2.0 * jnp.arange(half_dim, dtype=F32) / HD)
    angles = positions.astype(F32)[:, None] * inverse_freq[None, :]
    cosine, sine = jnp.cos(angles), jnp.sin(angles)
    return cat([cosine] * 4, 1), cat([-sine, sine] * 2, 1)


def lanes_of(shape):
    return lax.broadcasted_iota(jnp.int32, shape, 1)


def shuffle_halves(values):
    wide = values.shape[1]
    up = pltpu.roll(values, wide - HD // 2, 1)
    down = pltpu.roll(values, HD // 2, 1)
    return jnp.where(lanes_of(values.shape) % HD < HD // 2, up, down)


def tables(cos_ref, sin_ref, pairs):
    cosine, sine = cos_ref[...], sin_ref[...]
    is_key = lanes_of(cosine.shape) < HD
    return (
        cat([cosine] * pairs + [jnp.where(is_key, cosine, 1.0)], 1),
        cat([sine] * pairs + [jnp.where(is_key, sine, 0.0)], 1),
    )


def split_kv(both):
    is_key = lanes_of(both.shape) < HD
    blank = jnp.zeros_like(both)
    key_low = jnp.where(is_key, both, blank)
    value_high = jnp.where(is_key, blank, both)
    return (
        (key_low, pltpu.roll(key_low.astype(F32), HD, 1).astype(LOW)),
        (pltpu.roll(value_high.astype(F32), HD, 1).astype(LOW), value_high),
    )


def allowed_pairs(seg_col, seg_row):
    shape = (seg_col.shape[0], seg_row.shape[1])
    key_at = lax.broadcasted_iota(jnp.int32, shape, 1)
    query_at = lax.broadcasted_iota(jnp.int32, shape, 0)
    return (seg_col == seg_row) & (key_at <= query_at)


def attn_forward_kernel(pairs, loader, *refs):
    weights, refs = refs[: loader.count], refs[loader.count :]
    x_ref, cos_ref, sin_ref, col_ref, row_ref = refs[:5]
    part_ref, ctx_ref, q_ref, kv_ref, lse_ref, wout_ref, wqkv_ref, _, sems = refs[5:]

    @pl.when(pl.program_id(0) == 0)
    def _():
        loader.load(weights, wqkv_ref, wout_ref, sems)

    cosine, sine = tables(cos_ref, sin_ref, pairs)
    qkv = dot(x_ref[...], wqkv_ref[...], 1, 0)
    rotated = (qkv * cosine + shuffle_halves(qkv) * sine).astype(LOW)
    queries, both = rotated[:, : pairs * 128], rotated[:, pairs * 128 :]
    q_ref[...] = queries
    kv_ref[...] = both
    keys, values = split_kv(both)
    allowed = allowed_pairs(col_ref[...], row_ref[0])
    lane = lanes_of((both.shape[0], 128))
    log_sums = jnp.zeros((both.shape[0], 128), F32)
    contexts = []
    for pair in range(pairs):
        heads = queries[:, pair * 128 : (pair + 1) * 128]
        context = None
        for side in range(2):
            scores = dot(heads, keys[side], 1, 1) * HD**-0.5
            masked = jnp.where(allowed, scores, -1e30)
            top = jnp.max(masked, axis=1, keepdims=True)
            weights = jnp.exp(masked - top)
            totals = jnp.sum(weights, axis=1, keepdims=True)
            probs = (weights * (1.0 / totals)).astype(LOW)
            piece = dot(probs, values[side], 1, 0)
            context = piece if context is None else context + piece
            log_sums = jnp.where(lane == 2 * pair + side, top + jnp.log(totals), log_sums)
        contexts.append(context.astype(LOW))
    lse_ref[...] = log_sums
    context_low = cat(contexts, 1)
    ctx_ref[...] = context_low
    part_ref[...] = dot(context_low, wout_ref[...], 1, 0).astype(LOW)


def attn_backward_kernel(pairs, loader, *refs):
    weights, refs = refs[: loader.count], refs[loader.count :]
    cg_ref, x_ref, q_ref, kv_ref, lse_ref, cos_ref, sin_ref, col_ref, row_ref = refs[:9]
    part_ref, gain_ref, *grad_refs = refs[9:-4]
    wqkv_ref, wout_ref, sems, acc_qkv = refs[-4:]
    step = pl.program_id(0)

    @pl.when(step == 0)
    def _():
        loader.load(weights, wqkv_ref, wout_ref, sems)
        acc_qkv[...] = jnp.zeros_like(acc_qkv)

    cosine, sine = tables(cos_ref, sin_ref, pairs)
    scale = HD**-0.5
    ctx_grad = cg_ref[...]
    keys, values = split_kv(kv_ref[...])
    allowed = allowed_pairs(col_ref[...], row_ref[0])
    lane = lanes_of((ctx_grad.shape[0], 128))
    log_sums = lse_ref[...]
    query_grads, key_grad, value_grad = [], None, None
    for pair in range(pairs):
        heads = q_ref[:, pair * 128 : (pair + 1) * 128]
        grads = ctx_grad[:, pair * 128 : (pair + 1) * 128]
        query_grad = None
        for side in range(2):
            here = (lane < HD) if side == 0 else (lane >= HD)
            head = jnp.where(here, heads, jnp.zeros_like(heads))
            grad = jnp.where(here, grads, jnp.zeros_like(grads))
            at = 2 * pair + side
            scores = dot(heads, keys[side], 1, 1) * scale
            probs = jnp.where(allowed, jnp.exp(scores - log_sums[:, at : at + 1]), 0.0)
            prob_grad = dot(grads, values[side], 1, 1)
            delta = jnp.sum(probs * prob_grad, axis=1, keepdims=True)
            score_grad = (probs * (prob_grad - delta)).astype(LOW)
            to_value = dot(probs.astype(LOW), grad, 0, 0)
            to_key = dot(score_grad, head, 0, 0)
            to_query = dot(score_grad, keys[side], 1, 0)
            value_grad = to_value if value_grad is None else value_grad + to_value
            key_grad = to_key if key_grad is None else key_grad + to_key
            query_grad = to_query if query_grad is None else query_grad + to_query
        query_grads.append(query_grad * scale)
    key_grad = (key_grad + pltpu.roll(key_grad, HD, 1)) * scale
    value_grad = value_grad + pltpu.roll(value_grad, HD, 1)
    joined = cat(query_grads + [jnp.where(lane < HD, key_grad, value_grad)], 1)
    low = (joined * cosine - shuffle_halves(joined) * sine).astype(LOW)
    part_ref[...] = dot(low, wqkv_ref[...], 1, 1).astype(LOW)
    acc_qkv[...] += dot(x_ref[...], low, 0, 0)

    @pl.when(step == pl.num_programs(0) - 1)
    def _():
        cut = acc_qkv.shape[0] // len(grad_refs)
        for i, out in enumerate(grad_refs):
            out[...] = acc_qkv[i * cut : (i + 1) * cut, :].astype(LOW)
        gain_ref[...] = jnp.sum(acc_qkv[...] * wqkv_ref[...].astype(F32), axis=1, keepdims=True)


def once(shape):
    return pl.BlockSpec(shape, lambda i: (0,) * len(shape), pipeline_mode=pl.Buffered(1))


def per_seq(shape):
    return pl.BlockSpec(shape, lambda i: (i,) + (0,) * (len(shape) - 1))


def attn_forward(loader, normed, cosine, sine, seg_col, seg_row):
    rows, width = normed.shape
    heads = loader.col_shape[0]
    return pl.pallas_call(
        functools.partial(attn_forward_kernel, heads // 128, loader),
        grid=(rows // LEN,),
        in_specs=[
            *loader.specs(),
            per_seq((LEN, width)),
            per_seq((LEN, 128)),
            per_seq((LEN, 128)),
            per_seq((LEN, 1)),
            per_seq((1, 1, LEN)),
        ],
        out_specs=[
            per_seq((LEN, width)),
            per_seq((LEN, heads)),
            per_seq((LEN, heads)),
            per_seq((LEN, 128)),
            per_seq((LEN, 128)),
            once(loader.col_shape),
        ],
        out_shape=[
            jax.ShapeDtypeStruct((rows, width), LOW),
            jax.ShapeDtypeStruct((rows, heads), LOW),
            jax.ShapeDtypeStruct((rows, heads), LOW),
            jax.ShapeDtypeStruct((rows, 128), LOW),
            jax.ShapeDtypeStruct((rows, 128), F32),
            jax.ShapeDtypeStruct(loader.col_shape, LOW),
        ],
        scratch_shapes=loader.scratch(),
        compiler_params=pltpu.CompilerParams(vmem_limit_bytes=48 * MIB),
        cost_estimate=SMALL,
        name="attn_forward",
    )(*loader.operands, normed, cosine, sine, seg_col, seg_row)


def attn_backward(loader, ctx_grad, normed, queries, both, lse, cosine, sine, seg_col, seg_row):
    rows, width = normed.shape
    heads = loader.col_shape[0]
    cuts = loader.plan.cuts
    grad = (width // cuts, loader.row_shape[1])
    return pl.pallas_call(
        functools.partial(attn_backward_kernel, heads // 128, loader),
        grid=(rows // LEN,),
        in_specs=[
            *loader.specs(),
            per_seq((LEN, heads)),
            per_seq((LEN, width)),
            per_seq((LEN, heads)),
            per_seq((LEN, 128)),
            per_seq((LEN, 128)),
            per_seq((LEN, 128)),
            per_seq((LEN, 128)),
            per_seq((LEN, 1)),
            per_seq((1, 1, LEN)),
        ],
        out_specs=[per_seq((LEN, width)), once((width, 1))] + [once(grad)] * cuts,
        out_shape=[
            jax.ShapeDtypeStruct((rows, width), LOW),
            jax.ShapeDtypeStruct((width, 1), F32),
        ]
        + [jax.ShapeDtypeStruct(grad, LOW)] * cuts,
        scratch_shapes=[*loader.scratch(), pltpu.VMEM(loader.row_shape, F32)],
        compiler_params=pltpu.CompilerParams(vmem_limit_bytes=52 * MIB),
        cost_estimate=SMALL,
        name="attn_backward",
    )(*loader.operands, ctx_grad, normed, queries, both, lse, cosine, sine, seg_col, seg_row)


def out_weights_kernel(ctx_ref, res_ref, *refs):
    grad_refs, acc = refs[:-1], refs[-1]
    step = pl.program_id(0)

    @pl.when(step == 0)
    def _():
        acc[...] = jnp.zeros_like(acc)

    acc[...] += dot(ctx_ref[...], res_ref[...], 0, 0)

    @pl.when(step == pl.num_programs(0) - 1)
    def _():
        cut = acc.shape[1] // len(grad_refs)
        for i, out in enumerate(grad_refs):
            out[...] = acc[:, i * cut : (i + 1) * cut].astype(LOW)


def out_weights(plan, ctx, res_all):
    rows, width = res_all.shape
    heads = ctx.shape[1]
    grad = (heads, width // plan.cuts)
    return pl.pallas_call(
        out_weights_kernel,
        grid=(rows // LEN,),
        in_specs=[per_seq((LEN, heads)), per_seq((LEN, width))],
        out_specs=[once(grad)] * plan.cuts,
        out_shape=[jax.ShapeDtypeStruct(grad, LOW)] * plan.cuts,
        scratch_shapes=[pltpu.VMEM((heads, width), F32)],
        compiler_params=pltpu.CompilerParams(vmem_limit_bytes=40 * MIB),
        cost_estimate=SMALL,
        name="out_weights",
    )(ctx, res_all)


def residual_backward_kernel(
    back_ref, residual_ref, scale_ref, gain_ref, grad_ref, wout_ref, res_grad_ref, low_ref, ctx_ref
):
    @pl.when(pl.program_id(0) == 0)
    def _():
        back = norm_back(
            back_ref[...].astype(F32), residual_ref[...], scale_ref[...], gain_ref[...]
        )
        total = grad_ref[...].astype(F32) + back
        res_grad_ref[...] = total
        low_ref[...] = total.astype(LOW)

    ctx_ref[...] = dot(low_ref[...], wout_ref[...], 1, 1).astype(LOW)


def residual_backward(back_sum, residual, scale, gain, grad_low, wout_all):
    rows, width = residual.shape
    heads = wout_all.shape[0]
    step = 512
    return pl.pallas_call(
        residual_backward_kernel,
        grid=(heads // step,),
        in_specs=[
            once((rows, width)),
            once((rows, width)),
            once((rows, 1)),
            once((1, width)),
            once((rows, width)),
            per_seq((step, width)),
        ],
        out_specs=[
            once((rows, width)),
            once((rows, width)),
            pl.BlockSpec((rows, step), lambda i: (0, i)),
        ],
        out_shape=[
            jax.ShapeDtypeStruct((rows, width), F32),
            jax.ShapeDtypeStruct((rows, width), LOW),
            jax.ShapeDtypeStruct((rows, heads), LOW),
        ],
        compiler_params=pltpu.CompilerParams(vmem_limit_bytes=40 * MIB),
        cost_estimate=SMALL,
        name="residual_backward",
    )(back_sum, residual, scale, gain[None, :], grad_low, wout_all)


TILE = 512


def ffn_main_kernel(loader, more, *refs):
    weights, refs = refs[: loader.count], refs[loader.count :]
    x_ref, grad_ref = refs[:2]
    back_ref, act_ref, both_ref, gate_up_ref, down_ref, sems = refs[2 + more :]

    @pl.when(pl.program_id(0) == 0)
    def _():
        loader.load(weights, gate_up_ref, down_ref, sems)

    hidden = down_ref.shape[0]
    pre = dot(x_ref[...], gate_up_ref[...], 1, 0)
    gate_pre, lifted = pre[:, :hidden], pre[:, hidden:]
    sigmoid_gate = jax.nn.sigmoid(gate_pre)
    silu_gate = gate_pre * sigmoid_gate
    act_ref[...] = (silu_gate * lifted).astype(LOW)
    act_grad = dot(grad_ref[...], down_ref[...], 1, 1)
    gate_grad = act_grad * lifted * sigmoid_gate * (1.0 + gate_pre * (1.0 - sigmoid_gate))
    both_grad = cat([gate_grad.astype(LOW), (act_grad * silu_gate).astype(LOW)], 1)
    both_ref[...] = both_grad
    back = dot(both_grad, gate_up_ref[...], 1, 1)
    if more:
        back = back + refs[2][...].astype(F32)
    back_ref[...] = back.astype(LOW)


def ffn_main(loader, tokens, grads, earlier):
    rows, width = tokens.shape
    hidden = loader.col_shape[0]
    more = [] if earlier is None else [earlier]
    return pl.pallas_call(
        functools.partial(ffn_main_kernel, loader, len(more)),
        grid=(rows // TILE,),
        in_specs=[
            *loader.specs(),
            per_seq((TILE, width)),
            per_seq((TILE, width)),
            *[per_seq((TILE, width))] * len(more),
        ],
        out_specs=[
            per_seq((TILE, width)),
            per_seq((TILE, hidden)),
            per_seq((TILE, 2 * hidden)),
        ],
        out_shape=[
            jax.ShapeDtypeStruct((rows, width), LOW),
            jax.ShapeDtypeStruct((rows, hidden), LOW),
            jax.ShapeDtypeStruct((rows, 2 * hidden), LOW),
        ],
        scratch_shapes=loader.scratch(),
        compiler_params=pltpu.CompilerParams(vmem_limit_bytes=58 * MIB),
        cost_estimate=SMALL,
        name="ffn_main",
    )(*loader.operands, tokens, grads, *more)


def ffn_weights_kernel(loader, more, *refs):
    weights, refs = refs[: loader.count], refs[loader.count :]
    x_ref, grad_ref, act_ref, both_ref = refs[:4]
    out_ref, gain_ref, *grad_refs = refs[4 + more : -5]
    gate_up_ref, down_ref, sems, acc_gate_up, acc_down = refs[-5:]
    step = pl.program_id(0)

    @pl.when(step == 0)
    def _():
        loader.load(weights, gate_up_ref, down_ref, sems)
        acc_gate_up[...] = jnp.zeros_like(acc_gate_up)
        acc_down[...] = jnp.zeros_like(acc_down)

    act = act_ref[...]
    acc_down[...] += dot(act, grad_ref[...], 0, 0)
    acc_gate_up[...] += dot(x_ref[...], both_ref[...], 0, 0)
    out = dot(act, down_ref[...], 1, 0)
    if more:
        out = out + refs[4][...].astype(F32)
    out_ref[...] = out.astype(LOW)

    @pl.when(step == pl.num_programs(0) - 1)
    def _():
        pack_grads(loader.plan, acc_gate_up, acc_down, grad_refs)
        gain_ref[...] = jnp.sum(
            acc_gate_up[...] * gate_up_ref[...].astype(F32), axis=1, keepdims=True
        )


def ffn_weights(loader, tokens, grads, act, both_grad, earlier):
    rows, width = tokens.shape
    hidden = loader.col_shape[0]
    more = [] if earlier is None else [earlier]
    packed = packed_shapes(loader.plan, loader.row_shape, loader.col_shape)
    return pl.pallas_call(
        functools.partial(ffn_weights_kernel, loader, len(more)),
        grid=(rows // TILE,),
        in_specs=[
            *loader.specs(),
            per_seq((TILE, width)),
            per_seq((TILE, width)),
            per_seq((TILE, hidden)),
            per_seq((TILE, 2 * hidden)),
            *[per_seq((TILE, width))] * len(more),
        ],
        out_specs=[per_seq((TILE, width)), once((width, 1))] + [once(shape) for shape in packed],
        out_shape=[
            jax.ShapeDtypeStruct((rows, width), LOW),
            jax.ShapeDtypeStruct((width, 1), F32),
        ]
        + [jax.ShapeDtypeStruct(shape, LOW) for shape in packed],
        scratch_shapes=[
            *loader.scratch(),
            pltpu.VMEM(loader.row_shape, F32),
            pltpu.VMEM(loader.col_shape, F32),
        ],
        compiler_params=pltpu.CompilerParams(vmem_limit_bytes=60 * MIB),
        cost_estimate=SMALL,
        name="ffn_weights",
    )(*loader.operands, tokens, grads, act, both_grad, *more)


def norm_rows(values, gain_vec):
    row_scale = lax.rsqrt(jnp.mean(values * values, axis=1, keepdims=True) + NORM_EPS)
    return values * row_scale * gain_vec, row_scale


def norm_back(row_grad, values, row_scale, gain_vec):
    scaled_grad = row_grad * gain_vec
    return row_scale * scaled_grad - values * row_scale**3 * jnp.mean(
        scaled_grad * values, axis=1, keepdims=True
    )


def adamw_update(master, grad_sum, first_mom, second_mom, decay_rate, step_rate):
    next_first = BETA_ONE * first_mom + (1.0 - BETA_ONE) * grad_sum
    next_second = BETA_TWO * second_mom + (1.0 - BETA_TWO) * grad_sum * grad_sum
    first_hat = next_first / (1.0 - BETA_ONE**STEP)
    second_hat = next_second / (1.0 - BETA_TWO**STEP)
    next_master = master - step_rate * (
        first_hat / (jnp.sqrt(second_hat) + ADAM_EPS) + decay_rate * master
    )
    return (next_master, next_first, next_second)


def sum_everywhere(values, sizes):
    for axis, size in sizes:
        step = 1
        while step < size:
            values = values + lax.ppermute(values, axis, [(i, i ^ step) for i in range(size)])
            step *= 2
    return values


def pick(index, low, high):
    return jnp.where(index == 0, low, high)


class Plane:
    def __init__(self, tp):
        self.tp = tp
        self.half = tp // 2
        self.x = lax.axis_index("di")
        self.y = lax.axis_index("tp") // self.half
        self.far = [(i, (i + self.half) % tp) for i in range(tp)]

    def swap_y(self, value):
        return lax.ppermute(value, "tp", self.far)

    def swap_x(self, value):
        return lax.ppermute(value, "di", PAIR)

    def swap_core(self, value):
        return lax.ppermute(value, "tp", [(i, i ^ 1) for i in range(self.tp)])


def on_device(
    sizes,
    layer_input, out_grad, segment_ids, positions,
    w_query, w_key, w_value, w_out, w_gate, w_up, w_down,
    m_query, m_key, m_value, m_out, m_gate, m_up, m_down,
    v_query, v_key, v_value, v_out, v_gate, v_up, v_down,
    gain_attn, gain_ffn, m_gain_attn, m_gain_ffn, v_gain_attn, v_gain_ffn,
):
    width = layer_input.shape[1]
    plan = Plan(sizes["do"], w_query.shape[0])
    by_x = plan.by_x
    axes = ("di", "tp")
    plane = Plane(sizes["tp"])

    gain_one, gain_two = plan.reorder(gain_attn), plan.reorder(gain_ffn)
    inputs_f = plan.reorder(layer_input).astype(F32)
    grad_low = plan.reorder(out_grad)
    normed, scale_one = norm_rows(inputs_f, gain_one)
    normed_all = lax.all_gather(normed.astype(LOW), axes, axis=0, tiled=True)

    marks = cat([segment_ids[None, :], positions[None, :]], 0)
    marks_other = lax.ppermute(marks, "di", PAIR)
    marks_all = cat([by_x(marks, marks_other), by_x(marks_other, marks)], 1)
    seg_all, pos_all = marks_all[0], marks_all[1]
    rows = seg_all.shape[0]
    seqs = rows // LEN
    seg_col, seg_row = seg_all.reshape(rows, 1), seg_all.reshape(seqs, 1, LEN)
    cosine, sine = rope_tables(pos_all)

    def col_halves(weight):
        half = weight.shape[1] // 2
        low = weight.astype(LOW)
        return by_x(low[:, :half], low[:, half:]), by_x(low[:, half:], low[:, :half])

    def row_halves(weight):
        half = weight.shape[0] // 2
        low = weight.astype(LOW)
        return by_x(low[:half], low[half:]), by_x(low[half:], low[:half])

    def col_cut(pair, chunk):
        size = pair[0].shape[1] // CHUNKS
        return tuple(part[:, chunk * size : (chunk + 1) * size] for part in pair)

    def row_cut(pair, chunk):
        size = pair[0].shape[0] // CHUNKS
        return tuple(part[chunk * size : (chunk + 1) * size] for part in pair)

    halves_q, halves_k, halves_v = col_halves(w_query), col_halves(w_key), col_halves(w_value)
    qkv_parts = tuple(cat([q, k, v], 1) for q, k, v in zip(halves_q, halves_k, halves_v))
    out_parts = row_halves(w_out)
    halves_g, halves_u, halves_d = col_halves(w_gate), col_halves(w_up), row_halves(w_down)

    def ffn_parts(chunk):
        gate_up = tuple(
            cat([g, u], 1) for g, u in zip(col_cut(halves_g, chunk), col_cut(halves_u, chunk))
        )
        return gate_up, row_cut(halves_d, chunk)

    hidden = halves_d[0].shape[0] // CHUNKS
    attn_shapes = (width, qkv_parts[0].shape[1]), (out_parts[0].shape[0], width)
    ffn_shapes = (width, 2 * hidden), (hidden, width)
    own_rows = layer_input.shape[0]
    core = lax.axis_index("tp") % 2

    if plan.line:
        attn_own, attn_other = plan.pack(qkv_parts, out_parts)
        own_1, other_1 = plan.pack(*ffn_parts(0))
        own_2, other_2 = plan.pack(*ffn_parts(1))
        attn_theirs = plan.swap(attn_other)
        attn_theirs, marks_all = fence(attn_theirs, marks_all)
        attn_block = plan.join(attn_own, attn_theirs)
        near, across = line_near(attn_block)
        theirs_1 = plan.swap(other_1)
        near, across, theirs_1 = fence(near, across, theirs_1)
        across_near, out = line_far(near, across)
        theirs_2 = plan.swap(other_2)
        block_1 = plan.join(own_1, theirs_1)
        across_near, out, theirs_2, block_1 = fence(across_near, out, theirs_2, block_1)
        out_near = line_last(across_near)
        block_2 = plan.join(own_2, theirs_2)
        out_near, normed_all, cosine, sine, block_1, block_2 = fence(
            out_near, normed_all, cosine, sine, block_1, block_2
        )
        attn_weights = (attn_block, near, across_near, out, across, out_near)
        near_1, across_1 = line_near(block_1)
    else:
        attn_weights = plan.plain_gather(qkv_parts, out_parts)
        first_weights = plan.plain_gather(*ffn_parts(0))
        second_weights = plan.plain_gather(*ffn_parts(1))
    attn_loader = Loader(plan, attn_weights, *attn_shapes)

    attn_part, ctx, queries, both, lse, wout = attn_forward(
        attn_loader, normed_all, cosine, sine, seg_col, seg_row
    )
    grad_y, grad_x = plane.swap_y(grad_low), plane.swap_x(grad_low)
    if plan.line:
        attn_part, near_1, across_1, grad_y, grad_x = fence(
            attn_part, near_1, across_1, grad_y, grad_x
        )
        across_near_1, out_1 = line_far(near_1, across_1)
    attn_sum = lax.psum_scatter(attn_part, axes, scatter_dimension=0, tiled=True)
    grad_xy = plane.swap_x(grad_y)
    if plan.line:
        across_near_1, out_1, grad_xy, block_2 = fence(across_near_1, out_1, grad_xy, block_2)
        out_near_1 = line_last(across_near_1)
        across_2 = lax.ppermute(block_2, "do", MIDDLE)
    over_y = cat([pick(plane.y, grad_low, grad_y), pick(plane.y, grad_y, grad_low)], 0)
    over_xy = cat([pick(plane.y, grad_x, grad_xy), pick(plane.y, grad_xy, grad_x)], 0)
    grad_core = cat([by_x(over_y, over_xy), by_x(over_xy, over_y)], 0)
    grad_other = plane.swap_core(grad_core)
    groups = (rows // own_rows // 2, 1, own_rows, width)
    mine, theirs = grad_core.reshape(groups), grad_other.reshape(groups)
    grad_all = cat([pick(core, mine, theirs), pick(core, theirs, mine)], 1).reshape(rows, width)

    if plan.line:
        attn_sum, out_near_1, across_2, grad_all, block_2 = fence(
            attn_sum, out_near_1, across_2, grad_all, block_2
        )
        first_weights = (block_1, near_1, across_near_1, out_1, across_1, out_near_1)
        near_2 = lax.ppermute(block_2, "do", NEAR)
    residual = inputs_f + attn_sum.astype(F32)
    normed_two, scale_two = norm_rows(residual, gain_two)
    two_all = lax.all_gather(normed_two.astype(LOW), axes, axis=0, tiled=True)

    if plan.line:
        near_2, across_2 = fence(near_2, across_2)
        across_near_2, out_2 = line_far(near_2, across_2)
    first = Loader(plan, first_weights, *ffn_shapes)
    back_1, act_1, both_1 = ffn_main(first, two_all, grad_all, None)
    two_all, wout = fence(two_all, wout)
    wout_all = lax.all_gather(wout, axes, axis=0, tiled=True)
    if plan.line:
        back_1, act_1, both_1, across_near_2, out_2 = fence(
            back_1, act_1, both_1, across_near_2, out_2
        )
        out_near_2 = line_last(across_near_2)
    out_1_part, gain_1, *grads_1 = ffn_weights(first, two_all, grad_all, act_1, both_1, None)
    if plan.line:
        back_1, out_1_part, grads_1, out_near_2 = fence(back_1, out_1_part, grads_1, out_near_2)
        second_weights = (block_2, near_2, across_near_2, out_2, across_2, out_near_2)
        far_1 = sum_far(grads_1)
    second = Loader(plan, second_weights, *ffn_shapes)
    back_2, act_2, both_2 = ffn_main(second, two_all, grad_all, back_1)
    if plan.line:
        back_2, act_2, both_2, far_1, wout_all = fence(back_2, act_2, both_2, far_1, wout_all)
        crossed_1, inward_1 = sum_middle(grads_1, far_1)
    back_sum = lax.psum_scatter(back_2, axes, scatter_dimension=0, tiled=True)
    out_2_part, gain_2, *grads_2 = ffn_weights(second, two_all, grad_all, act_2, both_2, out_1_part)
    if plan.line:
        out_2_part, grads_2, crossed_1, inward_1 = fence(out_2_part, grads_2, crossed_1, inward_1)
        near_sum_1, across_sum_1 = sum_near(grads_1, crossed_1, inward_1)
        far_2 = sum_far(grads_2)
        back_sum, near_sum_1, across_sum_1 = fence(back_sum, near_sum_1, across_sum_1)

    out_shape = (rows // own_rows // 2, 2, own_rows, width)
    parts = out_2_part.reshape(out_shape)
    mine, theirs = pick(core, parts[:, 0], parts[:, 1]), pick(core, parts[:, 1], parts[:, 0])
    summed = add(mine, plane.swap_core(theirs)).astype(LOW)
    low, high = summed[: out_shape[0] // 2], summed[out_shape[0] // 2 :]
    summed = add(by_x(low, high), plane.swap_x(by_x(high, low))).astype(LOW)
    low, high = summed[: summed.shape[0] // 2], summed[summed.shape[0] // 2 :]
    summed = add(pick(plane.y, low, high), plane.swap_y(pick(plane.y, high, low)))
    out_value = (residual + summed.reshape(own_rows, width)).astype(LOW)

    residual_grad, res_low, ctx_grad = residual_backward(
        back_sum, residual, scale_two, gain_two, grad_low, wout_all
    )
    res_all = lax.all_gather(res_low, axes, axis=0, tiled=True)
    ctx_grad = lax.all_to_all(ctx_grad, axes, split_axis=1, concat_axis=0, tiled=True)
    if plan.line:
        ctx_grad, far_2 = fence(ctx_grad, far_2)
        crossed_2, inward_2 = sum_middle(grads_2, far_2)
    back_one_part, gain_one_part, *grads_qkv = attn_backward(
        attn_loader, ctx_grad, normed_all, queries, both, lse, cosine, sine, seg_col, seg_row
    )
    if plan.line:
        back_one_part, grads_qkv, crossed_2, inward_2 = fence(
            back_one_part, grads_qkv, crossed_2, inward_2
        )
    back_one = lax.psum_scatter(back_one_part, axes, scatter_dimension=0, tiled=True)
    grads_out = out_weights(plan, ctx, res_all)
    if plan.line:
        direct_qkv = send_direct(grads_qkv)
        gain_one_part, *direct_qkv = fence(gain_one_part, *direct_qkv)
        direct_out = send_direct(grads_out)
        near_sum_2, across_sum_2 = sum_near(grads_2, crossed_2, inward_2)
        total = add(grads_qkv[0], *direct_qkv)
        half = plan.rows
        qkv_pair = plan.trade(total[:half], total[half:])
        total = add(grads_out[0], *direct_out)
        out_pair = plan.trade(total[:, :half], total[:, half:])
        total_1 = sum_own(grads_1, near_sum_1, across_sum_1)
        total_2 = sum_own(grads_2, near_sum_2, across_sum_2)
        ffn_grads = [plan.unpack(each, 2 * hidden) for each in (total_1, total_2)]
    else:
        qkv_pair = plan.plain_sum_row(grads_qkv[0])
        out_pair = plan.plain_sum_col(grads_out[0])
        ffn_grads = [
            (plan.plain_sum_row(row), plan.plain_sum_col(col)) for row, col in (grads_1, grads_2)
        ]
    in_grad = residual_grad + norm_back(back_one.astype(F32), inputs_f, scale_one, gain_one)

    gain_parts = jnp.stack(
        [gain_one_part[:, 0] / gain_one, (gain_1[:, 0] + gain_2[:, 0]) / gain_two]
    )
    gain_sums = sum_everywhere(plan.reorder(gain_parts), list(sizes.items()))
    grad_gain_attn, grad_gain_ffn = gain_sums[0], gain_sums[1]

    def join(pair, axis):
        own, other = pair
        return by_x(cat([own, other], axis), cat([other, own], axis))

    def from_chunks(pairs, axis):
        own = cat([pair[0] for pair in pairs], axis)
        other = cat([pair[1] for pair in pairs], axis)
        return join((own, other), axis)

    def cut(pair, start, stop):
        return tuple(part[:, start:stop] for part in pair)

    at_k = halves_q[0].shape[1]
    at_v = at_k + halves_k[0].shape[1]
    end = at_v + halves_v[0].shape[1]
    grad_query = join(cut(qkv_pair, 0, at_k), 1)
    grad_key = join(cut(qkv_pair, at_k, at_v), 1)
    grad_value = join(cut(qkv_pair, at_v, end), 1)
    grad_out = join(out_pair, 0)
    grad_gate = from_chunks([cut(gu, 0, hidden) for gu, _ in ffn_grads], 1)
    grad_up = from_chunks([cut(gu, hidden, 2 * hidden) for gu, _ in ffn_grads], 1)
    grad_down = from_chunks([down for _, down in ffn_grads], 0)

    grads = (grad_query, grad_key, grad_value, grad_out, grad_gate, grad_up, grad_down)
    masters = (w_query, w_key, w_value, w_out, w_gate, w_up, w_down)
    firsts = (m_query, m_key, m_value, m_out, m_gate, m_up, m_down)
    seconds = (v_query, v_key, v_value, v_out, v_gate, v_up, v_down)
    updated = [
        adamw_update(w, g, m, v, WEIGHT_DECAY, LEARN_RATE)
        for w, g, m, v in zip(masters, grads, firsts, seconds)
    ]
    gain_updated = [
        adamw_update(gain_attn, grad_gain_attn, m_gain_attn, v_gain_attn, 0.0, GAIN_RATE),
        adamw_update(gain_ffn, grad_gain_ffn, m_gain_ffn, v_gain_ffn, 0.0, GAIN_RATE),
    ]
    return (
        plan.reorder(out_value),
        plan.reorder(in_grad),
        *grads,
        *[u[0] for u in updated],
        *[u[1] for u in updated],
        *[u[2] for u in updated],
        grad_gain_attn,
        grad_gain_ffn,
        *[u[0] for u in gain_updated],
        *[u[1] for u in gain_updated],
        *[u[2] for u in gain_updated],
    )


def solution(mesh):
    dp, tp = mesh.shape["dp"], mesh.shape["tp"]
    split = Mesh(mesh.devices.reshape(dp // 2, 2, tp), ("do", "di", "tp"))
    sizes = {"do": dp // 2, "di": 2, "tp": tp}
    dp_axes = ("do", "di")
    tokens = P(("do", "di", "tp"), None)
    by_rows, by_cols = P(dp_axes, "tp"), P("tp", dp_axes)
    weights = (by_rows, by_rows, by_rows, by_cols, by_rows, by_rows, by_cols)
    gains = (P(),) * 6
    in_specs = (tokens, tokens, P(dp_axes), P(dp_axes)) + weights * 3 + gains
    out_specs = (tokens, tokens) + weights * 4 + (P(),) * 2 + gains
    return jax.shard_map(
        functools.partial(on_device, sizes),
        mesh=split,
        in_specs=in_specs,
        out_specs=out_specs,
        check_vma=False,
    )
```

```python
import functools

import jax
import jax.numpy as jnp
from jax import lax
from jax.experimental import pallas as pl
from jax.experimental.pallas import tpu as pltpu
from jax.sharding import Mesh
from jax.sharding import PartitionSpec as P

HD = 64
LEN = 512
STEP = 5
CHUNKS = 2

NORM_EPS = 1e-05
ROPE_BASE = 500000.0
BETA_ONE = 0.9
BETA_TWO = 0.95
LEARN_RATE = 0.02
GAIN_RATE = 0.5
WEIGHT_DECAY = 0.1
ADAM_EPS = 1e-08

LOW = jnp.bfloat16
F32 = jnp.float32
MIB = 1024 * 1024

NEAR = [(0, 1), (1, 0), (2, 3), (3, 2)]
MIDDLE = [(1, 2), (2, 1)]
CROSS = [(0, 2), (1, 3), (2, 0), (3, 1)]
MIRROR = [(0, 3), (1, 2), (2, 1), (3, 0)]
PAIR = [(0, 1), (1, 0)]


def dot(lhs, rhs, lhs_dim, rhs_dim):
    return lax.dot_general(
        lhs, rhs, (((lhs_dim,), (rhs_dim,)), ((), ())), preferred_element_type=F32
    )


def cat(parts, axis):
    return jnp.concatenate(parts, axis)


def fence(*values):
    return lax.optimization_barrier(values)


def line_near(own):
    return lax.ppermute(own, "do", NEAR), lax.ppermute(own, "do", MIDDLE)


def line_far(near, across):
    return lax.ppermute(near, "do", MIDDLE), lax.ppermute(across, "do", NEAR)


def line_last(across_near):
    return lax.ppermute(across_near, "do", NEAR)


def add(part, *arrived):
    total = part.astype(F32)
    for piece in arrived:
        total = total + piece.astype(F32)
    return total


def is_inner():
    place = lax.axis_index("do")
    return (place == 1) | (place == 2)


def add_inner(part, arrived):
    return add(part, jnp.where(is_inner(), arrived, jnp.zeros_like(arrived)))


def sum_far(parts):
    return lax.ppermute(parts[3], "do", NEAR)


def sum_middle(parts, far):
    second = add_inner(parts[2], far).astype(LOW)
    return lax.ppermute(second, "do", MIDDLE), lax.ppermute(second, "do", NEAR)


def sum_near_parts(parts, crossed, inward):
    return add_inner(parts[1], crossed).astype(LOW), add_inner(parts[3], inward).astype(LOW)


def sum_near_send(first, third):
    return lax.ppermute(first, "do", NEAR), lax.ppermute(third, "do", MIDDLE)


def sum_own(parts, from_near, from_across):
    return add_inner(parts[0], from_across) + from_near.astype(F32)


def send_direct(parts):
    return [
        lax.ppermute(part, "do", perm) for part, perm in zip(parts[1:], (NEAR, CROSS, MIRROR))
    ]


class Plan:
    def __init__(self, outer, per_device):
        self.rows = per_device
        self.block = 2 * per_device
        self.line = outer == 4 and per_device == 256
        self.cuts = 4 if self.line else 1

    def reorder(self, values):
        if not self.line:
            return values
        place = lax.axis_index("do")
        quarter = values.shape[-1] // 4
        a, b, c, d = (values[..., i * quarter : (i + 1) * quarter] for i in range(4))
        values = jnp.where(place % 2 == 1, cat([b, a, d, c], -1), values)
        half = 2 * quarter
        turned = cat([values[..., half:], values[..., :half]], -1)
        return jnp.where(place >= 2, turned, values)

    def by_x(self, low, high):
        return jnp.where(lax.axis_index("di") == 0, low, high)

    def inner(self):
        return is_inner().astype(jnp.int32).reshape(1)

    def pack(self, row_part, col_part):
        rows, packs = self.rows, []
        for row_side, side in zip(row_part, col_part):
            pieces = [side[i : i + rows] for i in range(0, side.shape[0], rows)]
            packs.append(cat([row_side] + pieces, 1))
        return packs

    def swap(self, other):
        return lax.ppermute(other, "di", PAIR)

    def join(self, own, theirs, axis=0):
        return cat([self.by_x(own, theirs), self.by_x(theirs, own)], axis)

    def plain_gather(self, row_part, col_part):
        full = []
        for (own, other), axis in ((row_part, 0), (col_part, 1)):
            block = self.join(own, self.swap(other), axis)
            full.append(lax.all_gather(block, "do", axis=axis, tiled=True))
        return tuple(full)

    def unpack(self, total, wide):
        rows = self.rows
        mine, theirs = self.trade(total[:rows], total[rows:])
        cuts = range(wide, total.shape[1], rows)
        return (
            (mine[:, :wide], theirs[:, :wide]),
            tuple(cat([side[:, i : i + rows] for i in cuts], 0) for side in (mine, theirs)),
        )

    def plain_sum_row(self, grad):
        total = lax.psum_scatter(grad, "do", scatter_dimension=0, tiled=True)
        return self.trade(total[: self.rows], total[self.rows :])

    def plain_sum_col(self, grad):
        total = lax.psum_scatter(grad, "do", scatter_dimension=1, tiled=True)
        return self.trade(total[:, : self.rows], total[:, self.rows :])

    def trade(self, low, high):
        mine = self.by_x(low, high).astype(F32)
        theirs = lax.ppermute(self.by_x(high, low).astype(LOW), "di", PAIR)
        return mine, theirs.astype(F32)


ANY = pl.BlockSpec(memory_space=pl.ANY)
SMALL = pl.CostEstimate(flops=1, bytes_accessed=1, transcendentals=0)


class Loader:
    def __init__(self, plan, weights, row_shape, col_shape):
        self.plan, self.row_shape, self.col_shape = plan, row_shape, col_shape
        rows, wide = plan.rows, row_shape[1]
        self.moves = []
        if plan.line:
            self.operands = [plan.inner(), *weights]
            for k in range(4):
                at = k * plan.block
                self.moves.append((k, 0, (0, 0), (at, 0), (plan.block, wide)))
                for i in range(0, col_shape[0], rows):
                    for x in range(2):
                        self.moves.append(
                            (k, 1, (x * rows, wide + i), (i, at + x * rows), (rows, rows))
                        )
        else:
            self.operands = list(weights)
            self.moves.append((0, 0, (0, 0), (0, 0), row_shape))
            self.moves.append((1, 1, (0, 0), (0, 0), col_shape))
        self.count = len(self.operands)

    def specs(self):
        if not self.plan.line:
            return [ANY] * 2
        return [pl.BlockSpec(memory_space=pltpu.SMEM)] + [ANY] * 6

    def scratch(self):
        return [
            pltpu.VMEM(self.row_shape, LOW),
            pltpu.VMEM(self.col_shape, LOW),
            pltpu.SemaphoreType.DMA((len(self.moves),)),
        ]

    def load(self, refs, row_ref, col_ref, sems):
        def copies(sources, chosen):
            made = []
            for i, (k, which, here, there, size) in enumerate(self.moves):
                if k in chosen:
                    target = (row_ref, col_ref)[which]
                    made.append(
                        pltpu.make_async_copy(
                            sources[k].at[pl.ds(here[0], size[0]), pl.ds(here[1], size[1])],
                            target.at[pl.ds(there[0], size[0]), pl.ds(there[1], size[1])],
                            sems.at[i],
                        )
                    )
            return made

        if not self.plan.line:
            for copy in copies(refs, (0, 1)):
                copy.start()
            for copy in copies(refs, (0, 1)):
                copy.wait()
            return
        inner, own, near, across_near, out, across, out_near = refs
        is_inner = inner[0] == 1
        for copy in copies((own, near), (0, 1)):
            copy.start()

        @pl.when(is_inner)
        def _():
            for copy in copies((None, None, across_near, across), (2, 3)):
                copy.start()

        @pl.when(jnp.logical_not(is_inner))
        def _():
            for copy in copies((None, None, out, out_near), (2, 3)):
                copy.start()

        for copy in copies((own, near, out, out_near), (0, 1, 2, 3)):
            copy.wait()


def pack_grads(plan, row_grad, col_grad, out_refs):
    if not plan.line:
        out_refs[0][...] = row_grad[...].astype(LOW)
        out_refs[1][...] = col_grad[...].astype(LOW)
        return
    rows, block, wide = plan.rows, plan.block, row_grad.shape[1]
    for k, out in enumerate(out_refs):
        at = k * block
        out[:, :wide] = row_grad[at : at + block, :].astype(LOW)
        for i in range(0, col_grad.shape[0], rows):
            for x in range(2):
                out[x * rows : (x + 1) * rows, wide + i : wide + i + rows] = col_grad[
                    i : i + rows, at + x * rows : at + (x + 1) * rows
                ].astype(LOW)


def packed_shapes(plan, row_shape, col_shape):
    if not plan.line:
        return [row_shape, col_shape]
    return [(plan.block, row_shape[1] + col_shape[0])] * 4


def rope_tables(positions):
    half_dim = HD // 2
    inverse_freq = ROPE_BASE ** (-2.0 * jnp.arange(half_dim, dtype=F32) / HD)
    angles = positions.astype(F32)[:, None] * inverse_freq[None, :]
    cosine, sine = jnp.cos(angles), jnp.sin(angles)
    return cat([cosine] * 4, 1), cat([-sine, sine] * 2, 1)


def lanes_of(shape):
    return lax.broadcasted_iota(jnp.int32, shape, 1)


def shuffle_halves(values):
    wide = values.shape[1]
    up = pltpu.roll(values, wide - HD // 2, 1)
    down = pltpu.roll(values, HD // 2, 1)
    return jnp.where(lanes_of(values.shape) % HD < HD // 2, up, down)


def tables(cos_ref, sin_ref, pairs):
    cosine, sine = cos_ref[...], sin_ref[...]
    is_key = lanes_of(cosine.shape) < HD
    return (
        cat([cosine] * pairs + [jnp.where(is_key, cosine, 1.0)], 1),
        cat([sine] * pairs + [jnp.where(is_key, sine, 0.0)], 1),
    )


def split_kv(both):
    is_key = lanes_of(both.shape) < HD
    blank = jnp.zeros_like(both)
    key_low = jnp.where(is_key, both, blank)
    value_high = jnp.where(is_key, blank, both)
    return (
        (key_low, pltpu.roll(key_low.astype(F32), HD, 1).astype(LOW)),
        (pltpu.roll(value_high.astype(F32), HD, 1).astype(LOW), value_high),
    )


def allowed_pairs(seg_col, seg_row):
    shape = (seg_col.shape[0], seg_row.shape[1])
    key_at = lax.broadcasted_iota(jnp.int32, shape, 1)
    query_at = lax.broadcasted_iota(jnp.int32, shape, 0)
    return (seg_col == seg_row) & (key_at <= query_at)


def attn_forward_kernel(pairs, loader, *refs):
    weights, refs = refs[: loader.count], refs[loader.count :]
    x_ref, cos_ref, sin_ref, col_ref, row_ref = refs[:5]
    part_ref, ctx_ref, q_ref, kv_ref, lse_ref, wout_ref, wqkv_ref, _, sems = refs[5:]

    @pl.when(pl.program_id(0) == 0)
    def _():
        loader.load(weights, wqkv_ref, wout_ref, sems)

    cosine, sine = tables(cos_ref, sin_ref, pairs)
    qkv = dot(x_ref[...], wqkv_ref[...], 1, 0)
    rotated = (qkv * cosine + shuffle_halves(qkv) * sine).astype(LOW)
    queries, both = rotated[:, : pairs * 128], rotated[:, pairs * 128 :]
    q_ref[...] = queries
    kv_ref[...] = both
    keys, values = split_kv(both)
    allowed = allowed_pairs(col_ref[...], row_ref[0])
    lane = lanes_of((both.shape[0], 128))
    log_sums = jnp.zeros((both.shape[0], 128), F32)
    contexts = []
    for pair in range(pairs):
        heads = queries[:, pair * 128 : (pair + 1) * 128]
        context = None
        for side in range(2):
            scores = dot(heads, keys[side], 1, 1) * HD**-0.5
            masked = jnp.where(allowed, scores, -1e30)
            top = jnp.max(masked, axis=1, keepdims=True)
            weights = jnp.exp(masked - top)
            totals = jnp.sum(weights, axis=1, keepdims=True)
            probs = (weights * (1.0 / totals)).astype(LOW)
            piece = dot(probs, values[side], 1, 0)
            context = piece if context is None else context + piece
            log_sums = jnp.where(lane == 2 * pair + side, top + jnp.log(totals), log_sums)
        contexts.append(context.astype(LOW))
    lse_ref[...] = log_sums
    context_low = cat(contexts, 1)
    ctx_ref[...] = context_low
    part_ref[...] = dot(context_low, wout_ref[...], 1, 0).astype(LOW)


def attn_backward_kernel(pairs, loader, *refs):
    weights, refs = refs[: loader.count], refs[loader.count :]
    cg_ref, x_ref, q_ref, kv_ref, lse_ref, cos_ref, sin_ref, col_ref, row_ref = refs[:9]
    part_ref, gain_ref, *grad_refs = refs[9:-4]
    wqkv_ref, wout_ref, sems, acc_qkv = refs[-4:]
    step = pl.program_id(0)

    @pl.when(step == 0)
    def _():
        loader.load(weights, wqkv_ref, wout_ref, sems)
        acc_qkv[...] = jnp.zeros_like(acc_qkv)

    cosine, sine = tables(cos_ref, sin_ref, pairs)
    scale = HD**-0.5
    ctx_grad = cg_ref[...]
    keys, values = split_kv(kv_ref[...])
    allowed = allowed_pairs(col_ref[...], row_ref[0])
    lane = lanes_of((ctx_grad.shape[0], 128))
    log_sums = lse_ref[...]
    query_grads, key_grad, value_grad = [], None, None
    for pair in range(pairs):
        heads = q_ref[:, pair * 128 : (pair + 1) * 128]
        grads = ctx_grad[:, pair * 128 : (pair + 1) * 128]
        query_grad = None
        for side in range(2):
            here = (lane < HD) if side == 0 else (lane >= HD)
            head = jnp.where(here, heads, jnp.zeros_like(heads))
            grad = jnp.where(here, grads, jnp.zeros_like(grads))
            at = 2 * pair + side
            scores = dot(heads, keys[side], 1, 1) * scale
            probs = jnp.where(allowed, jnp.exp(scores - log_sums[:, at : at + 1]), 0.0)
            prob_grad = dot(grads, values[side], 1, 1)
            delta = jnp.sum(probs * prob_grad, axis=1, keepdims=True)
            score_grad = (probs * (prob_grad - delta)).astype(LOW)
            to_value = dot(probs.astype(LOW), grad, 0, 0)
            to_key = dot(score_grad, head, 0, 0)
            to_query = dot(score_grad, keys[side], 1, 0)
            value_grad = to_value if value_grad is None else value_grad + to_value
            key_grad = to_key if key_grad is None else key_grad + to_key
            query_grad = to_query if query_grad is None else query_grad + to_query
        query_grads.append(query_grad * scale)
    key_grad = (key_grad + pltpu.roll(key_grad, HD, 1)) * scale
    value_grad = value_grad + pltpu.roll(value_grad, HD, 1)
    joined = cat(query_grads + [jnp.where(lane < HD, key_grad, value_grad)], 1)
    low = (joined * cosine - shuffle_halves(joined) * sine).astype(LOW)
    part_ref[...] = dot(low, wqkv_ref[...], 1, 1).astype(LOW)
    acc_qkv[...] += dot(x_ref[...], low, 0, 0)

    @pl.when(step == pl.num_programs(0) - 1)
    def _():
        cut = acc_qkv.shape[0] // len(grad_refs)
        for i, out in enumerate(grad_refs):
            out[...] = acc_qkv[i * cut : (i + 1) * cut, :].astype(LOW)
        gain_ref[...] = jnp.sum(acc_qkv[...] * wqkv_ref[...].astype(F32), axis=1, keepdims=True)


def once(shape):
    return pl.BlockSpec(shape, lambda i: (0,) * len(shape), pipeline_mode=pl.Buffered(1))


def per_seq(shape):
    return pl.BlockSpec(shape, lambda i: (i,) + (0,) * (len(shape) - 1))


def attn_forward(loader, normed, cosine, sine, seg_col, seg_row):
    rows, width = normed.shape
    heads = loader.col_shape[0]
    return pl.pallas_call(
        functools.partial(attn_forward_kernel, heads // 128, loader),
        grid=(rows // LEN,),
        in_specs=[
            *loader.specs(),
            per_seq((LEN, width)),
            per_seq((LEN, 128)),
            per_seq((LEN, 128)),
            per_seq((LEN, 1)),
            per_seq((1, 1, LEN)),
        ],
        out_specs=[
            per_seq((LEN, width)),
            per_seq((LEN, heads)),
            per_seq((LEN, heads)),
            per_seq((LEN, 128)),
            per_seq((LEN, 128)),
            once(loader.col_shape),
        ],
        out_shape=[
            jax.ShapeDtypeStruct((rows, width), LOW),
            jax.ShapeDtypeStruct((rows, heads), LOW),
            jax.ShapeDtypeStruct((rows, heads), LOW),
            jax.ShapeDtypeStruct((rows, 128), LOW),
            jax.ShapeDtypeStruct((rows, 128), F32),
            jax.ShapeDtypeStruct(loader.col_shape, LOW),
        ],
        scratch_shapes=loader.scratch(),
        compiler_params=pltpu.CompilerParams(vmem_limit_bytes=48 * MIB),
        cost_estimate=SMALL,
        name="attn_forward",
    )(*loader.operands, normed, cosine, sine, seg_col, seg_row)


def attn_backward(loader, ctx_grad, normed, queries, both, lse, cosine, sine, seg_col, seg_row):
    rows, width = normed.shape
    heads = loader.col_shape[0]
    cuts = loader.plan.cuts
    grad = (width // cuts, loader.row_shape[1])
    return pl.pallas_call(
        functools.partial(attn_backward_kernel, heads // 128, loader),
        grid=(rows // LEN,),
        in_specs=[
            *loader.specs(),
            per_seq((LEN, heads)),
            per_seq((LEN, width)),
            per_seq((LEN, heads)),
            per_seq((LEN, 128)),
            per_seq((LEN, 128)),
            per_seq((LEN, 128)),
            per_seq((LEN, 128)),
            per_seq((LEN, 1)),
            per_seq((1, 1, LEN)),
        ],
        out_specs=[per_seq((LEN, width)), once((width, 1))] + [once(grad)] * cuts,
        out_shape=[
            jax.ShapeDtypeStruct((rows, width), LOW),
            jax.ShapeDtypeStruct((width, 1), F32),
        ]
        + [jax.ShapeDtypeStruct(grad, LOW)] * cuts,
        scratch_shapes=[*loader.scratch(), pltpu.VMEM(loader.row_shape, F32)],
        compiler_params=pltpu.CompilerParams(vmem_limit_bytes=52 * MIB),
        cost_estimate=SMALL,
        name="attn_backward",
    )(*loader.operands, ctx_grad, normed, queries, both, lse, cosine, sine, seg_col, seg_row)


def out_weights_kernel(ctx_ref, res_ref, *refs):
    grad_refs, acc = refs[:-1], refs[-1]
    step = pl.program_id(0)

    @pl.when(step == 0)
    def _():
        acc[...] = jnp.zeros_like(acc)

    acc[...] += dot(ctx_ref[...], res_ref[...], 0, 0)

    @pl.when(step == pl.num_programs(0) - 1)
    def _():
        cut = acc.shape[1] // len(grad_refs)
        for i, out in enumerate(grad_refs):
            out[...] = acc[:, i * cut : (i + 1) * cut].astype(LOW)


def out_weights(plan, ctx, res_all):
    rows, width = res_all.shape
    heads = ctx.shape[1]
    grad = (heads, width // plan.cuts)
    return pl.pallas_call(
        out_weights_kernel,
        grid=(rows // LEN,),
        in_specs=[per_seq((LEN, heads)), per_seq((LEN, width))],
        out_specs=[once(grad)] * plan.cuts,
        out_shape=[jax.ShapeDtypeStruct(grad, LOW)] * plan.cuts,
        scratch_shapes=[pltpu.VMEM((heads, width), F32)],
        compiler_params=pltpu.CompilerParams(vmem_limit_bytes=40 * MIB),
        cost_estimate=SMALL,
        name="out_weights",
    )(ctx, res_all)


def residual_backward_kernel(
    back_ref, residual_ref, scale_ref, gain_ref, grad_ref, wout_ref, res_grad_ref, low_ref, ctx_ref
):
    @pl.when(pl.program_id(0) == 0)
    def _():
        back = norm_back(
            back_ref[...].astype(F32), residual_ref[...], scale_ref[...], gain_ref[...]
        )
        total = grad_ref[...].astype(F32) + back
        res_grad_ref[...] = total
        low_ref[...] = total.astype(LOW)

    ctx_ref[...] = dot(low_ref[...], wout_ref[...], 1, 1).astype(LOW)


def residual_backward(back_sum, residual, scale, gain, grad_low, wout_all):
    rows, width = residual.shape
    heads = wout_all.shape[0]
    step = 512
    return pl.pallas_call(
        residual_backward_kernel,
        grid=(heads // step,),
        in_specs=[
            once((rows, width)),
            once((rows, width)),
            once((rows, 1)),
            once((1, width)),
            once((rows, width)),
            per_seq((step, width)),
        ],
        out_specs=[
            once((rows, width)),
            once((rows, width)),
            pl.BlockSpec((rows, step), lambda i: (0, i)),
        ],
        out_shape=[
            jax.ShapeDtypeStruct((rows, width), F32),
            jax.ShapeDtypeStruct((rows, width), LOW),
            jax.ShapeDtypeStruct((rows, heads), LOW),
        ],
        compiler_params=pltpu.CompilerParams(vmem_limit_bytes=40 * MIB),
        cost_estimate=SMALL,
        name="residual_backward",
    )(back_sum, residual, scale, gain[None, :], grad_low, wout_all)


TILE = 512


def ffn_main_kernel(loader, more, *refs):
    weights, refs = refs[: loader.count], refs[loader.count :]
    x_ref, grad_ref = refs[:2]
    back_ref, act_ref, both_ref, gate_up_ref, down_ref, sems = refs[2 + more :]

    @pl.when(pl.program_id(0) == 0)
    def _():
        loader.load(weights, gate_up_ref, down_ref, sems)

    hidden = down_ref.shape[0]
    pre = dot(x_ref[...], gate_up_ref[...], 1, 0)
    gate_pre, lifted = pre[:, :hidden], pre[:, hidden:]
    sigmoid_gate = jax.nn.sigmoid(gate_pre)
    silu_gate = gate_pre * sigmoid_gate
    act_ref[...] = (silu_gate * lifted).astype(LOW)
    act_grad = dot(grad_ref[...], down_ref[...], 1, 1)
    gate_grad = act_grad * lifted * sigmoid_gate * (1.0 + gate_pre * (1.0 - sigmoid_gate))
    both_grad = cat([gate_grad.astype(LOW), (act_grad * silu_gate).astype(LOW)], 1)
    both_ref[...] = both_grad
    back = dot(both_grad, gate_up_ref[...], 1, 1)
    if more:
        back = back + refs[2][...].astype(F32)
    back_ref[...] = back.astype(LOW)


def ffn_main(loader, tokens, grads, earlier):
    rows, width = tokens.shape
    hidden = loader.col_shape[0]
    more = [] if earlier is None else [earlier]
    return pl.pallas_call(
        functools.partial(ffn_main_kernel, loader, len(more)),
        grid=(rows // TILE,),
        in_specs=[
            *loader.specs(),
            per_seq((TILE, width)),
            per_seq((TILE, width)),
            *[per_seq((TILE, width))] * len(more),
        ],
        out_specs=[
            per_seq((TILE, width)),
            per_seq((TILE, hidden)),
            per_seq((TILE, 2 * hidden)),
        ],
        out_shape=[
            jax.ShapeDtypeStruct((rows, width), LOW),
            jax.ShapeDtypeStruct((rows, hidden), LOW),
            jax.ShapeDtypeStruct((rows, 2 * hidden), LOW),
        ],
        scratch_shapes=loader.scratch(),
        compiler_params=pltpu.CompilerParams(vmem_limit_bytes=58 * MIB),
        cost_estimate=SMALL,
        name="ffn_main",
    )(*loader.operands, tokens, grads, *more)


def ffn_weights_kernel(loader, more, *refs):
    weights, refs = refs[: loader.count], refs[loader.count :]
    x_ref, grad_ref, act_ref, both_ref = refs[:4]
    out_ref, gain_ref, *grad_refs = refs[4 + more : -5]
    gate_up_ref, down_ref, sems, acc_gate_up, acc_down = refs[-5:]
    step = pl.program_id(0)

    @pl.when(step == 0)
    def _():
        loader.load(weights, gate_up_ref, down_ref, sems)
        acc_gate_up[...] = jnp.zeros_like(acc_gate_up)
        acc_down[...] = jnp.zeros_like(acc_down)

    act = act_ref[...]
    acc_down[...] += dot(act, grad_ref[...], 0, 0)
    acc_gate_up[...] += dot(x_ref[...], both_ref[...], 0, 0)
    out = dot(act, down_ref[...], 1, 0)
    if more:
        out = out + refs[4][...].astype(F32)
    out_ref[...] = out.astype(LOW)

    @pl.when(step == pl.num_programs(0) - 1)
    def _():
        pack_grads(loader.plan, acc_gate_up, acc_down, grad_refs)
        gain_ref[...] = jnp.sum(
            acc_gate_up[...] * gate_up_ref[...].astype(F32), axis=1, keepdims=True
        )


def ffn_weights(loader, tokens, grads, act, both_grad, earlier):
    rows, width = tokens.shape
    hidden = loader.col_shape[0]
    more = [] if earlier is None else [earlier]
    packed = packed_shapes(loader.plan, loader.row_shape, loader.col_shape)
    return pl.pallas_call(
        functools.partial(ffn_weights_kernel, loader, len(more)),
        grid=(rows // TILE,),
        in_specs=[
            *loader.specs(),
            per_seq((TILE, width)),
            per_seq((TILE, width)),
            per_seq((TILE, hidden)),
            per_seq((TILE, 2 * hidden)),
            *[per_seq((TILE, width))] * len(more),
        ],
        out_specs=[per_seq((TILE, width)), once((width, 1))] + [once(shape) for shape in packed],
        out_shape=[
            jax.ShapeDtypeStruct((rows, width), LOW),
            jax.ShapeDtypeStruct((width, 1), F32),
        ]
        + [jax.ShapeDtypeStruct(shape, LOW) for shape in packed],
        scratch_shapes=[
            *loader.scratch(),
            pltpu.VMEM(loader.row_shape, F32),
            pltpu.VMEM(loader.col_shape, F32),
        ],
        compiler_params=pltpu.CompilerParams(vmem_limit_bytes=60 * MIB),
        cost_estimate=SMALL,
        name="ffn_weights",
    )(*loader.operands, tokens, grads, act, both_grad, *more)


def norm_rows(values, gain_vec):
    row_scale = lax.rsqrt(jnp.mean(values * values, axis=1, keepdims=True) + NORM_EPS)
    return values * row_scale * gain_vec, row_scale


def norm_back(row_grad, values, row_scale, gain_vec):
    scaled_grad = row_grad * gain_vec
    return row_scale * scaled_grad - values * row_scale**3 * jnp.mean(
        scaled_grad * values, axis=1, keepdims=True
    )


def adamw_update(master, grad_sum, first_mom, second_mom, decay_rate, step_rate):
    next_first = BETA_ONE * first_mom + (1.0 - BETA_ONE) * grad_sum
    next_second = BETA_TWO * second_mom + (1.0 - BETA_TWO) * grad_sum * grad_sum
    first_hat = next_first / (1.0 - BETA_ONE**STEP)
    second_hat = next_second / (1.0 - BETA_TWO**STEP)
    next_master = master - step_rate * (
        first_hat / (jnp.sqrt(second_hat) + ADAM_EPS) + decay_rate * master
    )
    return (next_master, next_first, next_second)


def sum_everywhere(values, sizes):
    for axis, size in sizes:
        step = 1
        while step < size:
            values = values + lax.ppermute(values, axis, [(i, i ^ step) for i in range(size)])
            step *= 2
    return values


def pick(index, low, high):
    return jnp.where(index == 0, low, high)


class Plane:
    def __init__(self, tp):
        self.tp, self.half = tp, tp // 2
        self.x = lax.axis_index("di")
        self.y = lax.axis_index("tp") // self.half
        self.core = lax.axis_index("tp") % 2
        self.place = self.x * 2 + self.y
        self.axes = ("di", "tp")

    def pairs(self, first):
        def other(index):
            x, t = divmod(index, self.tp)
            along_x = (t % 2 == 0) == first
            return (1 - x) * self.tp + t if along_x else x * self.tp + (t + self.half) % self.tp

        return [(index, other(index)) for index in range(2 * self.tp)]

    def swap_first(self, value):
        return lax.ppermute(value, self.axes, self.pairs(True))

    def swap_second(self, value):
        return lax.ppermute(value, self.axes, self.pairs(False))

    def swap_core(self, value):
        return lax.ppermute(value, "tp", [(i, i ^ 1) for i in range(self.tp)])

    def first_step(self):
        return jnp.where(self.core == 0, 2, 1)

    def at(self, blocks, step):
        return lax.dynamic_index_in_dim(blocks, self.place ^ step, 0, keepdims=False)


def on_device(
    sizes,
    layer_input, out_grad, segment_ids, positions,
    w_query, w_key, w_value, w_out, w_gate, w_up, w_down,
    m_query, m_key, m_value, m_out, m_gate, m_up, m_down,
    v_query, v_key, v_value, v_out, v_gate, v_up, v_down,
    gain_attn, gain_ffn, m_gain_attn, m_gain_ffn, v_gain_attn, v_gain_ffn,
):
    width = layer_input.shape[1]
    plan = Plan(sizes["do"], w_query.shape[0])
    by_x = plan.by_x
    axes = ("di", "tp")
    plane = Plane(sizes["tp"])

    gain_one, gain_two = plan.reorder(gain_attn), plan.reorder(gain_ffn)
    inputs_f = plan.reorder(layer_input).astype(F32)
    grad_low = plan.reorder(out_grad)
    normed, scale_one = norm_rows(inputs_f, gain_one)
    normed_all = lax.all_gather(normed.astype(LOW), axes, axis=0, tiled=True)

    marks = cat([segment_ids[None, :], positions[None, :]], 0)
    marks_other = lax.ppermute(marks, "di", PAIR)
    marks_all = cat([by_x(marks, marks_other), by_x(marks_other, marks)], 1)
    seg_all, pos_all = marks_all[0], marks_all[1]
    rows = seg_all.shape[0]
    seqs = rows // LEN
    seg_col, seg_row = seg_all.reshape(rows, 1), seg_all.reshape(seqs, 1, LEN)
    cosine, sine = rope_tables(pos_all)

    def col_halves(weight):
        half = weight.shape[1] // 2
        low = weight.astype(LOW)
        return by_x(low[:, :half], low[:, half:]), by_x(low[:, half:], low[:, :half])

    def row_halves(weight):
        half = weight.shape[0] // 2
        low = weight.astype(LOW)
        return by_x(low[:half], low[half:]), by_x(low[half:], low[:half])

    def col_cut(pair, chunk):
        size = pair[0].shape[1] // CHUNKS
        return tuple(part[:, chunk * size : (chunk + 1) * size] for part in pair)

    def row_cut(pair, chunk):
        size = pair[0].shape[0] // CHUNKS
        return tuple(part[chunk * size : (chunk + 1) * size] for part in pair)

    halves_q, halves_k, halves_v = col_halves(w_query), col_halves(w_key), col_halves(w_value)
    qkv_parts = tuple(cat([q, k, v], 1) for q, k, v in zip(halves_q, halves_k, halves_v))
    out_parts = row_halves(w_out)
    halves_g, halves_u, halves_d = col_halves(w_gate), col_halves(w_up), row_halves(w_down)

    def ffn_parts(chunk):
        gate_up = tuple(
            cat([g, u], 1) for g, u in zip(col_cut(halves_g, chunk), col_cut(halves_u, chunk))
        )
        return gate_up, row_cut(halves_d, chunk)

    hidden = halves_d[0].shape[0] // CHUNKS
    attn_shapes = (width, qkv_parts[0].shape[1]), (out_parts[0].shape[0], width)
    ffn_shapes = (width, 2 * hidden), (hidden, width)
    own_rows = layer_input.shape[0]
    core = lax.axis_index("tp") % 2

    if plan.line:
        attn_own, attn_other = plan.pack(qkv_parts, out_parts)
        own_1, other_1 = plan.pack(*ffn_parts(0))
        own_2, other_2 = plan.pack(*ffn_parts(1))
        attn_theirs = plan.swap(attn_other)
        attn_theirs, marks_all, own_1, other_1 = fence(attn_theirs, marks_all, own_1, other_1)
        attn_block = plan.join(attn_own, attn_theirs)
        near, across = line_near(attn_block)
        theirs_1 = plan.swap(other_1)
        near, across, cosine, sine, own_2, other_2 = fence(
            near, across, cosine, sine, own_2, other_2
        )
        across_near, out = line_far(near, across)
        across_near, out, theirs_1 = fence(across_near, out, theirs_1)
        out_near = line_last(across_near)
        out_near, normed_all, theirs_1, grad_low, other_2 = fence(
            out_near, normed_all, theirs_1, grad_low, other_2
        )
        block_1 = plan.join(own_1, theirs_1)
        attn_weights = (attn_block, near, across_near, out, across, out_near)
        near_1, across_1 = line_near(block_1)
    else:
        attn_weights = plan.plain_gather(qkv_parts, out_parts)
        first_weights = plan.plain_gather(*ffn_parts(0))
        second_weights = plan.plain_gather(*ffn_parts(1))
    attn_loader = Loader(plan, attn_weights, *attn_shapes)

    attn_part, ctx, queries, both, lse, wout = attn_forward(
        attn_loader, normed_all, cosine, sine, seg_col, seg_row
    )
    grad_second = plane.swap_second(grad_low)
    if plan.line:
        theirs_2 = plan.swap(other_2)
        attn_part, near_1, across_1, grad_second, theirs_2, grad_low = fence(
            attn_part, near_1, across_1, grad_second, theirs_2, grad_low
        )
        across_near_1, out_1 = line_far(near_1, across_1)
    grad_first = plane.swap_first(grad_low)
    attn_sum = lax.psum_scatter(attn_part, axes, scatter_dimension=0, tiled=True)
    grad_xy = plane.swap_first(grad_second)
    if plan.line:
        across_near_1, out_1, grad_xy, theirs_2, grad_first = fence(
            across_near_1, out_1, grad_xy, theirs_2, grad_first
        )
        block_2 = plan.join(own_2, theirs_2)
        out_near_1 = line_last(across_near_1)
        across_2 = lax.ppermute(block_2, "do", MIDDLE)
    grad_x = pick(core, grad_first, grad_second)
    grad_y = pick(core, grad_second, grad_first)
    over_y = cat([pick(plane.y, grad_low, grad_y), pick(plane.y, grad_y, grad_low)], 0)
    over_xy = cat([pick(plane.y, grad_x, grad_xy), pick(plane.y, grad_xy, grad_x)], 0)
    grad_core = cat([by_x(over_y, over_xy), by_x(over_xy, over_y)], 0)
    grad_other = plane.swap_core(grad_core)
    groups = (rows // own_rows // 2, 1, own_rows, width)
    mine, theirs = grad_core.reshape(groups), grad_other.reshape(groups)
    grad_all = cat([pick(core, mine, theirs), pick(core, theirs, mine)], 1).reshape(rows, width)

    if plan.line:
        attn_sum, grad_all = fence(attn_sum, grad_all)
    residual = inputs_f + attn_sum.astype(F32)
    normed_two, scale_two = norm_rows(residual, gain_two)
    two_low = normed_two.astype(LOW)
    two_all = lax.all_gather(two_low, axes, axis=0, tiled=True)

    if plan.line:
        out_near_1, across_2, block_2, _ = fence(out_near_1, across_2, block_2, two_low)
        first_weights = (block_1, near_1, across_near_1, out_1, across_1, out_near_1)
        near_2 = lax.ppermute(block_2, "do", NEAR)
        two_all, near_2, across_2 = fence(two_all, near_2, across_2)
        across_near_2, out_2 = line_far(near_2, across_2)
    two_all, wout = fence(two_all, wout)
    first = Loader(plan, first_weights, *ffn_shapes)
    back_1, act_1, both_1 = ffn_main(first, two_all, grad_all, None)
    wout_all = lax.all_gather(wout, axes, axis=0, tiled=True)
    if plan.line:
        back_1, act_1, both_1, across_near_2, out_2 = fence(
            back_1, act_1, both_1, across_near_2, out_2
        )
        out_near_2 = line_last(across_near_2)
    out_1_part, gain_1, *grads_1 = ffn_weights(first, two_all, grad_all, act_1, both_1, None)
    if plan.line:
        back_1, out_1_part, grads_1, out_near_2 = fence(back_1, out_1_part, grads_1, out_near_2)
        second_weights = (block_2, near_2, across_near_2, out_2, across_2, out_near_2)
        far_1 = sum_far(grads_1)
    second = Loader(plan, second_weights, *ffn_shapes)
    back_2, act_2, both_2 = ffn_main(second, two_all, grad_all, back_1)
    if plan.line:
        back_2, act_2, both_2, far_1, wout_all = fence(back_2, act_2, both_2, far_1, wout_all)
        crossed_1, inward_1 = sum_middle(grads_1, far_1)
    back_sum = lax.psum_scatter(back_2, axes, scatter_dimension=0, tiled=True)
    out_2_part, gain_2, *grads_2 = ffn_weights(second, two_all, grad_all, act_2, both_2, out_1_part)
    if plan.line:
        out_2_part, grads_2, crossed_1, inward_1 = fence(out_2_part, grads_2, crossed_1, inward_1)
        far_2 = sum_far(grads_2)

    residual_grad, res_low, ctx_grad = residual_backward(
        back_sum, residual, scale_two, gain_two, grad_low, wout_all
    )
    ctx_grad = lax.all_to_all(ctx_grad, axes, split_axis=1, concat_axis=0, tiled=True)

    out_shape = (rows // own_rows // 2, 2, own_rows, width)
    parts = out_2_part.reshape(out_shape)
    mine, theirs = pick(core, parts[:, 0], parts[:, 1]), pick(core, parts[:, 1], parts[:, 0])
    summed = add(mine, plane.swap_core(theirs)).astype(LOW)
    step = plane.first_step()
    goes = jnp.stack([plane.at(summed, step), plane.at(summed, 3)])
    goes_on, stays = plane.at(summed, 3 - step), plane.at(summed, 0)

    if plan.line:
        far_2, grads_1, _ = fence(far_2, grads_1, res_low)
        crossed_2, inward_2 = sum_middle(grads_2, far_2)
        first_1, third_1 = sum_near_parts(grads_1, crossed_1, inward_1)
        ctx_grad, res_low, stays, goes, goes_on, first_1, third_1 = fence(
            ctx_grad, res_low, stays, goes, goes_on, first_1, third_1
        )
        near_sum_1, across_sum_1 = sum_near_send(first_1, third_1)
    arrives = plane.swap_first(goes)
    res_all = lax.all_gather(res_low, axes, axis=0, tiled=True)
    back_one_part, gain_one_part, *grads_qkv = attn_backward(
        attn_loader, ctx_grad, normed_all, queries, both, lse, cosine, sine, seg_col, seg_row
    )
    if plan.line:
        back_one_part, grads_qkv, gain_one_part, crossed_2, inward_2, res_all = fence(
            back_one_part, grads_qkv, gain_one_part, crossed_2, inward_2, res_all
        )
        near_sum_1, across_sum_1, _ = fence(near_sum_1, across_sum_1, back_one_part)
        total_1 = sum_own(grads_1, near_sum_1, across_sum_1)
        ffn_grad_1 = plan.unpack(total_1, 2 * hidden)
    back_one = lax.psum_scatter(back_one_part, axes, scatter_dimension=0, tiled=True)
    grads_out = out_weights(plan, ctx, res_all)
    if plan.line:
        near_sum_2, across_sum_2 = sum_near_send(*sum_near_parts(grads_2, crossed_2, inward_2))
        near_sum_2, across_sum_2, grads_qkv, grads_out, arrives, ffn_grad_1 = fence(
            near_sum_2, across_sum_2, grads_qkv, grads_out, arrives, ffn_grad_1
        )
        direct_qkv, direct_out = send_direct(grads_qkv), send_direct(grads_out)
        total_2 = sum_own(grads_2, near_sum_2, across_sum_2)
        ffn_grad_2 = plan.unpack(total_2, 2 * hidden)
    summed = add(stays, arrives[0])
    arrives = plane.swap_second(add(goes_on, arrives[1]).astype(LOW))
    if plan.line:
        ffn_grad_2, direct_qkv, direct_out, arrives, gain_one_part = fence(
            ffn_grad_2, direct_qkv, direct_out, arrives, gain_one_part
        )
        half = plan.rows
        total = add(grads_qkv[0], *direct_qkv)
        qkv_pair = plan.trade(total[:half], total[half:])
        total = add(grads_out[0], *direct_out)
        out_pair = plan.trade(total[:, :half], total[:, half:])
        ffn_grads = [ffn_grad_1, ffn_grad_2]
    else:
        qkv_pair = plan.plain_sum_row(grads_qkv[0])
        out_pair = plan.plain_sum_col(grads_out[0])
        ffn_grads = [
            (plan.plain_sum_row(row), plan.plain_sum_col(col)) for row, col in (grads_1, grads_2)
        ]
    gain_parts = jnp.stack(
        [gain_one_part[:, 0] / gain_one, (gain_1[:, 0] + gain_2[:, 0]) / gain_two]
    )
    gain_sums = sum_everywhere(plan.reorder(gain_parts), list(sizes.items())[::-1])
    out_value = (residual + add(summed, arrives)).astype(LOW)
    in_grad = residual_grad + norm_back(back_one.astype(F32), inputs_f, scale_one, gain_one)

    grad_gain_attn, grad_gain_ffn = gain_sums[0], gain_sums[1]

    def join(pair, axis):
        own, other = pair
        return by_x(cat([own, other], axis), cat([other, own], axis))

    def from_chunks(pairs, axis):
        own = cat([pair[0] for pair in pairs], axis)
        other = cat([pair[1] for pair in pairs], axis)
        return join((own, other), axis)

    def cut(pair, start, stop):
        return tuple(part[:, start:stop] for part in pair)

    at_k = halves_q[0].shape[1]
    at_v = at_k + halves_k[0].shape[1]
    end = at_v + halves_v[0].shape[1]
    grad_query = join(cut(qkv_pair, 0, at_k), 1)
    grad_key = join(cut(qkv_pair, at_k, at_v), 1)
    grad_value = join(cut(qkv_pair, at_v, end), 1)
    grad_out = join(out_pair, 0)
    grad_gate = from_chunks([cut(gu, 0, hidden) for gu, _ in ffn_grads], 1)
    grad_up = from_chunks([cut(gu, hidden, 2 * hidden) for gu, _ in ffn_grads], 1)
    grad_down = from_chunks([down for _, down in ffn_grads], 0)

    grads = (grad_query, grad_key, grad_value, grad_out, grad_gate, grad_up, grad_down)
    masters = (w_query, w_key, w_value, w_out, w_gate, w_up, w_down)
    firsts = (m_query, m_key, m_value, m_out, m_gate, m_up, m_down)
    seconds = (v_query, v_key, v_value, v_out, v_gate, v_up, v_down)
    updated = [
        adamw_update(w, g, m, v, WEIGHT_DECAY, LEARN_RATE)
        for w, g, m, v in zip(masters, grads, firsts, seconds)
    ]
    gain_updated = [
        adamw_update(gain_attn, grad_gain_attn, m_gain_attn, v_gain_attn, 0.0, GAIN_RATE),
        adamw_update(gain_ffn, grad_gain_ffn, m_gain_ffn, v_gain_ffn, 0.0, GAIN_RATE),
    ]
    return (
        plan.reorder(out_value),
        plan.reorder(in_grad),
        *grads,
        *[u[0] for u in updated],
        *[u[1] for u in updated],
        *[u[2] for u in updated],
        grad_gain_attn,
        grad_gain_ffn,
        *[u[0] for u in gain_updated],
        *[u[1] for u in gain_updated],
        *[u[2] for u in gain_updated],
    )


def solution(mesh):
    dp, tp = mesh.shape["dp"], mesh.shape["tp"]
    split = Mesh(mesh.devices.reshape(dp // 2, 2, tp), ("do", "di", "tp"))
    sizes = {"do": dp // 2, "di": 2, "tp": tp}
    dp_axes = ("do", "di")
    tokens = P(("do", "di", "tp"), None)
    by_rows, by_cols = P(dp_axes, "tp"), P("tp", dp_axes)
    weights = (by_rows, by_rows, by_rows, by_cols, by_rows, by_rows, by_cols)
    gains = (P(),) * 6
    in_specs = (tokens, tokens, P(dp_axes), P(dp_axes)) + weights * 3 + gains
    out_specs = (tokens, tokens) + weights * 4 + (P(),) * 2 + gains
    return jax.shard_map(
        functools.partial(on_device, sizes),
        mesh=split,
        in_specs=in_specs,
        out_specs=out_specs,
        check_vma=False,
    )
```

```python
import functools

import jax
import jax.numpy as jnp
from jax import lax
from jax.experimental import pallas as pl
from jax.experimental.pallas import tpu as pltpu
from jax.sharding import Mesh
from jax.sharding import PartitionSpec as P

HD = 64
LEN = 512
STEP = 5
CHUNKS = 2

NORM_EPS = 1e-05
ROPE_BASE = 500000.0
BETA_ONE = 0.9
BETA_TWO = 0.95
LEARN_RATE = 0.02
GAIN_RATE = 0.5
WEIGHT_DECAY = 0.1
ADAM_EPS = 1e-08

LOW = jnp.bfloat16
F32 = jnp.float32
MIB = 1024 * 1024

NEAR = [(0, 1), (1, 0), (2, 3), (3, 2)]
MIDDLE = [(1, 2), (2, 1)]
CROSS = [(0, 2), (1, 3), (2, 0), (3, 1)]
MIRROR = [(0, 3), (1, 2), (2, 1), (3, 0)]
OUTWARD = [(1, 0), (2, 3)]
INWARD = [(0, 1), (3, 2)]
PAIR = [(0, 1), (1, 0)]


def dot(lhs, rhs, lhs_dim, rhs_dim):
    return lax.dot_general(
        lhs, rhs, (((lhs_dim,), (rhs_dim,)), ((), ())), preferred_element_type=F32
    )


def cat(parts, axis):
    return jnp.concatenate(parts, axis)


def fence(*values):
    return lax.optimization_barrier(values)


def line_near(own):
    return lax.ppermute(own, "do", NEAR), lax.ppermute(own, "do", MIDDLE)


def line_far(near, across):
    return lax.ppermute(near, "do", MIDDLE), lax.ppermute(across, "do", NEAR)


def line_last(across_near, perm=NEAR):
    return lax.ppermute(across_near, "do", perm)


def add(part, *arrived):
    total = part.astype(F32)
    for piece in arrived:
        total = total + piece.astype(F32)
    return total


def is_inner():
    place = lax.axis_index("do")
    return (place == 1) | (place == 2)


def add_inner(part, arrived):
    return add(part, jnp.where(is_inner(), arrived, jnp.zeros_like(arrived)))


def sum_far(part, perm=NEAR):
    return lax.ppermute(part, "do", perm)


def sum_middle(parts, far):
    second = add_inner(parts[2], far).astype(LOW)
    return lax.ppermute(second, "do", MIDDLE), lax.ppermute(second, "do", NEAR)


def sum_near_parts(parts, crossed, inward):
    return add_inner(parts[1], crossed).astype(LOW), add_inner(parts[3], inward).astype(LOW)


def sum_near_send(first, third):
    return lax.ppermute(first, "do", NEAR), lax.ppermute(third, "do", MIDDLE)


def sum_own(parts, from_near, from_across):
    return add_inner(parts[0], from_across) + from_near.astype(F32)


def send_direct(parts):
    return [
        lax.ppermute(part, "do", perm) for part, perm in zip(parts[1:], (NEAR, CROSS, MIRROR))
    ]


class Plan:
    def __init__(self, outer, per_device):
        self.rows = per_device
        self.block = 2 * per_device
        self.line = outer == 4 and per_device == 256
        self.cuts = 4 if self.line else 1

    def reorder(self, values):
        if not self.line:
            return values
        place = lax.axis_index("do")
        quarter = values.shape[-1] // 4
        a, b, c, d = (values[..., i * quarter : (i + 1) * quarter] for i in range(4))
        values = jnp.where(place % 2 == 1, cat([b, a, d, c], -1), values)
        half = 2 * quarter
        turned = cat([values[..., half:], values[..., :half]], -1)
        return jnp.where(place >= 2, turned, values)

    def by_x(self, low, high):
        return jnp.where(lax.axis_index("di") == 0, low, high)

    def inner(self):
        return is_inner().astype(jnp.int32).reshape(1)

    def pack(self, row_part, col_part):
        rows, packs = self.rows, []
        for row_side, side in zip(row_part, col_part):
            pieces = [side[i : i + rows] for i in range(0, side.shape[0], rows)]
            packs.append(cat([row_side] + pieces, 1))
        return packs

    def swap(self, other):
        return lax.ppermute(other, "di", PAIR)

    def join(self, own, theirs, axis=0):
        return cat([self.by_x(own, theirs), self.by_x(theirs, own)], axis)

    def plain_gather(self, row_part, col_part):
        full = []
        for (own, other), axis in ((row_part, 0), (col_part, 1)):
            block = self.join(own, self.swap(other), axis)
            full.append(lax.all_gather(block, "do", axis=axis, tiled=True))
        return tuple(full)

    def unpack(self, pair, wide):
        cuts = range(wide, pair[0].shape[1], self.rows)
        return (
            tuple(side[:, :wide] for side in pair),
            tuple(cat([side[:, i : i + self.rows] for i in cuts], 0) for side in pair),
        )

    def plain_sum_row(self, grad):
        total = lax.psum_scatter(grad, "do", scatter_dimension=0, tiled=True)
        return self.trade(total[: self.rows], total[self.rows :])

    def plain_sum_col(self, grad):
        total = lax.psum_scatter(grad, "do", scatter_dimension=1, tiled=True)
        return self.trade(total[:, : self.rows], total[:, self.rows :])

    def trade(self, low, high):
        theirs = lax.ppermute(self.by_x(high, low).astype(LOW), "di", PAIR)
        return self.by_x(low, high).astype(F32), theirs


ANY = pl.BlockSpec(memory_space=pl.ANY)
SMALL = pl.CostEstimate(flops=1, bytes_accessed=1, transcendentals=0)


class Loader:
    def __init__(self, plan, weights, row_shape, col_shape):
        self.plan, self.row_shape, self.col_shape = plan, row_shape, col_shape
        rows, wide = plan.rows, row_shape[1]
        self.moves = []
        if plan.line:
            *whole, last = weights
            self.operands = [plan.inner(), *whole, *last]
            for k in range(4):
                for x in range(2):
                    at = k * plan.block + x * rows
                    self.moves.append((k, x, 0, 0, (at, 0), wide))
                    for i in range(0, col_shape[0], rows):
                        self.moves.append((k, x, 1, wide + i, (i, at), rows))
        else:
            self.operands = list(weights)
            self.moves = [None, None]
        self.count = len(self.operands)

    def specs(self):
        if not self.plan.line:
            return [ANY] * 2
        return [pl.BlockSpec(memory_space=pltpu.SMEM)] + [ANY] * (self.count - 1)

    def scratch(self):
        return [
            pltpu.VMEM(self.row_shape, LOW),
            pltpu.VMEM(self.col_shape, LOW),
            pltpu.SemaphoreType.DMA((len(self.moves),)),
        ]

    def load(self, refs, row_ref, col_ref, sems):
        if not self.plan.line:
            pairs = zip(refs, (row_ref, col_ref))
            made = [pltpu.make_async_copy(*pair, sems.at[i]) for i, pair in enumerate(pairs)]
            for copy in made:
                copy.start()
            for copy in made:
                copy.wait()
            return
        rows = self.plan.rows

        def copies(sources):
            made = []
            for i, (k, x, which, column, there, wide) in enumerate(self.moves):
                if sources[k] is None:
                    continue
                if isinstance(sources[k], tuple):
                    source, row = sources[k][x], 0
                else:
                    source, row = sources[k], x * rows
                target = (row_ref, col_ref)[which]
                made.append(
                    pltpu.make_async_copy(
                        source.at[pl.ds(row, rows), pl.ds(column, wide)],
                        target.at[pl.ds(there[0], rows), pl.ds(there[1], wide)],
                        sems.at[i],
                    )
                )
            return made

        inner, own, near, across_near, out, across, *last = refs
        out_near = tuple(last) if len(last) == 2 else last[0]
        is_inner = inner[0] == 1
        for copy in copies((own, near, None, None)):
            copy.start()

        @pl.when(is_inner)
        def _():
            for copy in copies((None, None, across_near, across)):
                copy.start()

        @pl.when(jnp.logical_not(is_inner))
        def _():
            for copy in copies((None, None, out, out_near)):
                copy.start()

        for copy in copies((own, near, out, out_near)):
            copy.wait()


def rope_tables(positions):
    half_dim = HD // 2
    inverse_freq = ROPE_BASE ** (-2.0 * jnp.arange(half_dim, dtype=F32) / HD)
    angles = positions.astype(F32)[:, None] * inverse_freq[None, :]
    cosine, sine = jnp.cos(angles), jnp.sin(angles)
    return cat([cosine] * 4, 1), cat([-sine, sine] * 2, 1)


def lanes_of(shape):
    return lax.broadcasted_iota(jnp.int32, shape, 1)


def shuffle_halves(values):
    wide = values.shape[1]
    up = pltpu.roll(values, wide - HD // 2, 1)
    down = pltpu.roll(values, HD // 2, 1)
    return jnp.where(lanes_of(values.shape) % HD < HD // 2, up, down)


def tables(cos_ref, sin_ref, pairs):
    cosine, sine = cos_ref[...], sin_ref[...]
    is_key = lanes_of(cosine.shape) < HD
    return (
        cat([cosine] * pairs + [jnp.where(is_key, cosine, 1.0)], 1),
        cat([sine] * pairs + [jnp.where(is_key, sine, 0.0)], 1),
    )


def split_kv(both):
    is_key = lanes_of(both.shape) < HD
    blank = jnp.zeros_like(both)
    key_low = jnp.where(is_key, both, blank)
    value_high = jnp.where(is_key, blank, both)
    return (
        (key_low, pltpu.roll(key_low.astype(F32), HD, 1).astype(LOW)),
        (pltpu.roll(value_high.astype(F32), HD, 1).astype(LOW), value_high),
    )


def allowed_pairs(seg_col, seg_row):
    shape = (seg_col.shape[0], seg_row.shape[1])
    key_at = lax.broadcasted_iota(jnp.int32, shape, 1)
    query_at = lax.broadcasted_iota(jnp.int32, shape, 0)
    return (seg_col == seg_row) & (key_at <= query_at)


def attn_forward_kernel(pairs, loader, *refs):
    weights, refs = refs[: loader.count], refs[loader.count :]
    x_ref, cos_ref, sin_ref, col_ref, row_ref = refs[:5]
    part_ref, ctx_ref, q_ref, kv_ref, lse_ref, wout_ref, wqkv_ref, _, sems = refs[5:]

    @pl.when(pl.program_id(0) == 0)
    def _():
        loader.load(weights, wqkv_ref, wout_ref, sems)

    cosine, sine = tables(cos_ref, sin_ref, pairs)
    qkv = dot(x_ref[...], wqkv_ref[...], 1, 0)
    rotated = (qkv * cosine + shuffle_halves(qkv) * sine).astype(LOW)
    queries, both = rotated[:, : pairs * 128], rotated[:, pairs * 128 :]
    q_ref[...] = queries
    kv_ref[...] = both
    keys, values = split_kv(both)
    allowed = allowed_pairs(col_ref[...], row_ref[0])
    lane = lanes_of((both.shape[0], 128))
    log_sums = jnp.zeros((both.shape[0], 128), F32)
    contexts = []
    for pair in range(pairs):
        heads = queries[:, pair * 128 : (pair + 1) * 128]
        context = None
        for side in range(2):
            scores = dot(heads, keys[side], 1, 1) * HD**-0.5
            masked = jnp.where(allowed, scores, -1e30)
            top = jnp.max(masked, axis=1, keepdims=True)
            weights = jnp.exp(masked - top)
            totals = jnp.sum(weights, axis=1, keepdims=True)
            probs = (weights * (1.0 / totals)).astype(LOW)
            piece = dot(probs, values[side], 1, 0)
            context = piece if context is None else context + piece
            log_sums = jnp.where(lane == 2 * pair + side, top + jnp.log(totals), log_sums)
        contexts.append(context.astype(LOW))
    lse_ref[...] = log_sums
    context_low = cat(contexts, 1)
    ctx_ref[...] = context_low
    part_ref[...] = dot(context_low, wout_ref[...], 1, 0).astype(LOW)


def attn_backward_kernel(pairs, loader, *refs):
    weights, refs = refs[: loader.count], refs[loader.count :]
    cg_ref, x_ref, q_ref, kv_ref, lse_ref, cos_ref, sin_ref, col_ref, row_ref = refs[:9]
    part_ref, gain_ref, *grad_refs = refs[9:-4]
    wqkv_ref, wout_ref, sems, acc_qkv = refs[-4:]
    step = pl.program_id(0)

    @pl.when(step == 0)
    def _():
        loader.load(weights, wqkv_ref, wout_ref, sems)
        acc_qkv[...] = jnp.zeros_like(acc_qkv)
        gain_ref[...] = jnp.zeros_like(gain_ref)

    cosine, sine = tables(cos_ref, sin_ref, pairs)
    scale = HD**-0.5
    ctx_grad = cg_ref[...]
    keys, values = split_kv(kv_ref[...])
    allowed = allowed_pairs(col_ref[...], row_ref[0])
    lane = lanes_of((ctx_grad.shape[0], 128))
    log_sums = lse_ref[...]
    query_grads, key_grad, value_grad = [], None, None
    for pair in range(pairs):
        heads = q_ref[:, pair * 128 : (pair + 1) * 128]
        grads = ctx_grad[:, pair * 128 : (pair + 1) * 128]
        query_grad = None
        for side in range(2):
            here = (lane < HD) if side == 0 else (lane >= HD)
            head = jnp.where(here, heads, jnp.zeros_like(heads))
            grad = jnp.where(here, grads, jnp.zeros_like(grads))
            at = 2 * pair + side
            scores = dot(heads, keys[side], 1, 1) * scale
            probs = jnp.where(allowed, jnp.exp(scores - log_sums[:, at : at + 1]), 0.0)
            prob_grad = dot(grads, values[side], 1, 1)
            delta = jnp.sum(probs * prob_grad, axis=1, keepdims=True)
            score_grad = (probs * (prob_grad - delta)).astype(LOW)
            to_value = dot(probs.astype(LOW), grad, 0, 0)
            to_key = dot(score_grad, head, 0, 0)
            to_query = dot(score_grad, keys[side], 1, 0)
            value_grad = to_value if value_grad is None else value_grad + to_value
            key_grad = to_key if key_grad is None else key_grad + to_key
            query_grad = to_query if query_grad is None else query_grad + to_query
        query_grads.append(query_grad * scale)
    key_grad = (key_grad + pltpu.roll(key_grad, HD, 1)) * scale
    value_grad = value_grad + pltpu.roll(value_grad, HD, 1)
    joined = cat(query_grads + [jnp.where(lane < HD, key_grad, value_grad)], 1)
    low = (joined * cosine - shuffle_halves(joined) * sine).astype(LOW)
    part = dot(low, wqkv_ref[...], 1, 1)
    part_ref[...] = part.astype(LOW)
    gain_ref[...] += jnp.sum(part * x_ref[...].astype(F32), axis=0, keepdims=True)
    acc_qkv[...] += dot(x_ref[...], low, 0, 0)

    @pl.when(step == pl.num_programs(0) - 1)
    def _():
        cut = acc_qkv.shape[0] // len(grad_refs)
        for i, out in enumerate(grad_refs):
            out[...] = acc_qkv[i * cut : (i + 1) * cut, :].astype(LOW)


def once(shape):
    return pl.BlockSpec(shape, lambda i: (0,) * len(shape), pipeline_mode=pl.Buffered(1))


def per_seq(shape):
    return pl.BlockSpec(shape, lambda i: (i,) + (0,) * (len(shape) - 1))


def attn_forward(loader, normed, cosine, sine, seg_col, seg_row):
    rows, width = normed.shape
    heads = loader.col_shape[0]
    return pl.pallas_call(
        functools.partial(attn_forward_kernel, heads // 128, loader),
        grid=(rows // LEN,),
        in_specs=[
            *loader.specs(),
            per_seq((LEN, width)),
            per_seq((LEN, 128)),
            per_seq((LEN, 128)),
            per_seq((LEN, 1)),
            per_seq((1, 1, LEN)),
        ],
        out_specs=[
            per_seq((LEN, width)),
            per_seq((LEN, heads)),
            per_seq((LEN, heads)),
            per_seq((LEN, 128)),
            per_seq((LEN, 128)),
            once(loader.col_shape),
        ],
        out_shape=[
            jax.ShapeDtypeStruct((rows, width), LOW),
            jax.ShapeDtypeStruct((rows, heads), LOW),
            jax.ShapeDtypeStruct((rows, heads), LOW),
            jax.ShapeDtypeStruct((rows, 128), LOW),
            jax.ShapeDtypeStruct((rows, 128), F32),
            jax.ShapeDtypeStruct(loader.col_shape, LOW),
        ],
        scratch_shapes=loader.scratch(),
        compiler_params=pltpu.CompilerParams(vmem_limit_bytes=60 * MIB),
        cost_estimate=SMALL,
        name="attn_forward",
    )(*loader.operands, normed, cosine, sine, seg_col, seg_row)


def attn_backward(loader, ctx_grad, normed, queries, both, lse, cosine, sine, seg_col, seg_row):
    rows, width = normed.shape
    heads = loader.col_shape[0]
    cuts = loader.plan.cuts
    grad = (width // cuts, loader.row_shape[1])
    return pl.pallas_call(
        functools.partial(attn_backward_kernel, heads // 128, loader),
        grid=(rows // LEN,),
        in_specs=[
            *loader.specs(),
            per_seq((LEN, heads)),
            per_seq((LEN, width)),
            per_seq((LEN, heads)),
            per_seq((LEN, 128)),
            per_seq((LEN, 128)),
            per_seq((LEN, 128)),
            per_seq((LEN, 128)),
            per_seq((LEN, 1)),
            per_seq((1, 1, LEN)),
        ],
        out_specs=[per_seq((LEN, width)), once((1, width))] + [once(grad)] * cuts,
        out_shape=[
            jax.ShapeDtypeStruct((rows, width), LOW),
            jax.ShapeDtypeStruct((1, width), F32),
        ]
        + [jax.ShapeDtypeStruct(grad, LOW)] * cuts,
        scratch_shapes=[*loader.scratch(), pltpu.VMEM(loader.row_shape, F32)],
        compiler_params=pltpu.CompilerParams(vmem_limit_bytes=60 * MIB),
        cost_estimate=SMALL,
        name="attn_backward",
    )(*loader.operands, ctx_grad, normed, queries, both, lse, cosine, sine, seg_col, seg_row)


def out_weights_kernel(plan, ctx_ref, res_ref, *refs):
    count = plan.cuts
    qkv_refs, grad_refs, acc = refs[:-1][: count * plan.line], refs[-1 - count : -1], refs[-1]
    step = pl.program_id(0)

    @pl.when(step == 0)
    def _():
        acc[...] = jnp.zeros_like(acc)

    acc[...] += dot(ctx_ref[...], res_ref[...], 0, 0)

    @pl.when(step == pl.num_programs(0) - 1)
    def _():
        if not plan.line:
            grad_refs[0][...] = acc[...].astype(LOW)
            return
        rows = plan.rows
        for k, (qkv, out) in enumerate(zip(qkv_refs, grad_refs)):
            wide = qkv.shape[1]
            out[:, :wide] = qkv[...]
            for x in range(2):
                at = k * plan.block + x * rows
                out[x * rows : (x + 1) * rows, wide:] = acc[:, at : at + rows].astype(LOW)


def out_weights(plan, ctx, res_all, grads_qkv):
    rows, width = res_all.shape
    heads = ctx.shape[1]
    extra = list(grads_qkv) if plan.line else []
    shape = (plan.block, extra[0].shape[1] + heads) if plan.line else (heads, width)
    return pl.pallas_call(
        functools.partial(out_weights_kernel, plan),
        grid=(rows // LEN,),
        in_specs=[per_seq((LEN, heads)), per_seq((LEN, width))] + [once(g.shape) for g in extra],
        out_specs=[once(shape)] * plan.cuts,
        out_shape=[jax.ShapeDtypeStruct(shape, LOW)] * plan.cuts,
        scratch_shapes=[pltpu.VMEM((heads, width), F32)],
        compiler_params=pltpu.CompilerParams(vmem_limit_bytes=40 * MIB),
        cost_estimate=SMALL,
        name="out_weights",
    )(ctx, res_all, *extra)


def residual_backward_kernel(
    back_ref, residual_ref, scale_ref, gain_ref, grad_ref, wout_ref, res_grad_ref, low_ref, ctx_ref
):
    @pl.when(pl.program_id(0) == 0)
    def _():
        back = norm_back(
            back_ref[...].astype(F32), residual_ref[...], scale_ref[...], gain_ref[...]
        )
        total = grad_ref[...].astype(F32) + back
        res_grad_ref[...] = total
        low_ref[...] = total.astype(LOW)

    ctx_ref[...] = dot(low_ref[...], wout_ref[...], 1, 1).astype(LOW)


def residual_backward(back_sum, residual, scale, gain, grad_low, wout_all):
    rows, width = residual.shape
    heads = wout_all.shape[0]
    step = 512
    return pl.pallas_call(
        residual_backward_kernel,
        grid=(heads // step,),
        in_specs=[
            once((rows, width)),
            once((rows, width)),
            once((rows, 1)),
            once((1, width)),
            once((rows, width)),
            per_seq((step, width)),
        ],
        out_specs=[
            once((rows, width)),
            once((rows, width)),
            pl.BlockSpec((rows, step), lambda i: (0, i)),
        ],
        out_shape=[
            jax.ShapeDtypeStruct((rows, width), F32),
            jax.ShapeDtypeStruct((rows, width), LOW),
            jax.ShapeDtypeStruct((rows, heads), LOW),
        ],
        compiler_params=pltpu.CompilerParams(vmem_limit_bytes=60 * MIB),
        cost_estimate=SMALL,
        name="residual_backward",
    )(back_sum, residual, scale, gain[None, :], grad_low, wout_all)


TILE = 512


def ffn_main_kernel(loader, more, *refs):
    weights, refs = refs[: loader.count], refs[loader.count :]
    x_ref, grad_ref = refs[:2]
    back_ref, act_ref, both_ref, down_ref, gate_up_ref, _, sems = refs[2 + more :]

    @pl.when(pl.program_id(0) == 0)
    def _():
        loader.load(weights, gate_up_ref, down_ref, sems)

    hidden = down_ref.shape[0]
    pre = dot(x_ref[...], gate_up_ref[...], 1, 0)
    gate_pre, lifted = pre[:, :hidden], pre[:, hidden:]
    sigmoid_gate = jax.nn.sigmoid(gate_pre)
    silu_gate = gate_pre * sigmoid_gate
    act_ref[...] = (silu_gate * lifted).astype(LOW)
    act_grad = dot(grad_ref[...], down_ref[...], 1, 1)
    gate_grad = act_grad * lifted * sigmoid_gate * (1.0 + gate_pre * (1.0 - sigmoid_gate))
    both_grad = cat([gate_grad.astype(LOW), (act_grad * silu_gate).astype(LOW)], 1)
    both_ref[...] = both_grad
    back = dot(both_grad, gate_up_ref[...], 1, 1)
    if more:
        back = back + refs[2][...].astype(F32)
    back_ref[...] = back.astype(LOW)


def ffn_main(loader, tokens, grads, earlier):
    rows, width = tokens.shape
    hidden = loader.col_shape[0]
    more = [] if earlier is None else [earlier]
    return pl.pallas_call(
        functools.partial(ffn_main_kernel, loader, len(more)),
        grid=(rows // TILE,),
        in_specs=[
            *loader.specs(),
            per_seq((TILE, width)),
            per_seq((TILE, width)),
            *[per_seq((TILE, width))] * len(more),
        ],
        out_specs=[
            per_seq((TILE, width)),
            per_seq((TILE, hidden)),
            per_seq((TILE, 2 * hidden)),
            once(loader.col_shape),
        ],
        out_shape=[
            jax.ShapeDtypeStruct((rows, width), LOW),
            jax.ShapeDtypeStruct((rows, hidden), LOW),
            jax.ShapeDtypeStruct((rows, 2 * hidden), LOW),
            jax.ShapeDtypeStruct(loader.col_shape, LOW),
        ],
        scratch_shapes=loader.scratch(),
        compiler_params=pltpu.CompilerParams(vmem_limit_bytes=60 * MIB),
        cost_estimate=SMALL,
        name="ffn_main",
    )(*loader.operands, tokens, grads, *more)


def ffn_weights_kernel(plan, x_ref, grad_ref, act_ref, both_ref, *out_refs):
    row = dot(x_ref[...], both_ref[...], 0, 0).astype(LOW)
    col = dot(act_ref[...], grad_ref[...], 0, 0).astype(LOW)
    if not plan.line:
        out_refs[0][...], out_refs[1][...] = row, col
        return
    rows, wide, out = plan.rows, row.shape[1], out_refs[0]
    out[:, :wide] = row
    for i in range(0, col.shape[0], rows):
        for x in range(2):
            out[x * rows : (x + 1) * rows, wide + i : wide + i + rows] = col[
                i : i + rows, x * rows : (x + 1) * rows
            ]


def ffn_weights(plan, tokens, grads, act, both_grad, first, count):
    rows, width = tokens.shape
    block = width // 4
    wide, hidden = both_grad.shape[1], act.shape[1]

    def columns(shift):
        return pl.BlockSpec((rows, block), lambda i: (0, i + shift))

    if plan.line:
        out_specs = [pl.BlockSpec((block, wide + hidden), lambda i: (i, 0))]
        out_shape = [jax.ShapeDtypeStruct((count * block, wide + hidden), LOW)]
    else:
        out_specs = [
            pl.BlockSpec((block, wide), lambda i: (i, 0)),
            pl.BlockSpec((hidden, block), lambda i: (0, i)),
        ]
        out_shape = [
            jax.ShapeDtypeStruct((count * block, wide), LOW),
            jax.ShapeDtypeStruct((hidden, count * block), LOW),
        ]
    return pl.pallas_call(
        functools.partial(ffn_weights_kernel, plan),
        grid=(count,),
        in_specs=[columns(first), columns(first), once(act.shape), once(both_grad.shape)],
        out_specs=out_specs,
        out_shape=out_shape,
        compiler_params=pltpu.CompilerParams(vmem_limit_bytes=60 * MIB),
        cost_estimate=SMALL,
        name="ffn_weights",
    )(tokens, grads, act, both_grad)


def ffn_out_kernel(act_1, act_2, down_1, down_2, back_ref, x_ref, out_ref, gain_ref):
    @pl.when(pl.program_id(0) == 0)
    def _():
        gain_ref[...] = jnp.zeros_like(gain_ref)

    out = dot(act_1[...], down_1[...], 1, 0) + dot(act_2[...], down_2[...], 1, 0)
    out_ref[...] = out.astype(LOW)
    product = back_ref[...].astype(F32) * x_ref[...].astype(F32)
    gain_ref[...] += jnp.sum(product, axis=0, keepdims=True)


def ffn_out(act_1, act_2, down_1, down_2, back, tokens):
    rows, width = tokens.shape
    hidden = act_1.shape[1]
    return pl.pallas_call(
        ffn_out_kernel,
        grid=(rows // TILE,),
        in_specs=[
            per_seq((TILE, hidden)),
            per_seq((TILE, hidden)),
            once(down_1.shape),
            once(down_2.shape),
            per_seq((TILE, width)),
            per_seq((TILE, width)),
        ],
        out_specs=[per_seq((TILE, width)), once((1, width))],
        out_shape=[
            jax.ShapeDtypeStruct((rows, width), LOW),
            jax.ShapeDtypeStruct((1, width), F32),
        ],
        compiler_params=pltpu.CompilerParams(vmem_limit_bytes=60 * MIB),
        cost_estimate=SMALL,
        name="ffn_out",
    )(act_1, act_2, down_1, down_2, back, tokens)


def norm_rows(values, gain_vec):
    row_scale = lax.rsqrt(jnp.mean(values * values, axis=1, keepdims=True) + NORM_EPS)
    return values * row_scale * gain_vec, row_scale


def norm_back(row_grad, values, row_scale, gain_vec):
    scaled_grad = row_grad * gain_vec
    return row_scale * scaled_grad - values * row_scale**3 * jnp.mean(
        scaled_grad * values, axis=1, keepdims=True
    )


def adamw_update(master, grad_sum, first_mom, second_mom, decay_rate, step_rate):
    next_first = BETA_ONE * first_mom + (1.0 - BETA_ONE) * grad_sum
    next_second = BETA_TWO * second_mom + (1.0 - BETA_TWO) * grad_sum * grad_sum
    first_hat = next_first / (1.0 - BETA_ONE**STEP)
    second_hat = next_second / (1.0 - BETA_TWO**STEP)
    next_master = master - step_rate * (
        first_hat / (jnp.sqrt(second_hat) + ADAM_EPS) + decay_rate * master
    )
    return (next_master, next_first, next_second)


def sum_over(values, sizes):
    for axis, size in sizes:
        step = 1
        while step < size:
            values = values + lax.ppermute(values, axis, [(i, i ^ step) for i in range(size)])
            step *= 2
    return values


def pick(index, low, high):
    return jnp.where(index == 0, low, high)


class Plane:
    def __init__(self, tp):
        self.tp, self.half = tp, tp // 2
        self.x = lax.axis_index("di")
        self.y = lax.axis_index("tp") // self.half
        self.core = lax.axis_index("tp") % 2
        self.place = self.x * 2 + self.y
        self.axes = ("di", "tp")

    def pairs(self, first):
        def other(index):
            x, t = divmod(index, self.tp)
            along_x = (t % 2 == 0) == first
            return (1 - x) * self.tp + t if along_x else x * self.tp + (t + self.half) % self.tp

        return [(index, other(index)) for index in range(2 * self.tp)]

    def swap_first(self, value):
        return lax.ppermute(value, self.axes, self.pairs(True))

    def swap_second(self, value):
        return lax.ppermute(value, self.axes, self.pairs(False))

    def swap_core(self, value):
        return lax.ppermute(value, "tp", [(i, i ^ 1) for i in range(self.tp)])

    def first_step(self):
        return jnp.where(self.core == 0, 2, 1)

    def at(self, blocks, step):
        return lax.dynamic_index_in_dim(blocks, self.place ^ step, 0, keepdims=False)


def on_device(
    sizes,
    layer_input, out_grad, segment_ids, positions,
    w_query, w_key, w_value, w_out, w_gate, w_up, w_down,
    m_query, m_key, m_value, m_out, m_gate, m_up, m_down,
    v_query, v_key, v_value, v_out, v_gate, v_up, v_down,
    gain_attn, gain_ffn, m_gain_attn, m_gain_ffn, v_gain_attn, v_gain_ffn,
):
    width = layer_input.shape[1]
    plan = Plan(sizes["do"], w_query.shape[0])
    by_x = plan.by_x
    axes = ("di", "tp")
    plane = Plane(sizes["tp"])
    plane_sizes = (("tp", sizes["tp"]), ("di", sizes["di"]))

    gain_one, gain_two = plan.reorder(gain_attn), plan.reorder(gain_ffn)
    inputs_f = plan.reorder(layer_input).astype(F32)
    grad_low = plan.reorder(out_grad)
    normed, scale_one = norm_rows(inputs_f, gain_one)
    normed_all = lax.all_gather(normed.astype(LOW), axes, axis=0, tiled=True)

    marks = cat([segment_ids[None, :], positions[None, :]], 0)
    marks_other = lax.ppermute(marks, "di", PAIR)
    marks_all = cat([by_x(marks, marks_other), by_x(marks_other, marks)], 1)
    seg_all, pos_all = marks_all[0], marks_all[1]
    rows = seg_all.shape[0]
    seqs = rows // LEN
    seg_col, seg_row = seg_all.reshape(rows, 1), seg_all.reshape(seqs, 1, LEN)
    cosine, sine = rope_tables(pos_all)

    def col_halves(weight):
        half = weight.shape[1] // 2
        low = weight.astype(LOW)
        return by_x(low[:, :half], low[:, half:]), by_x(low[:, half:], low[:, :half])

    def row_halves(weight):
        half = weight.shape[0] // 2
        low = weight.astype(LOW)
        return by_x(low[:half], low[half:]), by_x(low[half:], low[:half])

    def col_cut(pair, chunk):
        size = pair[0].shape[1] // CHUNKS
        return tuple(part[:, chunk * size : (chunk + 1) * size] for part in pair)

    def row_cut(pair, chunk):
        size = pair[0].shape[0] // CHUNKS
        return tuple(part[chunk * size : (chunk + 1) * size] for part in pair)

    halves_q, halves_k, halves_v = col_halves(w_query), col_halves(w_key), col_halves(w_value)
    qkv_parts = tuple(cat([q, k, v], 1) for q, k, v in zip(halves_q, halves_k, halves_v))
    out_parts = row_halves(w_out)
    halves_g, halves_u, halves_d = col_halves(w_gate), col_halves(w_up), row_halves(w_down)

    def ffn_parts(chunk):
        gate_up = tuple(
            cat([g, u], 1) for g, u in zip(col_cut(halves_g, chunk), col_cut(halves_u, chunk))
        )
        return gate_up, row_cut(halves_d, chunk)

    hidden = halves_d[0].shape[0] // CHUNKS
    attn_shapes = (width, qkv_parts[0].shape[1]), (out_parts[0].shape[0], width)
    ffn_shapes = (width, 2 * hidden), (hidden, width)
    own_rows = layer_input.shape[0]
    core = lax.axis_index("tp") % 2

    if plan.line:
        attn_own, attn_other = plan.pack(qkv_parts, out_parts)
        own_1, other_1 = plan.pack(*ffn_parts(0))
        own_2, other_2 = plan.pack(*ffn_parts(1))
        attn_theirs = plan.swap(attn_other)
        attn_theirs, marks_all, own_1, other_1 = fence(attn_theirs, marks_all, own_1, other_1)
        attn_block = plan.join(attn_own, attn_theirs)
        near, across = line_near(attn_block)
        theirs_1 = plan.swap(other_1)
        near, across, cosine, sine, own_2, other_2 = fence(
            near, across, cosine, sine, own_2, other_2
        )
        across_near, out = line_far(near, across)
        across_near, out, theirs_1 = fence(across_near, out, theirs_1)
        out_near = line_last(across_near)
        block_1 = plan.join(own_1, theirs_1)
        out_near, normed_all, block_1, grad_low, other_2, seg_col, seg_row = fence(
            out_near, normed_all, block_1, grad_low, other_2, seg_col, seg_row
        )
        attn_weights = (attn_block, near, across_near, out, across, (out_near,))
        near_1, across_1 = line_near(block_1)
    else:
        attn_weights = plan.plain_gather(qkv_parts, out_parts)
        first_weights = plan.plain_gather(*ffn_parts(0))
        second_weights = plan.plain_gather(*ffn_parts(1))
    attn_loader = Loader(plan, attn_weights, *attn_shapes)

    attn_part, ctx, queries, both, lse, wout = attn_forward(
        attn_loader, normed_all, cosine, sine, seg_col, seg_row
    )
    grad_second = plane.swap_second(grad_low)
    if plan.line:
        theirs_2 = plan.swap(other_2)
        attn_part, near_1, across_1, grad_second, theirs_2, grad_low = fence(
            attn_part, near_1, across_1, grad_second, theirs_2, grad_low
        )
        across_near_1, out_1 = line_far(near_1, across_1)
    grad_first = plane.swap_first(grad_low)
    attn_sum = lax.psum_scatter(attn_part, axes, scatter_dimension=0, tiled=True)
    grad_xy = plane.swap_first(grad_second)
    if plan.line:
        across_near_1, out_1, grad_xy, theirs_2, grad_first = fence(
            across_near_1, out_1, grad_xy, theirs_2, grad_first
        )
        block_2 = plan.join(own_2, theirs_2)
        half = plan.rows
        out_near_low = line_last(across_near_1[:half])
        across_2 = lax.ppermute(block_2, "do", MIDDLE)
    grad_x = pick(core, grad_first, grad_second)
    grad_y = pick(core, grad_second, grad_first)
    over_y = cat([pick(plane.y, grad_low, grad_y), pick(plane.y, grad_y, grad_low)], 0)
    over_xy = cat([pick(plane.y, grad_x, grad_xy), pick(plane.y, grad_xy, grad_x)], 0)
    grad_core = cat([by_x(over_y, over_xy), by_x(over_xy, over_y)], 0)
    grad_other = plane.swap_core(grad_core)
    groups = (rows // own_rows // 2, 1, own_rows, width)
    mine, theirs = grad_core.reshape(groups), grad_other.reshape(groups)
    grad_all = cat([pick(core, mine, theirs), pick(core, theirs, mine)], 1).reshape(rows, width)

    if plan.line:
        attn_sum, grad_all, out_near_low, across_2 = fence(
            attn_sum, grad_all, out_near_low, across_2
        )
    residual = inputs_f + attn_sum.astype(F32)
    normed_two, scale_two = norm_rows(residual, gain_two)
    two_low = normed_two.astype(LOW)
    two_all = lax.all_gather(two_low, axes, axis=0, tiled=True)

    if plan.line:
        across_near_1, across_2, block_2, _ = fence(across_near_1, across_2, block_2, two_low)
        out_near_high = line_last(across_near_1[half:])
        near_2 = lax.ppermute(block_2, "do", NEAR)
        near_2, across_2, wout, out_near_high = fence(near_2, across_2, wout, out_near_high)
        across_near_2, out_2 = line_far(near_2, across_2)
        out_near_1 = (out_near_low, out_near_high)
        first_weights = (block_1, near_1, across_near_1, out_1, across_1, out_near_1)
    wout_all = lax.all_gather(wout, axes, axis=0, tiled=True)
    first = Loader(plan, first_weights, *ffn_shapes)
    back_1, act_1, both_1, down_1 = ffn_main(first, two_all, grad_all, None)
    if plan.line:
        back_1, act_1, both_1, across_near_2, out_2 = fence(
            back_1, act_1, both_1, across_near_2, out_2
        )
        out_near_2 = line_last(across_near_2, OUTWARD)
        (last_1,) = ffn_weights(plan, two_all, grad_all, act_1, both_1, 3, 1)
        last_1, both_1 = fence(last_1, both_1)
        far_1 = sum_far(last_1, INWARD)
        (rest_1,) = ffn_weights(plan, two_all, grad_all, act_1, both_1, 0, 3)
        back_1, rest_1, out_near_2 = fence(back_1, rest_1, out_near_2)
        second_weights = (block_2, near_2, across_near_2, out_2, across_2, (out_near_2,))
    else:
        grads_1 = ffn_weights(plan, two_all, grad_all, act_1, both_1, 0, 4)
    second = Loader(plan, second_weights, *ffn_shapes)
    back_2, act_2, both_2, down_2 = ffn_main(second, two_all, grad_all, back_1)
    if plan.line:
        back_2, act_2, both_2, far_1, wout_all = fence(back_2, act_2, both_2, far_1, wout_all)
        block = plan.block
        grads_1 = [rest_1[:block], rest_1[block : 2 * block], rest_1[2 * block :], last_1]
        crossed_1, inward_1 = sum_middle(grads_1, far_1)
    back_sum = lax.psum_scatter(back_2, axes, scatter_dimension=0, tiled=True)
    grads_2 = ffn_weights(plan, two_all, grad_all, act_2, both_2, 0, 4)
    if plan.line:
        grads_2, act_2, crossed_1, inward_1 = fence(grads_2, act_2, crossed_1, inward_1)
        (grads_2,) = grads_2
        grads_2 = [grads_2[k * block : (k + 1) * block] for k in range(4)]
        far_2 = sum_far(grads_2[3])
    out_part, gain_two_part = ffn_out(act_1, act_2, down_1, down_2, back_2, two_all)
    if plan.line:
        back_sum, out_part, far_2 = fence(back_sum, out_part, far_2)

    residual_grad, res_low, ctx_grad = residual_backward(
        back_sum, residual, scale_two, gain_two, grad_low, wout_all
    )
    ctx_grad = lax.all_to_all(ctx_grad, axes, split_axis=1, concat_axis=0, tiled=True)

    out_shape = (rows // own_rows // 2, 2, own_rows, width)
    parts = out_part.reshape(out_shape)
    mine, theirs = pick(core, parts[:, 0], parts[:, 1]), pick(core, parts[:, 1], parts[:, 0])
    summed = add(mine, plane.swap_core(theirs)).astype(LOW)
    step = plane.first_step()
    goes = jnp.stack([plane.at(summed, step), plane.at(summed, 3)])
    goes_on, stays = plane.at(summed, 3 - step), plane.at(summed, 0)

    if plan.line:
        crossed_2, inward_2 = sum_middle(grads_2, far_2)
        near_sum_1, across_sum_1 = sum_near_send(*sum_near_parts(grads_1, crossed_1, inward_1))
        ctx_grad, res_low, goes, goes_on, stays, near_sum_1, across_sum_1 = fence(
            ctx_grad, res_low, goes, goes_on, stays, near_sum_1, across_sum_1
        )
    arrives = plane.swap_first(goes)
    res_all = lax.all_gather(res_low, axes, axis=0, tiled=True)
    back_one_part, gain_one_part, *grads_qkv = attn_backward(
        attn_loader, ctx_grad, normed_all, queries, both, lse, cosine, sine, seg_col, seg_row
    )
    if plan.line:
        gain_parts = jnp.stack([gain_one_part[0] / gain_one, gain_two_part[0] / gain_two])
        gain_parts = sum_over(plan.reorder(gain_parts), plane_sizes + (("do", sizes["do"]),))
        back_one_part, grads_qkv, res_all, crossed_2, inward_2, gain_parts, arrives = fence(
            back_one_part, grads_qkv, res_all, crossed_2, inward_2, gain_parts, arrives
        )
    else:
        gain_parts = jnp.stack([gain_one_part[0] / gain_one, gain_two_part[0] / gain_two])
        gain_parts = sum_over(gain_parts, plane_sizes)
    back_one = lax.psum_scatter(back_one_part, axes, scatter_dimension=0, tiled=True)
    grads_attn = out_weights(plan, ctx, res_all, grads_qkv)
    if plan.line:

        def trade(total):
            return plan.trade(total[:half], total[half:])

        near_sum_2, across_sum_2 = sum_near_send(*sum_near_parts(grads_2, crossed_2, inward_2))
        ffn_pair_1 = trade(sum_own(grads_1, near_sum_1, across_sum_1))
        near_sum_2, across_sum_2, grads_attn = fence(near_sum_2, across_sum_2, grads_attn)
        direct = send_direct(grads_attn)
        ffn_pair_2 = trade(sum_own(grads_2, near_sum_2, across_sum_2))
    summed = add(stays, arrives[0])
    arrives = plane.swap_second(add(goes_on, arrives[1]).astype(LOW))
    if plan.line:
        direct, ffn_pair_1, ffn_pair_2, arrives, back_one, gain_parts = fence(
            direct, ffn_pair_1, ffn_pair_2, arrives, back_one, gain_parts
        )
        attn_pair = trade(add(grads_attn[0], *direct))
        gain_sums = gain_parts
        qkv_pair, out_pair = plan.unpack(attn_pair, attn_shapes[0][1])
        ffn_grads = [plan.unpack(pair, 2 * hidden) for pair in (ffn_pair_1, ffn_pair_2)]
    else:
        qkv_pair = plan.plain_sum_row(grads_qkv[0])
        out_pair = plan.plain_sum_col(grads_attn[0])
        ffn_grads = [
            (plan.plain_sum_row(row), plan.plain_sum_col(col)) for row, col in (grads_1, grads_2)
        ]
        gain_sums = sum_over(gain_parts, (("do", sizes["do"]),))
    in_grad = residual_grad + norm_back(back_one.astype(F32), inputs_f, scale_one, gain_one)
    out_value = residual + add(summed, arrives)
    grad_gain_attn, grad_gain_ffn = gain_sums[0], gain_sums[1]

    def join(pair, axis):
        own, other = pair[0], pair[1].astype(F32)
        return by_x(cat([own, other], axis), cat([other, own], axis))

    def from_chunks(pairs, axis):
        own = cat([pair[0] for pair in pairs], axis)
        other = cat([pair[1] for pair in pairs], axis)
        return join((own, other), axis)

    def cut(pair, start, stop):
        return tuple(part[:, start:stop] for part in pair)

    at_k = halves_q[0].shape[1]
    at_v = at_k + halves_k[0].shape[1]
    end = at_v + halves_v[0].shape[1]
    grad_query = join(cut(qkv_pair, 0, at_k), 1)
    grad_key = join(cut(qkv_pair, at_k, at_v), 1)
    grad_value = join(cut(qkv_pair, at_v, end), 1)
    grad_out = join(out_pair, 0)
    grad_gate = from_chunks([cut(gu, 0, hidden) for gu, _ in ffn_grads], 1)
    grad_up = from_chunks([cut(gu, hidden, 2 * hidden) for gu, _ in ffn_grads], 1)
    grad_down = from_chunks([down for _, down in ffn_grads], 0)

    grads = (grad_query, grad_key, grad_value, grad_out, grad_gate, grad_up, grad_down)
    masters = (w_query, w_key, w_value, w_out, w_gate, w_up, w_down)
    firsts = (m_query, m_key, m_value, m_out, m_gate, m_up, m_down)
    seconds = (v_query, v_key, v_value, v_out, v_gate, v_up, v_down)
    updated = [
        adamw_update(w, g, m, v, WEIGHT_DECAY, LEARN_RATE)
        for w, g, m, v in zip(masters, grads, firsts, seconds)
    ]
    gain_updated = [
        adamw_update(gain_attn, grad_gain_attn, m_gain_attn, v_gain_attn, 0.0, GAIN_RATE),
        adamw_update(gain_ffn, grad_gain_ffn, m_gain_ffn, v_gain_ffn, 0.0, GAIN_RATE),
    ]
    return (
        plan.reorder(out_value.astype(LOW)),
        plan.reorder(in_grad),
        *grads,
        *[u[0] for u in updated],
        *[u[1] for u in updated],
        *[u[2] for u in updated],
        grad_gain_attn,
        grad_gain_ffn,
        *[u[0] for u in gain_updated],
        *[u[1] for u in gain_updated],
        *[u[2] for u in gain_updated],
    )


def solution(mesh):
    dp, tp = mesh.shape["dp"], mesh.shape["tp"]
    split = Mesh(mesh.devices.reshape(dp // 2, 2, tp), ("do", "di", "tp"))
    sizes = {"do": dp // 2, "di": 2, "tp": tp}
    dp_axes = ("do", "di")
    tokens = P(("do", "di", "tp"), None)
    by_rows, by_cols = P(dp_axes, "tp"), P("tp", dp_axes)
    weights = (by_rows, by_rows, by_rows, by_cols, by_rows, by_rows, by_cols)
    gains = (P(),) * 6
    in_specs = (tokens, tokens, P(dp_axes), P(dp_axes)) + weights * 3 + gains
    out_specs = (tokens, tokens) + weights * 4 + (P(),) * 2 + gains
    return jax.shard_map(
        functools.partial(on_device, sizes),
        mesh=split,
        in_specs=in_specs,
        out_specs=out_specs,
        check_vma=False,
    )
```

```python
import functools

import jax
import jax.numpy as jnp
from jax import lax
from jax.experimental import pallas as pl
from jax.experimental.pallas import tpu as pltpu
from jax.sharding import Mesh
from jax.sharding import PartitionSpec as P

HD = 64
LEN = 512
STEP = 5
CHUNKS = 2

NORM_EPS = 1e-05
ROPE_BASE = 500000.0
BETA_ONE = 0.9
BETA_TWO = 0.95
LEARN_RATE = 0.02
GAIN_RATE = 0.5
WEIGHT_DECAY = 0.1
ADAM_EPS = 1e-08

LOW = jnp.bfloat16
F32 = jnp.float32
MIB = 1024 * 1024

NEAR = [(0, 1), (1, 0), (2, 3), (3, 2)]
MIDDLE = [(1, 2), (2, 1)]
CROSS = [(0, 2), (1, 3), (2, 0), (3, 1)]
MIRROR = [(0, 3), (1, 2), (2, 1), (3, 0)]
OUTWARD = [(1, 0), (2, 3)]
INWARD = [(0, 1), (3, 2)]
PAIR = [(0, 1), (1, 0)]


def dot(lhs, rhs, lhs_dim, rhs_dim):
    return lax.dot_general(
        lhs, rhs, (((lhs_dim,), (rhs_dim,)), ((), ())), preferred_element_type=F32
    )


def cat(parts, axis):
    return jnp.concatenate(parts, axis)


def fence(*values):
    return lax.optimization_barrier(values)


def line_near(own):
    return lax.ppermute(own, "do", NEAR), lax.ppermute(own, "do", MIDDLE)


def line_far(near, across):
    return lax.ppermute(near, "do", MIDDLE), lax.ppermute(across, "do", NEAR)


def line_last(across_near, perm=NEAR):
    return lax.ppermute(across_near, "do", perm)


def add(part, *arrived):
    total = part.astype(F32)
    for piece in arrived:
        total = total + piece.astype(F32)
    return total


def is_inner():
    place = lax.axis_index("do")
    return (place == 1) | (place == 2)


def add_inner(part, arrived):
    return add(part, jnp.where(is_inner(), arrived, jnp.zeros_like(arrived)))


def sum_middle(parts, far):
    second = add_inner(parts[2], cat(far, 0)).astype(LOW)
    return lax.ppermute(second, "do", MIDDLE), lax.ppermute(second, "do", NEAR)


def sum_near_parts(parts, crossed, inward):
    return add_inner(parts[1], crossed).astype(LOW), add_inner(parts[3], inward).astype(LOW)


def sum_near_send(first, third):
    return lax.ppermute(first, "do", NEAR), lax.ppermute(third, "do", MIDDLE)


def sum_own(parts, from_near, from_across):
    return add_inner(parts[0], from_across) + from_near.astype(F32)


def send_direct(parts):
    return [
        lax.ppermute(part, "do", perm) for part, perm in zip(parts[1:], (NEAR, CROSS, MIRROR))
    ]


class Plan:
    def __init__(self, outer, per_device):
        self.rows = per_device
        self.block = 2 * per_device
        self.line = outer == 4 and per_device == 256
        self.cuts = 4 if self.line else 1

    def reorder(self, values):
        if not self.line:
            return values
        place = lax.axis_index("do")
        quarter = values.shape[-1] // 4
        a, b, c, d = (values[..., i * quarter : (i + 1) * quarter] for i in range(4))
        values = jnp.where(place % 2 == 1, cat([b, a, d, c], -1), values)
        half = 2 * quarter
        turned = cat([values[..., half:], values[..., :half]], -1)
        return jnp.where(place >= 2, turned, values)

    def by_x(self, low, high):
        return jnp.where(lax.axis_index("di") == 0, low, high)

    def inner(self):
        return is_inner().astype(jnp.int32).reshape(1)

    def pack(self, row_part, col_part):
        rows, packs = self.rows, []
        for row_side, side in zip(row_part, col_part):
            pieces = [side[i : i + rows] for i in range(0, side.shape[0], rows)]
            packs.append(cat([row_side] + pieces, 1))
        return packs

    def swap(self, other):
        return lax.ppermute(other, "di", PAIR)

    def join(self, own, theirs, axis=0):
        return cat([self.by_x(own, theirs), self.by_x(theirs, own)], axis)

    def plain_gather(self, row_part, col_part):
        full = []
        for (own, other), axis in ((row_part, 0), (col_part, 1)):
            block = self.join(own, self.swap(other), axis)
            full.append(lax.all_gather(block, "do", axis=axis, tiled=True))
        return tuple(full)

    def unpack(self, pair, wide):
        cuts = range(wide, pair[0].shape[1], self.rows)
        return (
            tuple(side[:, :wide] for side in pair),
            tuple(cat([side[:, i : i + self.rows] for i in cuts], 0) for side in pair),
        )

    def plain_sum_row(self, grad):
        total = lax.psum_scatter(grad, "do", scatter_dimension=0, tiled=True)
        return self.trade(total[: self.rows], total[self.rows :])

    def plain_sum_col(self, grad):
        total = lax.psum_scatter(grad, "do", scatter_dimension=1, tiled=True)
        return self.trade(total[:, : self.rows], total[:, self.rows :])

    def trade(self, low, high):
        theirs = lax.ppermute(self.by_x(high, low).astype(LOW), "di", PAIR)
        return self.by_x(low, high).astype(F32), theirs


ANY = pl.BlockSpec(memory_space=pl.ANY)
SMALL = pl.CostEstimate(flops=1, bytes_accessed=1, transcendentals=0)


class Loader:
    def __init__(self, plan, weights, row_shape, col_shape):
        self.plan, self.row_shape, self.col_shape = plan, row_shape, col_shape
        rows, wide = plan.rows, row_shape[1]
        self.moves = []
        if plan.line:
            *whole, last = weights
            self.operands = [plan.inner(), *whole, *last]
            for k in range(4):
                for x in range(2):
                    at = k * plan.block + x * rows
                    self.moves.append((k, x, 0, 0, (at, 0), wide))
                    for i in range(0, col_shape[0], rows):
                        self.moves.append((k, x, 1, wide + i, (i, at), rows))
        else:
            self.operands = list(weights)
            self.moves = [None, None]
        self.count = len(self.operands)

    def specs(self):
        if not self.plan.line:
            return [ANY] * 2
        return [pl.BlockSpec(memory_space=pltpu.SMEM)] + [ANY] * (self.count - 1)

    def scratch(self):
        return [
            pltpu.VMEM(self.row_shape, LOW),
            pltpu.VMEM(self.col_shape, LOW),
            pltpu.SemaphoreType.DMA((len(self.moves),)),
        ]

    def load(self, refs, row_ref, col_ref, sems):
        if not self.plan.line:
            pairs = zip(refs, (row_ref, col_ref))
            made = [pltpu.make_async_copy(*pair, sems.at[i]) for i, pair in enumerate(pairs)]
            for copy in made:
                copy.start()
            for copy in made:
                copy.wait()
            return
        rows = self.plan.rows

        def copies(sources):
            made = []
            for i, (k, x, which, column, there, wide) in enumerate(self.moves):
                if sources[k] is None:
                    continue
                if isinstance(sources[k], tuple):
                    source, row = sources[k][x], 0
                else:
                    source, row = sources[k], x * rows
                target = (row_ref, col_ref)[which]
                made.append(
                    pltpu.make_async_copy(
                        source.at[pl.ds(row, rows), pl.ds(column, wide)],
                        target.at[pl.ds(there[0], rows), pl.ds(there[1], wide)],
                        sems.at[i],
                    )
                )
            return made

        inner, own, near, across_near, out, across, *last = refs
        out_near = tuple(last) if len(last) == 2 else last[0]
        is_inner = inner[0] == 1
        for copy in copies((own, near, None, None)):
            copy.start()

        @pl.when(is_inner)
        def _():
            for copy in copies((None, None, across_near, across)):
                copy.start()

        @pl.when(jnp.logical_not(is_inner))
        def _():
            for copy in copies((None, None, out, out_near)):
                copy.start()

        for copy in copies((own, near, out, out_near)):
            copy.wait()


def rope_tables(positions):
    half_dim = HD // 2
    inverse_freq = ROPE_BASE ** (-2.0 * jnp.arange(half_dim, dtype=F32) / HD)
    angles = positions.astype(F32)[:, None] * inverse_freq[None, :]
    cosine, sine = jnp.cos(angles), jnp.sin(angles)
    return cat([cosine] * 4, 1), cat([-sine, sine] * 2, 1)


def lanes_of(shape):
    return lax.broadcasted_iota(jnp.int32, shape, 1)


def shuffle_halves(values):
    wide = values.shape[1]
    up = pltpu.roll(values, wide - HD // 2, 1)
    down = pltpu.roll(values, HD // 2, 1)
    return jnp.where(lanes_of(values.shape) % HD < HD // 2, up, down)


def tables(cos_ref, sin_ref, pairs):
    cosine, sine = cos_ref[...], sin_ref[...]
    is_key = lanes_of(cosine.shape) < HD
    return (
        cat([cosine] * pairs + [jnp.where(is_key, cosine, 1.0)], 1),
        cat([sine] * pairs + [jnp.where(is_key, sine, 0.0)], 1),
    )


def split_kv(both):
    is_key = lanes_of(both.shape) < HD
    blank = jnp.zeros_like(both)
    key_low = jnp.where(is_key, both, blank)
    value_high = jnp.where(is_key, blank, both)
    return (
        (key_low, pltpu.roll(key_low.astype(F32), HD, 1).astype(LOW)),
        (pltpu.roll(value_high.astype(F32), HD, 1).astype(LOW), value_high),
    )


def allowed_pairs(seg_col, seg_row):
    shape = (seg_col.shape[0], seg_row.shape[1])
    key_at = lax.broadcasted_iota(jnp.int32, shape, 1)
    query_at = lax.broadcasted_iota(jnp.int32, shape, 0)
    return (seg_col == seg_row) & (key_at <= query_at)


def attn_forward_kernel(pairs, loader, *refs):
    weights, refs = refs[: loader.count], refs[loader.count :]
    x_ref, cos_ref, sin_ref, col_ref, row_ref = refs[:5]
    part_ref, ctx_ref, q_ref, kv_ref, lse_ref, wout_ref, wqkv_ref, _, sems = refs[5:]

    @pl.when(pl.program_id(0) == 0)
    def _():
        loader.load(weights, wqkv_ref, wout_ref, sems)

    cosine, sine = tables(cos_ref, sin_ref, pairs)
    qkv = dot(x_ref[...], wqkv_ref[...], 1, 0)
    rotated = (qkv * cosine + shuffle_halves(qkv) * sine).astype(LOW)
    queries, both = rotated[:, : pairs * 128], rotated[:, pairs * 128 :]
    q_ref[...] = queries
    kv_ref[...] = both
    keys, values = split_kv(both)
    allowed = allowed_pairs(col_ref[...], row_ref[0])
    lane = lanes_of((both.shape[0], 128))
    log_sums = jnp.zeros((both.shape[0], 128), F32)
    contexts = []
    for pair in range(pairs):
        heads = queries[:, pair * 128 : (pair + 1) * 128]
        context = None
        for side in range(2):
            scores = dot(heads, keys[side], 1, 1) * HD**-0.5
            masked = jnp.where(allowed, scores, -1e30)
            top = jnp.max(masked, axis=1, keepdims=True)
            weights = jnp.exp(masked - top)
            totals = jnp.sum(weights, axis=1, keepdims=True)
            probs = (weights * (1.0 / totals)).astype(LOW)
            piece = dot(probs, values[side], 1, 0)
            context = piece if context is None else context + piece
            log_sums = jnp.where(lane == 2 * pair + side, top + jnp.log(totals), log_sums)
        contexts.append(context.astype(LOW))
    lse_ref[...] = log_sums
    context_low = cat(contexts, 1)
    ctx_ref[...] = context_low
    part_ref[...] = dot(context_low, wout_ref[...], 1, 0).astype(LOW)


def attn_backward_kernel(pairs, loader, *refs):
    weights, refs = refs[: loader.count], refs[loader.count :]
    cg_ref, x_ref, q_ref, kv_ref, lse_ref, cos_ref, sin_ref, col_ref, row_ref = refs[:9]
    part_ref, gain_ref, *grad_refs = refs[9:-4]
    wqkv_ref, wout_ref, sems, acc_qkv = refs[-4:]
    step = pl.program_id(0)

    @pl.when(step == 0)
    def _():
        loader.load(weights, wqkv_ref, wout_ref, sems)
        acc_qkv[...] = jnp.zeros_like(acc_qkv)
        gain_ref[...] = jnp.zeros_like(gain_ref)

    cosine, sine = tables(cos_ref, sin_ref, pairs)
    scale = HD**-0.5
    ctx_grad = cg_ref[...]
    keys, values = split_kv(kv_ref[...])
    allowed = allowed_pairs(col_ref[...], row_ref[0])
    lane = lanes_of((ctx_grad.shape[0], 128))
    log_sums = lse_ref[...]
    query_grads, key_grad, value_grad = [], None, None
    for pair in range(pairs):
        heads = q_ref[:, pair * 128 : (pair + 1) * 128]
        grads = ctx_grad[:, pair * 128 : (pair + 1) * 128]
        query_grad = None
        for side in range(2):
            here = (lane < HD) if side == 0 else (lane >= HD)
            head = jnp.where(here, heads, jnp.zeros_like(heads))
            grad = jnp.where(here, grads, jnp.zeros_like(grads))
            at = 2 * pair + side
            scores = dot(heads, keys[side], 1, 1) * scale
            probs = jnp.where(allowed, jnp.exp(scores - log_sums[:, at : at + 1]), 0.0)
            prob_grad = dot(grads, values[side], 1, 1)
            delta = jnp.sum(probs * prob_grad, axis=1, keepdims=True)
            score_grad = (probs * (prob_grad - delta)).astype(LOW)
            to_value = dot(probs.astype(LOW), grad, 0, 0)
            to_key = dot(score_grad, head, 0, 0)
            to_query = dot(score_grad, keys[side], 1, 0)
            value_grad = to_value if value_grad is None else value_grad + to_value
            key_grad = to_key if key_grad is None else key_grad + to_key
            query_grad = to_query if query_grad is None else query_grad + to_query
        query_grads.append(query_grad * scale)
    key_grad = (key_grad + pltpu.roll(key_grad, HD, 1)) * scale
    value_grad = value_grad + pltpu.roll(value_grad, HD, 1)
    joined = cat(query_grads + [jnp.where(lane < HD, key_grad, value_grad)], 1)
    low = (joined * cosine - shuffle_halves(joined) * sine).astype(LOW)
    part = dot(low, wqkv_ref[...], 1, 1)
    part_ref[...] = part.astype(LOW)
    gain_ref[...] += jnp.sum(part * x_ref[...].astype(F32), axis=0, keepdims=True)
    acc_qkv[...] += dot(x_ref[...], low, 0, 0)

    @pl.when(step == pl.num_programs(0) - 1)
    def _():
        cut = acc_qkv.shape[0] // len(grad_refs)
        for i, out in enumerate(grad_refs):
            out[...] = acc_qkv[i * cut : (i + 1) * cut, :].astype(LOW)


def once(shape):
    return pl.BlockSpec(shape, lambda i: (0,) * len(shape), pipeline_mode=pl.Buffered(1))


def per_seq(shape):
    return pl.BlockSpec(shape, lambda i: (i,) + (0,) * (len(shape) - 1))


def attn_forward(loader, normed, cosine, sine, seg_col, seg_row):
    rows, width = normed.shape
    heads = loader.col_shape[0]
    return pl.pallas_call(
        functools.partial(attn_forward_kernel, heads // 128, loader),
        grid=(rows // LEN,),
        in_specs=[
            *loader.specs(),
            per_seq((LEN, width)),
            per_seq((LEN, 128)),
            per_seq((LEN, 128)),
            per_seq((LEN, 1)),
            per_seq((1, 1, LEN)),
        ],
        out_specs=[
            per_seq((LEN, width)),
            per_seq((LEN, heads)),
            per_seq((LEN, heads)),
            per_seq((LEN, 128)),
            per_seq((LEN, 128)),
            once(loader.col_shape),
        ],
        out_shape=[
            jax.ShapeDtypeStruct((rows, width), LOW),
            jax.ShapeDtypeStruct((rows, heads), LOW),
            jax.ShapeDtypeStruct((rows, heads), LOW),
            jax.ShapeDtypeStruct((rows, 128), LOW),
            jax.ShapeDtypeStruct((rows, 128), F32),
            jax.ShapeDtypeStruct(loader.col_shape, LOW),
        ],
        scratch_shapes=loader.scratch(),
        compiler_params=pltpu.CompilerParams(vmem_limit_bytes=60 * MIB),
        cost_estimate=SMALL,
        name="attn_forward",
    )(*loader.operands, normed, cosine, sine, seg_col, seg_row)


def attn_backward(loader, ctx_grad, normed, queries, both, lse, cosine, sine, seg_col, seg_row):
    rows, width = normed.shape
    heads = loader.col_shape[0]
    cuts = loader.plan.cuts
    grad = (width // cuts, loader.row_shape[1])
    return pl.pallas_call(
        functools.partial(attn_backward_kernel, heads // 128, loader),
        grid=(rows // LEN,),
        in_specs=[
            *loader.specs(),
            per_seq((LEN, heads)),
            per_seq((LEN, width)),
            per_seq((LEN, heads)),
            per_seq((LEN, 128)),
            per_seq((LEN, 128)),
            per_seq((LEN, 128)),
            per_seq((LEN, 128)),
            per_seq((LEN, 1)),
            per_seq((1, 1, LEN)),
        ],
        out_specs=[per_seq((LEN, width)), once((1, width))] + [once(grad)] * cuts,
        out_shape=[
            jax.ShapeDtypeStruct((rows, width), LOW),
            jax.ShapeDtypeStruct((1, width), F32),
        ]
        + [jax.ShapeDtypeStruct(grad, LOW)] * cuts,
        scratch_shapes=[*loader.scratch(), pltpu.VMEM(loader.row_shape, F32)],
        compiler_params=pltpu.CompilerParams(vmem_limit_bytes=60 * MIB),
        cost_estimate=SMALL,
        name="attn_backward",
    )(*loader.operands, ctx_grad, normed, queries, both, lse, cosine, sine, seg_col, seg_row)


def out_weights_kernel(plan, ctx_ref, res_ref, *refs):
    count = plan.cuts
    qkv_refs, grad_refs, acc = refs[:-1][: count * plan.line], refs[-1 - count : -1], refs[-1]
    step = pl.program_id(0)

    @pl.when(step == 0)
    def _():
        acc[...] = jnp.zeros_like(acc)

    acc[...] += dot(ctx_ref[...], res_ref[...], 0, 0)

    @pl.when(step == pl.num_programs(0) - 1)
    def _():
        if not plan.line:
            grad_refs[0][...] = acc[...].astype(LOW)
            return
        rows = plan.rows
        for k, (qkv, out) in enumerate(zip(qkv_refs, grad_refs)):
            wide = qkv.shape[1]
            out[:, :wide] = qkv[...]
            for x in range(2):
                at = k * plan.block + x * rows
                out[x * rows : (x + 1) * rows, wide:] = acc[:, at : at + rows].astype(LOW)


def out_weights(plan, ctx, res_all, grads_qkv):
    rows, width = res_all.shape
    heads = ctx.shape[1]
    extra = list(grads_qkv) if plan.line else []
    shape = (plan.block, extra[0].shape[1] + heads) if plan.line else (heads, width)
    return pl.pallas_call(
        functools.partial(out_weights_kernel, plan),
        grid=(rows // LEN,),
        in_specs=[per_seq((LEN, heads)), per_seq((LEN, width))] + [once(g.shape) for g in extra],
        out_specs=[once(shape)] * plan.cuts,
        out_shape=[jax.ShapeDtypeStruct(shape, LOW)] * plan.cuts,
        scratch_shapes=[pltpu.VMEM((heads, width), F32)],
        compiler_params=pltpu.CompilerParams(vmem_limit_bytes=40 * MIB),
        cost_estimate=SMALL,
        name="out_weights",
    )(ctx, res_all, *extra)


def residual_backward_kernel(
    back_ref, residual_ref, scale_ref, gain_ref, grad_ref, wout_ref, res_grad_ref, low_ref, ctx_ref
):
    @pl.when(pl.program_id(0) == 0)
    def _():
        back = norm_back(
            back_ref[...].astype(F32), residual_ref[...], scale_ref[...], gain_ref[...]
        )
        total = grad_ref[...].astype(F32) + back
        res_grad_ref[...] = total
        low_ref[...] = total.astype(LOW)

    ctx_ref[...] = dot(low_ref[...], wout_ref[...], 1, 1).astype(LOW)


def residual_backward(back_sum, residual, scale, gain, grad_low, wout_all):
    rows, width = residual.shape
    heads = wout_all.shape[0]
    step = 512
    return pl.pallas_call(
        residual_backward_kernel,
        grid=(heads // step,),
        in_specs=[
            once((rows, width)),
            once((rows, width)),
            once((rows, 1)),
            once((1, width)),
            once((rows, width)),
            per_seq((step, width)),
        ],
        out_specs=[
            once((rows, width)),
            once((rows, width)),
            pl.BlockSpec((rows, step), lambda i: (0, i)),
        ],
        out_shape=[
            jax.ShapeDtypeStruct((rows, width), F32),
            jax.ShapeDtypeStruct((rows, width), LOW),
            jax.ShapeDtypeStruct((rows, heads), LOW),
        ],
        compiler_params=pltpu.CompilerParams(vmem_limit_bytes=60 * MIB),
        cost_estimate=SMALL,
        name="residual_backward",
    )(back_sum, residual, scale, gain[None, :], grad_low, wout_all)


TILE = 512


def ffn_main_kernel(loader, more, *refs):
    weights, refs = refs[: loader.count], refs[loader.count :]
    x_ref, grad_ref = refs[:2]
    back_ref, act_ref, both_ref, down_ref, gate_up_ref, _, sems = refs[2 + more :]

    @pl.when(pl.program_id(0) == 0)
    def _():
        loader.load(weights, gate_up_ref, down_ref, sems)

    hidden = down_ref.shape[0]
    pre = dot(x_ref[...], gate_up_ref[...], 1, 0)
    gate_pre, lifted = pre[:, :hidden], pre[:, hidden:]
    sigmoid_gate = jax.nn.sigmoid(gate_pre)
    silu_gate = gate_pre * sigmoid_gate
    act_ref[...] = (silu_gate * lifted).astype(LOW)
    act_grad = dot(grad_ref[...], down_ref[...], 1, 1)
    gate_grad = act_grad * lifted * sigmoid_gate * (1.0 + gate_pre * (1.0 - sigmoid_gate))
    both_grad = cat([gate_grad.astype(LOW), (act_grad * silu_gate).astype(LOW)], 1)
    both_ref[...] = both_grad
    back = dot(both_grad, gate_up_ref[...], 1, 1)
    if more:
        back = back + refs[2][...].astype(F32)
    back_ref[...] = back.astype(LOW)


def ffn_main(loader, tokens, grads, earlier):
    rows, width = tokens.shape
    hidden = loader.col_shape[0]
    more = [] if earlier is None else [earlier]
    return pl.pallas_call(
        functools.partial(ffn_main_kernel, loader, len(more)),
        grid=(rows // TILE,),
        in_specs=[
            *loader.specs(),
            per_seq((TILE, width)),
            per_seq((TILE, width)),
            *[per_seq((TILE, width))] * len(more),
        ],
        out_specs=[
            per_seq((TILE, width)),
            per_seq((TILE, hidden)),
            per_seq((TILE, 2 * hidden)),
            once(loader.col_shape),
        ],
        out_shape=[
            jax.ShapeDtypeStruct((rows, width), LOW),
            jax.ShapeDtypeStruct((rows, hidden), LOW),
            jax.ShapeDtypeStruct((rows, 2 * hidden), LOW),
            jax.ShapeDtypeStruct(loader.col_shape, LOW),
        ],
        scratch_shapes=loader.scratch(),
        compiler_params=pltpu.CompilerParams(vmem_limit_bytes=60 * MIB),
        cost_estimate=SMALL,
        name="ffn_main",
    )(*loader.operands, tokens, grads, *more)


def ffn_weights_kernel(plan, x_ref, grad_ref, act_ref, both_ref, *out_refs):
    row = dot(x_ref[...], both_ref[...], 0, 0).astype(LOW)
    col = dot(act_ref[...], grad_ref[...], 0, 0).astype(LOW)
    if not plan.line:
        out_refs[0][...], out_refs[1][...] = row, col
        return
    rows, wide = plan.rows, row.shape[1]

    def pack(halves):
        for x, (out, at) in enumerate(halves):
            out[at : at + rows, :wide] = row[x * rows : (x + 1) * rows]
            for i in range(0, col.shape[0], rows):
                out[at : at + rows, wide + i : wide + i + rows] = col[
                    i : i + rows, x * rows : (x + 1) * rows
                ]

    if len(out_refs) == 1:
        pack([(out_refs[0], 0), (out_refs[0], rows)])
        return

    @pl.when(pl.program_id(0) == 0)
    def _():
        pack([(out_refs[0], 0), (out_refs[1], 0)])

    @pl.when(pl.program_id(0) > 0)
    def _():
        pack([(out_refs[2], 0), (out_refs[2], rows)])


def ffn_weights(plan, tokens, grads, act, both_grad, order):
    rows, width = tokens.shape
    block = width // 4
    wide, hidden = both_grad.shape[1], act.shape[1]
    count, begin = len(order), order[0]
    step = order[1] - order[0] if begin < 3 else (order[1] - 3) % 4
    assert all(order[i] == (begin + step * i) % 4 for i in range(count))

    def columns():
        return pl.BlockSpec((rows, block), lambda i: (0, (begin + step * i) % 4))

    if not plan.line:
        out_specs = [
            pl.BlockSpec((block, wide), lambda i: ((begin + step * i) % 4, 0)),
            pl.BlockSpec((hidden, block), lambda i: (0, (begin + step * i) % 4)),
        ]
        shapes = [(count * block, wide), (hidden, count * block)]
    elif begin == 3:
        out_specs = [once((plan.rows, wide + hidden))] * 2 + [
            pl.BlockSpec((block, wide + hidden), lambda i: (jnp.maximum(i - 1, 0), 0))
        ]
        shapes = [(plan.rows, wide + hidden)] * 2 + [((count - 1) * block, wide + hidden)]
    else:
        out_specs = [pl.BlockSpec((block, wide + hidden), lambda i: (i, 0))]
        shapes = [(count * block, wide + hidden)]
    return pl.pallas_call(
        functools.partial(ffn_weights_kernel, plan),
        grid=(count,),
        in_specs=[columns(), columns(), once(act.shape), once(both_grad.shape)],
        out_specs=out_specs,
        out_shape=[jax.ShapeDtypeStruct(shape, LOW) for shape in shapes],
        compiler_params=pltpu.CompilerParams(vmem_limit_bytes=60 * MIB),
        cost_estimate=SMALL,
        name="ffn_weights",
    )(tokens, grads, act, both_grad)


def ffn_out_kernel(act_1, act_2, down_1, down_2, back_ref, x_ref, out_ref, gain_ref):
    @pl.when(pl.program_id(0) == 0)
    def _():
        gain_ref[...] = jnp.zeros_like(gain_ref)

    out = dot(act_1[...], down_1[...], 1, 0) + dot(act_2[...], down_2[...], 1, 0)
    out_ref[...] = out.astype(LOW)
    product = back_ref[...].astype(F32) * x_ref[...].astype(F32)
    gain_ref[...] += jnp.sum(product, axis=0, keepdims=True)


def ffn_out(act_1, act_2, down_1, down_2, back, tokens):
    rows, width = tokens.shape
    hidden = act_1.shape[1]
    return pl.pallas_call(
        ffn_out_kernel,
        grid=(rows // TILE,),
        in_specs=[
            per_seq((TILE, hidden)),
            per_seq((TILE, hidden)),
            once(down_1.shape),
            once(down_2.shape),
            per_seq((TILE, width)),
            per_seq((TILE, width)),
        ],
        out_specs=[per_seq((TILE, width)), once((1, width))],
        out_shape=[
            jax.ShapeDtypeStruct((rows, width), LOW),
            jax.ShapeDtypeStruct((1, width), F32),
        ],
        compiler_params=pltpu.CompilerParams(vmem_limit_bytes=60 * MIB),
        cost_estimate=SMALL,
        name="ffn_out",
    )(act_1, act_2, down_1, down_2, back, tokens)


def norm_rows(values, gain_vec):
    row_scale = lax.rsqrt(jnp.mean(values * values, axis=1, keepdims=True) + NORM_EPS)
    return values * row_scale * gain_vec, row_scale


def norm_back(row_grad, values, row_scale, gain_vec):
    scaled_grad = row_grad * gain_vec
    return row_scale * scaled_grad - values * row_scale**3 * jnp.mean(
        scaled_grad * values, axis=1, keepdims=True
    )


def adamw_update(master, grad_sum, first_mom, second_mom, decay_rate, step_rate):
    next_first = BETA_ONE * first_mom + (1.0 - BETA_ONE) * grad_sum
    next_second = BETA_TWO * second_mom + (1.0 - BETA_TWO) * grad_sum * grad_sum
    first_hat = next_first / (1.0 - BETA_ONE**STEP)
    second_hat = next_second / (1.0 - BETA_TWO**STEP)
    next_master = master - step_rate * (
        first_hat / (jnp.sqrt(second_hat) + ADAM_EPS) + decay_rate * master
    )
    return (next_master, next_first, next_second)


def sum_over(values, sizes):
    for axis, size in sizes:
        step = 1
        while step < size:
            values = values + lax.ppermute(values, axis, [(i, i ^ step) for i in range(size)])
            step *= 2
    return values


def adamw_write(refs, grad, master, first, second):
    refs[0][...] = grad
    refs[1][...], refs[2][...], refs[3][...] = adamw_update(
        master[...], grad, first[...], second[...], WEIGHT_DECAY, LEARN_RATE
    )


def adamw_ffn_kernel(x_ref, mine_1, theirs_1, mine_2, theirs_2, *refs):
    step = pl.program_id(0)
    low_is_own = x_ref[0] == 0
    states, outs = refs[:9], refs[9:]
    rows = states[0].shape[0]
    hidden = states[0].shape[1] // 4
    here = pl.ds(pl.multiple_of(step * rows, rows), rows)
    for i in range(2):
        lanes = slice(i * hidden, (i + 1) * hidden)
        own = cat([mine_1[here, lanes], mine_2[here, lanes]], 1)
        other = cat([theirs_1[here, lanes], theirs_2[here, lanes]], 1).astype(F32)
        low = jnp.where(low_is_own, own, other)
        high = jnp.where(low_is_own, other, own)
        adamw_write(outs[4 * i : 4 * i + 4], cat([low, high], 1), *states[3 * i : 3 * i + 3])
    lanes = slice(2 * hidden, 3 * hidden)
    first = step % 2 == 0
    own = jnp.where(first, mine_1[:, lanes], mine_2[:, lanes])
    other = jnp.where(first, theirs_1[:, lanes], theirs_2[:, lanes]).astype(F32)
    grad = jnp.where(step // 2 == x_ref[0], own, other)
    width = states[6].shape[1]
    grad = cat([grad[:, j : j + width] for j in range(0, hidden, width)], 0)
    adamw_write(outs[8:], grad, *states[6:])


def adamw_ffn(x, pair_1, pair_2, states):
    steps = 4

    def cut(array):
        return pl.BlockSpec((array.shape[0] // steps, array.shape[1]), lambda i: (i, 0))

    packs = [*pair_1, *pair_2]
    flat = [array for triple in states for array in triple]
    outs = [triple[0] for triple in states for _ in range(4)]
    result = pl.pallas_call(
        adamw_ffn_kernel,
        grid=(steps,),
        in_specs=[pl.BlockSpec(memory_space=pltpu.SMEM)]
        + [once(pack.shape) for pack in packs]
        + [cut(array) for array in flat],
        out_specs=[cut(array) for array in outs],
        out_shape=[jax.ShapeDtypeStruct(array.shape, F32) for array in outs],
        compiler_params=pltpu.CompilerParams(vmem_limit_bytes=60 * MIB),
        cost_estimate=SMALL,
        name="adamw_ffn",
    )(x.astype(jnp.int32).reshape(1), *packs, *flat)
    return [result[4 * i : 4 * i + 4] for i in range(3)]


def adamw_attn_kernel(x_ref, mine_ref, theirs_ref, *refs):
    low_is_own = x_ref[0] == 0
    states, outs = refs[:12], refs[12:]
    own, other = mine_ref[...], theirs_ref[...].astype(F32)
    low = jnp.where(low_is_own, own, other)
    high = jnp.where(low_is_own, other, own)
    wide = states[0].shape[1] // 2
    adamw_write(outs[:4], cat([low[:, :wide], high[:, :wide]], 1), *states[:3])
    low_kv, high_kv = low[:, wide : wide + 128], high[:, wide : wide + 128]
    is_key = lanes_of(low_kv.shape) < HD
    key = jnp.where(is_key, low_kv, pltpu.roll(high_kv, HD, 1))
    adamw_write(outs[4:8], key, *states[3:6])
    value = jnp.where(is_key, pltpu.roll(low_kv, HD, 1), high_kv)
    adamw_write(outs[8:12], value, *states[6:9])
    adamw_write(outs[12:], cat([low[:, wide + 128 :], high[:, wide + 128 :]], 0), *states[9:])


def adamw_attn(x, pair, states):
    flat = [array for triple in states for array in triple]
    outs = [triple[0] for triple in states for _ in range(4)]
    result = pl.pallas_call(
        adamw_attn_kernel,
        grid=(1,),
        in_specs=[pl.BlockSpec(memory_space=pltpu.SMEM)]
        + [once(array.shape) for array in [*pair, *flat]],
        out_specs=[once(array.shape) for array in outs],
        out_shape=[jax.ShapeDtypeStruct(array.shape, F32) for array in outs],
        compiler_params=pltpu.CompilerParams(vmem_limit_bytes=60 * MIB),
        cost_estimate=SMALL,
        name="adamw_attn",
    )(x.astype(jnp.int32).reshape(1), *pair, *flat)
    return [result[4 * i : 4 * i + 4] for i in range(4)]


def finish_kernel(
    place_ref, back_ref, inputs_ref, scale_ref, gain_ref, res_grad_ref, residual_ref, stays_ref,
    first_ref, second_ref, out_ref, in_grad_ref,
):
    back = norm_back(
        back_ref[...].astype(F32), inputs_ref[...].astype(F32), scale_ref[...], gain_ref[...]
    )
    in_grad = res_grad_ref[...] + back
    summed = add(stays_ref[...], first_ref[0], second_ref[...])
    out = (residual_ref[...] + summed).astype(LOW)
    quarter = out.shape[1] // 4
    for k in range(4):
        there = pl.ds(pl.multiple_of((place_ref[0] ^ k) * quarter, quarter), quarter)
        out_ref[:, there] = out[:, k * quarter : (k + 1) * quarter]
        in_grad_ref[:, there] = in_grad[:, k * quarter : (k + 1) * quarter]


def finish(place, back, inputs, scale, gain, res_grad, residual, stays, first, second):
    arrays = [back, inputs, scale, gain[None, :], res_grad, residual, stays, first, second]
    return pl.pallas_call(
        finish_kernel,
        grid=(1,),
        in_specs=[pl.BlockSpec(memory_space=pltpu.SMEM)] + [once(a.shape) for a in arrays],
        out_specs=[once(inputs.shape)] * 2,
        out_shape=[
            jax.ShapeDtypeStruct(inputs.shape, LOW),
            jax.ShapeDtypeStruct(inputs.shape, F32),
        ],
        compiler_params=pltpu.CompilerParams(vmem_limit_bytes=60 * MIB),
        cost_estimate=SMALL,
        name="finish",
    )(place.astype(jnp.int32).reshape(1), *arrays)


def pick(index, low, high):
    return jnp.where(index == 0, low, high)


class Plane:
    def __init__(self, tp):
        self.tp, self.half = tp, tp // 2
        self.x = lax.axis_index("di")
        self.y = lax.axis_index("tp") // self.half
        self.core = lax.axis_index("tp") % 2
        self.place = self.x * 2 + self.y
        self.axes = ("di", "tp")

    def pairs(self, first):
        def other(index):
            x, t = divmod(index, self.tp)
            along_x = (t % 2 == 0) == first
            return (1 - x) * self.tp + t if along_x else x * self.tp + (t + self.half) % self.tp

        return [(index, other(index)) for index in range(2 * self.tp)]

    def swap_first(self, value):
        return lax.ppermute(value, self.axes, self.pairs(True))

    def swap_second(self, value):
        return lax.ppermute(value, self.axes, self.pairs(False))

    def swap_core(self, value):
        return lax.ppermute(value, "tp", [(i, i ^ 1) for i in range(self.tp)])

    def first_step(self):
        return jnp.where(self.core == 0, 2, 1)

    def at(self, blocks, step):
        return lax.dynamic_index_in_dim(blocks, self.place ^ step, 0, keepdims=False)


def on_device(
    sizes,
    layer_input, out_grad, segment_ids, positions,
    w_query, w_key, w_value, w_out, w_gate, w_up, w_down,
    m_query, m_key, m_value, m_out, m_gate, m_up, m_down,
    v_query, v_key, v_value, v_out, v_gate, v_up, v_down,
    gain_attn, gain_ffn, m_gain_attn, m_gain_ffn, v_gain_attn, v_gain_ffn,
):
    width = layer_input.shape[1]
    plan = Plan(sizes["do"], w_query.shape[0])
    by_x = plan.by_x
    axes = ("di", "tp")
    plane = Plane(sizes["tp"])
    plane_sizes = (("tp", sizes["tp"]), ("di", sizes["di"]))

    gain_one, gain_two = plan.reorder(gain_attn), plan.reorder(gain_ffn)
    inputs_low = plan.reorder(layer_input)
    inputs_f = inputs_low.astype(F32)
    grad_low = plan.reorder(out_grad)
    normed, scale_one = norm_rows(inputs_f, gain_one)
    normed_all = lax.all_gather(normed.astype(LOW), axes, axis=0, tiled=True)

    marks = cat([segment_ids[None, :], positions[None, :]], 0)
    marks_other = lax.ppermute(marks, "di", PAIR)
    marks_all = cat([by_x(marks, marks_other), by_x(marks_other, marks)], 1)
    seg_all, pos_all = marks_all[0], marks_all[1]
    rows = seg_all.shape[0]
    seqs = rows // LEN
    seg_col, seg_row = seg_all.reshape(rows, 1), seg_all.reshape(seqs, 1, LEN)
    cosine, sine = rope_tables(pos_all)

    def col_halves(weight):
        half = weight.shape[1] // 2
        low = weight.astype(LOW)
        return by_x(low[:, :half], low[:, half:]), by_x(low[:, half:], low[:, :half])

    def row_halves(weight):
        half = weight.shape[0] // 2
        low = weight.astype(LOW)
        return by_x(low[:half], low[half:]), by_x(low[half:], low[:half])

    def col_cut(pair, chunk):
        size = pair[0].shape[1] // CHUNKS
        return tuple(part[:, chunk * size : (chunk + 1) * size] for part in pair)

    def row_cut(pair, chunk):
        size = pair[0].shape[0] // CHUNKS
        return tuple(part[chunk * size : (chunk + 1) * size] for part in pair)

    halves_q, halves_k, halves_v = col_halves(w_query), col_halves(w_key), col_halves(w_value)
    qkv_parts = tuple(cat([q, k, v], 1) for q, k, v in zip(halves_q, halves_k, halves_v))
    out_parts = row_halves(w_out)
    halves_g, halves_u, halves_d = col_halves(w_gate), col_halves(w_up), row_halves(w_down)

    def ffn_parts(chunk):
        gate_up = tuple(
            cat([g, u], 1) for g, u in zip(col_cut(halves_g, chunk), col_cut(halves_u, chunk))
        )
        return gate_up, row_cut(halves_d, chunk)

    hidden = halves_d[0].shape[0] // CHUNKS
    attn_shapes = (width, qkv_parts[0].shape[1]), (out_parts[0].shape[0], width)
    ffn_shapes = (width, 2 * hidden), (hidden, width)
    own_rows = layer_input.shape[0]
    core = lax.axis_index("tp") % 2

    if plan.line:
        attn_own, attn_other = plan.pack(qkv_parts, out_parts)
        own_1, other_1 = plan.pack(*ffn_parts(0))
        own_2, other_2 = plan.pack(*ffn_parts(1))
        attn_theirs = plan.swap(attn_other)
        attn_theirs, marks_all, own_1, other_1 = fence(attn_theirs, marks_all, own_1, other_1)
        attn_block = plan.join(attn_own, attn_theirs)
        near, across = line_near(attn_block)
        theirs_1 = plan.swap(other_1)
        near, across, cosine, sine, own_2, other_2 = fence(
            near, across, cosine, sine, own_2, other_2
        )
        across_near, out = line_far(near, across)
        across_near, out, theirs_1 = fence(across_near, out, theirs_1)
        out_near = line_last(across_near)
        block_1 = plan.join(own_1, theirs_1)
        out_near, normed_all, block_1, grad_low, other_2, seg_col, seg_row = fence(
            out_near, normed_all, block_1, grad_low, other_2, seg_col, seg_row
        )
        attn_weights = (attn_block, near, across_near, out, across, (out_near,))
        near_1, across_1 = line_near(block_1)
    else:
        attn_weights = plan.plain_gather(qkv_parts, out_parts)
        first_weights = plan.plain_gather(*ffn_parts(0))
        second_weights = plan.plain_gather(*ffn_parts(1))
    attn_loader = Loader(plan, attn_weights, *attn_shapes)

    attn_part, ctx, queries, both, lse, wout = attn_forward(
        attn_loader, normed_all, cosine, sine, seg_col, seg_row
    )
    grad_second = plane.swap_second(grad_low)
    if plan.line:
        theirs_2 = plan.swap(other_2)
        attn_part, near_1, across_1, grad_second, theirs_2, grad_low = fence(
            attn_part, near_1, across_1, grad_second, theirs_2, grad_low
        )
        across_near_1, out_1 = line_far(near_1, across_1)
    grad_first = plane.swap_first(grad_low)
    attn_sum = lax.psum_scatter(attn_part, axes, scatter_dimension=0, tiled=True)
    grad_xy = plane.swap_first(grad_second)
    if plan.line:
        across_near_1, out_1, grad_xy, theirs_2, grad_first = fence(
            across_near_1, out_1, grad_xy, theirs_2, grad_first
        )
        block_2 = plan.join(own_2, theirs_2)
        out_near_1 = line_last(across_near_1)
    grad_x = pick(core, grad_first, grad_second)
    grad_y = pick(core, grad_second, grad_first)
    over_y = cat([pick(plane.y, grad_low, grad_y), pick(plane.y, grad_y, grad_low)], 0)
    over_xy = cat([pick(plane.y, grad_x, grad_xy), pick(plane.y, grad_xy, grad_x)], 0)
    grad_core = cat([by_x(over_y, over_xy), by_x(over_xy, over_y)], 0)
    grad_other = plane.swap_core(grad_core)
    groups = (rows // own_rows // 2, 1, own_rows, width)
    mine, theirs = grad_core.reshape(groups), grad_other.reshape(groups)
    grad_all = cat([pick(core, mine, theirs), pick(core, theirs, mine)], 1).reshape(rows, width)

    if plan.line:
        attn_sum, grad_all, out_near_1 = fence(attn_sum, grad_all, out_near_1)
    residual = inputs_f + attn_sum.astype(F32)
    normed_two, scale_two = norm_rows(residual, gain_two)
    two_low = normed_two.astype(LOW)
    two_all = lax.all_gather(two_low, axes, axis=0, tiled=True)

    if plan.line:
        first_weights = (block_1, near_1, across_near_1, out_1, across_1, (out_near_1,))
        block_2, _ = fence(block_2, two_low)
        near_2, across_2 = line_near(block_2)
        near_2, across_2, wout = fence(near_2, across_2, wout)
        across_near_2, out_2 = line_far(near_2, across_2)
    wout_all = lax.all_gather(wout, axes, axis=0, tiled=True)
    if plan.line:
        two_all, across_near_2, out_2 = fence(two_all, across_near_2, out_2)
        out_near_2 = line_last(across_near_2)
    first = Loader(plan, first_weights, *ffn_shapes)
    back_1, act_1, both_1, down_1 = ffn_main(first, two_all, grad_all, None)
    if plan.line:
        *last_1, third_1 = ffn_weights(plan, two_all, grad_all, act_1, both_1, (3, 2))
        back_1, last_1, out_near_2 = fence(back_1, last_1, out_near_2)
        far_1 = [lax.ppermute(part, "do", NEAR) for part in last_1]
        second_weights = (block_2, near_2, across_near_2, out_2, across_2, (out_near_2,))
    else:
        grads_1 = ffn_weights(plan, two_all, grad_all, act_1, both_1, (0, 1, 2, 3))
    second = Loader(plan, second_weights, *ffn_shapes)
    back_2, act_2, both_2, down_2 = ffn_main(second, two_all, grad_all, back_1)
    if plan.line:
        back_2, act_2, both_2, far_1, wout_all, act_1 = fence(
            back_2, act_2, both_2, far_1, wout_all, act_1
        )
        block = plan.block
        crossed_1, inward_1 = sum_middle([None, None, third_1], far_1)
    back_sum = lax.psum_scatter(back_2, axes, scatter_dimension=0, tiled=True)
    order = (3, 0, 1, 2) if plan.line else (0, 1, 2, 3)
    grads_2 = ffn_weights(plan, two_all, grad_all, act_2, both_2, order)
    if plan.line:
        *last_2, rest_2 = grads_2
        act_1, rest_2 = fence(act_1, rest_2)
        (rest_1,) = ffn_weights(plan, two_all, grad_all, act_1, both_1, (0, 1))
        act_2, rest_1, crossed_1, inward_1, last_2 = fence(
            act_2, rest_1, crossed_1, inward_1, last_2
        )
        grads_1 = [rest_1[:block], rest_1[block:], third_1, cat(last_1, 0)]
        grads_2 = [rest_2[:block], rest_2[block : 2 * block], rest_2[2 * block :], cat(last_2, 0)]
        far_low = lax.ppermute(last_2[0], "do", NEAR)
    out_part, gain_two_part = ffn_out(act_1, act_2, down_1, down_2, back_2, two_all)
    if plan.line:
        out_part, far_low, last_high = fence(out_part, far_low, last_2[1])
        far_high = lax.ppermute(last_high, "do", NEAR)

    if plan.line:
        back_sum, out_part = fence(back_sum, out_part)

    residual_grad, res_low, ctx_grad = residual_backward(
        back_sum, residual, scale_two, gain_two, grad_low, wout_all
    )
    if plan.line:
        ctx_grad, res_low, far_high = fence(ctx_grad, res_low, far_high)
        second = add_inner(grads_2[2], cat([far_low, far_high], 0)).astype(LOW)
        first_1, third_1 = sum_near_parts(grads_1, crossed_1, inward_1)
        ctx_grad, near_both, across_both = fence(
            ctx_grad, cat([second, first_1], 0), cat([second, third_1], 0)
        )
        near_both = lax.ppermute(near_both, "do", NEAR)
        across_both = lax.ppermute(across_both, "do", MIDDLE)
    ctx_grad = lax.all_to_all(ctx_grad, axes, split_axis=1, concat_axis=0, tiled=True)
    if plan.line:
        ctx_grad, res_low, out_part = fence(ctx_grad, res_low, out_part)

    out_shape = (rows // own_rows // 2, 2, own_rows, width)
    parts = out_part.reshape(out_shape)
    mine, theirs = pick(core, parts[:, 0], parts[:, 1]), pick(core, parts[:, 1], parts[:, 0])
    summed = add(mine, plane.swap_core(theirs)).astype(LOW)
    step = plane.first_step()
    goes = jnp.stack([plane.at(summed, step), plane.at(summed, 3)])
    goes_on, stays = plane.at(summed, 3 - step), plane.at(summed, 0)
    if plan.line:
        ctx_grad, goes, goes_on, stays = fence(ctx_grad, goes, goes_on, stays)
    arrives = plane.swap_first(goes)
    res_all = lax.all_gather(res_low, axes, axis=0, tiled=True)
    back_one_part, gain_one_part, *grads_qkv = attn_backward(
        attn_loader, ctx_grad, normed_all, queries, both, lse, cosine, sine, seg_col, seg_row
    )
    if plan.line:
        gain_parts = jnp.stack([gain_one_part[0] / gain_one, gain_two_part[0] / gain_two])
        gain_sums = sum_over(plan.reorder(gain_parts), plane_sizes + (("do", sizes["do"]),))
        back_one_part, grads_qkv, res_all, gain_sums, arrives, near_both, across_both = fence(
            back_one_part, grads_qkv, res_all, gain_sums, arrives, near_both, across_both
        )
        crossed_2, inward_2 = across_both[:block], near_both[:block]
        near_sum_1, across_sum_1 = near_both[block:], across_both[block:]
    else:
        gain_parts = jnp.stack([gain_one_part[0] / gain_one, gain_two_part[0] / gain_two])
        gain_sums = sum_over(gain_parts, (("do", sizes["do"]),) + plane_sizes)
    back_one = lax.psum_scatter(back_one_part, axes, scatter_dimension=0, tiled=True)
    grads_attn = out_weights(plan, ctx, res_all, grads_qkv)
    if plan.line:
        half = plan.rows

        def trade(total):
            return plan.trade(total[:half], total[half:])

        near_sum_2, across_sum_2 = sum_near_send(*sum_near_parts(grads_2, crossed_2, inward_2))
        ffn_pair_1 = trade(sum_own(grads_1, near_sum_1, across_sum_1))
        near_sum_2, across_sum_2, grads_attn = fence(near_sum_2, across_sum_2, grads_attn)
        direct = send_direct(grads_attn)
        ffn_pair_2 = trade(sum_own(grads_2, near_sum_2, across_sum_2))
    second = plane.swap_second(add(goes_on, arrives[1]).astype(LOW))
    place = lax.axis_index("do") if plan.line else jnp.zeros((), jnp.int32)
    states = {
        "attn": [
            (w_query, m_query, v_query), (w_key, m_key, v_key),
            (w_value, m_value, v_value), (w_out, m_out, v_out),
        ],
        "ffn": [(w_gate, m_gate, v_gate), (w_up, m_up, v_up), (w_down, m_down, v_down)],
    }
    if plan.line:
        ffn_updated = adamw_ffn(lax.axis_index("di"), ffn_pair_1, ffn_pair_2, states["ffn"])
        direct, ffn_updated, second, back_one = fence(direct, ffn_updated, second, back_one)
        attn_pair = trade(add(grads_attn[0], *direct))
        attn_updated = adamw_attn(lax.axis_index("di"), attn_pair, states["attn"])
    else:

        def join(pair, axis):
            own, other = pair[0], pair[1].astype(F32)
            return by_x(cat([own, other], axis), cat([other, own], axis))

        def from_chunks(pairs, axis):
            return join([cat([pair[i] for pair in pairs], axis) for i in range(2)], axis)

        def cut(pair, start, stop):
            return tuple(part[:, start:stop] for part in pair)

        def update(grad, state):
            return (grad, *adamw_update(state[0], grad, *state[1:], WEIGHT_DECAY, LEARN_RATE))

        qkv_pair = plan.plain_sum_row(grads_qkv[0])
        out_pair = plan.plain_sum_col(grads_attn[0])
        ffn_pairs = [
            (plan.plain_sum_row(row), plan.plain_sum_col(col)) for row, col in (grads_1, grads_2)
        ]
        at_k = halves_q[0].shape[1]
        at_v = at_k + halves_k[0].shape[1]
        end = at_v + halves_v[0].shape[1]
        attn_grads = [
            join(cut(qkv_pair, 0, at_k), 1),
            join(cut(qkv_pair, at_k, at_v), 1),
            join(cut(qkv_pair, at_v, end), 1),
            join(out_pair, 0),
        ]
        ffn_grads = [
            from_chunks([cut(row, 0, hidden) for row, _ in ffn_pairs], 1),
            from_chunks([cut(row, hidden, 2 * hidden) for row, _ in ffn_pairs], 1),
            from_chunks([col for _, col in ffn_pairs], 0),
        ]
        attn_updated = [update(g, s) for g, s in zip(attn_grads, states["attn"])]
        ffn_updated = [update(g, s) for g, s in zip(ffn_grads, states["ffn"])]
    out_value, in_grad = finish(
        place, back_one, inputs_low, scale_one, gain_one, residual_grad, residual, stays, arrives,
        second,
    )
    grad_gain_attn, grad_gain_ffn = gain_sums[0], gain_sums[1]
    updated = attn_updated + ffn_updated
    gain_updated = [
        adamw_update(gain_attn, grad_gain_attn, m_gain_attn, v_gain_attn, 0.0, GAIN_RATE),
        adamw_update(gain_ffn, grad_gain_ffn, m_gain_ffn, v_gain_ffn, 0.0, GAIN_RATE),
    ]
    return (
        out_value,
        in_grad,
        *[u[0] for u in updated],
        *[u[1] for u in updated],
        *[u[2] for u in updated],
        *[u[3] for u in updated],
        grad_gain_attn,
        grad_gain_ffn,
        *[u[0] for u in gain_updated],
        *[u[1] for u in gain_updated],
        *[u[2] for u in gain_updated],
    )


def solution(mesh):
    dp, tp = mesh.shape["dp"], mesh.shape["tp"]
    split = Mesh(mesh.devices.reshape(dp // 2, 2, tp), ("do", "di", "tp"))
    sizes = {"do": dp // 2, "di": 2, "tp": tp}
    dp_axes = ("do", "di")
    tokens = P(("do", "di", "tp"), None)
    by_rows, by_cols = P(dp_axes, "tp"), P("tp", dp_axes)
    weights = (by_rows, by_rows, by_rows, by_cols, by_rows, by_rows, by_cols)
    gains = (P(),) * 6
    in_specs = (tokens, tokens, P(dp_axes), P(dp_axes)) + weights * 3 + gains
    out_specs = (tokens, tokens) + weights * 4 + (P(),) * 2 + gains
    return jax.shard_map(
        functools.partial(on_device, sizes),
        mesh=split,
        in_specs=in_specs,
        out_specs=out_specs,
        check_vma=False,
    )
```

```python
import functools

import jax
import jax.numpy as jnp
from jax import lax
from jax.experimental import pallas as pl
from jax.experimental.pallas import tpu as pltpu
from jax.sharding import Mesh
from jax.sharding import PartitionSpec as P

HD = 64
LEN = 512
STEP = 5
CHUNKS = 2

NORM_EPS = 1e-05
ROPE_BASE = 500000.0
BETA_ONE = 0.9
BETA_TWO = 0.95
LEARN_RATE = 0.02
GAIN_RATE = 0.5
WEIGHT_DECAY = 0.1
ADAM_EPS = 1e-08

LOW = jnp.bfloat16
F32 = jnp.float32
MIB = 1024 * 1024

NEAR = [(0, 1), (1, 0), (2, 3), (3, 2)]
MIDDLE = [(1, 2), (2, 1)]
CROSS = [(0, 2), (1, 3), (2, 0), (3, 1)]
MIRROR = [(0, 3), (1, 2), (2, 1), (3, 0)]
OUTWARD = [(1, 0), (2, 3)]
INWARD = [(0, 1), (3, 2)]
PAIR = [(0, 1), (1, 0)]


def dot(lhs, rhs, lhs_dim, rhs_dim):
    return lax.dot_general(
        lhs, rhs, (((lhs_dim,), (rhs_dim,)), ((), ())), preferred_element_type=F32
    )


def cat(parts, axis):
    return jnp.concatenate(parts, axis)


def fence(*values):
    return lax.optimization_barrier(values)


def line_near(own):
    return lax.ppermute(own, "do", NEAR), lax.ppermute(own, "do", MIDDLE)


def line_far(near, across):
    out = lax.ppermute(across, "do", NEAR)
    return lax.ppermute(near, "do", MIDDLE), out


def line_last(across_near, perm=NEAR):
    return lax.ppermute(across_near, "do", perm)


def add(part, *arrived):
    total = part.astype(F32)
    for piece in arrived:
        total = total + piece.astype(F32)
    return total


def is_inner():
    place = lax.axis_index("do")
    return (place == 1) | (place == 2)


def add_inner(part, arrived):
    return add(part, jnp.where(is_inner(), arrived, jnp.zeros_like(arrived)))


def sum_middle(parts, far):
    second = add_inner(parts[2], cat(far, 0)).astype(LOW)
    inward = lax.ppermute(second, "do", NEAR)
    return lax.ppermute(second, "do", MIDDLE), inward


def sum_near_parts(parts, crossed, inward):
    return add_inner(parts[1], crossed).astype(LOW), add_inner(parts[3], inward).astype(LOW)


def sum_near_send(first, third):
    return lax.ppermute(first, "do", NEAR), lax.ppermute(third, "do", MIDDLE)


def sum_own(parts, from_near, from_across):
    return add_inner(parts[0], from_across) + from_near.astype(F32)


def send_direct(parts):
    return [
        lax.ppermute(part, "do", perm) for part, perm in zip(parts[1:], (NEAR, CROSS, MIRROR))
    ]


class Plan:
    def __init__(self, outer, per_device):
        self.rows = per_device
        self.block = 2 * per_device
        self.line = outer == 4 and per_device == 256
        self.cuts = 4 if self.line else 1

    def reorder(self, values):
        if not self.line:
            return values
        place = lax.axis_index("do")
        quarter = values.shape[-1] // 4
        a, b, c, d = (values[..., i * quarter : (i + 1) * quarter] for i in range(4))
        values = jnp.where(place % 2 == 1, cat([b, a, d, c], -1), values)
        half = 2 * quarter
        turned = cat([values[..., half:], values[..., :half]], -1)
        return jnp.where(place >= 2, turned, values)

    def by_x(self, low, high):
        return jnp.where(lax.axis_index("di") == 0, low, high)

    def inner(self):
        return is_inner().astype(jnp.int32).reshape(1)

    def pack(self, row_part, col_part):
        rows, packs = self.rows, []
        for row_side, side in zip(row_part, col_part):
            pieces = [side[i : i + rows] for i in range(0, side.shape[0], rows)]
            packs.append(cat([row_side] + pieces, 1))
        return packs

    def swap(self, other):
        return lax.ppermute(other, "di", PAIR)

    def join(self, own, theirs, axis=0):
        return cat([self.by_x(own, theirs), self.by_x(theirs, own)], axis)

    def plain_gather(self, row_part, col_part):
        full = []
        for (own, other), axis in ((row_part, 0), (col_part, 1)):
            block = self.join(own, self.swap(other), axis)
            full.append(lax.all_gather(block, "do", axis=axis, tiled=True))
        return tuple(full)

    def unpack(self, pair, wide):
        cuts = range(wide, pair[0].shape[1], self.rows)
        return (
            tuple(side[:, :wide] for side in pair),
            tuple(cat([side[:, i : i + self.rows] for i in cuts], 0) for side in pair),
        )

    def plain_sum_row(self, grad):
        total = lax.psum_scatter(grad, "do", scatter_dimension=0, tiled=True)
        return self.trade(total[: self.rows], total[self.rows :])

    def plain_sum_col(self, grad):
        total = lax.psum_scatter(grad, "do", scatter_dimension=1, tiled=True)
        return self.trade(total[:, : self.rows], total[:, self.rows :])

    def trade(self, low, high):
        theirs = lax.ppermute(self.by_x(high, low).astype(LOW), "di", PAIR)
        return self.by_x(low, high).astype(F32), theirs


ANY = pl.BlockSpec(memory_space=pl.ANY)
SMALL = pl.CostEstimate(flops=1, bytes_accessed=1, transcendentals=0)


class Loader:
    def __init__(self, plan, weights, row_shape, col_shape):
        self.plan, self.row_shape, self.col_shape = plan, row_shape, col_shape
        rows, wide = plan.rows, row_shape[1]
        self.moves = []
        if plan.line:
            *whole, last = weights
            self.operands = [plan.inner(), *whole, *last]
            for k in range(4):
                for x in range(2):
                    at = k * plan.block + x * rows
                    self.moves.append((k, x, 0, 0, (at, 0), wide))
                    for i in range(0, col_shape[0], rows):
                        self.moves.append((k, x, 1, wide + i, (i, at), rows))
        else:
            self.operands = list(weights)
            self.moves = [None, None]
        self.count = len(self.operands)

    def specs(self):
        if not self.plan.line:
            return [ANY] * 2
        return [pl.BlockSpec(memory_space=pltpu.SMEM)] + [ANY] * (self.count - 1)

    def scratch(self):
        return [
            pltpu.VMEM(self.row_shape, LOW),
            pltpu.VMEM(self.col_shape, LOW),
            pltpu.SemaphoreType.DMA((len(self.moves),)),
        ]

    def load(self, refs, row_ref, col_ref, sems):
        if not self.plan.line:
            pairs = zip(refs, (row_ref, col_ref))
            made = [pltpu.make_async_copy(*pair, sems.at[i]) for i, pair in enumerate(pairs)]
            for copy in made:
                copy.start()
            for copy in made:
                copy.wait()
            return
        rows = self.plan.rows

        def copies(sources):
            made = []
            for i, (k, x, which, column, there, wide) in enumerate(self.moves):
                if sources[k] is None:
                    continue
                if isinstance(sources[k], tuple):
                    source, row = sources[k][x], 0
                else:
                    source, row = sources[k], x * rows
                target = (row_ref, col_ref)[which]
                made.append(
                    pltpu.make_async_copy(
                        source.at[pl.ds(row, rows), pl.ds(column, wide)],
                        target.at[pl.ds(there[0], rows), pl.ds(there[1], wide)],
                        sems.at[i],
                    )
                )
            return made

        inner, own, near, across_near, out, across, *last = refs
        out_near = tuple(last) if len(last) == 2 else last[0]
        is_inner = inner[0] == 1
        for copy in copies((own, near, None, None)):
            copy.start()

        @pl.when(is_inner)
        def _():
            for copy in copies((None, None, across_near, across)):
                copy.start()

        @pl.when(jnp.logical_not(is_inner))
        def _():
            for copy in copies((None, None, out, out_near)):
                copy.start()

        for copy in copies((own, near, out, out_near)):
            copy.wait()


def rope_tables(positions):
    half_dim = HD // 2
    inverse_freq = ROPE_BASE ** (-2.0 * jnp.arange(half_dim, dtype=F32) / HD)
    angles = positions.astype(F32)[:, None] * inverse_freq[None, :]
    cosine, sine = jnp.cos(angles), jnp.sin(angles)
    return cat([cosine] * 4, 1), cat([-sine, sine] * 2, 1)


def lanes_of(shape):
    return lax.broadcasted_iota(jnp.int32, shape, 1)


def shuffle_halves(values):
    wide = values.shape[1]
    up = pltpu.roll(values, wide - HD // 2, 1)
    down = pltpu.roll(values, HD // 2, 1)
    return jnp.where(lanes_of(values.shape) % HD < HD // 2, up, down)


def tables(cos_ref, sin_ref, pairs):
    cosine, sine = cos_ref[...], sin_ref[...]
    is_key = lanes_of(cosine.shape) < HD
    return (
        cat([cosine] * pairs + [jnp.where(is_key, cosine, 1.0)], 1),
        cat([sine] * pairs + [jnp.where(is_key, sine, 0.0)], 1),
    )


def split_kv(both):
    is_key = lanes_of(both.shape) < HD
    blank = jnp.zeros_like(both)
    key_low = jnp.where(is_key, both, blank)
    value_high = jnp.where(is_key, blank, both)
    return (
        (key_low, pltpu.roll(key_low.astype(F32), HD, 1).astype(LOW)),
        (pltpu.roll(value_high.astype(F32), HD, 1).astype(LOW), value_high),
    )


def allowed_pairs(seg_col, seg_row):
    shape = (seg_col.shape[0], seg_row.shape[1])
    key_at = lax.broadcasted_iota(jnp.int32, shape, 1)
    query_at = lax.broadcasted_iota(jnp.int32, shape, 0)
    return (seg_col == seg_row) & (key_at <= query_at)


def attn_forward_kernel(pairs, loader, *refs):
    weights, refs = refs[: loader.count], refs[loader.count :]
    x_ref, cos_ref, sin_ref, col_ref, row_ref = refs[:5]
    part_ref, ctx_ref, q_ref, kv_ref, lse_ref, wout_ref, wqkv_ref, _, sems = refs[5:]

    @pl.when(pl.program_id(0) == 0)
    def _():
        loader.load(weights, wqkv_ref, wout_ref, sems)

    cosine, sine = tables(cos_ref, sin_ref, pairs)
    qkv = dot(x_ref[...], wqkv_ref[...], 1, 0)
    rotated = (qkv * cosine + shuffle_halves(qkv) * sine).astype(LOW)
    queries, both = rotated[:, : pairs * 128], rotated[:, pairs * 128 :]
    q_ref[...] = queries
    kv_ref[...] = both
    keys, values = split_kv(both)
    allowed = allowed_pairs(col_ref[...], row_ref[0])
    lane = lanes_of((both.shape[0], 128))
    log_sums = [jnp.zeros((both.shape[0] // 2, 128), F32)] * 2
    contexts = []
    half = both.shape[0] // 2
    for pair in range(pairs):
        bands = []
        for low, high in ((0, half), (half, 2 * half)):
            heads = queries[low:high, pair * 128 : (pair + 1) * 128]
            context = None
            for side in range(2):
                scores = dot(heads, keys[side][:high], 1, 1) * HD**-0.5
                masked = jnp.where(allowed[low:high, :high], scores, -1e30)
                top = jnp.max(masked, axis=1, keepdims=True)
                weights = jnp.exp(masked - top)
                totals = jnp.sum(weights, axis=1, keepdims=True)
                probs = (weights * (1.0 / totals)).astype(LOW)
                piece = dot(probs, values[side][:high], 1, 0)
                context = piece if context is None else context + piece
                at = 2 * pair + side
                log_sums[low // half] = jnp.where(
                    lane[:half] == at, top + jnp.log(totals), log_sums[low // half]
                )
            bands.append(context.astype(LOW))
        contexts.append(cat(bands, 0))
    lse_ref[...] = cat(log_sums, 0)
    context_low = cat(contexts, 1)
    ctx_ref[...] = context_low
    part_ref[...] = dot(context_low, wout_ref[...], 1, 0).astype(LOW)


def attn_backward_kernel(pairs, loader, *refs):
    weights, refs = refs[: loader.count], refs[loader.count :]
    cg_ref, x_ref, q_ref, kv_ref, lse_ref, cos_ref, sin_ref, col_ref, row_ref = refs[:9]
    part_ref, gain_ref, *grad_refs = refs[9:-4]
    wqkv_ref, wout_ref, sems, acc_qkv = refs[-4:]
    step = pl.program_id(0)

    @pl.when(step == 0)
    def _():
        loader.load(weights, wqkv_ref, wout_ref, sems)
        acc_qkv[...] = jnp.zeros_like(acc_qkv)
        gain_ref[...] = jnp.zeros_like(gain_ref)

    cosine, sine = tables(cos_ref, sin_ref, pairs)
    scale = HD**-0.5
    ctx_grad = cg_ref[...]
    keys, values = split_kv(kv_ref[...])
    allowed = allowed_pairs(col_ref[...], row_ref[0])
    lane = lanes_of((ctx_grad.shape[0], 128))
    log_sums = lse_ref[...]
    query_grads, key_grad, value_grad = [], None, None
    for pair in range(pairs):
        heads = q_ref[:, pair * 128 : (pair + 1) * 128]
        grads = ctx_grad[:, pair * 128 : (pair + 1) * 128]
        query_grad = None
        for side in range(2):
            here = (lane < HD) if side == 0 else (lane >= HD)
            head = jnp.where(here, heads, jnp.zeros_like(heads))
            grad = jnp.where(here, grads, jnp.zeros_like(grads))
            at = 2 * pair + side
            scores = dot(heads, keys[side], 1, 1) * scale
            probs = jnp.where(allowed, jnp.exp(scores - log_sums[:, at : at + 1]), 0.0)
            prob_grad = dot(grads, values[side], 1, 1)
            delta = jnp.sum(probs * prob_grad, axis=1, keepdims=True)
            score_grad = (probs * (prob_grad - delta)).astype(LOW)
            to_value = dot(probs.astype(LOW), grad, 0, 0)
            to_key = dot(score_grad, head, 0, 0)
            to_query = dot(score_grad, keys[side], 1, 0)
            value_grad = to_value if value_grad is None else value_grad + to_value
            key_grad = to_key if key_grad is None else key_grad + to_key
            query_grad = to_query if query_grad is None else query_grad + to_query
        query_grads.append(query_grad * scale)
    key_grad = (key_grad + pltpu.roll(key_grad, HD, 1)) * scale
    value_grad = value_grad + pltpu.roll(value_grad, HD, 1)
    joined = cat(query_grads + [jnp.where(lane < HD, key_grad, value_grad)], 1)
    low = (joined * cosine - shuffle_halves(joined) * sine).astype(LOW)
    part = dot(low, wqkv_ref[...], 1, 1)
    part_ref[...] = part.astype(LOW)
    gain_ref[...] += jnp.sum(part * x_ref[...].astype(F32), axis=0, keepdims=True)
    acc_qkv[...] += dot(x_ref[...], low, 0, 0)

    @pl.when(step == pl.num_programs(0) - 1)
    def _():
        cut = acc_qkv.shape[0] // len(grad_refs)
        for i, out in enumerate(grad_refs):
            out[...] = acc_qkv[i * cut : (i + 1) * cut, :].astype(LOW)


def once(shape):
    return pl.BlockSpec(shape, lambda i: (0,) * len(shape), pipeline_mode=pl.Buffered(1))


def per_seq(shape):
    return pl.BlockSpec(shape, lambda i: (i,) + (0,) * (len(shape) - 1))


def attn_forward(loader, normed, cosine, sine, seg_col, seg_row):
    rows, width = normed.shape
    heads = loader.col_shape[0]
    return pl.pallas_call(
        functools.partial(attn_forward_kernel, heads // 128, loader),
        grid=(rows // LEN,),
        in_specs=[
            *loader.specs(),
            per_seq((LEN, width)),
            per_seq((LEN, 128)),
            per_seq((LEN, 128)),
            per_seq((LEN, 1)),
            per_seq((1, 1, LEN)),
        ],
        out_specs=[
            per_seq((LEN, width)),
            per_seq((LEN, heads)),
            per_seq((LEN, heads)),
            per_seq((LEN, 128)),
            per_seq((LEN, 128)),
            once(loader.col_shape),
        ],
        out_shape=[
            jax.ShapeDtypeStruct((rows, width), LOW),
            jax.ShapeDtypeStruct((rows, heads), LOW),
            jax.ShapeDtypeStruct((rows, heads), LOW),
            jax.ShapeDtypeStruct((rows, 128), LOW),
            jax.ShapeDtypeStruct((rows, 128), F32),
            jax.ShapeDtypeStruct(loader.col_shape, LOW),
        ],
        scratch_shapes=loader.scratch(),
        compiler_params=pltpu.CompilerParams(vmem_limit_bytes=60 * MIB),
        cost_estimate=SMALL,
        name="attn_forward",
    )(*loader.operands, normed, cosine, sine, seg_col, seg_row)


def attn_backward(loader, ctx_grad, normed, queries, both, lse, cosine, sine, seg_col, seg_row):
    rows, width = normed.shape
    heads = loader.col_shape[0]
    cuts = loader.plan.cuts
    grad = (width // cuts, loader.row_shape[1])
    return pl.pallas_call(
        functools.partial(attn_backward_kernel, heads // 128, loader),
        grid=(rows // LEN,),
        in_specs=[
            *loader.specs(),
            per_seq((LEN, heads)),
            per_seq((LEN, width)),
            per_seq((LEN, heads)),
            per_seq((LEN, 128)),
            per_seq((LEN, 128)),
            per_seq((LEN, 128)),
            per_seq((LEN, 128)),
            per_seq((LEN, 1)),
            per_seq((1, 1, LEN)),
        ],
        out_specs=[per_seq((LEN, width)), once((1, width))] + [once(grad)] * cuts,
        out_shape=[
            jax.ShapeDtypeStruct((rows, width), LOW),
            jax.ShapeDtypeStruct((1, width), F32),
        ]
        + [jax.ShapeDtypeStruct(grad, LOW)] * cuts,
        scratch_shapes=[*loader.scratch(), pltpu.VMEM(loader.row_shape, F32)],
        compiler_params=pltpu.CompilerParams(vmem_limit_bytes=60 * MIB),
        cost_estimate=SMALL,
        name="attn_backward",
    )(*loader.operands, ctx_grad, normed, queries, both, lse, cosine, sine, seg_col, seg_row)


def out_weights_kernel(plan, ctx_ref, res_ref, *refs):
    count = plan.cuts
    qkv_refs, grad_refs, acc = refs[:-1][: count * plan.line], refs[-1 - count : -1], refs[-1]
    step = pl.program_id(0)

    @pl.when(step == 0)
    def _():
        acc[...] = jnp.zeros_like(acc)

    acc[...] += dot(ctx_ref[...], res_ref[...], 0, 0)

    @pl.when(step == pl.num_programs(0) - 1)
    def _():
        if not plan.line:
            grad_refs[0][...] = acc[...].astype(LOW)
            return
        rows = plan.rows
        for k, (qkv, out) in enumerate(zip(qkv_refs, grad_refs)):
            wide = qkv.shape[1]
            out[:, :wide] = qkv[...]
            for x in range(2):
                at = k * plan.block + x * rows
                out[x * rows : (x + 1) * rows, wide:] = acc[:, at : at + rows].astype(LOW)


def out_weights(plan, ctx, res_all, grads_qkv):
    rows, width = res_all.shape
    heads = ctx.shape[1]
    extra = list(grads_qkv) if plan.line else []
    shape = (plan.block, extra[0].shape[1] + heads) if plan.line else (heads, width)
    return pl.pallas_call(
        functools.partial(out_weights_kernel, plan),
        grid=(rows // LEN,),
        in_specs=[per_seq((LEN, heads)), per_seq((LEN, width))] + [once(g.shape) for g in extra],
        out_specs=[once(shape)] * plan.cuts,
        out_shape=[jax.ShapeDtypeStruct(shape, LOW)] * plan.cuts,
        scratch_shapes=[pltpu.VMEM((heads, width), F32)],
        compiler_params=pltpu.CompilerParams(vmem_limit_bytes=40 * MIB),
        cost_estimate=SMALL,
        name="out_weights",
    )(ctx, res_all, *extra)


def residual_backward_kernel(
    back_ref, residual_ref, scale_ref, gain_ref, grad_ref, wout_ref, res_grad_ref, low_ref, ctx_ref
):
    @pl.when(pl.program_id(0) == 0)
    def _():
        back = norm_back(
            back_ref[...].astype(F32), residual_ref[...], scale_ref[...], gain_ref[...]
        )
        total = grad_ref[...].astype(F32) + back
        res_grad_ref[...] = total
        low_ref[...] = total.astype(LOW)

    ctx_ref[...] = dot(low_ref[...], wout_ref[...], 1, 1).astype(LOW)


def residual_backward(back_sum, residual, scale, gain, grad_low, wout_all):
    rows, width = residual.shape
    heads = wout_all.shape[0]
    step = 512
    return pl.pallas_call(
        residual_backward_kernel,
        grid=(heads // step,),
        in_specs=[
            once((rows, width)),
            once((rows, width)),
            once((rows, 1)),
            once((1, width)),
            once((rows, width)),
            per_seq((step, width)),
        ],
        out_specs=[
            once((rows, width)),
            once((rows, width)),
            pl.BlockSpec((rows, step), lambda i: (0, i)),
        ],
        out_shape=[
            jax.ShapeDtypeStruct((rows, width), F32),
            jax.ShapeDtypeStruct((rows, width), LOW),
            jax.ShapeDtypeStruct((rows, heads), LOW),
        ],
        compiler_params=pltpu.CompilerParams(vmem_limit_bytes=60 * MIB),
        cost_estimate=SMALL,
        name="residual_backward",
    )(back_sum, residual, scale, gain[None, :], grad_low, wout_all)


TILE = 512


def ffn_main_kernel(loader, more, *refs):
    weights, refs = refs[: loader.count], refs[loader.count :]
    x_ref, grad_ref = refs[:2]
    back_ref, act_ref, both_ref, down_ref, gate_up_ref, _, sems = refs[2 + more :]

    @pl.when(pl.program_id(0) == 0)
    def _():
        loader.load(weights, gate_up_ref, down_ref, sems)

    hidden = down_ref.shape[0]
    pre = dot(x_ref[...], gate_up_ref[...], 1, 0)
    gate_pre, lifted = pre[:, :hidden], pre[:, hidden:]
    sigmoid_gate = jax.nn.sigmoid(gate_pre)
    silu_gate = gate_pre * sigmoid_gate
    act_ref[...] = (silu_gate * lifted).astype(LOW)
    act_grad = dot(grad_ref[...], down_ref[...], 1, 1)
    gate_grad = act_grad * lifted * sigmoid_gate * (1.0 + gate_pre * (1.0 - sigmoid_gate))
    both_grad = cat([gate_grad.astype(LOW), (act_grad * silu_gate).astype(LOW)], 1)
    both_ref[...] = both_grad
    back = dot(both_grad, gate_up_ref[...], 1, 1)
    if more:
        back = back + refs[2][...].astype(F32)
    back_ref[...] = back.astype(LOW)


def ffn_main(loader, tokens, grads, earlier):
    rows, width = tokens.shape
    hidden = loader.col_shape[0]
    more = [] if earlier is None else [earlier]
    return pl.pallas_call(
        functools.partial(ffn_main_kernel, loader, len(more)),
        grid=(rows // TILE,),
        in_specs=[
            *loader.specs(),
            per_seq((TILE, width)),
            per_seq((TILE, width)),
            *[per_seq((TILE, width))] * len(more),
        ],
        out_specs=[
            per_seq((TILE, width)),
            per_seq((TILE, hidden)),
            per_seq((TILE, 2 * hidden)),
            once(loader.col_shape),
        ],
        out_shape=[
            jax.ShapeDtypeStruct((rows, width), LOW),
            jax.ShapeDtypeStruct((rows, hidden), LOW),
            jax.ShapeDtypeStruct((rows, 2 * hidden), LOW),
            jax.ShapeDtypeStruct(loader.col_shape, LOW),
        ],
        scratch_shapes=loader.scratch(),
        compiler_params=pltpu.CompilerParams(vmem_limit_bytes=60 * MIB),
        cost_estimate=SMALL,
        name="ffn_main",
    )(*loader.operands, tokens, grads, *more)


def ffn_weights_kernel(plan, x_ref, grad_ref, act_ref, both_ref, *out_refs):
    row = dot(x_ref[...], both_ref[...], 0, 0).astype(LOW)
    col = dot(act_ref[...], grad_ref[...], 0, 0).astype(LOW)
    if not plan.line:
        out_refs[0][...], out_refs[1][...] = row, col
        return
    rows, wide = plan.rows, row.shape[1]

    def pack(halves):
        for x, (out, at) in enumerate(halves):
            out[at : at + rows, :wide] = row[x * rows : (x + 1) * rows]
            for i in range(0, col.shape[0], rows):
                out[at : at + rows, wide + i : wide + i + rows] = col[
                    i : i + rows, x * rows : (x + 1) * rows
                ]

    if len(out_refs) == 1:
        pack([(out_refs[0], 0), (out_refs[0], rows)])
        return

    @pl.when(pl.program_id(0) == 0)
    def _():
        pack([(out_refs[0], 0), (out_refs[1], 0)])

    @pl.when(pl.program_id(0) > 0)
    def _():
        pack([(out_refs[2], 0), (out_refs[2], rows)])


def ffn_weights(plan, tokens, grads, act, both_grad, order):
    rows, width = tokens.shape
    block = width // 4
    wide, hidden = both_grad.shape[1], act.shape[1]
    count, begin = len(order), order[0]
    step = order[1] - order[0] if begin < 3 else (order[1] - 3) % 4
    assert all(order[i] == (begin + step * i) % 4 for i in range(count))

    def columns():
        return pl.BlockSpec((rows, block), lambda i: (0, (begin + step * i) % 4))

    if not plan.line:
        out_specs = [
            pl.BlockSpec((block, wide), lambda i: ((begin + step * i) % 4, 0)),
            pl.BlockSpec((hidden, block), lambda i: (0, (begin + step * i) % 4)),
        ]
        shapes = [(count * block, wide), (hidden, count * block)]
    elif begin == 3:
        out_specs = [once((plan.rows, wide + hidden))] * 2 + [
            pl.BlockSpec((block, wide + hidden), lambda i: (jnp.maximum(i - 1, 0), 0))
        ]
        shapes = [(plan.rows, wide + hidden)] * 2 + [((count - 1) * block, wide + hidden)]
    else:
        out_specs = [pl.BlockSpec((block, wide + hidden), lambda i: (i, 0))]
        shapes = [(count * block, wide + hidden)]
    return pl.pallas_call(
        functools.partial(ffn_weights_kernel, plan),
        grid=(count,),
        in_specs=[columns(), columns(), once(act.shape), once(both_grad.shape)],
        out_specs=out_specs,
        out_shape=[jax.ShapeDtypeStruct(shape, LOW) for shape in shapes],
        compiler_params=pltpu.CompilerParams(vmem_limit_bytes=60 * MIB),
        cost_estimate=SMALL,
        name="ffn_weights",
    )(tokens, grads, act, both_grad)


def ffn_out_kernel(act_1, act_2, down_1, down_2, back_ref, x_ref, out_ref, gain_ref):
    @pl.when(pl.program_id(0) == 0)
    def _():
        gain_ref[...] = jnp.zeros_like(gain_ref)

    out = dot(act_1[...], down_1[...], 1, 0) + dot(act_2[...], down_2[...], 1, 0)
    out_ref[...] = out.astype(LOW)
    product = back_ref[...].astype(F32) * x_ref[...].astype(F32)
    gain_ref[...] += jnp.sum(product, axis=0, keepdims=True)


def ffn_out(act_1, act_2, down_1, down_2, back, tokens):
    rows, width = tokens.shape
    hidden = act_1.shape[1]
    return pl.pallas_call(
        ffn_out_kernel,
        grid=(rows // TILE,),
        in_specs=[
            per_seq((TILE, hidden)),
            per_seq((TILE, hidden)),
            once(down_1.shape),
            once(down_2.shape),
            per_seq((TILE, width)),
            per_seq((TILE, width)),
        ],
        out_specs=[per_seq((TILE, width)), once((1, width))],
        out_shape=[
            jax.ShapeDtypeStruct((rows, width), LOW),
            jax.ShapeDtypeStruct((1, width), F32),
        ],
        compiler_params=pltpu.CompilerParams(vmem_limit_bytes=60 * MIB),
        cost_estimate=SMALL,
        name="ffn_out",
    )(act_1, act_2, down_1, down_2, back, tokens)


def norm_rows(values, gain_vec):
    row_scale = lax.rsqrt(jnp.mean(values * values, axis=1, keepdims=True) + NORM_EPS)
    return values * row_scale * gain_vec, row_scale


def norm_back(row_grad, values, row_scale, gain_vec):
    scaled_grad = row_grad * gain_vec
    return row_scale * scaled_grad - values * row_scale**3 * jnp.mean(
        scaled_grad * values, axis=1, keepdims=True
    )


def adamw_update(master, grad_sum, first_mom, second_mom, decay_rate, step_rate):
    next_first = BETA_ONE * first_mom + (1.0 - BETA_ONE) * grad_sum
    next_second = BETA_TWO * second_mom + (1.0 - BETA_TWO) * grad_sum * grad_sum
    first_hat = next_first / (1.0 - BETA_ONE**STEP)
    second_hat = next_second / (1.0 - BETA_TWO**STEP)
    next_master = master - step_rate * (
        first_hat / (jnp.sqrt(second_hat) + ADAM_EPS) + decay_rate * master
    )
    return (next_master, next_first, next_second)


def sum_over(values, sizes):
    for axis, size in sizes:
        step = 1
        while step < size:
            values = values + lax.ppermute(values, axis, [(i, i ^ step) for i in range(size)])
            step *= 2
    return values


def adamw_write(refs, grad, master, first, second):
    refs[0][...] = grad
    refs[1][...], refs[2][...], refs[3][...] = adamw_update(
        master[...], grad, first[...], second[...], WEIGHT_DECAY, LEARN_RATE
    )


def adamw_ffn_kernel(x_ref, mine_1, theirs_1, mine_2, theirs_2, *refs):
    step = pl.program_id(0)
    low_is_own = x_ref[0] == 0
    states, outs = refs[:9], refs[9:]
    rows = states[0].shape[0]
    hidden = states[0].shape[1] // 4
    here = pl.ds(pl.multiple_of(step * rows, rows), rows)
    for i in range(2):
        lanes = slice(i * hidden, (i + 1) * hidden)
        own = cat([mine_1[here, lanes], mine_2[here, lanes]], 1)
        other = cat([theirs_1[here, lanes], theirs_2[here, lanes]], 1).astype(F32)
        low = jnp.where(low_is_own, own, other)
        high = jnp.where(low_is_own, other, own)
        adamw_write(outs[4 * i : 4 * i + 4], cat([low, high], 1), *states[3 * i : 3 * i + 3])
    lanes = slice(2 * hidden, 3 * hidden)
    first = step % 2 == 0
    own = jnp.where(first, mine_1[:, lanes], mine_2[:, lanes])
    other = jnp.where(first, theirs_1[:, lanes], theirs_2[:, lanes]).astype(F32)
    grad = jnp.where(step // 2 == x_ref[0], own, other)
    width = states[6].shape[1]
    grad = cat([grad[:, j : j + width] for j in range(0, hidden, width)], 0)
    adamw_write(outs[8:], grad, *states[6:])


def adamw_ffn(x, pair_1, pair_2, states):
    steps = 4

    def cut(array):
        return pl.BlockSpec((array.shape[0] // steps, array.shape[1]), lambda i: (i, 0))

    packs = [*pair_1, *pair_2]
    flat = [array for triple in states for array in triple]
    outs = [triple[0] for triple in states for _ in range(4)]
    result = pl.pallas_call(
        adamw_ffn_kernel,
        grid=(steps,),
        in_specs=[pl.BlockSpec(memory_space=pltpu.SMEM)]
        + [once(pack.shape) for pack in packs]
        + [cut(array) for array in flat],
        out_specs=[cut(array) for array in outs],
        out_shape=[jax.ShapeDtypeStruct(array.shape, F32) for array in outs],
        compiler_params=pltpu.CompilerParams(vmem_limit_bytes=60 * MIB),
        cost_estimate=SMALL,
        name="adamw_ffn",
    )(x.astype(jnp.int32).reshape(1), *packs, *flat)
    return [result[4 * i : 4 * i + 4] for i in range(3)]


def adamw_attn_kernel(x_ref, mine_ref, theirs_ref, *refs):
    low_is_own = x_ref[0] == 0
    states, outs = refs[:12], refs[12:]
    own, other = mine_ref[...], theirs_ref[...].astype(F32)
    low = jnp.where(low_is_own, own, other)
    high = jnp.where(low_is_own, other, own)
    wide = states[0].shape[1] // 2
    adamw_write(outs[:4], cat([low[:, :wide], high[:, :wide]], 1), *states[:3])
    low_kv, high_kv = low[:, wide : wide + 128], high[:, wide : wide + 128]
    is_key = lanes_of(low_kv.shape) < HD
    key = jnp.where(is_key, low_kv, pltpu.roll(high_kv, HD, 1))
    adamw_write(outs[4:8], key, *states[3:6])
    value = jnp.where(is_key, pltpu.roll(low_kv, HD, 1), high_kv)
    adamw_write(outs[8:12], value, *states[6:9])
    adamw_write(outs[12:], cat([low[:, wide + 128 :], high[:, wide + 128 :]], 0), *states[9:])


def adamw_attn(x, pair, states):
    flat = [array for triple in states for array in triple]
    outs = [triple[0] for triple in states for _ in range(4)]
    result = pl.pallas_call(
        adamw_attn_kernel,
        grid=(1,),
        in_specs=[pl.BlockSpec(memory_space=pltpu.SMEM)]
        + [once(array.shape) for array in [*pair, *flat]],
        out_specs=[once(array.shape) for array in outs],
        out_shape=[jax.ShapeDtypeStruct(array.shape, F32) for array in outs],
        compiler_params=pltpu.CompilerParams(vmem_limit_bytes=60 * MIB),
        cost_estimate=SMALL,
        name="adamw_attn",
    )(x.astype(jnp.int32).reshape(1), *pair, *flat)
    return [result[4 * i : 4 * i + 4] for i in range(4)]


def finish_kernel(
    place_ref, back_ref, inputs_ref, scale_ref, gain_ref, res_grad_ref, residual_ref, stays_ref,
    first_ref, second_ref, out_ref, in_grad_ref,
):
    back = norm_back(
        back_ref[...].astype(F32), inputs_ref[...].astype(F32), scale_ref[...], gain_ref[...]
    )
    in_grad = res_grad_ref[...] + back
    summed = add(stays_ref[...], first_ref[0], second_ref[...])
    out = (residual_ref[...] + summed).astype(LOW)
    quarter = out.shape[1] // 4
    for k in range(4):
        there = pl.ds(pl.multiple_of((place_ref[0] ^ k) * quarter, quarter), quarter)
        out_ref[:, there] = out[:, k * quarter : (k + 1) * quarter]
        in_grad_ref[:, there] = in_grad[:, k * quarter : (k + 1) * quarter]


def finish(place, back, inputs, scale, gain, res_grad, residual, stays, first, second):
    arrays = [back, inputs, scale, gain[None, :], res_grad, residual, stays, first, second]
    return pl.pallas_call(
        finish_kernel,
        grid=(1,),
        in_specs=[pl.BlockSpec(memory_space=pltpu.SMEM)] + [once(a.shape) for a in arrays],
        out_specs=[once(inputs.shape)] * 2,
        out_shape=[
            jax.ShapeDtypeStruct(inputs.shape, LOW),
            jax.ShapeDtypeStruct(inputs.shape, F32),
        ],
        compiler_params=pltpu.CompilerParams(vmem_limit_bytes=60 * MIB),
        cost_estimate=SMALL,
        name="finish",
    )(place.astype(jnp.int32).reshape(1), *arrays)


def pick(index, low, high):
    return jnp.where(index == 0, low, high)


class Plane:
    def __init__(self, tp):
        self.tp, self.half = tp, tp // 2
        self.x = lax.axis_index("di")
        self.y = lax.axis_index("tp") // self.half
        self.core = lax.axis_index("tp") % 2
        self.place = self.x * 2 + self.y
        self.axes = ("di", "tp")

    def pairs(self, first):
        def other(index):
            x, t = divmod(index, self.tp)
            along_x = (t % 2 == 0) == first
            return (1 - x) * self.tp + t if along_x else x * self.tp + (t + self.half) % self.tp

        return [(index, other(index)) for index in range(2 * self.tp)]

    def swap_first(self, value):
        return lax.ppermute(value, self.axes, self.pairs(True))

    def swap_second(self, value):
        return lax.ppermute(value, self.axes, self.pairs(False))

    def swap_core(self, value):
        return lax.ppermute(value, "tp", [(i, i ^ 1) for i in range(self.tp)])

    def first_step(self):
        return jnp.where(self.core == 0, 2, 1)

    def at(self, blocks, step):
        return lax.dynamic_index_in_dim(blocks, self.place ^ step, 0, keepdims=False)


def on_device(
    sizes,
    layer_input, out_grad, segment_ids, positions,
    w_query, w_key, w_value, w_out, w_gate, w_up, w_down,
    m_query, m_key, m_value, m_out, m_gate, m_up, m_down,
    v_query, v_key, v_value, v_out, v_gate, v_up, v_down,
    gain_attn, gain_ffn, m_gain_attn, m_gain_ffn, v_gain_attn, v_gain_ffn,
):
    width = layer_input.shape[1]
    plan = Plan(sizes["do"], w_query.shape[0])
    by_x = plan.by_x
    axes = ("di", "tp")
    plane = Plane(sizes["tp"])
    plane_sizes = (("tp", sizes["tp"]), ("di", sizes["di"]))

    gain_one, gain_two = plan.reorder(gain_attn), plan.reorder(gain_ffn)
    inputs_low = plan.reorder(layer_input)
    inputs_f = inputs_low.astype(F32)
    grad_low = plan.reorder(out_grad)
    normed, scale_one = norm_rows(inputs_f, gain_one)
    normed_all = lax.all_gather(normed.astype(LOW), axes, axis=0, tiled=True)

    marks = cat([segment_ids[None, :], positions[None, :]], 0)
    marks_other = lax.ppermute(marks, "di", PAIR)
    marks_all = cat([by_x(marks, marks_other), by_x(marks_other, marks)], 1)
    seg_all, pos_all = marks_all[0], marks_all[1]
    rows = seg_all.shape[0]
    seqs = rows // LEN
    seg_col, seg_row = seg_all.reshape(rows, 1), seg_all.reshape(seqs, 1, LEN)
    cosine, sine = rope_tables(pos_all)

    def col_halves(weight):
        half = weight.shape[1] // 2
        low = weight.astype(LOW)
        return by_x(low[:, :half], low[:, half:]), by_x(low[:, half:], low[:, :half])

    def row_halves(weight):
        half = weight.shape[0] // 2
        low = weight.astype(LOW)
        return by_x(low[:half], low[half:]), by_x(low[half:], low[:half])

    def col_cut(pair, chunk):
        size = pair[0].shape[1] // CHUNKS
        return tuple(part[:, chunk * size : (chunk + 1) * size] for part in pair)

    def row_cut(pair, chunk):
        size = pair[0].shape[0] // CHUNKS
        return tuple(part[chunk * size : (chunk + 1) * size] for part in pair)

    halves_q, halves_k, halves_v = col_halves(w_query), col_halves(w_key), col_halves(w_value)
    qkv_parts = tuple(cat([q, k, v], 1) for q, k, v in zip(halves_q, halves_k, halves_v))
    out_parts = row_halves(w_out)
    halves_g, halves_u, halves_d = col_halves(w_gate), col_halves(w_up), row_halves(w_down)

    def ffn_parts(chunk):
        gate_up = tuple(
            cat([g, u], 1) for g, u in zip(col_cut(halves_g, chunk), col_cut(halves_u, chunk))
        )
        return gate_up, row_cut(halves_d, chunk)

    hidden = halves_d[0].shape[0] // CHUNKS
    attn_shapes = (width, qkv_parts[0].shape[1]), (out_parts[0].shape[0], width)
    ffn_shapes = (width, 2 * hidden), (hidden, width)
    own_rows = layer_input.shape[0]
    core = lax.axis_index("tp") % 2

    if plan.line:
        attn_own, attn_other = plan.pack(qkv_parts, out_parts)
        own_1, other_1 = plan.pack(*ffn_parts(0))
        own_2, other_2 = plan.pack(*ffn_parts(1))
        attn_theirs = plan.swap(attn_other)
        attn_theirs, marks_all, own_1, other_1 = fence(attn_theirs, marks_all, own_1, other_1)
        attn_block = plan.join(attn_own, attn_theirs)
        near, across = line_near(attn_block)
        theirs_1 = plan.swap(other_1)
        near, across, cosine, sine, own_2, other_2 = fence(
            near, across, cosine, sine, own_2, other_2
        )
        across_near, out = line_far(near, across)
        out, across_near, theirs_1 = fence(out, across_near, theirs_1)
        out_near = line_last(across_near)
        block_1 = plan.join(own_1, theirs_1)
        out_near, block_1, grad_low, other_2, seg_col, seg_row = fence(
            out_near, block_1, grad_low, other_2, seg_col, seg_row
        )
        attn_weights = (attn_block, near, across_near, out, across, (out_near,))
        near_1, across_1 = line_near(block_1)
    else:
        attn_weights = plan.plain_gather(qkv_parts, out_parts)
        first_weights = plan.plain_gather(*ffn_parts(0))
        second_weights = plan.plain_gather(*ffn_parts(1))
    attn_loader = Loader(plan, attn_weights, *attn_shapes)

    attn_part, ctx, queries, both, lse, wout = attn_forward(
        attn_loader, normed_all, cosine, sine, seg_col, seg_row
    )
    grad_second = plane.swap_second(grad_low)
    if plan.line:
        theirs_2 = plan.swap(other_2)
        attn_part, near_1, across_1, grad_second, theirs_2, grad_low = fence(
            attn_part, near_1, across_1, grad_second, theirs_2, grad_low
        )
        across_near_1, out_1 = line_far(near_1, across_1)
    grad_first = plane.swap_first(grad_low)
    attn_sum = lax.psum_scatter(attn_part, axes, scatter_dimension=0, tiled=True)
    grad_xy = plane.swap_first(grad_second)
    if plan.line:
        out_1, across_near_1, grad_xy, theirs_2, grad_first = fence(
            out_1, across_near_1, grad_xy, theirs_2, grad_first
        )
        block_2 = plan.join(own_2, theirs_2)
        out_near_1 = line_last(across_near_1)
    grad_x = pick(core, grad_first, grad_second)
    grad_y = pick(core, grad_second, grad_first)
    over_y = cat([pick(plane.y, grad_low, grad_y), pick(plane.y, grad_y, grad_low)], 0)
    over_xy = cat([pick(plane.y, grad_x, grad_xy), pick(plane.y, grad_xy, grad_x)], 0)
    grad_core = cat([by_x(over_y, over_xy), by_x(over_xy, over_y)], 0)
    if plan.line:
        attn_sum, out_near_1, grad_core, block_2 = fence(
            attn_sum, out_near_1, grad_core, block_2
        )
    grad_other = plane.swap_core(grad_core)
    groups = (rows // own_rows // 2, 1, own_rows, width)
    mine, theirs = grad_core.reshape(groups), grad_other.reshape(groups)
    grad_all = cat([pick(core, mine, theirs), pick(core, theirs, mine)], 1).reshape(rows, width)
    residual = inputs_f + attn_sum.astype(F32)
    normed_two, scale_two = norm_rows(residual, gain_two)
    two_low = normed_two.astype(LOW)
    two_all = lax.all_gather(two_low, axes, axis=0, tiled=True)

    if plan.line:
        first_weights = (block_1, near_1, across_near_1, out_1, across_1, (out_near_1,))
        block_2, _ = fence(block_2, two_low)
        near_2, across_2 = line_near(block_2)
        near_2, across_2, wout, grad_all = fence(near_2, across_2, wout, grad_all)
        across_near_2, out_2 = line_far(near_2, across_2)
    wout_all = lax.all_gather(wout, axes, axis=0, tiled=True)
    first = Loader(plan, first_weights, *ffn_shapes)
    back_1, act_1, both_1, down_1 = ffn_main(first, two_all, grad_all, None)
    if plan.line:
        back_1, act_1, both_1, out_2, across_near_2 = fence(
            back_1, act_1, both_1, out_2, across_near_2
        )
        out_near_2 = line_last(across_near_2, OUTWARD)
        *last_1, third_1 = ffn_weights(plan, two_all, grad_all, act_1, both_1, (3, 2))
        last_1, both_1 = fence(last_1, both_1)
        far_1 = [lax.ppermute(part, "do", INWARD) for part in last_1]
        (rest_1,) = ffn_weights(plan, two_all, grad_all, act_1, both_1, (0, 1))
        back_1, rest_1, out_near_2 = fence(back_1, rest_1, out_near_2)
        second_weights = (block_2, near_2, across_near_2, out_2, across_2, (out_near_2,))
    else:
        grads_1 = ffn_weights(plan, two_all, grad_all, act_1, both_1, (0, 1, 2, 3))
    second = Loader(plan, second_weights, *ffn_shapes)
    back_2, act_2, both_2, down_2 = ffn_main(second, two_all, grad_all, back_1)
    if plan.line:
        back_2, act_2, both_2, far_1, wout_all, act_1 = fence(
            back_2, act_2, both_2, far_1, wout_all, act_1
        )
        block = plan.block
        crossed_1, inward_1 = sum_middle([None, None, third_1], far_1)
    back_sum = lax.psum_scatter(back_2, axes, scatter_dimension=0, tiled=True)
    order = (3, 0, 1, 2) if plan.line else (0, 1, 2, 3)
    grads_2 = ffn_weights(plan, two_all, grad_all, act_2, both_2, order)
    if plan.line:
        *last_2, rest_2 = grads_2
        act_2, rest_2, inward_1, crossed_1, last_2 = fence(
            act_2, rest_2, inward_1, crossed_1, last_2
        )
        grads_1 = [rest_1[:block], rest_1[block:], third_1, cat(last_1, 0)]
        grads_2 = [rest_2[:block], rest_2[block : 2 * block], rest_2[2 * block :], cat(last_2, 0)]
        far_low = lax.ppermute(last_2[0], "do", NEAR)
    out_part, gain_two_part = ffn_out(act_1, act_2, down_1, down_2, back_2, two_all)
    if plan.line:
        out_part, far_low, last_high = fence(out_part, far_low, last_2[1])
        far_high = lax.ppermute(last_high, "do", NEAR)

    if plan.line:
        back_sum, out_part = fence(back_sum, out_part)

    residual_grad, res_low, ctx_grad = residual_backward(
        back_sum, residual, scale_two, gain_two, grad_low, wout_all
    )
    if plan.line:
        ctx_grad, res_low, far_high = fence(ctx_grad, res_low, far_high)
        second = add_inner(grads_2[2], cat([far_low, far_high], 0)).astype(LOW)
        first_1, third_1 = sum_near_parts(grads_1, crossed_1, inward_1)
        ctx_grad, near_both, across_both = fence(
            ctx_grad, cat([second, first_1], 0), cat([second, third_1], 0)
        )
        near_both = lax.ppermute(near_both, "do", NEAR)
        across_both = lax.ppermute(across_both, "do", MIDDLE)
    ctx_grad = lax.all_to_all(ctx_grad, axes, split_axis=1, concat_axis=0, tiled=True)
    if plan.line:
        ctx_grad, res_low, out_part = fence(ctx_grad, res_low, out_part)

    out_shape = (rows // own_rows // 2, 2, own_rows, width)
    parts = out_part.reshape(out_shape)
    mine, theirs = pick(core, parts[:, 0], parts[:, 1]), pick(core, parts[:, 1], parts[:, 0])
    summed = add(mine, plane.swap_core(theirs)).astype(LOW)
    step = plane.first_step()
    goes = jnp.stack([plane.at(summed, step), plane.at(summed, 3)])
    goes_on, stays = plane.at(summed, 3 - step), plane.at(summed, 0)
    if plan.line:
        ctx_grad, goes, goes_on, stays = fence(ctx_grad, goes, goes_on, stays)
    arrives = plane.swap_first(goes)
    res_all = lax.all_gather(res_low, axes, axis=0, tiled=True)
    back_one_part, gain_one_part, *grads_qkv = attn_backward(
        attn_loader, ctx_grad, normed_all, queries, both, lse, cosine, sine, seg_col, seg_row
    )
    if plan.line:
        gain_parts = jnp.stack([gain_one_part[0] / gain_one, gain_two_part[0] / gain_two])
        gain_sums = sum_over(plan.reorder(gain_parts), plane_sizes + (("do", sizes["do"]),))
        back_one_part, grads_qkv, res_all, gain_sums, arrives, near_both, across_both = fence(
            back_one_part, grads_qkv, res_all, gain_sums, arrives, near_both, across_both
        )
        crossed_2, inward_2 = across_both[:block], near_both[:block]
        near_sum_1, across_sum_1 = near_both[block:], across_both[block:]
    else:
        gain_parts = jnp.stack([gain_one_part[0] / gain_one, gain_two_part[0] / gain_two])
        gain_sums = sum_over(gain_parts, (("do", sizes["do"]),) + plane_sizes)
    back_one = lax.psum_scatter(back_one_part, axes, scatter_dimension=0, tiled=True)
    grads_attn = out_weights(plan, ctx, res_all, grads_qkv)
    if plan.line:
        half = plan.rows

        def trade(total):
            return plan.trade(total[:half], total[half:])

        near_sum_2, across_sum_2 = sum_near_send(*sum_near_parts(grads_2, crossed_2, inward_2))
        ffn_pair_1 = trade(sum_own(grads_1, near_sum_1, across_sum_1))
        near_sum_2, across_sum_2, grads_attn = fence(near_sum_2, across_sum_2, grads_attn)
        direct = send_direct(grads_attn)
        ffn_pair_2 = trade(sum_own(grads_2, near_sum_2, across_sum_2))
    second = plane.swap_second(add(goes_on, arrives[1]).astype(LOW))
    place = lax.axis_index("do") if plan.line else jnp.zeros((), jnp.int32)
    states = {
        "attn": [
            (w_query, m_query, v_query), (w_key, m_key, v_key),
            (w_value, m_value, v_value), (w_out, m_out, v_out),
        ],
        "ffn": [(w_gate, m_gate, v_gate), (w_up, m_up, v_up), (w_down, m_down, v_down)],
    }
    if plan.line:
        ffn_updated = adamw_ffn(lax.axis_index("di"), ffn_pair_1, ffn_pair_2, states["ffn"])
        direct, ffn_updated, second, back_one = fence(direct, ffn_updated, second, back_one)
        attn_pair = trade(add(grads_attn[0], *direct))
        attn_updated = adamw_attn(lax.axis_index("di"), attn_pair, states["attn"])
    else:

        def join(pair, axis):
            own, other = pair[0], pair[1].astype(F32)
            return by_x(cat([own, other], axis), cat([other, own], axis))

        def from_chunks(pairs, axis):
            return join([cat([pair[i] for pair in pairs], axis) for i in range(2)], axis)

        def cut(pair, start, stop):
            return tuple(part[:, start:stop] for part in pair)

        def update(grad, state):
            return (grad, *adamw_update(state[0], grad, *state[1:], WEIGHT_DECAY, LEARN_RATE))

        qkv_pair = plan.plain_sum_row(grads_qkv[0])
        out_pair = plan.plain_sum_col(grads_attn[0])
        ffn_pairs = [
            (plan.plain_sum_row(row), plan.plain_sum_col(col)) for row, col in (grads_1, grads_2)
        ]
        at_k = halves_q[0].shape[1]
        at_v = at_k + halves_k[0].shape[1]
        end = at_v + halves_v[0].shape[1]
        attn_grads = [
            join(cut(qkv_pair, 0, at_k), 1),
            join(cut(qkv_pair, at_k, at_v), 1),
            join(cut(qkv_pair, at_v, end), 1),
            join(out_pair, 0),
        ]
        ffn_grads = [
            from_chunks([cut(row, 0, hidden) for row, _ in ffn_pairs], 1),
            from_chunks([cut(row, hidden, 2 * hidden) for row, _ in ffn_pairs], 1),
            from_chunks([col for _, col in ffn_pairs], 0),
        ]
        attn_updated = [update(g, s) for g, s in zip(attn_grads, states["attn"])]
        ffn_updated = [update(g, s) for g, s in zip(ffn_grads, states["ffn"])]
    out_value, in_grad = finish(
        place, back_one, inputs_low, scale_one, gain_one, residual_grad, residual, stays, arrives,
        second,
    )
    grad_gain_attn, grad_gain_ffn = gain_sums[0], gain_sums[1]
    updated = attn_updated + ffn_updated
    gain_updated = [
        adamw_update(gain_attn, grad_gain_attn, m_gain_attn, v_gain_attn, 0.0, GAIN_RATE),
        adamw_update(gain_ffn, grad_gain_ffn, m_gain_ffn, v_gain_ffn, 0.0, GAIN_RATE),
    ]
    return (
        out_value,
        in_grad,
        *[u[0] for u in updated],
        *[u[1] for u in updated],
        *[u[2] for u in updated],
        *[u[3] for u in updated],
        grad_gain_attn,
        grad_gain_ffn,
        *[u[0] for u in gain_updated],
        *[u[1] for u in gain_updated],
        *[u[2] for u in gain_updated],
    )


def solution(mesh):
    dp, tp = mesh.shape["dp"], mesh.shape["tp"]
    split = Mesh(mesh.devices.reshape(dp // 2, 2, tp), ("do", "di", "tp"))
    sizes = {"do": dp // 2, "di": 2, "tp": tp}
    dp_axes = ("do", "di")
    tokens = P(("do", "di", "tp"), None)
    by_rows, by_cols = P(dp_axes, "tp"), P("tp", dp_axes)
    weights = (by_rows, by_rows, by_rows, by_cols, by_rows, by_rows, by_cols)
    gains = (P(),) * 6
    in_specs = (tokens, tokens, P(dp_axes), P(dp_axes)) + weights * 3 + gains
    out_specs = (tokens, tokens) + weights * 4 + (P(),) * 2 + gains
    return jax.shard_map(
        functools.partial(on_device, sizes),
        mesh=split,
        in_specs=in_specs,
        out_specs=out_specs,
        check_vma=False,
    )
```

```python
import functools

import jax
import jax.numpy as jnp
from jax import lax
from jax.experimental import pallas as pl
from jax.experimental.pallas import tpu as pltpu
from jax.sharding import Mesh
from jax.sharding import PartitionSpec as P

HD = 64
LEN = 512
STEP = 5
CHUNKS = 2

NORM_EPS = 1e-05
ROPE_BASE = 500000.0
BETA_ONE = 0.9
BETA_TWO = 0.95
LEARN_RATE = 0.02
GAIN_RATE = 0.5
WEIGHT_DECAY = 0.1
ADAM_EPS = 1e-08

LOW = jnp.bfloat16
F32 = jnp.float32
MIB = 1024 * 1024

NEAR = [(0, 1), (1, 0), (2, 3), (3, 2)]
MIDDLE = [(1, 2), (2, 1)]
CROSS = [(0, 2), (1, 3), (2, 0), (3, 1)]
MIRROR = [(0, 3), (1, 2), (2, 1), (3, 0)]
OUTWARD = [(1, 0), (2, 3)]
INWARD = [(0, 1), (3, 2)]
PAIR = [(0, 1), (1, 0)]


def dot(lhs, rhs, lhs_dim, rhs_dim):
    return lax.dot_general(
        lhs, rhs, (((lhs_dim,), (rhs_dim,)), ((), ())), preferred_element_type=F32
    )


def cat(parts, axis):
    return jnp.concatenate(parts, axis)


def fence(*values):
    return lax.optimization_barrier(values)


def line_near(own):
    return lax.ppermute(own, "do", NEAR), lax.ppermute(own, "do", MIDDLE)


def line_far(near, across):
    out = lax.ppermute(across, "do", NEAR)
    return lax.ppermute(near, "do", MIDDLE), out


def line_last(across_near, perm=NEAR):
    return lax.ppermute(across_near, "do", perm)


def add(part, *arrived):
    total = part.astype(F32)
    for piece in arrived:
        total = total + piece.astype(F32)
    return total


def is_inner():
    place = lax.axis_index("do")
    return (place == 1) | (place == 2)


def add_inner(part, arrived):
    return add(part, jnp.where(is_inner(), arrived, jnp.zeros_like(arrived)))


def sum_middle(parts, far):
    second = add_inner(parts[2], cat(far, 0)).astype(LOW)
    inward = lax.ppermute(second, "do", NEAR)
    return lax.ppermute(second, "do", MIDDLE), inward


def sum_near_parts(parts, crossed, inward):
    return add_inner(parts[1], crossed).astype(LOW), add_inner(parts[3], inward).astype(LOW)


def sum_near_send(first, third):
    return lax.ppermute(first, "do", NEAR), lax.ppermute(third, "do", MIDDLE)


def sum_own(parts, from_near, from_across):
    return add_inner(parts[0], from_across) + from_near.astype(F32)


class Plan:
    def __init__(self, outer, per_device):
        self.rows = per_device
        self.block = 2 * per_device
        self.line = outer == 4 and per_device == 256
        self.cuts = 4 if self.line else 1

    def reorder(self, values):
        if not self.line:
            return values
        place = lax.axis_index("do")
        quarter = values.shape[-1] // 4
        a, b, c, d = (values[..., i * quarter : (i + 1) * quarter] for i in range(4))
        values = jnp.where(place % 2 == 1, cat([b, a, d, c], -1), values)
        half = 2 * quarter
        turned = cat([values[..., half:], values[..., :half]], -1)
        return jnp.where(place >= 2, turned, values)

    def by_x(self, low, high):
        return jnp.where(lax.axis_index("di") == 0, low, high)

    def inner(self):
        return is_inner().astype(jnp.int32).reshape(1)

    def pack(self, row_part, col_part):
        rows, packs = self.rows, []
        for row_side, side in zip(row_part, col_part):
            pieces = [side[i : i + rows] for i in range(0, side.shape[0], rows)]
            packs.append(cat([row_side] + pieces, 1))
        return packs

    def swap(self, other):
        return lax.ppermute(other, "di", PAIR)

    def join(self, own, theirs, axis=0):
        return cat([self.by_x(own, theirs), self.by_x(theirs, own)], axis)

    def plain_gather(self, row_part, col_part):
        full = []
        for (own, other), axis in ((row_part, 0), (col_part, 1)):
            block = self.join(own, self.swap(other), axis)
            full.append(lax.all_gather(block, "do", axis=axis, tiled=True))
        return tuple(full)

    def unpack(self, pair, wide):
        cuts = range(wide, pair[0].shape[1], self.rows)
        return (
            tuple(side[:, :wide] for side in pair),
            tuple(cat([side[:, i : i + self.rows] for i in cuts], 0) for side in pair),
        )

    def plain_sum_row(self, grad):
        total = lax.psum_scatter(grad, "do", scatter_dimension=0, tiled=True)
        return self.trade(total[: self.rows], total[self.rows :])

    def plain_sum_col(self, grad):
        total = lax.psum_scatter(grad, "do", scatter_dimension=1, tiled=True)
        return self.trade(total[:, : self.rows], total[:, self.rows :])

    def trade(self, low, high):
        theirs = lax.ppermute(self.by_x(high, low).astype(LOW), "di", PAIR)
        return self.by_x(low, high).astype(F32), theirs


ANY = pl.BlockSpec(memory_space=pl.ANY)
SMALL = pl.CostEstimate(flops=1, bytes_accessed=1, transcendentals=0)


class Loader:
    def __init__(self, plan, weights, row_shape, col_shape):
        self.plan, self.row_shape, self.col_shape = plan, row_shape, col_shape
        rows, wide = plan.rows, row_shape[1]
        self.moves = []
        if plan.line:
            *whole, last = weights
            self.operands = [plan.inner(), *whole, *last]
            for k in range(4):
                for x in range(2):
                    at = k * plan.block + x * rows
                    self.moves.append((k, x, 0, 0, (at, 0), wide))
                    for i in range(0, col_shape[0], rows):
                        self.moves.append((k, x, 1, wide + i, (i, at), rows))
        else:
            self.operands = list(weights)
            self.moves = [None, None]
        self.count = len(self.operands)

    def specs(self):
        if not self.plan.line:
            return [ANY] * 2
        return [pl.BlockSpec(memory_space=pltpu.SMEM)] + [ANY] * (self.count - 1)

    def scratch(self):
        return [
            pltpu.VMEM(self.row_shape, LOW),
            pltpu.VMEM(self.col_shape, LOW),
            pltpu.SemaphoreType.DMA((len(self.moves),)),
        ]

    def load(self, refs, row_ref, col_ref, sems):
        if not self.plan.line:
            pairs = zip(refs, (row_ref, col_ref))
            made = [pltpu.make_async_copy(*pair, sems.at[i]) for i, pair in enumerate(pairs)]
            for copy in made:
                copy.start()
            for copy in made:
                copy.wait()
            return
        rows = self.plan.rows

        def copies(sources):
            made = []
            for i, (k, x, which, column, there, wide) in enumerate(self.moves):
                if sources[k] is None:
                    continue
                if isinstance(sources[k], tuple):
                    source, row = sources[k][x], 0
                else:
                    source, row = sources[k], x * rows
                target = (row_ref, col_ref)[which]
                made.append(
                    pltpu.make_async_copy(
                        source.at[pl.ds(row, rows), pl.ds(column, wide)],
                        target.at[pl.ds(there[0], rows), pl.ds(there[1], wide)],
                        sems.at[i],
                    )
                )
            return made

        inner, own, near, across_near, out, across, *last = refs
        out_near = tuple(last) if len(last) == 2 else last[0]
        is_inner = inner[0] == 1
        for copy in copies((own, near, None, None)):
            copy.start()

        @pl.when(is_inner)
        def _():
            for copy in copies((None, None, across_near, across)):
                copy.start()

        @pl.when(jnp.logical_not(is_inner))
        def _():
            for copy in copies((None, None, out, out_near)):
                copy.start()

        for copy in copies((own, near, out, out_near)):
            copy.wait()


def rope_tables(positions):
    half_dim = HD // 2
    inverse_freq = ROPE_BASE ** (-2.0 * jnp.arange(half_dim, dtype=F32) / HD)
    angles = positions.astype(F32)[:, None] * inverse_freq[None, :]
    cosine, sine = jnp.cos(angles), jnp.sin(angles)
    return cat([cosine] * 4, 1), cat([-sine, sine] * 2, 1)


def lanes_of(shape):
    return lax.broadcasted_iota(jnp.int32, shape, 1)


def shuffle_halves(values):
    wide = values.shape[1]
    up = pltpu.roll(values, wide - HD // 2, 1)
    down = pltpu.roll(values, HD // 2, 1)
    return jnp.where(lanes_of(values.shape) % HD < HD // 2, up, down)


def tables(cos_ref, sin_ref, pairs):
    cosine, sine = cos_ref[...], sin_ref[...]
    is_key = lanes_of(cosine.shape) < HD
    return (
        cat([cosine] * pairs + [jnp.where(is_key, cosine, 1.0)], 1),
        cat([sine] * pairs + [jnp.where(is_key, sine, 0.0)], 1),
    )


def split_kv(both):
    is_key = lanes_of(both.shape) < HD
    blank = jnp.zeros_like(both)
    key_low = jnp.where(is_key, both, blank)
    value_high = jnp.where(is_key, blank, both)
    return (
        (key_low, pltpu.roll(key_low.astype(F32), HD, 1).astype(LOW)),
        (pltpu.roll(value_high.astype(F32), HD, 1).astype(LOW), value_high),
    )


def allowed_pairs(seg_col, seg_row):
    shape = (seg_col.shape[0], seg_row.shape[1])
    key_at = lax.broadcasted_iota(jnp.int32, shape, 1)
    query_at = lax.broadcasted_iota(jnp.int32, shape, 0)
    return (seg_col == seg_row) & (key_at <= query_at)


def attn_forward_kernel(pairs, loader, *refs):
    weights, refs = refs[: loader.count], refs[loader.count :]
    x_ref, cos_ref, sin_ref, col_ref, row_ref = refs[:5]
    part_ref, ctx_ref, q_ref, kv_ref, lse_ref, wout_ref, wqkv_ref, _, sems = refs[5:]

    @pl.when(pl.program_id(0) == 0)
    def _():
        loader.load(weights, wqkv_ref, wout_ref, sems)

    cosine, sine = tables(cos_ref, sin_ref, pairs)
    qkv = dot(x_ref[...], wqkv_ref[...], 1, 0)
    rotated = (qkv * cosine + shuffle_halves(qkv) * sine).astype(LOW)
    queries, both = rotated[:, : pairs * 128], rotated[:, pairs * 128 :]
    q_ref[...] = queries
    kv_ref[...] = both
    keys, values = split_kv(both)
    allowed = allowed_pairs(col_ref[...], row_ref[0])
    lane = lanes_of((both.shape[0], 128))
    log_sums = [jnp.zeros((both.shape[0] // 2, 128), F32)] * 2
    contexts = []
    half = both.shape[0] // 2
    for pair in range(pairs):
        bands = []
        for low, high in ((0, half), (half, 2 * half)):
            heads = queries[low:high, pair * 128 : (pair + 1) * 128]
            context = None
            for side in range(2):
                scores = dot(heads, keys[side][:high], 1, 1) * HD**-0.5
                masked = jnp.where(allowed[low:high, :high], scores, -1e30)
                top = jnp.max(masked, axis=1, keepdims=True)
                weights = jnp.exp(masked - top)
                totals = jnp.sum(weights, axis=1, keepdims=True)
                probs = (weights * (1.0 / totals)).astype(LOW)
                piece = dot(probs, values[side][:high], 1, 0)
                context = piece if context is None else context + piece
                at = 2 * pair + side
                log_sums[low // half] = jnp.where(
                    lane[:half] == at, top + jnp.log(totals), log_sums[low // half]
                )
            bands.append(context.astype(LOW))
        contexts.append(cat(bands, 0))
    lse_ref[...] = cat(log_sums, 0)
    context_low = cat(contexts, 1)
    ctx_ref[...] = context_low
    part_ref[...] = dot(context_low, wout_ref[...], 1, 0).astype(LOW)


def attn_backward_kernel(pairs, loader, *refs):
    weights, refs = refs[: loader.count], refs[loader.count :]
    cg_ref, x_ref, q_ref, kv_ref, lse_ref, cos_ref, sin_ref, col_ref, row_ref = refs[:9]
    part_ref, gain_ref, *grad_refs = refs[9:-4]
    wqkv_ref, wout_ref, sems, acc_qkv = refs[-4:]
    step = pl.program_id(0)

    @pl.when(step == 0)
    def _():
        loader.load(weights, wqkv_ref, wout_ref, sems)
        acc_qkv[...] = jnp.zeros_like(acc_qkv)
        gain_ref[...] = jnp.zeros_like(gain_ref)

    cosine, sine = tables(cos_ref, sin_ref, pairs)
    scale = HD**-0.5
    ctx_grad = cg_ref[...]
    keys, values = split_kv(kv_ref[...])
    allowed = allowed_pairs(col_ref[...], row_ref[0])
    lane = lanes_of((ctx_grad.shape[0], 128))
    log_sums = lse_ref[...]
    query_grads, key_grad, value_grad = [], None, None
    for pair in range(pairs):
        heads = q_ref[:, pair * 128 : (pair + 1) * 128]
        grads = ctx_grad[:, pair * 128 : (pair + 1) * 128]
        query_grad = None
        for side in range(2):
            here = (lane < HD) if side == 0 else (lane >= HD)
            head = jnp.where(here, heads, jnp.zeros_like(heads))
            grad = jnp.where(here, grads, jnp.zeros_like(grads))
            at = 2 * pair + side
            scores = dot(heads, keys[side], 1, 1) * scale
            probs = jnp.where(allowed, jnp.exp(scores - log_sums[:, at : at + 1]), 0.0)
            prob_grad = dot(grads, values[side], 1, 1)
            delta = jnp.sum(probs * prob_grad, axis=1, keepdims=True)
            score_grad = (probs * (prob_grad - delta)).astype(LOW)
            to_value = dot(probs.astype(LOW), grad, 0, 0)
            to_key = dot(score_grad, head, 0, 0)
            to_query = dot(score_grad, keys[side], 1, 0)
            value_grad = to_value if value_grad is None else value_grad + to_value
            key_grad = to_key if key_grad is None else key_grad + to_key
            query_grad = to_query if query_grad is None else query_grad + to_query
        query_grads.append(query_grad * scale)
    key_grad = (key_grad + pltpu.roll(key_grad, HD, 1)) * scale
    value_grad = value_grad + pltpu.roll(value_grad, HD, 1)
    joined = cat(query_grads + [jnp.where(lane < HD, key_grad, value_grad)], 1)
    low = (joined * cosine - shuffle_halves(joined) * sine).astype(LOW)
    part = dot(low, wqkv_ref[...], 1, 1)
    part_ref[...] = part.astype(LOW)
    gain_ref[...] += jnp.sum(part * x_ref[...].astype(F32), axis=0, keepdims=True)
    acc_qkv[...] += dot(x_ref[...], low, 0, 0)

    @pl.when(step == pl.num_programs(0) - 1)
    def _():
        cut = acc_qkv.shape[0] // len(grad_refs)
        for i, out in enumerate(grad_refs):
            out[...] = acc_qkv[i * cut : (i + 1) * cut, :].astype(LOW)


def once(shape):
    return pl.BlockSpec(shape, lambda i: (0,) * len(shape), pipeline_mode=pl.Buffered(1))


def per_seq(shape):
    return pl.BlockSpec(shape, lambda i: (i,) + (0,) * (len(shape) - 1))


def attn_forward(loader, normed, cosine, sine, seg_col, seg_row):
    rows, width = normed.shape
    heads = loader.col_shape[0]
    return pl.pallas_call(
        functools.partial(attn_forward_kernel, heads // 128, loader),
        grid=(rows // LEN,),
        in_specs=[
            *loader.specs(),
            per_seq((LEN, width)),
            per_seq((LEN, 128)),
            per_seq((LEN, 128)),
            per_seq((LEN, 1)),
            per_seq((1, 1, LEN)),
        ],
        out_specs=[
            per_seq((LEN, width)),
            per_seq((LEN, heads)),
            per_seq((LEN, heads)),
            per_seq((LEN, 128)),
            per_seq((LEN, 128)),
            once(loader.col_shape),
        ],
        out_shape=[
            jax.ShapeDtypeStruct((rows, width), LOW),
            jax.ShapeDtypeStruct((rows, heads), LOW),
            jax.ShapeDtypeStruct((rows, heads), LOW),
            jax.ShapeDtypeStruct((rows, 128), LOW),
            jax.ShapeDtypeStruct((rows, 128), F32),
            jax.ShapeDtypeStruct(loader.col_shape, LOW),
        ],
        scratch_shapes=loader.scratch(),
        compiler_params=pltpu.CompilerParams(vmem_limit_bytes=60 * MIB),
        cost_estimate=SMALL,
        name="attn_forward",
    )(*loader.operands, normed, cosine, sine, seg_col, seg_row)


def attn_backward(loader, ctx_grad, normed, queries, both, lse, cosine, sine, seg_col, seg_row):
    rows, width = normed.shape
    heads = loader.col_shape[0]
    cuts = loader.plan.cuts
    grad = (width // cuts, loader.row_shape[1])
    return pl.pallas_call(
        functools.partial(attn_backward_kernel, heads // 128, loader),
        grid=(rows // LEN,),
        in_specs=[
            *loader.specs(),
            per_seq((LEN, heads)),
            per_seq((LEN, width)),
            per_seq((LEN, heads)),
            per_seq((LEN, 128)),
            per_seq((LEN, 128)),
            per_seq((LEN, 128)),
            per_seq((LEN, 128)),
            per_seq((LEN, 1)),
            per_seq((1, 1, LEN)),
        ],
        out_specs=[per_seq((LEN, width)), once((1, width))] + [once(grad)] * cuts,
        out_shape=[
            jax.ShapeDtypeStruct((rows, width), LOW),
            jax.ShapeDtypeStruct((1, width), F32),
        ]
        + [jax.ShapeDtypeStruct(grad, LOW)] * cuts,
        scratch_shapes=[*loader.scratch(), pltpu.VMEM(loader.row_shape, F32)],
        compiler_params=pltpu.CompilerParams(vmem_limit_bytes=60 * MIB),
        cost_estimate=SMALL,
        name="attn_backward",
    )(*loader.operands, ctx_grad, normed, queries, both, lse, cosine, sine, seg_col, seg_row)


PACKS = (
    ((0, 0), (0, 1)),
    ((1, 0), (1, 1), (2, 1)),
    ((2, 0),),
    ((3, 0),),
    ((3, 1),),
)


def out_weights_kernel(plan, ctx_ref, res_ref, *refs):
    count = plan.cuts * plan.line
    qkv_refs, grad_refs, acc = refs[:count], refs[count:-1], refs[-1]
    step = pl.program_id(0)

    @pl.when(step == 0)
    def _():
        acc[...] = jnp.zeros_like(acc)

    acc[...] += dot(ctx_ref[...], res_ref[...], 0, 0)

    @pl.when(step == pl.num_programs(0) - 1)
    def _():
        if not plan.line:
            grad_refs[0][...] = acc[...].astype(LOW)
            return
        rows = plan.rows
        for out, halves in zip(grad_refs, PACKS):
            for i, (k, x) in enumerate(halves):
                wide = qkv_refs[k].shape[1]
                here, at = slice(i * rows, (i + 1) * rows), k * plan.block + x * rows
                out[here, :wide] = qkv_refs[k][x * rows : (x + 1) * rows, :]
                out[here, wide:] = acc[:, at : at + rows].astype(LOW)


def out_weights(plan, ctx, res_all, grads_qkv):
    rows, width = res_all.shape
    heads = ctx.shape[1]
    extra = list(grads_qkv) if plan.line else []
    shapes = [(heads, width)]
    if plan.line:
        shapes = [(len(halves) * plan.rows, extra[0].shape[1] + heads) for halves in PACKS]
    return pl.pallas_call(
        functools.partial(out_weights_kernel, plan),
        grid=(rows // LEN,),
        in_specs=[per_seq((LEN, heads)), per_seq((LEN, width))] + [once(g.shape) for g in extra],
        out_specs=[once(shape) for shape in shapes],
        out_shape=[jax.ShapeDtypeStruct(shape, LOW) for shape in shapes],
        scratch_shapes=[pltpu.VMEM((heads, width), F32)],
        compiler_params=pltpu.CompilerParams(vmem_limit_bytes=40 * MIB),
        cost_estimate=SMALL,
        name="out_weights",
    )(ctx, res_all, *extra)


def residual_backward_kernel(
    back_ref, residual_ref, scale_ref, gain_ref, grad_ref, wout_ref, res_grad_ref, low_ref, ctx_ref
):
    @pl.when(pl.program_id(0) == 0)
    def _():
        back = norm_back(
            back_ref[...].astype(F32), residual_ref[...], scale_ref[...], gain_ref[...]
        )
        total = grad_ref[...].astype(F32) + back
        res_grad_ref[...] = total
        low_ref[...] = total.astype(LOW)

    ctx_ref[...] = dot(low_ref[...], wout_ref[...], 1, 1).astype(LOW)


def residual_backward(back_sum, residual, scale, gain, grad_low, wout_all):
    rows, width = residual.shape
    heads = wout_all.shape[0]
    step = 512
    return pl.pallas_call(
        residual_backward_kernel,
        grid=(heads // step,),
        in_specs=[
            once((rows, width)),
            once((rows, width)),
            once((rows, 1)),
            once((1, width)),
            once((rows, width)),
            per_seq((step, width)),
        ],
        out_specs=[
            once((rows, width)),
            once((rows, width)),
            pl.BlockSpec((rows, step), lambda i: (0, i)),
        ],
        out_shape=[
            jax.ShapeDtypeStruct((rows, width), F32),
            jax.ShapeDtypeStruct((rows, width), LOW),
            jax.ShapeDtypeStruct((rows, heads), LOW),
        ],
        compiler_params=pltpu.CompilerParams(vmem_limit_bytes=60 * MIB),
        cost_estimate=SMALL,
        name="residual_backward",
    )(back_sum, residual, scale, gain[None, :], grad_low, wout_all)


TILE = 512


def ffn_main_kernel(loader, more, *refs):
    weights, refs = refs[: loader.count], refs[loader.count :]
    x_ref, grad_ref = refs[:2]
    back_ref, act_ref, both_ref, down_ref, gate_up_ref, _, sems = refs[2 + more :]

    @pl.when(pl.program_id(0) == 0)
    def _():
        loader.load(weights, gate_up_ref, down_ref, sems)

    hidden = down_ref.shape[0]
    pre = dot(x_ref[...], gate_up_ref[...], 1, 0)
    gate_pre, lifted = pre[:, :hidden], pre[:, hidden:]
    sigmoid_gate = jax.nn.sigmoid(gate_pre)
    silu_gate = gate_pre * sigmoid_gate
    act_ref[...] = (silu_gate * lifted).astype(LOW)
    act_grad = dot(grad_ref[...], down_ref[...], 1, 1)
    gate_grad = act_grad * lifted * sigmoid_gate * (1.0 + gate_pre * (1.0 - sigmoid_gate))
    both_grad = cat([gate_grad.astype(LOW), (act_grad * silu_gate).astype(LOW)], 1)
    both_ref[...] = both_grad
    back = dot(both_grad, gate_up_ref[...], 1, 1)
    if more:
        back = back + refs[2][...].astype(F32)
    back_ref[...] = back.astype(LOW)


def ffn_main(loader, tokens, grads, earlier):
    rows, width = tokens.shape
    hidden = loader.col_shape[0]
    more = [] if earlier is None else [earlier]
    return pl.pallas_call(
        functools.partial(ffn_main_kernel, loader, len(more)),
        grid=(rows // TILE,),
        in_specs=[
            *loader.specs(),
            per_seq((TILE, width)),
            per_seq((TILE, width)),
            *[per_seq((TILE, width))] * len(more),
        ],
        out_specs=[
            per_seq((TILE, width)),
            per_seq((TILE, hidden)),
            per_seq((TILE, 2 * hidden)),
            once(loader.col_shape),
        ],
        out_shape=[
            jax.ShapeDtypeStruct((rows, width), LOW),
            jax.ShapeDtypeStruct((rows, hidden), LOW),
            jax.ShapeDtypeStruct((rows, 2 * hidden), LOW),
            jax.ShapeDtypeStruct(loader.col_shape, LOW),
        ],
        scratch_shapes=loader.scratch(),
        compiler_params=pltpu.CompilerParams(vmem_limit_bytes=60 * MIB),
        cost_estimate=SMALL,
        name="ffn_main",
    )(*loader.operands, tokens, grads, *more)


def ffn_weights_kernel(plan, x_ref, grad_ref, act_ref, both_ref, *out_refs):
    row = dot(x_ref[...], both_ref[...], 0, 0).astype(LOW)
    col = dot(act_ref[...], grad_ref[...], 0, 0).astype(LOW)
    if not plan.line:
        out_refs[0][...], out_refs[1][...] = row, col
        return
    rows, wide = plan.rows, row.shape[1]

    def pack(halves):
        for x, (out, at) in enumerate(halves):
            out[at : at + rows, :wide] = row[x * rows : (x + 1) * rows]
            for i in range(0, col.shape[0], rows):
                out[at : at + rows, wide + i : wide + i + rows] = col[
                    i : i + rows, x * rows : (x + 1) * rows
                ]

    if len(out_refs) == 1:
        pack([(out_refs[0], 0), (out_refs[0], rows)])
        return

    @pl.when(pl.program_id(0) == 0)
    def _():
        pack([(out_refs[0], 0), (out_refs[1], 0)])

    @pl.when(pl.program_id(0) > 0)
    def _():
        pack([(out_refs[2], 0), (out_refs[2], rows)])


def ffn_weights(plan, tokens, grads, act, both_grad, order):
    rows, width = tokens.shape
    block = width // 4
    wide, hidden = both_grad.shape[1], act.shape[1]
    count, begin = len(order), order[0]
    step = order[1] - order[0] if begin < 3 else (order[1] - 3) % 4
    assert all(order[i] == (begin + step * i) % 4 for i in range(count))

    def columns():
        return pl.BlockSpec((rows, block), lambda i: (0, (begin + step * i) % 4))

    if not plan.line:
        out_specs = [
            pl.BlockSpec((block, wide), lambda i: ((begin + step * i) % 4, 0)),
            pl.BlockSpec((hidden, block), lambda i: (0, (begin + step * i) % 4)),
        ]
        shapes = [(count * block, wide), (hidden, count * block)]
    elif begin == 3:
        out_specs = [once((plan.rows, wide + hidden))] * 2 + [
            pl.BlockSpec((block, wide + hidden), lambda i: (jnp.maximum(i - 1, 0), 0))
        ]
        shapes = [(plan.rows, wide + hidden)] * 2 + [((count - 1) * block, wide + hidden)]
    else:
        out_specs = [pl.BlockSpec((block, wide + hidden), lambda i: (i, 0))]
        shapes = [(count * block, wide + hidden)]
    return pl.pallas_call(
        functools.partial(ffn_weights_kernel, plan),
        grid=(count,),
        in_specs=[columns(), columns(), once(act.shape), once(both_grad.shape)],
        out_specs=out_specs,
        out_shape=[jax.ShapeDtypeStruct(shape, LOW) for shape in shapes],
        compiler_params=pltpu.CompilerParams(vmem_limit_bytes=60 * MIB),
        cost_estimate=SMALL,
        name="ffn_weights",
    )(tokens, grads, act, both_grad)


def ffn_out_kernel(act_1, act_2, down_1, down_2, back_ref, x_ref, out_ref, gain_ref):
    @pl.when(pl.program_id(0) == 0)
    def _():
        gain_ref[...] = jnp.zeros_like(gain_ref)

    out = dot(act_1[...], down_1[...], 1, 0) + dot(act_2[...], down_2[...], 1, 0)
    out_ref[...] = out.astype(LOW)
    product = back_ref[...].astype(F32) * x_ref[...].astype(F32)
    gain_ref[...] += jnp.sum(product, axis=0, keepdims=True)


def ffn_out(act_1, act_2, down_1, down_2, back, tokens):
    rows, width = tokens.shape
    hidden = act_1.shape[1]
    return pl.pallas_call(
        ffn_out_kernel,
        grid=(rows // TILE,),
        in_specs=[
            per_seq((TILE, hidden)),
            per_seq((TILE, hidden)),
            once(down_1.shape),
            once(down_2.shape),
            per_seq((TILE, width)),
            per_seq((TILE, width)),
        ],
        out_specs=[per_seq((TILE, width)), once((1, width))],
        out_shape=[
            jax.ShapeDtypeStruct((rows, width), LOW),
            jax.ShapeDtypeStruct((1, width), F32),
        ],
        compiler_params=pltpu.CompilerParams(vmem_limit_bytes=60 * MIB),
        cost_estimate=SMALL,
        name="ffn_out",
    )(act_1, act_2, down_1, down_2, back, tokens)


def norm_rows(values, gain_vec):
    row_scale = lax.rsqrt(jnp.mean(values * values, axis=1, keepdims=True) + NORM_EPS)
    return values * row_scale * gain_vec, row_scale


def norm_back(row_grad, values, row_scale, gain_vec):
    scaled_grad = row_grad * gain_vec
    return row_scale * scaled_grad - values * row_scale**3 * jnp.mean(
        scaled_grad * values, axis=1, keepdims=True
    )


def adamw_update(master, grad_sum, first_mom, second_mom, decay_rate, step_rate):
    next_first = BETA_ONE * first_mom + (1.0 - BETA_ONE) * grad_sum
    next_second = BETA_TWO * second_mom + (1.0 - BETA_TWO) * grad_sum * grad_sum
    first_hat = next_first / (1.0 - BETA_ONE**STEP)
    second_hat = next_second / (1.0 - BETA_TWO**STEP)
    next_master = master - step_rate * (
        first_hat / (jnp.sqrt(second_hat) + ADAM_EPS) + decay_rate * master
    )
    return (next_master, next_first, next_second)


def sum_over(values, sizes):
    for axis, size in sizes:
        step = 1
        while step < size:
            values = values + lax.ppermute(values, axis, [(i, i ^ step) for i in range(size)])
            step *= 2
    return values


def adamw_write(refs, grad, master, first, second):
    refs[0][...] = grad
    refs[1][...], refs[2][...], refs[3][...] = adamw_update(
        master[...], grad, first[...], second[...], WEIGHT_DECAY, LEARN_RATE
    )


def adamw_ffn_kernel(x_ref, mine_1, theirs_1, mine_2, theirs_2, *refs):
    step = pl.program_id(0)
    low_is_own = x_ref[0] == 0
    states, outs = refs[:9], refs[9:]
    rows = states[0].shape[0]
    hidden = states[0].shape[1] // 4
    here = pl.ds(pl.multiple_of(step * rows, rows), rows)
    for i in range(2):
        lanes = slice(i * hidden, (i + 1) * hidden)
        own = cat([mine_1[here, lanes], mine_2[here, lanes]], 1)
        other = cat([theirs_1[here, lanes], theirs_2[here, lanes]], 1).astype(F32)
        low = jnp.where(low_is_own, own, other)
        high = jnp.where(low_is_own, other, own)
        adamw_write(outs[4 * i : 4 * i + 4], cat([low, high], 1), *states[3 * i : 3 * i + 3])
    lanes = slice(2 * hidden, 3 * hidden)
    first = step % 2 == 0
    own = jnp.where(first, mine_1[:, lanes], mine_2[:, lanes])
    other = jnp.where(first, theirs_1[:, lanes], theirs_2[:, lanes]).astype(F32)
    grad = jnp.where(step // 2 == x_ref[0], own, other)
    width = states[6].shape[1]
    grad = cat([grad[:, j : j + width] for j in range(0, hidden, width)], 0)
    adamw_write(outs[8:], grad, *states[6:])


def adamw_ffn(x, pair_1, pair_2, states):
    steps = 4

    def cut(array):
        return pl.BlockSpec((array.shape[0] // steps, array.shape[1]), lambda i: (i, 0))

    packs = [*pair_1, *pair_2]
    flat = [array for triple in states for array in triple]
    outs = [triple[0] for triple in states for _ in range(4)]
    result = pl.pallas_call(
        adamw_ffn_kernel,
        grid=(steps,),
        in_specs=[pl.BlockSpec(memory_space=pltpu.SMEM)]
        + [once(pack.shape) for pack in packs]
        + [cut(array) for array in flat],
        out_specs=[cut(array) for array in outs],
        out_shape=[jax.ShapeDtypeStruct(array.shape, F32) for array in outs],
        compiler_params=pltpu.CompilerParams(vmem_limit_bytes=60 * MIB),
        cost_estimate=SMALL,
        name="adamw_ffn",
    )(x.astype(jnp.int32).reshape(1), *packs, *flat)
    return [result[4 * i : 4 * i + 4] for i in range(3)]


def adamw_attn_kernel(x_ref, mine_ref, theirs_ref, *refs):
    low_is_own = x_ref[0] == 0
    states, outs = refs[:12], refs[12:]
    own, other = mine_ref[...], theirs_ref[...].astype(F32)
    low = jnp.where(low_is_own, own, other)
    high = jnp.where(low_is_own, other, own)
    wide = states[0].shape[1] // 2
    adamw_write(outs[:4], cat([low[:, :wide], high[:, :wide]], 1), *states[:3])
    low_kv, high_kv = low[:, wide : wide + 128], high[:, wide : wide + 128]
    is_key = lanes_of(low_kv.shape) < HD
    key = jnp.where(is_key, low_kv, pltpu.roll(high_kv, HD, 1))
    adamw_write(outs[4:8], key, *states[3:6])
    value = jnp.where(is_key, pltpu.roll(low_kv, HD, 1), high_kv)
    adamw_write(outs[8:12], value, *states[6:9])
    adamw_write(outs[12:], cat([low[:, wide + 128 :], high[:, wide + 128 :]], 0), *states[9:])


def adamw_attn(x, pair, states):
    flat = [array for triple in states for array in triple]
    outs = [triple[0] for triple in states for _ in range(4)]
    result = pl.pallas_call(
        adamw_attn_kernel,
        grid=(1,),
        in_specs=[pl.BlockSpec(memory_space=pltpu.SMEM)]
        + [once(array.shape) for array in [*pair, *flat]],
        out_specs=[once(array.shape) for array in outs],
        out_shape=[jax.ShapeDtypeStruct(array.shape, F32) for array in outs],
        compiler_params=pltpu.CompilerParams(vmem_limit_bytes=60 * MIB),
        cost_estimate=SMALL,
        name="adamw_attn",
    )(x.astype(jnp.int32).reshape(1), *pair, *flat)
    return [result[4 * i : 4 * i + 4] for i in range(4)]


def finish_kernel(
    place_ref, back_ref, inputs_ref, scale_ref, gain_ref, res_grad_ref, residual_ref, stays_ref,
    first_ref, second_ref, out_ref, in_grad_ref,
):
    back = norm_back(
        back_ref[...].astype(F32), inputs_ref[...].astype(F32), scale_ref[...], gain_ref[...]
    )
    in_grad = res_grad_ref[...] + back
    summed = add(stays_ref[...], first_ref[0], second_ref[...])
    out = (residual_ref[...] + summed).astype(LOW)
    quarter = out.shape[1] // 4
    for k in range(4):
        there = pl.ds(pl.multiple_of((place_ref[0] ^ k) * quarter, quarter), quarter)
        out_ref[:, there] = out[:, k * quarter : (k + 1) * quarter]
        in_grad_ref[:, there] = in_grad[:, k * quarter : (k + 1) * quarter]


def finish(place, back, inputs, scale, gain, res_grad, residual, stays, first, second):
    arrays = [back, inputs, scale, gain[None, :], res_grad, residual, stays, first, second]
    return pl.pallas_call(
        finish_kernel,
        grid=(1,),
        in_specs=[pl.BlockSpec(memory_space=pltpu.SMEM)] + [once(a.shape) for a in arrays],
        out_specs=[once(inputs.shape)] * 2,
        out_shape=[
            jax.ShapeDtypeStruct(inputs.shape, LOW),
            jax.ShapeDtypeStruct(inputs.shape, F32),
        ],
        compiler_params=pltpu.CompilerParams(vmem_limit_bytes=60 * MIB),
        cost_estimate=SMALL,
        name="finish",
    )(place.astype(jnp.int32).reshape(1), *arrays)


def pick(index, low, high):
    return jnp.where(index == 0, low, high)


class Plane:
    def __init__(self, tp):
        self.tp, self.half = tp, tp // 2
        self.x = lax.axis_index("di")
        self.y = lax.axis_index("tp") // self.half
        self.core = lax.axis_index("tp") % 2
        self.place = self.x * 2 + self.y
        self.axes = ("di", "tp")

    def pairs(self, first):
        def other(index):
            x, t = divmod(index, self.tp)
            along_x = (t % 2 == 0) == first
            return (1 - x) * self.tp + t if along_x else x * self.tp + (t + self.half) % self.tp

        return [(index, other(index)) for index in range(2 * self.tp)]

    def swap_first(self, value):
        return lax.ppermute(value, self.axes, self.pairs(True))

    def swap_second(self, value):
        return lax.ppermute(value, self.axes, self.pairs(False))

    def swap_core(self, value):
        return lax.ppermute(value, "tp", [(i, i ^ 1) for i in range(self.tp)])

    def first_step(self):
        return jnp.where(self.core == 0, 2, 1)

    def at(self, blocks, step):
        return lax.dynamic_index_in_dim(blocks, self.place ^ step, 0, keepdims=False)


def on_device(
    sizes,
    layer_input, out_grad, segment_ids, positions,
    w_query, w_key, w_value, w_out, w_gate, w_up, w_down,
    m_query, m_key, m_value, m_out, m_gate, m_up, m_down,
    v_query, v_key, v_value, v_out, v_gate, v_up, v_down,
    gain_attn, gain_ffn, m_gain_attn, m_gain_ffn, v_gain_attn, v_gain_ffn,
):
    width = layer_input.shape[1]
    plan = Plan(sizes["do"], w_query.shape[0])
    by_x = plan.by_x
    axes = ("di", "tp")
    plane = Plane(sizes["tp"])
    plane_sizes = (("tp", sizes["tp"]), ("di", sizes["di"]))

    gain_one, gain_two = plan.reorder(gain_attn), plan.reorder(gain_ffn)
    inputs_low = plan.reorder(layer_input)
    inputs_f = inputs_low.astype(F32)
    grad_low = plan.reorder(out_grad)
    normed, scale_one = norm_rows(inputs_f, gain_one)
    normed_all = lax.all_gather(normed.astype(LOW), axes, axis=0, tiled=True)

    marks = cat([segment_ids[None, :], positions[None, :]], 0)
    marks_other = lax.ppermute(marks, "di", PAIR)
    marks_all = cat([by_x(marks, marks_other), by_x(marks_other, marks)], 1)
    seg_all, pos_all = marks_all[0], marks_all[1]
    rows = seg_all.shape[0]
    seqs = rows // LEN
    seg_col, seg_row = seg_all.reshape(rows, 1), seg_all.reshape(seqs, 1, LEN)
    cosine, sine = rope_tables(pos_all)

    def col_halves(weight):
        half = weight.shape[1] // 2
        low = weight.astype(LOW)
        return by_x(low[:, :half], low[:, half:]), by_x(low[:, half:], low[:, :half])

    def row_halves(weight):
        half = weight.shape[0] // 2
        low = weight.astype(LOW)
        return by_x(low[:half], low[half:]), by_x(low[half:], low[:half])

    def col_cut(pair, chunk):
        size = pair[0].shape[1] // CHUNKS
        return tuple(part[:, chunk * size : (chunk + 1) * size] for part in pair)

    def row_cut(pair, chunk):
        size = pair[0].shape[0] // CHUNKS
        return tuple(part[chunk * size : (chunk + 1) * size] for part in pair)

    halves_q, halves_k, halves_v = col_halves(w_query), col_halves(w_key), col_halves(w_value)
    qkv_parts = tuple(cat([q, k, v], 1) for q, k, v in zip(halves_q, halves_k, halves_v))
    out_parts = row_halves(w_out)
    halves_g, halves_u, halves_d = col_halves(w_gate), col_halves(w_up), row_halves(w_down)

    def ffn_parts(chunk):
        gate_up = tuple(
            cat([g, u], 1) for g, u in zip(col_cut(halves_g, chunk), col_cut(halves_u, chunk))
        )
        return gate_up, row_cut(halves_d, chunk)

    hidden = halves_d[0].shape[0] // CHUNKS
    attn_shapes = (width, qkv_parts[0].shape[1]), (out_parts[0].shape[0], width)
    ffn_shapes = (width, 2 * hidden), (hidden, width)
    own_rows = layer_input.shape[0]
    core = lax.axis_index("tp") % 2

    if plan.line:
        attn_own, attn_other = plan.pack(qkv_parts, out_parts)
        own_1, other_1 = plan.pack(*ffn_parts(0))
        own_2, other_2 = plan.pack(*ffn_parts(1))
        attn_theirs = plan.swap(attn_other)
        attn_theirs, marks_all, own_1, other_1 = fence(attn_theirs, marks_all, own_1, other_1)
        attn_block = plan.join(attn_own, attn_theirs)
        near, across = line_near(attn_block)
        theirs_1 = plan.swap(other_1)
        near, across, cosine, sine, own_2, other_2 = fence(
            near, across, cosine, sine, own_2, other_2
        )
        across_near, out = line_far(near, across)
        out, across_near, theirs_1 = fence(out, across_near, theirs_1)
        out_near = line_last(across_near)
        block_1 = plan.join(own_1, theirs_1)
        out_near, block_1, grad_low, other_2, seg_col, seg_row = fence(
            out_near, block_1, grad_low, other_2, seg_col, seg_row
        )
        attn_weights = (attn_block, near, across_near, out, across, (out_near,))
        near_1, across_1 = line_near(block_1)
    else:
        attn_weights = plan.plain_gather(qkv_parts, out_parts)
        first_weights = plan.plain_gather(*ffn_parts(0))
        second_weights = plan.plain_gather(*ffn_parts(1))
    attn_loader = Loader(plan, attn_weights, *attn_shapes)

    attn_part, ctx, queries, both, lse, wout = attn_forward(
        attn_loader, normed_all, cosine, sine, seg_col, seg_row
    )
    grad_second = plane.swap_second(grad_low)
    if plan.line:
        theirs_2 = plan.swap(other_2)
        attn_part, near_1, across_1, grad_second, theirs_2, grad_low = fence(
            attn_part, near_1, across_1, grad_second, theirs_2, grad_low
        )
        across_near_1, out_1 = line_far(near_1, across_1)
    grad_first = plane.swap_first(grad_low)
    attn_sum = lax.psum_scatter(attn_part, axes, scatter_dimension=0, tiled=True)
    grad_xy = plane.swap_first(grad_second)
    if plan.line:
        out_1, across_near_1, grad_xy, theirs_2, grad_first = fence(
            out_1, across_near_1, grad_xy, theirs_2, grad_first
        )
        block_2 = plan.join(own_2, theirs_2)
        out_near_1 = line_last(across_near_1)
    grad_x = pick(core, grad_first, grad_second)
    grad_y = pick(core, grad_second, grad_first)
    over_y = cat([pick(plane.y, grad_low, grad_y), pick(plane.y, grad_y, grad_low)], 0)
    over_xy = cat([pick(plane.y, grad_x, grad_xy), pick(plane.y, grad_xy, grad_x)], 0)
    grad_core = cat([by_x(over_y, over_xy), by_x(over_xy, over_y)], 0)
    if plan.line:
        attn_sum, out_near_1, grad_core, block_2 = fence(
            attn_sum, out_near_1, grad_core, block_2
        )
    grad_other = plane.swap_core(grad_core)
    groups = (rows // own_rows // 2, 1, own_rows, width)
    mine, theirs = grad_core.reshape(groups), grad_other.reshape(groups)
    grad_all = cat([pick(core, mine, theirs), pick(core, theirs, mine)], 1).reshape(rows, width)
    residual = inputs_f + attn_sum.astype(F32)
    normed_two, scale_two = norm_rows(residual, gain_two)
    two_low = normed_two.astype(LOW)
    two_all = lax.all_gather(two_low, axes, axis=0, tiled=True)

    if plan.line:
        first_weights = (block_1, near_1, across_near_1, out_1, across_1, (out_near_1,))
        block_2, _ = fence(block_2, two_low)
        near_2, across_2 = line_near(block_2)
        near_2, across_2, wout, grad_all = fence(near_2, across_2, wout, grad_all)
        across_near_2, out_2 = line_far(near_2, across_2)
    wout_all = lax.all_gather(wout, axes, axis=0, tiled=True)
    first = Loader(plan, first_weights, *ffn_shapes)
    back_1, act_1, both_1, down_1 = ffn_main(first, two_all, grad_all, None)
    if plan.line:
        back_1, act_1, both_1, out_2, across_near_2 = fence(
            back_1, act_1, both_1, out_2, across_near_2
        )
        out_near_2 = line_last(across_near_2, OUTWARD)
        *last_1, third_1 = ffn_weights(plan, two_all, grad_all, act_1, both_1, (3, 2))
        last_1, both_1 = fence(last_1, both_1)
        far_1 = [lax.ppermute(part, "do", INWARD) for part in last_1]
        (rest_1,) = ffn_weights(plan, two_all, grad_all, act_1, both_1, (0, 1))
        back_1, rest_1, out_near_2 = fence(back_1, rest_1, out_near_2)
        second_weights = (block_2, near_2, across_near_2, out_2, across_2, (out_near_2,))
    else:
        grads_1 = ffn_weights(plan, two_all, grad_all, act_1, both_1, (0, 1, 2, 3))
    second = Loader(plan, second_weights, *ffn_shapes)
    back_2, act_2, both_2, down_2 = ffn_main(second, two_all, grad_all, back_1)
    if plan.line:
        back_2, act_2, both_2, far_1, wout_all, act_1 = fence(
            back_2, act_2, both_2, far_1, wout_all, act_1
        )
        block = plan.block
        crossed_1, inward_1 = sum_middle([None, None, third_1], far_1)
    back_sum = lax.psum_scatter(back_2, axes, scatter_dimension=0, tiled=True)
    order = (3, 0, 1, 2) if plan.line else (0, 1, 2, 3)
    grads_2 = ffn_weights(plan, two_all, grad_all, act_2, both_2, order)
    if plan.line:
        *last_2, rest_2 = grads_2
        act_2, rest_2, inward_1, crossed_1, last_2 = fence(
            act_2, rest_2, inward_1, crossed_1, last_2
        )
        grads_1 = [rest_1[:block], rest_1[block:], third_1, cat(last_1, 0)]
        grads_2 = [rest_2[:block], rest_2[block : 2 * block], rest_2[2 * block :], cat(last_2, 0)]
        far_low = lax.ppermute(last_2[0], "do", NEAR)
    out_part, gain_two_part = ffn_out(act_1, act_2, down_1, down_2, back_2, two_all)
    if plan.line:
        out_part, far_low, last_high = fence(out_part, far_low, last_2[1])
        far_high = lax.ppermute(last_high, "do", NEAR)

    if plan.line:
        back_sum, out_part = fence(back_sum, out_part)

    residual_grad, res_low, ctx_grad = residual_backward(
        back_sum, residual, scale_two, gain_two, grad_low, wout_all
    )
    if plan.line:
        ctx_grad, res_low, far_high = fence(ctx_grad, res_low, far_high)
        second = add_inner(grads_2[2], cat([far_low, far_high], 0)).astype(LOW)
        first_1, third_1 = sum_near_parts(grads_1, crossed_1, inward_1)
        ctx_grad, near_both, across_both = fence(
            ctx_grad, cat([second, first_1], 0), cat([second, third_1], 0)
        )
        near_both = lax.ppermute(near_both, "do", NEAR)
        across_both = lax.ppermute(across_both, "do", MIDDLE)
    ctx_grad = lax.all_to_all(ctx_grad, axes, split_axis=1, concat_axis=0, tiled=True)
    if plan.line:
        ctx_grad, res_low, out_part = fence(ctx_grad, res_low, out_part)

    out_shape = (rows // own_rows // 2, 2, own_rows, width)
    parts = out_part.reshape(out_shape)
    mine, theirs = pick(core, parts[:, 0], parts[:, 1]), pick(core, parts[:, 1], parts[:, 0])
    summed = add(mine, plane.swap_core(theirs)).astype(LOW)
    step = plane.first_step()
    goes = jnp.stack([plane.at(summed, step), plane.at(summed, 3)])
    goes_on, stays = plane.at(summed, 3 - step), plane.at(summed, 0)
    if plan.line:
        ctx_grad, goes, goes_on, stays = fence(ctx_grad, goes, goes_on, stays)
    arrives = plane.swap_first(goes)
    res_all = lax.all_gather(res_low, axes, axis=0, tiled=True)
    back_one_part, gain_one_part, *grads_qkv = attn_backward(
        attn_loader, ctx_grad, normed_all, queries, both, lse, cosine, sine, seg_col, seg_row
    )
    if plan.line:
        gain_parts = jnp.stack([gain_one_part[0] / gain_one, gain_two_part[0] / gain_two])
        gain_sums = sum_over(plan.reorder(gain_parts), plane_sizes + (("do", sizes["do"]),))
        back_one_part, grads_qkv, res_all, gain_sums, arrives, near_both, across_both = fence(
            back_one_part, grads_qkv, res_all, gain_sums, arrives, near_both, across_both
        )
        crossed_2, inward_2 = across_both[:block], near_both[:block]
        near_sum_1, across_sum_1 = near_both[block:], across_both[block:]
    else:
        gain_parts = jnp.stack([gain_one_part[0] / gain_one, gain_two_part[0] / gain_two])
        gain_sums = sum_over(gain_parts, (("do", sizes["do"]),) + plane_sizes)
    back_one = lax.psum_scatter(back_one_part, axes, scatter_dimension=0, tiled=True)
    grads_attn = out_weights(plan, ctx, res_all, grads_qkv)
    if plan.line:
        half = plan.rows

        def trade(total):
            return plan.trade(total[:half], total[half:])

        near_sum_2, across_sum_2 = sum_near_send(*sum_near_parts(grads_2, crossed_2, inward_2))
        ffn_pair_1 = trade(sum_own(grads_1, near_sum_1, across_sum_1))
        near_sum_2, across_sum_2, grads_attn = fence(near_sum_2, across_sum_2, grads_attn)
        own_attn, to_near, to_cross, to_mirror, kept = grads_attn
        from_near = lax.ppermute(to_near, "do", NEAR)
        direct = [lax.ppermute(to_cross, "do", CROSS), lax.ppermute(to_mirror, "do", MIRROR)]
        ffn_pair_2 = trade(sum_own(grads_2, near_sum_2, across_sum_2))
    second = plane.swap_second(add(goes_on, arrives[1]).astype(LOW))
    place = lax.axis_index("do") if plan.line else jnp.zeros((), jnp.int32)
    states = {
        "attn": [
            (w_query, m_query, v_query), (w_key, m_key, v_key),
            (w_value, m_value, v_value), (w_out, m_out, v_out),
        ],
        "ffn": [(w_gate, m_gate, v_gate), (w_up, m_up, v_up), (w_down, m_down, v_down)],
    }
    if plan.line:
        from_near, ffn_pair_1, ffn_pair_2 = fence(from_near, ffn_pair_1, ffn_pair_2)
        passed = add(kept, from_near[2 * half :]).astype(LOW)
        direct.append(lax.ppermute(passed, "do", MIRROR))
        ffn_updated = adamw_ffn(lax.axis_index("di"), ffn_pair_1, ffn_pair_2, states["ffn"])
        direct, ffn_updated, second, back_one = fence(direct, ffn_updated, second, back_one)
        low = add(own_attn[:half], from_near[:half], direct[0], direct[1])
        high = add(own_attn[half:], from_near[half : 2 * half], direct[2])
        attn_pair = plan.trade(low, high)
        attn_updated = adamw_attn(lax.axis_index("di"), attn_pair, states["attn"])
    else:

        def join(pair, axis):
            own, other = pair[0], pair[1].astype(F32)
            return by_x(cat([own, other], axis), cat([other, own], axis))

        def from_chunks(pairs, axis):
            return join([cat([pair[i] for pair in pairs], axis) for i in range(2)], axis)

        def cut(pair, start, stop):
            return tuple(part[:, start:stop] for part in pair)

        def update(grad, state):
            return (grad, *adamw_update(state[0], grad, *state[1:], WEIGHT_DECAY, LEARN_RATE))

        qkv_pair = plan.plain_sum_row(grads_qkv[0])
        out_pair = plan.plain_sum_col(grads_attn[0])
        ffn_pairs = [
            (plan.plain_sum_row(row), plan.plain_sum_col(col)) for row, col in (grads_1, grads_2)
        ]
        at_k = halves_q[0].shape[1]
        at_v = at_k + halves_k[0].shape[1]
        end = at_v + halves_v[0].shape[1]
        attn_grads = [
            join(cut(qkv_pair, 0, at_k), 1),
            join(cut(qkv_pair, at_k, at_v), 1),
            join(cut(qkv_pair, at_v, end), 1),
            join(out_pair, 0),
        ]
        ffn_grads = [
            from_chunks([cut(row, 0, hidden) for row, _ in ffn_pairs], 1),
            from_chunks([cut(row, hidden, 2 * hidden) for row, _ in ffn_pairs], 1),
            from_chunks([col for _, col in ffn_pairs], 0),
        ]
        attn_updated = [update(g, s) for g, s in zip(attn_grads, states["attn"])]
        ffn_updated = [update(g, s) for g, s in zip(ffn_grads, states["ffn"])]
    out_value, in_grad = finish(
        place, back_one, inputs_low, scale_one, gain_one, residual_grad, residual, stays, arrives,
        second,
    )
    grad_gain_attn, grad_gain_ffn = gain_sums[0], gain_sums[1]
    updated = attn_updated + ffn_updated
    gain_updated = [
        adamw_update(gain_attn, grad_gain_attn, m_gain_attn, v_gain_attn, 0.0, GAIN_RATE),
        adamw_update(gain_ffn, grad_gain_ffn, m_gain_ffn, v_gain_ffn, 0.0, GAIN_RATE),
    ]
    return (
        out_value,
        in_grad,
        *[u[0] for u in updated],
        *[u[1] for u in updated],
        *[u[2] for u in updated],
        *[u[3] for u in updated],
        grad_gain_attn,
        grad_gain_ffn,
        *[u[0] for u in gain_updated],
        *[u[1] for u in gain_updated],
        *[u[2] for u in gain_updated],
    )


def solution(mesh):
    dp, tp = mesh.shape["dp"], mesh.shape["tp"]
    split = Mesh(mesh.devices.reshape(dp // 2, 2, tp), ("do", "di", "tp"))
    sizes = {"do": dp // 2, "di": 2, "tp": tp}
    dp_axes = ("do", "di")
    tokens = P(("do", "di", "tp"), None)
    by_rows, by_cols = P(dp_axes, "tp"), P("tp", dp_axes)
    weights = (by_rows, by_rows, by_rows, by_cols, by_rows, by_rows, by_cols)
    gains = (P(),) * 6
    in_specs = (tokens, tokens, P(dp_axes), P(dp_axes)) + weights * 3 + gains
    out_specs = (tokens, tokens) + weights * 4 + (P(),) * 2 + gains
    return jax.shard_map(
        functools.partial(on_device, sizes),
        mesh=split,
        in_specs=in_specs,
        out_specs=out_specs,
        check_vma=False,
    )
```

```python
import functools

import jax
import jax.numpy as jnp
from jax import lax
from jax.experimental import pallas as pl
from jax.experimental.pallas import tpu as pltpu
from jax.sharding import Mesh
from jax.sharding import PartitionSpec as P

HD = 64
LEN = 512
STEP = 5
CHUNKS = 2

NORM_EPS = 1e-05
ROPE_BASE = 500000.0
BETA_ONE = 0.9
BETA_TWO = 0.95
LEARN_RATE = 0.02
GAIN_RATE = 0.5
WEIGHT_DECAY = 0.1
ADAM_EPS = 1e-08

LOW = jnp.bfloat16
F32 = jnp.float32
MIB = 1024 * 1024

NEAR = [(0, 1), (1, 0), (2, 3), (3, 2)]
MIDDLE = [(1, 2), (2, 1)]
CROSS = [(0, 2), (1, 3), (2, 0), (3, 1)]
MIRROR = [(0, 3), (1, 2), (2, 1), (3, 0)]
OUTWARD = [(1, 0), (2, 3)]
INWARD = [(0, 1), (3, 2)]
PAIR = [(0, 1), (1, 0)]


def dot(lhs, rhs, lhs_dim, rhs_dim):
    return lax.dot_general(
        lhs, rhs, (((lhs_dim,), (rhs_dim,)), ((), ())), preferred_element_type=F32
    )


def cat(parts, axis):
    return jnp.concatenate(parts, axis)


def fence(*values):
    return lax.optimization_barrier(values)


def line_near(own):
    return lax.ppermute(own, "do", NEAR), lax.ppermute(own, "do", MIDDLE)


def line_far(near, across):
    out = lax.ppermute(across, "do", NEAR)
    return lax.ppermute(near, "do", MIDDLE), out


def line_last(across_near, perm=NEAR):
    return lax.ppermute(across_near, "do", perm)


def add(part, *arrived):
    total = part.astype(F32)
    for piece in arrived:
        total = total + piece.astype(F32)
    return total


def is_inner():
    place = lax.axis_index("do")
    return (place == 1) | (place == 2)


def add_inner(part, arrived):
    return add(part, jnp.where(is_inner(), arrived, jnp.zeros_like(arrived)))


def sum_middle(parts, far):
    second = add_inner(parts[2], cat(far, 0)).astype(LOW)
    inward = lax.ppermute(second, "do", NEAR)
    return lax.ppermute(second, "do", MIDDLE), inward


def sum_near_parts(parts, crossed, inward):
    return add_inner(parts[1], crossed).astype(LOW), add_inner(parts[3], inward).astype(LOW)


def sum_near_send(first, third):
    return lax.ppermute(first, "do", NEAR), lax.ppermute(third, "do", MIDDLE)


def sum_own(parts, from_near, from_across):
    return add_inner(parts[0], from_across) + from_near.astype(F32)


class Plan:
    def __init__(self, outer, per_device):
        self.rows = per_device
        self.block = 2 * per_device
        self.line = outer == 4 and per_device == 256
        self.cuts = 4 if self.line else 1

    def reorder(self, values):
        if not self.line:
            return values
        place = lax.axis_index("do")
        quarter = values.shape[-1] // 4
        a, b, c, d = (values[..., i * quarter : (i + 1) * quarter] for i in range(4))
        values = jnp.where(place % 2 == 1, cat([b, a, d, c], -1), values)
        half = 2 * quarter
        turned = cat([values[..., half:], values[..., :half]], -1)
        return jnp.where(place >= 2, turned, values)

    def by_x(self, low, high):
        return jnp.where(lax.axis_index("di") == 0, low, high)

    def inner(self):
        return is_inner().astype(jnp.int32).reshape(1)

    def pack(self, row_part, col_part):
        rows, packs = self.rows, []
        for row_side, side in zip(row_part, col_part):
            pieces = [side[i : i + rows] for i in range(0, side.shape[0], rows)]
            packs.append(cat([row_side] + pieces, 1))
        return packs

    def swap(self, other):
        return lax.ppermute(other, "di", PAIR)

    def join(self, own, theirs, axis=0):
        return cat([self.by_x(own, theirs), self.by_x(theirs, own)], axis)

    def plain_gather(self, row_part, col_part):
        full = []
        for (own, other), axis in ((row_part, 0), (col_part, 1)):
            block = self.join(own, self.swap(other), axis)
            full.append(lax.all_gather(block, "do", axis=axis, tiled=True))
        return tuple(full)

    def unpack(self, pair, wide):
        cuts = range(wide, pair[0].shape[1], self.rows)
        return (
            tuple(side[:, :wide] for side in pair),
            tuple(cat([side[:, i : i + self.rows] for i in cuts], 0) for side in pair),
        )

    def plain_sum_row(self, grad):
        total = lax.psum_scatter(grad, "do", scatter_dimension=0, tiled=True)
        return self.trade(total[: self.rows], total[self.rows :])

    def plain_sum_col(self, grad):
        total = lax.psum_scatter(grad, "do", scatter_dimension=1, tiled=True)
        return self.trade(total[:, : self.rows], total[:, self.rows :])

    def trade(self, low, high):
        theirs = lax.ppermute(self.by_x(high, low).astype(LOW), "di", PAIR)
        return self.by_x(low, high).astype(F32), theirs


ANY = pl.BlockSpec(memory_space=pl.ANY)
SMALL = pl.CostEstimate(flops=1, bytes_accessed=1, transcendentals=0)


class Loader:
    def __init__(self, plan, weights, row_shape, col_shape):
        self.plan, self.row_shape, self.col_shape = plan, row_shape, col_shape
        rows, wide = plan.rows, row_shape[1]
        self.moves = []
        if plan.line:
            *whole, last = weights
            self.operands = [plan.inner(), *whole, *last]
            for k in range(4):
                for x in range(2):
                    at = k * plan.block + x * rows
                    self.moves.append((k, x, 0, 0, (at, 0), wide))
                    for i in range(0, col_shape[0], rows):
                        self.moves.append((k, x, 1, wide + i, (i, at), rows))
        else:
            self.operands = list(weights)
            self.moves = [None, None]
        self.count = len(self.operands)

    def specs(self):
        if not self.plan.line:
            return [ANY] * 2
        return [pl.BlockSpec(memory_space=pltpu.SMEM)] + [ANY] * (self.count - 1)

    def scratch(self):
        return [
            pltpu.VMEM(self.row_shape, LOW),
            pltpu.VMEM(self.col_shape, LOW),
            pltpu.SemaphoreType.DMA((len(self.moves),)),
        ]

    def load(self, refs, row_ref, col_ref, sems):
        if not self.plan.line:
            pairs = zip(refs, (row_ref, col_ref))
            made = [pltpu.make_async_copy(*pair, sems.at[i]) for i, pair in enumerate(pairs)]
            for copy in made:
                copy.start()
            for copy in made:
                copy.wait()
            return
        rows = self.plan.rows

        def copies(sources):
            made = []
            for i, (k, x, which, column, there, wide) in enumerate(self.moves):
                if sources[k] is None:
                    continue
                if isinstance(sources[k], tuple):
                    source, row = sources[k][x], 0
                else:
                    source, row = sources[k], x * rows
                target = (row_ref, col_ref)[which]
                made.append(
                    pltpu.make_async_copy(
                        source.at[pl.ds(row, rows), pl.ds(column, wide)],
                        target.at[pl.ds(there[0], rows), pl.ds(there[1], wide)],
                        sems.at[i],
                    )
                )
            return made

        inner, own, near, across_near, out, across, *last = refs
        out_near = tuple(last) if len(last) == 2 else last[0]
        is_inner = inner[0] == 1
        for copy in copies((own, near, None, None)):
            copy.start()

        @pl.when(is_inner)
        def _():
            for copy in copies((None, None, across_near, across)):
                copy.start()

        @pl.when(jnp.logical_not(is_inner))
        def _():
            for copy in copies((None, None, out, out_near)):
                copy.start()

        for copy in copies((own, near, out, out_near)):
            copy.wait()


def rope_tables(positions):
    half_dim = HD // 2
    inverse_freq = ROPE_BASE ** (-2.0 * jnp.arange(half_dim, dtype=F32) / HD)
    angles = positions.astype(F32)[:, None] * inverse_freq[None, :]
    cosine, sine = jnp.cos(angles), jnp.sin(angles)
    return cat([cosine] * 4, 1), cat([-sine, sine] * 2, 1)


def lanes_of(shape):
    return lax.broadcasted_iota(jnp.int32, shape, 1)


def shuffle_halves(values):
    wide = values.shape[1]
    up = pltpu.roll(values, wide - HD // 2, 1)
    down = pltpu.roll(values, HD // 2, 1)
    return jnp.where(lanes_of(values.shape) % HD < HD // 2, up, down)


def tables(cos_ref, sin_ref, pairs):
    cosine, sine = cos_ref[...], sin_ref[...]
    is_key = lanes_of(cosine.shape) < HD
    return (
        cat([cosine] * pairs + [jnp.where(is_key, cosine, 1.0)], 1),
        cat([sine] * pairs + [jnp.where(is_key, sine, 0.0)], 1),
    )


def split_kv(both):
    is_key = lanes_of(both.shape) < HD
    blank = jnp.zeros_like(both)
    key_low = jnp.where(is_key, both, blank)
    value_high = jnp.where(is_key, blank, both)
    return (
        (key_low, pltpu.roll(key_low.astype(F32), HD, 1).astype(LOW)),
        (pltpu.roll(value_high.astype(F32), HD, 1).astype(LOW), value_high),
    )


def allowed_pairs(seg_col, seg_row):
    shape = (seg_col.shape[0], seg_row.shape[1])
    key_at = lax.broadcasted_iota(jnp.int32, shape, 1)
    query_at = lax.broadcasted_iota(jnp.int32, shape, 0)
    return (seg_col == seg_row) & (key_at <= query_at)


def attn_forward_kernel(pairs, loader, *refs):
    weights, refs = refs[: loader.count], refs[loader.count :]
    x_ref, cos_ref, sin_ref, col_ref, row_ref = refs[:5]
    part_ref, ctx_ref, q_ref, kv_ref, lse_ref, wout_ref, wqkv_ref, _, sems = refs[5:]

    @pl.when(pl.program_id(0) == 0)
    def _():
        loader.load(weights, wqkv_ref, wout_ref, sems)

    cosine, sine = tables(cos_ref, sin_ref, pairs)
    qkv = dot(x_ref[...], wqkv_ref[...], 1, 0)
    rotated = (qkv * cosine + shuffle_halves(qkv) * sine).astype(LOW)
    queries, both = rotated[:, : pairs * 128], rotated[:, pairs * 128 :]
    q_ref[...] = queries
    kv_ref[...] = both
    keys, values = split_kv(both)
    allowed = allowed_pairs(col_ref[...], row_ref[0])
    lane = lanes_of((both.shape[0], 128))
    log_sums = [jnp.zeros((both.shape[0] // 2, 128), F32)] * 2
    contexts = []
    half = both.shape[0] // 2
    for pair in range(pairs):
        bands = []
        for low, high in ((0, half), (half, 2 * half)):
            heads = queries[low:high, pair * 128 : (pair + 1) * 128]
            context = None
            for side in range(2):
                scores = dot(heads, keys[side][:high], 1, 1) * HD**-0.5
                masked = jnp.where(allowed[low:high, :high], scores, -1e30)
                top = jnp.max(masked, axis=1, keepdims=True)
                weights = jnp.exp(masked - top)
                totals = jnp.sum(weights, axis=1, keepdims=True)
                probs = (weights * (1.0 / totals)).astype(LOW)
                piece = dot(probs, values[side][:high], 1, 0)
                context = piece if context is None else context + piece
                at = 2 * pair + side
                log_sums[low // half] = jnp.where(
                    lane[:half] == at, top + jnp.log(totals), log_sums[low // half]
                )
            bands.append(context.astype(LOW))
        contexts.append(cat(bands, 0))
    lse_ref[...] = cat(log_sums, 0)
    context_low = cat(contexts, 1)
    ctx_ref[...] = context_low
    part_ref[...] = dot(context_low, wout_ref[...], 1, 0).astype(LOW)


def attn_backward_kernel(pairs, loader, *refs):
    weights, refs = refs[: loader.count], refs[loader.count :]
    cg_ref, x_ref, q_ref, kv_ref, lse_ref, cos_ref, sin_ref, col_ref, row_ref = refs[:9]
    part_ref, gain_ref, *grad_refs = refs[9:-4]
    wqkv_ref, wout_ref, sems, acc_qkv = refs[-4:]
    step = pl.program_id(0)

    @pl.when(step == 0)
    def _():
        loader.load(weights, wqkv_ref, wout_ref, sems)
        acc_qkv[...] = jnp.zeros_like(acc_qkv)
        gain_ref[...] = jnp.zeros_like(gain_ref)

    cosine, sine = tables(cos_ref, sin_ref, pairs)
    scale = HD**-0.5
    ctx_grad = cg_ref[...]
    keys, values = split_kv(kv_ref[...])
    allowed = allowed_pairs(col_ref[...], row_ref[0])
    lane = lanes_of((ctx_grad.shape[0], 128))
    log_sums = lse_ref[...]
    query_grads, key_grad, value_grad = [], None, None
    for pair in range(pairs):
        heads = q_ref[:, pair * 128 : (pair + 1) * 128]
        grads = ctx_grad[:, pair * 128 : (pair + 1) * 128]
        query_grad = None
        for side in range(2):
            here = (lane < HD) if side == 0 else (lane >= HD)
            head = jnp.where(here, heads, jnp.zeros_like(heads))
            grad = jnp.where(here, grads, jnp.zeros_like(grads))
            at = 2 * pair + side
            scores = dot(heads, keys[side], 1, 1) * scale
            probs = jnp.where(allowed, jnp.exp(scores - log_sums[:, at : at + 1]), 0.0)
            prob_grad = dot(grads, values[side], 1, 1)
            delta = jnp.sum(probs * prob_grad, axis=1, keepdims=True)
            score_grad = (probs * (prob_grad - delta)).astype(LOW)
            to_value = dot(probs.astype(LOW), grad, 0, 0)
            to_key = dot(score_grad, head, 0, 0)
            to_query = dot(score_grad, keys[side], 1, 0)
            value_grad = to_value if value_grad is None else value_grad + to_value
            key_grad = to_key if key_grad is None else key_grad + to_key
            query_grad = to_query if query_grad is None else query_grad + to_query
        query_grads.append(query_grad * scale)
    key_grad = (key_grad + pltpu.roll(key_grad, HD, 1)) * scale
    value_grad = value_grad + pltpu.roll(value_grad, HD, 1)
    joined = cat(query_grads + [jnp.where(lane < HD, key_grad, value_grad)], 1)
    low = (joined * cosine - shuffle_halves(joined) * sine).astype(LOW)
    part = dot(low, wqkv_ref[...], 1, 1)
    part_ref[...] = part.astype(LOW)
    gain_ref[...] += jnp.sum(part * x_ref[...].astype(F32), axis=0, keepdims=True)
    acc_qkv[...] += dot(x_ref[...], low, 0, 0)

    @pl.when(step == pl.num_programs(0) - 1)
    def _():
        cut = acc_qkv.shape[0] // len(grad_refs)
        for i, out in enumerate(grad_refs):
            out[...] = acc_qkv[i * cut : (i + 1) * cut, :].astype(LOW)


def once(shape):
    return pl.BlockSpec(shape, lambda i: (0,) * len(shape), pipeline_mode=pl.Buffered(1))


def per_seq(shape):
    return pl.BlockSpec(shape, lambda i: (i,) + (0,) * (len(shape) - 1))


def attn_forward(loader, normed, cosine, sine, seg_col, seg_row):
    rows, width = normed.shape
    heads = loader.col_shape[0]
    return pl.pallas_call(
        functools.partial(attn_forward_kernel, heads // 128, loader),
        grid=(rows // LEN,),
        in_specs=[
            *loader.specs(),
            per_seq((LEN, width)),
            per_seq((LEN, 128)),
            per_seq((LEN, 128)),
            per_seq((LEN, 1)),
            per_seq((1, 1, LEN)),
        ],
        out_specs=[
            per_seq((LEN, width)),
            per_seq((LEN, heads)),
            per_seq((LEN, heads)),
            per_seq((LEN, 128)),
            per_seq((LEN, 128)),
            once(loader.col_shape),
        ],
        out_shape=[
            jax.ShapeDtypeStruct((rows, width), LOW),
            jax.ShapeDtypeStruct((rows, heads), LOW),
            jax.ShapeDtypeStruct((rows, heads), LOW),
            jax.ShapeDtypeStruct((rows, 128), LOW),
            jax.ShapeDtypeStruct((rows, 128), F32),
            jax.ShapeDtypeStruct(loader.col_shape, LOW),
        ],
        scratch_shapes=loader.scratch(),
        compiler_params=pltpu.CompilerParams(vmem_limit_bytes=60 * MIB),
        cost_estimate=SMALL,
        name="attn_forward",
    )(*loader.operands, normed, cosine, sine, seg_col, seg_row)


def attn_backward(loader, ctx_grad, normed, queries, both, lse, cosine, sine, seg_col, seg_row):
    rows, width = normed.shape
    heads = loader.col_shape[0]
    cuts = loader.plan.cuts
    grad = (width // cuts, loader.row_shape[1])
    return pl.pallas_call(
        functools.partial(attn_backward_kernel, heads // 128, loader),
        grid=(rows // LEN,),
        in_specs=[
            *loader.specs(),
            per_seq((LEN, heads)),
            per_seq((LEN, width)),
            per_seq((LEN, heads)),
            per_seq((LEN, 128)),
            per_seq((LEN, 128)),
            per_seq((LEN, 128)),
            per_seq((LEN, 128)),
            per_seq((LEN, 1)),
            per_seq((1, 1, LEN)),
        ],
        out_specs=[per_seq((LEN, width)), once((1, width))] + [once(grad)] * cuts,
        out_shape=[
            jax.ShapeDtypeStruct((rows, width), LOW),
            jax.ShapeDtypeStruct((1, width), F32),
        ]
        + [jax.ShapeDtypeStruct(grad, LOW)] * cuts,
        scratch_shapes=[*loader.scratch(), pltpu.VMEM(loader.row_shape, F32)],
        compiler_params=pltpu.CompilerParams(vmem_limit_bytes=60 * MIB),
        cost_estimate=SMALL,
        name="attn_backward",
    )(*loader.operands, ctx_grad, normed, queries, both, lse, cosine, sine, seg_col, seg_row)


PACKS = (
    ((0, 0), (0, 1)),
    ((1, 0), (1, 1), (2, 1)),
    ((2, 0),),
    ((3, 0),),
    ((3, 1),),
)


def out_weights_kernel(plan, ctx_ref, res_ref, *refs):
    count = plan.cuts * plan.line
    qkv_refs, grad_refs, acc = refs[:count], refs[count:-1], refs[-1]
    step = pl.program_id(0)

    @pl.when(step == 0)
    def _():
        acc[...] = jnp.zeros_like(acc)

    acc[...] += dot(ctx_ref[...], res_ref[...], 0, 0)

    @pl.when(step == pl.num_programs(0) - 1)
    def _():
        if not plan.line:
            grad_refs[0][...] = acc[...].astype(LOW)
            return
        rows = plan.rows
        for out, halves in zip(grad_refs, PACKS):
            for i, (k, x) in enumerate(halves):
                wide = qkv_refs[k].shape[1]
                here, at = slice(i * rows, (i + 1) * rows), k * plan.block + x * rows
                out[here, :wide] = qkv_refs[k][x * rows : (x + 1) * rows, :]
                out[here, wide:] = acc[:, at : at + rows].astype(LOW)


def out_weights(plan, ctx, res_all, grads_qkv):
    rows, width = res_all.shape
    heads = ctx.shape[1]
    extra = list(grads_qkv) if plan.line else []
    shapes = [(heads, width)]
    if plan.line:
        shapes = [(len(halves) * plan.rows, extra[0].shape[1] + heads) for halves in PACKS]
    return pl.pallas_call(
        functools.partial(out_weights_kernel, plan),
        grid=(rows // LEN,),
        in_specs=[per_seq((LEN, heads)), per_seq((LEN, width))] + [once(g.shape) for g in extra],
        out_specs=[once(shape) for shape in shapes],
        out_shape=[jax.ShapeDtypeStruct(shape, LOW) for shape in shapes],
        scratch_shapes=[pltpu.VMEM((heads, width), F32)],
        compiler_params=pltpu.CompilerParams(vmem_limit_bytes=40 * MIB),
        cost_estimate=SMALL,
        name="out_weights",
    )(ctx, res_all, *extra)


def residual_backward_kernel(
    back_ref, residual_ref, scale_ref, gain_ref, grad_ref, wout_ref, res_grad_ref, low_ref, ctx_ref
):
    @pl.when(pl.program_id(0) == 0)
    def _():
        back = norm_back(
            back_ref[...].astype(F32), residual_ref[...], scale_ref[...], gain_ref[...]
        )
        total = grad_ref[...].astype(F32) + back
        res_grad_ref[...] = total
        low_ref[...] = total.astype(LOW)

    ctx_ref[...] = dot(low_ref[...], wout_ref[...], 1, 1).astype(LOW)


def residual_backward(back_sum, residual, scale, gain, grad_low, wout_all):
    rows, width = residual.shape
    heads = wout_all.shape[0]
    step = 512
    return pl.pallas_call(
        residual_backward_kernel,
        grid=(heads // step,),
        in_specs=[
            once((rows, width)),
            once((rows, width)),
            once((rows, 1)),
            once((1, width)),
            once((rows, width)),
            per_seq((step, width)),
        ],
        out_specs=[
            once((rows, width)),
            once((rows, width)),
            pl.BlockSpec((rows, step), lambda i: (0, i)),
        ],
        out_shape=[
            jax.ShapeDtypeStruct((rows, width), F32),
            jax.ShapeDtypeStruct((rows, width), LOW),
            jax.ShapeDtypeStruct((rows, heads), LOW),
        ],
        compiler_params=pltpu.CompilerParams(vmem_limit_bytes=60 * MIB),
        cost_estimate=SMALL,
        name="residual_backward",
    )(back_sum, residual, scale, gain[None, :], grad_low, wout_all)


TILE = 512


def ffn_main_kernel(loader, more, *refs):
    weights, refs = refs[: loader.count], refs[loader.count :]
    x_ref, grad_ref = refs[:2]
    back_ref, act_ref, both_ref, down_ref, gate_up_ref, _, sems = refs[2 + more :]

    @pl.when(pl.program_id(0) == 0)
    def _():
        loader.load(weights, gate_up_ref, down_ref, sems)

    hidden = down_ref.shape[0]
    pre = dot(x_ref[...], gate_up_ref[...], 1, 0)
    gate_pre, lifted = pre[:, :hidden], pre[:, hidden:]
    sigmoid_gate = jax.nn.sigmoid(gate_pre)
    silu_gate = gate_pre * sigmoid_gate
    act_ref[...] = (silu_gate * lifted).astype(LOW)
    act_grad = dot(grad_ref[...], down_ref[...], 1, 1)
    gate_grad = act_grad * lifted * sigmoid_gate * (1.0 + gate_pre * (1.0 - sigmoid_gate))
    both_grad = cat([gate_grad.astype(LOW), (act_grad * silu_gate).astype(LOW)], 1)
    both_ref[...] = both_grad
    back = dot(both_grad, gate_up_ref[...], 1, 1)
    if more:
        back = back + refs[2][...].astype(F32)
    back_ref[...] = back.astype(LOW)


def ffn_main(loader, tokens, grads, earlier):
    rows, width = tokens.shape
    hidden = loader.col_shape[0]
    more = [] if earlier is None else [earlier]
    return pl.pallas_call(
        functools.partial(ffn_main_kernel, loader, len(more)),
        grid=(rows // TILE,),
        in_specs=[
            *loader.specs(),
            per_seq((TILE, width)),
            per_seq((TILE, width)),
            *[per_seq((TILE, width))] * len(more),
        ],
        out_specs=[
            per_seq((TILE, width)),
            per_seq((TILE, hidden)),
            per_seq((TILE, 2 * hidden)),
            once(loader.col_shape),
        ],
        out_shape=[
            jax.ShapeDtypeStruct((rows, width), LOW),
            jax.ShapeDtypeStruct((rows, hidden), LOW),
            jax.ShapeDtypeStruct((rows, 2 * hidden), LOW),
            jax.ShapeDtypeStruct(loader.col_shape, LOW),
        ],
        scratch_shapes=loader.scratch(),
        compiler_params=pltpu.CompilerParams(vmem_limit_bytes=60 * MIB),
        cost_estimate=SMALL,
        name="ffn_main",
    )(*loader.operands, tokens, grads, *more)


def ffn_weights_kernel(plan, x_ref, grad_ref, act_ref, both_ref, *out_refs):
    row = dot(x_ref[...], both_ref[...], 0, 0).astype(LOW)
    col = dot(act_ref[...], grad_ref[...], 0, 0).astype(LOW)
    if not plan.line:
        out_refs[0][...], out_refs[1][...] = row, col
        return
    rows, wide = plan.rows, row.shape[1]

    def pack(halves):
        for x, (out, at) in enumerate(halves):
            out[at : at + rows, :wide] = row[x * rows : (x + 1) * rows]
            for i in range(0, col.shape[0], rows):
                out[at : at + rows, wide + i : wide + i + rows] = col[
                    i : i + rows, x * rows : (x + 1) * rows
                ]

    if len(out_refs) == 1:
        pack([(out_refs[0], 0), (out_refs[0], rows)])
        return

    @pl.when(pl.program_id(0) == 0)
    def _():
        pack([(out_refs[0], 0), (out_refs[1], 0)])

    @pl.when(pl.program_id(0) > 0)
    def _():
        pack([(out_refs[2], 0), (out_refs[2], rows)])


def ffn_weights(plan, tokens, grads, act, both_grad, order):
    rows, width = tokens.shape
    block = width // 4
    wide, hidden = both_grad.shape[1], act.shape[1]
    count, begin = len(order), order[0]
    step = order[1] - order[0] if begin < 3 else (order[1] - 3) % 4
    assert all(order[i] == (begin + step * i) % 4 for i in range(count))

    def columns():
        return pl.BlockSpec((rows, block), lambda i: (0, (begin + step * i) % 4))

    if not plan.line:
        out_specs = [
            pl.BlockSpec((block, wide), lambda i: ((begin + step * i) % 4, 0)),
            pl.BlockSpec((hidden, block), lambda i: (0, (begin + step * i) % 4)),
        ]
        shapes = [(count * block, wide), (hidden, count * block)]
    elif begin == 3:
        out_specs = [once((plan.rows, wide + hidden))] * 2 + [
            pl.BlockSpec((block, wide + hidden), lambda i: (jnp.maximum(i - 1, 0), 0))
        ]
        shapes = [(plan.rows, wide + hidden)] * 2 + [((count - 1) * block, wide + hidden)]
    else:
        out_specs = [pl.BlockSpec((block, wide + hidden), lambda i: (i, 0))]
        shapes = [(count * block, wide + hidden)]
    return pl.pallas_call(
        functools.partial(ffn_weights_kernel, plan),
        grid=(count,),
        in_specs=[columns(), columns(), once(act.shape), once(both_grad.shape)],
        out_specs=out_specs,
        out_shape=[jax.ShapeDtypeStruct(shape, LOW) for shape in shapes],
        compiler_params=pltpu.CompilerParams(vmem_limit_bytes=60 * MIB),
        cost_estimate=SMALL,
        name="ffn_weights",
    )(tokens, grads, act, both_grad)


def ffn_out_kernel(act_1, act_2, down_1, down_2, back_ref, x_ref, out_ref, gain_ref):
    @pl.when(pl.program_id(0) == 0)
    def _():
        gain_ref[...] = jnp.zeros_like(gain_ref)

    out = dot(act_1[...], down_1[...], 1, 0) + dot(act_2[...], down_2[...], 1, 0)
    out_ref[...] = out.astype(LOW)
    product = back_ref[...].astype(F32) * x_ref[...].astype(F32)
    gain_ref[...] += jnp.sum(product, axis=0, keepdims=True)


def ffn_out(act_1, act_2, down_1, down_2, back, tokens):
    rows, width = tokens.shape
    hidden = act_1.shape[1]
    return pl.pallas_call(
        ffn_out_kernel,
        grid=(rows // TILE,),
        in_specs=[
            per_seq((TILE, hidden)),
            per_seq((TILE, hidden)),
            once(down_1.shape),
            once(down_2.shape),
            per_seq((TILE, width)),
            per_seq((TILE, width)),
        ],
        out_specs=[per_seq((TILE, width)), once((1, width))],
        out_shape=[
            jax.ShapeDtypeStruct((rows, width), LOW),
            jax.ShapeDtypeStruct((1, width), F32),
        ],
        compiler_params=pltpu.CompilerParams(vmem_limit_bytes=60 * MIB),
        cost_estimate=SMALL,
        name="ffn_out",
    )(act_1, act_2, down_1, down_2, back, tokens)


def norm_rows(values, gain_vec):
    row_scale = lax.rsqrt(jnp.mean(values * values, axis=1, keepdims=True) + NORM_EPS)
    return values * row_scale * gain_vec, row_scale


def norm_back(row_grad, values, row_scale, gain_vec):
    scaled_grad = row_grad * gain_vec
    return row_scale * scaled_grad - values * row_scale**3 * jnp.mean(
        scaled_grad * values, axis=1, keepdims=True
    )


def adamw_update(master, grad_sum, first_mom, second_mom, decay_rate, step_rate):
    next_first = BETA_ONE * first_mom + (1.0 - BETA_ONE) * grad_sum
    next_second = BETA_TWO * second_mom + (1.0 - BETA_TWO) * grad_sum * grad_sum
    first_hat = next_first / (1.0 - BETA_ONE**STEP)
    second_hat = next_second / (1.0 - BETA_TWO**STEP)
    next_master = master - step_rate * (
        first_hat / (jnp.sqrt(second_hat) + ADAM_EPS) + decay_rate * master
    )
    return (next_master, next_first, next_second)


def sum_over(values, sizes):
    for axis, size in sizes:
        step = 1
        while step < size:
            values = values + lax.ppermute(values, axis, [(i, i ^ step) for i in range(size)])
            step *= 2
    return values


def adamw_write(refs, grad, master, first, second):
    refs[0][...] = grad
    refs[1][...], refs[2][...], refs[3][...] = adamw_update(
        master[...], grad, first[...], second[...], WEIGHT_DECAY, LEARN_RATE
    )


def adamw_ffn_kernel(x_ref, mine_1, theirs_1, mine_2, theirs_2, *refs):
    step = pl.program_id(0)
    low_is_own = x_ref[0] == 0
    states, outs = refs[:9], refs[9:]
    rows = states[0].shape[0]
    hidden = states[0].shape[1] // 4
    here = pl.ds(pl.multiple_of(step * rows, rows), rows)
    for i in range(2):
        lanes = slice(i * hidden, (i + 1) * hidden)
        own = cat([mine_1[here, lanes], mine_2[here, lanes]], 1)
        other = cat([theirs_1[here, lanes], theirs_2[here, lanes]], 1).astype(F32)
        low = jnp.where(low_is_own, own, other)
        high = jnp.where(low_is_own, other, own)
        adamw_write(outs[4 * i : 4 * i + 4], cat([low, high], 1), *states[3 * i : 3 * i + 3])
    lanes = slice(2 * hidden, 3 * hidden)
    first = step % 2 == 0
    own = jnp.where(first, mine_1[:, lanes], mine_2[:, lanes])
    other = jnp.where(first, theirs_1[:, lanes], theirs_2[:, lanes]).astype(F32)
    grad = jnp.where(step // 2 == x_ref[0], own, other)
    width = states[6].shape[1]
    grad = cat([grad[:, j : j + width] for j in range(0, hidden, width)], 0)
    adamw_write(outs[8:], grad, *states[6:])


def adamw_ffn(x, pair_1, pair_2, states):
    steps = 4

    def cut(array):
        return pl.BlockSpec((array.shape[0] // steps, array.shape[1]), lambda i: (i, 0))

    packs = [*pair_1, *pair_2]
    flat = [array for triple in states for array in triple]
    outs = [triple[0] for triple in states for _ in range(4)]
    result = pl.pallas_call(
        adamw_ffn_kernel,
        grid=(steps,),
        in_specs=[pl.BlockSpec(memory_space=pltpu.SMEM)]
        + [once(pack.shape) for pack in packs]
        + [cut(array) for array in flat],
        out_specs=[cut(array) for array in outs],
        out_shape=[jax.ShapeDtypeStruct(array.shape, F32) for array in outs],
        compiler_params=pltpu.CompilerParams(vmem_limit_bytes=60 * MIB),
        cost_estimate=SMALL,
        name="adamw_ffn",
    )(x.astype(jnp.int32).reshape(1), *packs, *flat)
    return [result[4 * i : 4 * i + 4] for i in range(3)]


def adamw_attn_kernel(x_ref, mine_ref, theirs_ref, *refs):
    step = pl.program_id(0)
    low_is_own = x_ref[0] == 0
    states, outs = refs[:12], refs[12:]
    rows, wide = states[0].shape[0], states[0].shape[1] // 2
    here = pl.ds(pl.multiple_of(step * rows, rows), rows)
    end = wide + 128
    own, other = mine_ref[here, :end], theirs_ref[here, :end].astype(F32)
    low = jnp.where(low_is_own, own, other)
    high = jnp.where(low_is_own, other, own)
    adamw_write(outs[:4], cat([low[:, :wide], high[:, :wide]], 1), *states[:3])
    low_kv, high_kv = low[:, wide:], high[:, wide:]
    is_key = lanes_of(low_kv.shape) < HD
    key = jnp.where(is_key, low_kv, pltpu.roll(high_kv, HD, 1))
    adamw_write(outs[4:8], key, *states[3:6])
    value = jnp.where(is_key, pltpu.roll(low_kv, HD, 1), high_kv)
    adamw_write(outs[8:12], value, *states[6:9])
    grad = jnp.where(step == x_ref[0], mine_ref[:, end:], theirs_ref[:, end:].astype(F32))
    adamw_write(outs[12:], grad, *states[9:])


def adamw_attn(x, pair, states):
    flat = [array for triple in states for array in triple]
    outs = [triple[0] for triple in states for _ in range(4)]

    def cut(array):
        return per_seq((array.shape[0] // 2, array.shape[1]))

    result = pl.pallas_call(
        adamw_attn_kernel,
        grid=(2,),
        in_specs=[pl.BlockSpec(memory_space=pltpu.SMEM)]
        + [once(array.shape) for array in pair]
        + [cut(array) for array in flat],
        out_specs=[cut(array) for array in outs],
        out_shape=[jax.ShapeDtypeStruct(array.shape, F32) for array in outs],
        compiler_params=pltpu.CompilerParams(vmem_limit_bytes=60 * MIB),
        cost_estimate=SMALL,
        name="adamw_attn",
    )(x.astype(jnp.int32).reshape(1), *pair, *flat)
    return [result[4 * i : 4 * i + 4] for i in range(4)]


def finish_kernel(
    place_ref, back_ref, inputs_ref, scale_ref, gain_ref, res_grad_ref, residual_ref, stays_ref,
    first_ref, second_ref, out_ref, in_grad_ref,
):
    back = norm_back(
        back_ref[...].astype(F32), inputs_ref[...].astype(F32), scale_ref[...], gain_ref[...]
    )
    in_grad = res_grad_ref[...] + back
    summed = add(stays_ref[...], first_ref[0], second_ref[...])
    out = (residual_ref[...] + summed).astype(LOW)
    quarter = out.shape[1] // 4
    for k in range(4):
        there = pl.ds(pl.multiple_of((place_ref[0] ^ k) * quarter, quarter), quarter)
        out_ref[:, there] = out[:, k * quarter : (k + 1) * quarter]
        in_grad_ref[:, there] = in_grad[:, k * quarter : (k + 1) * quarter]


def finish(place, back, inputs, scale, gain, res_grad, residual, stays, first, second):
    arrays = [back, inputs, scale, gain[None, :], res_grad, residual, stays, first, second]
    rows, width = inputs.shape
    cut = per_seq((rows // 4, width))
    specs = [cut, cut, per_seq((rows // 4, 1)), once((1, width)), cut, cut, cut]
    specs += [pl.BlockSpec((1, rows // 4, width), lambda i: (0, i, 0)), cut]
    return pl.pallas_call(
        finish_kernel,
        grid=(4,),
        in_specs=[pl.BlockSpec(memory_space=pltpu.SMEM)] + specs,
        out_specs=[cut] * 2,
        out_shape=[
            jax.ShapeDtypeStruct(inputs.shape, LOW),
            jax.ShapeDtypeStruct(inputs.shape, F32),
        ],
        compiler_params=pltpu.CompilerParams(vmem_limit_bytes=60 * MIB),
        cost_estimate=SMALL,
        name="finish",
    )(place.astype(jnp.int32).reshape(1), *arrays)


def pick(index, low, high):
    return jnp.where(index == 0, low, high)


class Plane:
    def __init__(self, tp):
        self.tp, self.half = tp, tp // 2
        self.x = lax.axis_index("di")
        self.y = lax.axis_index("tp") // self.half
        self.core = lax.axis_index("tp") % 2
        self.place = self.x * 2 + self.y
        self.axes = ("di", "tp")

    def pairs(self, first):
        def other(index):
            x, t = divmod(index, self.tp)
            along_x = (t % 2 == 0) == first
            return (1 - x) * self.tp + t if along_x else x * self.tp + (t + self.half) % self.tp

        return [(index, other(index)) for index in range(2 * self.tp)]

    def swap_first(self, value):
        return lax.ppermute(value, self.axes, self.pairs(True))

    def swap_second(self, value):
        return lax.ppermute(value, self.axes, self.pairs(False))

    def swap_core(self, value):
        return lax.ppermute(value, "tp", [(i, i ^ 1) for i in range(self.tp)])

    def first_step(self):
        return jnp.where(self.core == 0, 2, 1)

    def at(self, blocks, step):
        return lax.dynamic_index_in_dim(blocks, self.place ^ step, 0, keepdims=False)


def on_device(
    sizes,
    layer_input, out_grad, segment_ids, positions,
    w_query, w_key, w_value, w_out, w_gate, w_up, w_down,
    m_query, m_key, m_value, m_out, m_gate, m_up, m_down,
    v_query, v_key, v_value, v_out, v_gate, v_up, v_down,
    gain_attn, gain_ffn, m_gain_attn, m_gain_ffn, v_gain_attn, v_gain_ffn,
):
    width = layer_input.shape[1]
    plan = Plan(sizes["do"], w_query.shape[0])
    by_x = plan.by_x
    axes = ("di", "tp")
    plane = Plane(sizes["tp"])
    plane_sizes = (("tp", sizes["tp"]), ("di", sizes["di"]))

    gain_one, gain_two = plan.reorder(gain_attn), plan.reorder(gain_ffn)
    inputs_low = plan.reorder(layer_input)
    inputs_f = inputs_low.astype(F32)
    grad_low = plan.reorder(out_grad)
    normed, scale_one = norm_rows(inputs_f, gain_one)
    normed_all = lax.all_gather(normed.astype(LOW), axes, axis=0, tiled=True)

    marks = cat([segment_ids[None, :], positions[None, :]], 0)
    marks_other = lax.ppermute(marks, "di", PAIR)
    marks_all = cat([by_x(marks, marks_other), by_x(marks_other, marks)], 1)
    seg_all, pos_all = marks_all[0], marks_all[1]
    rows = seg_all.shape[0]
    seqs = rows // LEN
    seg_col, seg_row = seg_all.reshape(rows, 1), seg_all.reshape(seqs, 1, LEN)
    cosine, sine = rope_tables(pos_all)

    def col_halves(weight):
        half = weight.shape[1] // 2
        low = weight.astype(LOW)
        return by_x(low[:, :half], low[:, half:]), by_x(low[:, half:], low[:, :half])

    def row_halves(weight):
        half = weight.shape[0] // 2
        low = weight.astype(LOW)
        return by_x(low[:half], low[half:]), by_x(low[half:], low[:half])

    def col_cut(pair, chunk):
        size = pair[0].shape[1] // CHUNKS
        return tuple(part[:, chunk * size : (chunk + 1) * size] for part in pair)

    def row_cut(pair, chunk):
        size = pair[0].shape[0] // CHUNKS
        return tuple(part[chunk * size : (chunk + 1) * size] for part in pair)

    halves_q, halves_k, halves_v = col_halves(w_query), col_halves(w_key), col_halves(w_value)
    qkv_parts = tuple(cat([q, k, v], 1) for q, k, v in zip(halves_q, halves_k, halves_v))
    out_parts = row_halves(w_out)
    halves_g, halves_u, halves_d = col_halves(w_gate), col_halves(w_up), row_halves(w_down)

    def ffn_parts(chunk):
        gate_up = tuple(
            cat([g, u], 1) for g, u in zip(col_cut(halves_g, chunk), col_cut(halves_u, chunk))
        )
        return gate_up, row_cut(halves_d, chunk)

    hidden = halves_d[0].shape[0] // CHUNKS
    attn_shapes = (width, qkv_parts[0].shape[1]), (out_parts[0].shape[0], width)
    ffn_shapes = (width, 2 * hidden), (hidden, width)
    own_rows = layer_input.shape[0]
    core = lax.axis_index("tp") % 2

    if plan.line:
        attn_own, attn_other = plan.pack(qkv_parts, out_parts)
        own_1, other_1 = plan.pack(*ffn_parts(0))
        own_2, other_2 = plan.pack(*ffn_parts(1))
        attn_theirs = plan.swap(attn_other)
        attn_theirs, marks_all, own_1, other_1 = fence(attn_theirs, marks_all, own_1, other_1)
        attn_block = plan.join(attn_own, attn_theirs)
        near, across = line_near(attn_block)
        theirs_1 = plan.swap(other_1)
        near, across, cosine, sine, own_2, other_2 = fence(
            near, across, cosine, sine, own_2, other_2
        )
        across_near, out = line_far(near, across)
        out, across_near, theirs_1 = fence(out, across_near, theirs_1)
        out_near = line_last(across_near)
        block_1 = plan.join(own_1, theirs_1)
        out_near, block_1, grad_low, other_2, seg_col, seg_row = fence(
            out_near, block_1, grad_low, other_2, seg_col, seg_row
        )
        attn_weights = (attn_block, near, across_near, out, across, (out_near,))
        near_1, across_1 = line_near(block_1)
    else:
        attn_weights = plan.plain_gather(qkv_parts, out_parts)
        first_weights = plan.plain_gather(*ffn_parts(0))
        second_weights = plan.plain_gather(*ffn_parts(1))
    attn_loader = Loader(plan, attn_weights, *attn_shapes)

    attn_part, ctx, queries, both, lse, wout = attn_forward(
        attn_loader, normed_all, cosine, sine, seg_col, seg_row
    )
    grad_second = plane.swap_second(grad_low)
    if plan.line:
        theirs_2 = plan.swap(other_2)
        attn_part, near_1, across_1, grad_second, theirs_2, grad_low = fence(
            attn_part, near_1, across_1, grad_second, theirs_2, grad_low
        )
        across_near_1, out_1 = line_far(near_1, across_1)
    grad_first = plane.swap_first(grad_low)
    attn_sum = lax.psum_scatter(attn_part, axes, scatter_dimension=0, tiled=True)
    grad_xy = plane.swap_first(grad_second)
    if plan.line:
        out_1, across_near_1, grad_xy, theirs_2, grad_first = fence(
            out_1, across_near_1, grad_xy, theirs_2, grad_first
        )
        block_2 = plan.join(own_2, theirs_2)
        out_near_1 = line_last(across_near_1)
    grad_x = pick(core, grad_first, grad_second)
    grad_y = pick(core, grad_second, grad_first)
    over_y = cat([pick(plane.y, grad_low, grad_y), pick(plane.y, grad_y, grad_low)], 0)
    over_xy = cat([pick(plane.y, grad_x, grad_xy), pick(plane.y, grad_xy, grad_x)], 0)
    grad_core = cat([by_x(over_y, over_xy), by_x(over_xy, over_y)], 0)
    if plan.line:
        attn_sum, out_near_1, grad_core, block_2 = fence(
            attn_sum, out_near_1, grad_core, block_2
        )
    grad_other = plane.swap_core(grad_core)
    groups = (rows // own_rows // 2, 1, own_rows, width)
    mine, theirs = grad_core.reshape(groups), grad_other.reshape(groups)
    grad_all = cat([pick(core, mine, theirs), pick(core, theirs, mine)], 1).reshape(rows, width)
    residual = inputs_f + attn_sum.astype(F32)
    normed_two, scale_two = norm_rows(residual, gain_two)
    two_low = normed_two.astype(LOW)
    two_all = lax.all_gather(two_low, axes, axis=0, tiled=True)

    if plan.line:
        first_weights = (block_1, near_1, across_near_1, out_1, across_1, (out_near_1,))
        block_2, _ = fence(block_2, two_low)
        near_2, across_2 = line_near(block_2)
        near_2, across_2, wout, grad_all = fence(near_2, across_2, wout, grad_all)
        across_near_2, out_2 = line_far(near_2, across_2)
    wout_all = lax.all_gather(wout, axes, axis=0, tiled=True)
    first = Loader(plan, first_weights, *ffn_shapes)
    back_1, act_1, both_1, down_1 = ffn_main(first, two_all, grad_all, None)
    if plan.line:
        back_1, act_1, both_1, out_2, across_near_2 = fence(
            back_1, act_1, both_1, out_2, across_near_2
        )
        out_near_2 = line_last(across_near_2, OUTWARD)
        *last_1, third_1 = ffn_weights(plan, two_all, grad_all, act_1, both_1, (3, 2))
        last_1, both_1 = fence(last_1, both_1)
        far_1 = [lax.ppermute(part, "do", INWARD) for part in last_1]
        (rest_1,) = ffn_weights(plan, two_all, grad_all, act_1, both_1, (0, 1))
        back_1, rest_1, out_near_2 = fence(back_1, rest_1, out_near_2)
        second_weights = (block_2, near_2, across_near_2, out_2, across_2, (out_near_2,))
    else:
        grads_1 = ffn_weights(plan, two_all, grad_all, act_1, both_1, (0, 1, 2, 3))
    second = Loader(plan, second_weights, *ffn_shapes)
    back_2, act_2, both_2, down_2 = ffn_main(second, two_all, grad_all, back_1)
    if plan.line:
        back_2, act_2, both_2, far_1, wout_all, act_1 = fence(
            back_2, act_2, both_2, far_1, wout_all, act_1
        )
        block = plan.block
        crossed_1, inward_1 = sum_middle([None, None, third_1], far_1)
    back_sum = lax.psum_scatter(back_2, axes, scatter_dimension=0, tiled=True)
    order = (3, 0, 1, 2) if plan.line else (0, 1, 2, 3)
    grads_2 = ffn_weights(plan, two_all, grad_all, act_2, both_2, order)
    if plan.line:
        *last_2, rest_2 = grads_2
        act_2, rest_2, inward_1, crossed_1, last_2 = fence(
            act_2, rest_2, inward_1, crossed_1, last_2
        )
        grads_1 = [rest_1[:block], rest_1[block:], third_1, cat(last_1, 0)]
        grads_2 = [rest_2[:block], rest_2[block : 2 * block], rest_2[2 * block :], cat(last_2, 0)]
        far_low = lax.ppermute(last_2[0], "do", NEAR)
    out_part, gain_two_part = ffn_out(act_1, act_2, down_1, down_2, back_2, two_all)
    if plan.line:
        out_part, far_low, last_high = fence(out_part, far_low, last_2[1])
        far_high = lax.ppermute(last_high, "do", NEAR)

    if plan.line:
        back_sum, out_part = fence(back_sum, out_part)

    residual_grad, res_low, ctx_grad = residual_backward(
        back_sum, residual, scale_two, gain_two, grad_low, wout_all
    )
    if plan.line:
        ctx_grad, res_low, far_high = fence(ctx_grad, res_low, far_high)
        second = add_inner(grads_2[2], cat([far_low, far_high], 0)).astype(LOW)
        first_1, third_1 = sum_near_parts(grads_1, crossed_1, inward_1)
        ctx_grad, near_both, across_both = fence(
            ctx_grad, cat([second, first_1], 0), cat([second, third_1], 0)
        )
        near_both = lax.ppermute(near_both, "do", NEAR)
        across_both = lax.ppermute(across_both, "do", MIDDLE)
    ctx_grad = lax.all_to_all(ctx_grad, axes, split_axis=1, concat_axis=0, tiled=True)
    if plan.line:
        ctx_grad, res_low, out_part = fence(ctx_grad, res_low, out_part)

    out_shape = (rows // own_rows // 2, 2, own_rows, width)
    parts = out_part.reshape(out_shape)
    mine, theirs = pick(core, parts[:, 0], parts[:, 1]), pick(core, parts[:, 1], parts[:, 0])
    summed = add(mine, plane.swap_core(theirs)).astype(LOW)
    step = plane.first_step()
    goes = jnp.stack([plane.at(summed, step), plane.at(summed, 3)])
    goes_on, stays = plane.at(summed, 3 - step), plane.at(summed, 0)
    if plan.line:
        ctx_grad, goes, goes_on, stays = fence(ctx_grad, goes, goes_on, stays)
    arrives = plane.swap_first(goes)
    res_all = lax.all_gather(res_low, axes, axis=0, tiled=True)
    back_one_part, gain_one_part, *grads_qkv = attn_backward(
        attn_loader, ctx_grad, normed_all, queries, both, lse, cosine, sine, seg_col, seg_row
    )
    if plan.line:
        gain_parts = jnp.stack([gain_one_part[0] / gain_one, gain_two_part[0] / gain_two])
        gain_sums = sum_over(plan.reorder(gain_parts), plane_sizes + (("do", sizes["do"]),))
        back_one_part, grads_qkv, res_all, gain_sums, arrives, near_both, across_both = fence(
            back_one_part, grads_qkv, res_all, gain_sums, arrives, near_both, across_both
        )
        crossed_2, inward_2 = across_both[:block], near_both[:block]
        near_sum_1, across_sum_1 = near_both[block:], across_both[block:]
    else:
        gain_parts = jnp.stack([gain_one_part[0] / gain_one, gain_two_part[0] / gain_two])
        gain_sums = sum_over(gain_parts, (("do", sizes["do"]),) + plane_sizes)
    back_one = lax.psum_scatter(back_one_part, axes, scatter_dimension=0, tiled=True)
    grads_attn = out_weights(plan, ctx, res_all, grads_qkv)
    if plan.line:
        half = plan.rows

        def trade(total):
            return plan.trade(total[:half], total[half:])

        near_sum_2, across_sum_2 = sum_near_send(*sum_near_parts(grads_2, crossed_2, inward_2))
        ffn_pair_1 = trade(sum_own(grads_1, near_sum_1, across_sum_1))
        near_sum_2, across_sum_2, grads_attn = fence(near_sum_2, across_sum_2, grads_attn)
        own_attn, to_near, to_cross, to_mirror, kept = grads_attn
        from_near = lax.ppermute(to_near, "do", NEAR)
        direct = [lax.ppermute(to_cross, "do", CROSS), lax.ppermute(to_mirror, "do", MIRROR)]
        ffn_pair_2 = trade(sum_own(grads_2, near_sum_2, across_sum_2))
    second = plane.swap_second(add(goes_on, arrives[1]).astype(LOW))
    place = lax.axis_index("do") if plan.line else jnp.zeros((), jnp.int32)
    states = {
        "attn": [
            (w_query, m_query, v_query), (w_key, m_key, v_key),
            (w_value, m_value, v_value), (w_out, m_out, v_out),
        ],
        "ffn": [(w_gate, m_gate, v_gate), (w_up, m_up, v_up), (w_down, m_down, v_down)],
    }
    if plan.line:
        from_near, ffn_pair_1, ffn_pair_2 = fence(from_near, ffn_pair_1, ffn_pair_2)
        passed = add(kept, from_near[2 * half :]).astype(LOW)
        direct.append(lax.ppermute(passed, "do", MIRROR))
        ffn_updated = adamw_ffn(lax.axis_index("di"), ffn_pair_1, ffn_pair_2, states["ffn"])
        direct, ffn_updated, second, back_one = fence(direct, ffn_updated, second, back_one)
        low = add(own_attn[:half], from_near[:half], direct[0], direct[1])
        high = add(own_attn[half:], from_near[half : 2 * half], direct[2])
        attn_pair = plan.trade(low, high)
        attn_updated = adamw_attn(lax.axis_index("di"), attn_pair, states["attn"])
    else:

        def join(pair, axis):
            own, other = pair[0], pair[1].astype(F32)
            return by_x(cat([own, other], axis), cat([other, own], axis))

        def from_chunks(pairs, axis):
            return join([cat([pair[i] for pair in pairs], axis) for i in range(2)], axis)

        def cut(pair, start, stop):
            return tuple(part[:, start:stop] for part in pair)

        def update(grad, state):
            return (grad, *adamw_update(state[0], grad, *state[1:], WEIGHT_DECAY, LEARN_RATE))

        qkv_pair = plan.plain_sum_row(grads_qkv[0])
        out_pair = plan.plain_sum_col(grads_attn[0])
        ffn_pairs = [
            (plan.plain_sum_row(row), plan.plain_sum_col(col)) for row, col in (grads_1, grads_2)
        ]
        at_k = halves_q[0].shape[1]
        at_v = at_k + halves_k[0].shape[1]
        end = at_v + halves_v[0].shape[1]
        attn_grads = [
            join(cut(qkv_pair, 0, at_k), 1),
            join(cut(qkv_pair, at_k, at_v), 1),
            join(cut(qkv_pair, at_v, end), 1),
            join(out_pair, 0),
        ]
        ffn_grads = [
            from_chunks([cut(row, 0, hidden) for row, _ in ffn_pairs], 1),
            from_chunks([cut(row, hidden, 2 * hidden) for row, _ in ffn_pairs], 1),
            from_chunks([col for _, col in ffn_pairs], 0),
        ]
        attn_updated = [update(g, s) for g, s in zip(attn_grads, states["attn"])]
        ffn_updated = [update(g, s) for g, s in zip(ffn_grads, states["ffn"])]
    out_value, in_grad = finish(
        place, back_one, inputs_low, scale_one, gain_one, residual_grad, residual, stays, arrives,
        second,
    )
    grad_gain_attn, grad_gain_ffn = gain_sums[0], gain_sums[1]
    updated = attn_updated + ffn_updated
    gain_updated = [
        adamw_update(gain_attn, grad_gain_attn, m_gain_attn, v_gain_attn, 0.0, GAIN_RATE),
        adamw_update(gain_ffn, grad_gain_ffn, m_gain_ffn, v_gain_ffn, 0.0, GAIN_RATE),
    ]
    return (
        out_value,
        in_grad,
        *[u[0] for u in updated],
        *[u[1] for u in updated],
        *[u[2] for u in updated],
        *[u[3] for u in updated],
        grad_gain_attn,
        grad_gain_ffn,
        *[u[0] for u in gain_updated],
        *[u[1] for u in gain_updated],
        *[u[2] for u in gain_updated],
    )


def solution(mesh):
    dp, tp = mesh.shape["dp"], mesh.shape["tp"]
    split = Mesh(mesh.devices.reshape(dp // 2, 2, tp), ("do", "di", "tp"))
    sizes = {"do": dp // 2, "di": 2, "tp": tp}
    dp_axes = ("do", "di")
    tokens = P(("do", "di", "tp"), None)
    by_rows, by_cols = P(dp_axes, "tp"), P("tp", dp_axes)
    weights = (by_rows, by_rows, by_rows, by_cols, by_rows, by_rows, by_cols)
    gains = (P(),) * 6
    in_specs = (tokens, tokens, P(dp_axes), P(dp_axes)) + weights * 3 + gains
    out_specs = (tokens, tokens) + weights * 4 + (P(),) * 2 + gains
    return jax.shard_map(
        functools.partial(on_device, sizes),
        mesh=split,
        in_specs=in_specs,
        out_specs=out_specs,
        check_vma=False,
    )
```
